32 devices in a mesh: band: 4 (over y, core), fft: 8 (over z, x).
Axes of the slice: x: 2, y: 2, z: 4, core: 2. Of those that a mesh axis runs over, the one named last changes fastest.
Arguments:
- wave_coeffs: bfloat16 [4, 2, 192, 192, 256], P('band', None, None, 'fft'), may hold values from -4 to 4
- occupation: float32 [4, 2], P('band'), may hold values from 0.05 to 0.2
- potential: bfloat16 [192, 192, 256], P('fft'), may hold values from -1.5 to 1.5
- projectors: bfloat16 [32, 8, 64, 128], P('fft'), may hold values from -0.0625 to 0.0625
- coupling: float32 [8, 8], replicated, may hold values from -4 to 4
- sphere_blocks: int32 [32, 64], replicated, may hold values from 0 to 73727, as said below
Outputs:
- applied: bfloat16 [4, 2, 192, 192, 256], P('band', None, None, 'fft')
- rho: bfloat16 [192, 192, 256], P('fft')
- projections: float32 [4, 32, 2, 8], P('band', 'fft')
The draws below stay inside these ranges and needn't reach their ends.
Inputs may be any that keep to these rules, and one draw needn't show every extreme that they name: `sphere_blocks`: row a holds 64 distinct block numbers. The first-dimension planes of all of them lie among the planes b * 24 - 6 to b * 24 + 29, counted around the periodic grid, with b = a // 4; every row has 16 blocks in the lowest of these planes and 16 in the highest.
All inputs are finite; a program needn't handle non-finite values.
Results may differ from the reference program's by a relative error of at most 0.025.
Values may be sent and summed in bfloat16 or wider, within the bound.
No kernel may reach another device: no remote copies, remote signals or barrier semaphores. Data moves between devices by JAX's collectives and lax.ppermute only.
A program may use at most 128 MiB of HBM per device.

```python
import math
import jax
import jax.numpy as jnp
from jax import lax

NX = 192
NY = 192
NZ = 256
BLOCK = 128
NPROJ = 8
SB = 64
HALO = 6
ATOM_DEV = 4
SLAB = 24
ATOMS = 32
PAIRS = 4


def draw_sphere_blocks(key, part):
    zblocks = NZ // BLOCK
    plane_blocks = NY * zblocks
    ext_planes = SLAB + 2 * HALO
    inner_count = (ext_planes - 2) * plane_blocks
    edge_count = SB // 4

    def one_atom(atom_key, atom_number):
        key_low, key_high, key_rest, key_order = jax.random.split(atom_key, 4)
        lowest = jax.random.permutation(key_low, plane_blocks)[:edge_count]
        highest = (ext_planes - 1) * plane_blocks + jax.random.permutation(key_high, plane_blocks)[:edge_count]
        others = plane_blocks + jax.random.permutation(key_rest, inner_count)[:SB - 2 * edge_count]
        chosen = jnp.concatenate([lowest, highest, others]).astype(jnp.int32)
        chosen = chosen[jax.random.permutation(key_order, SB)]
        ext_plane = chosen // plane_blocks
        within = chosen % plane_blocks
        owner = atom_number // ATOM_DEV
        plane_index = (owner * SLAB - HALO + ext_plane + NX) % NX
        return (plane_index * plane_blocks + within).astype(jnp.int32)
    atom_keys = jax.random.split(key, ATOMS)
    return jax.vmap(one_atom)(atom_keys, jnp.arange(ATOMS, dtype=jnp.int32))


def block_levels(key, dims, shards, smallest, top_value):
    loudness = 1.0
    for position, shards_of in shards:
        steps = jax.random.uniform(jax.random.fold_in(jax.random.fold_in(key, 6), position), (shards_of,), jnp.float32, smallest / len(shards), top_value / len(shards))
        loudness = loudness * jnp.repeat(jnp.exp(steps), dims[position] // shards_of).reshape((-1,) + (1,) * (len(dims) - 1 - position))
    return loudness


def noise(own_key, extent, width, bound, cuts=(), kind=jnp.bfloat16):
    drawn = width * jax.random.normal(own_key, extent, jnp.float32)
    if cuts:
        drawn = drawn * block_levels(own_key, extent, cuts, -0.22, 0.18)
    return jnp.clip(drawn, -bound, bound).astype(kind)


def setup_inputs(seed: int = 0) -> dict:
    keys = jax.random.split(jax.random.key(seed), 7)
    return {
        "wave_coeffs": noise(keys[0], (PAIRS, 2, NX, NY, NZ), 1.0, 4.0, ((0, 4), (3, 8))),
        "occupation": jnp.clip(0.05 + 0.15 * jax.random.uniform(keys[1], (PAIRS, 2), jnp.float32) ** block_levels(keys[1], (PAIRS, 2), ((0, 4),), -0.2, 0.2), 0.05, 0.2),
        "potential": jnp.clip(jax.random.uniform(keys[2], (NX, NY, NZ), jnp.float32, -1.5, 1.5) * block_levels(keys[2], (NX, NY, NZ), ((0, 8),), -0.4, 0.0), -1.5, 1.5).astype(jnp.bfloat16),
        "projectors": noise(keys[3], (ATOMS, NPROJ, SB, BLOCK), (SB * BLOCK) ** -0.5, 0.0625, ((0, 8),)),
        "coupling": noise(keys[4], (NPROJ, NPROJ), 1.0, 4.0, (), jnp.float32),
        "sphere_blocks": draw_sphere_blocks(jax.random.fold_in(keys[6], 71), 0),
    }


def to_complex(pair_values):
    return pair_values[0].astype(jnp.float32) + 1j * pair_values[1].astype(jnp.float32)

def to_pair(values):
    return jnp.stack([jnp.real(values), jnp.imag(values)]).astype(jnp.bfloat16)

def wave_squares(length):
    indices = jnp.arange(length, dtype=jnp.int32)
    frequency = jnp.where(2 * indices < length, indices, indices - length).astype(jnp.float32) / length
    return frequency * frequency

def reference(wave_coeffs, occupation, potential, projectors, coupling, sphere_blocks):
    plane_blocks = NY * (NZ // BLOCK)
    strength = 3.0 * math.sqrt(BLOCK * SB) / NPROJ
    coupled = (coupling + coupling.T) * (0.5 * strength)
    kinetic = wave_squares(NX)[:, None, None] + wave_squares(NY)[None, :, None] + wave_squares(NZ)[None, None, :]
    beta_values = projectors.astype(jnp.float32)
    local_potential = potential.astype(jnp.float32)

    def one_pair(density, inputs):
        coeffs, weights = inputs
        section = to_pair(jnp.fft.ifft(to_complex(coeffs), axis=0, norm='ortho'))
        section = to_pair(jnp.fft.ifft(to_complex(section), axis=1, norm='ortho'))
        wave_field = to_pair(jnp.fft.ifft(to_complex(section), axis=2, norm='ortho'))
        real_part = wave_field[0].astype(jnp.float32)
        imag_part = wave_field[1].astype(jnp.float32)
        density = density + weights[0] * real_part * real_part + weights[1] * imag_part * imag_part
        blocks = wave_field.astype(jnp.float32).reshape(2, NX * plane_blocks, BLOCK)[:, sphere_blocks]
        projected = jnp.einsum('ajsk,bask->abj', beta_values, blocks, precision=lax.Precision.HIGHEST)
        energy = jnp.einsum('ij,abj->abi', coupled, projected, precision=lax.Precision.HIGHEST)
        spread = jnp.einsum('ajsk,abj->bask', beta_values, energy, precision=lax.Precision.HIGHEST)
        nonlocal_term = jnp.zeros((2, NX * plane_blocks, BLOCK), jnp.float32).at[:, sphere_blocks].add(spread)
        nonlocal_term = nonlocal_term.reshape(2, NX, NY, NZ)
        total_field = (local_potential[None] * wave_field.astype(jnp.float32) + nonlocal_term).astype(jnp.bfloat16)
        section = to_pair(jnp.fft.fft(to_complex(total_field), axis=2, norm='ortho'))
        section = to_pair(jnp.fft.fft(to_complex(section), axis=1, norm='ortho'))
        last = jnp.fft.fft(to_complex(section), axis=0, norm='ortho')
        transformed = jnp.stack([jnp.real(last), jnp.imag(last)]).astype(jnp.float32)
        applied = (transformed + kinetic[None] * coeffs.astype(jnp.float32)).astype(jnp.bfloat16)
        return (density, (applied, projected))
    start = jnp.zeros((NX, NY, NZ), jnp.float32)
    density, (applied, projections) = lax.scan(one_pair, start, (wave_coeffs, occupation))
    return (applied, density.astype(jnp.bfloat16), projections)
```

```python
import functools
import math

import jax
import jax.numpy as jnp
import numpy as np
from jax import lax
from jax.experimental import pallas as pl
from jax.experimental.pallas import tpu as pltpu
from jax.sharding import PartitionSpec as P

HALO = 6
EDGE = 8
VMEM_BYTES = 56 * 1024 * 1024


def extended(shard, sides, width):
    for axis, dim in sides:
        count, length = (lax.axis_size(axis), shard.shape[dim])
        up = [(i, (i + 1) % count) for i in range(count)]
        down = [(j, i) for i, j in up]
        last = lax.slice_in_dim(shard, length - width, length, axis=dim)
        first = lax.slice_in_dim(shard, 0, width, axis=dim)
        before = lax.ppermute(last, axis, up)
        after = lax.ppermute(first, axis, down)
        shard = jnp.concatenate([before, shard, after], axis=dim)
    return shard


def dft_table(length, sign_value):
    indices = jnp.arange(length, dtype=jnp.int32)
    phases = indices[:, None] * indices[None, :] % length
    angles = 2.0 * math.pi / length * phases.astype(jnp.float32)
    factor = 1.0 / math.sqrt(length)
    cosine = jnp.cos(angles) * factor
    sine_part = jnp.sin(angles) * (sign_value * factor)
    upper_rows = jnp.stack([cosine, -sine_part])
    bottom = jnp.stack([sine_part, cosine])
    return jnp.stack([upper_rows, bottom]).astype(jnp.bfloat16)


def wave_squares(indices, length):
    frequency = (
        jnp.where(2 * indices < length, indices, indices - length).astype(jnp.float32) / length
    )
    return frequency * frequency


def per_device_plain(wave_coeffs, occupation, potential, projectors, coupling, sphere_blocks):
    pieces = lax.axis_size("fft")
    slab_index = lax.axis_index("fft")
    coeffs = wave_coeffs[0]
    size_x = coeffs.shape[1]
    columns = coeffs.shape[2]
    size_z = coeffs.shape[3]
    slab_planes = potential.shape[0]
    size_y = potential.shape[1]
    atom_dev = projectors.shape[0]
    nproj_count = projectors.shape[1]
    block_cells = projectors.shape[3]
    zblocks = size_z // block_cells
    plane_blocks = size_y * zblocks
    total_atoms = atom_dev * pieces
    table_x = dft_table(size_x, 1.0).transpose(0, 2, 1, 3).reshape(2 * size_x, 2 * size_x)
    inverse_y = dft_table(size_y, 1.0)
    inverse_z = dft_table(size_z, 1.0)
    flattened = coeffs.reshape(2 * size_x, columns * size_z)
    along_x = jnp.dot(table_x, flattened, preferred_element_type=jnp.float32)
    along_x = along_x.reshape(2, size_x, columns, size_z).astype(jnp.bfloat16)
    along_y = jnp.einsum(
        "abyk,bxkz->axyz",
        inverse_y,
        lax.all_to_all(along_x, "fft", split_axis=1, concat_axis=2, tiled=True),
        preferred_element_type=jnp.float32,
    ).astype(jnp.bfloat16)
    wave_field = jnp.einsum(
        "abzk,bxyk->axyz", inverse_z, along_y, preferred_element_type=jnp.float32
    ).astype(jnp.bfloat16)
    weights = occupation[0]
    real_part = wave_field[0].astype(jnp.float32)
    imag_part = wave_field[1].astype(jnp.float32)
    partial_density = weights[0] * real_part * real_part + weights[1] * imag_part * imag_part
    density = lax.psum(partial_density.astype(jnp.bfloat16), "band")
    strength = 3.0 * math.sqrt(block_cells * projectors.shape[2]) / nproj_count
    coupled = (coupling + coupling.T) * (0.5 * strength)
    nearby = extended(projectors, (("fft", 0),), atom_dev)
    atom_rows = (
        slab_index * atom_dev - atom_dev + jnp.arange(3 * atom_dev, dtype=jnp.int32) + total_atoms
    ) % total_atoms
    near_blocks = sphere_blocks[atom_rows]
    plane_index = near_blocks // plane_blocks
    inside = plane_index // slab_planes == slab_index
    local_index = jnp.where(
        inside,
        (plane_index - slab_index * slab_planes) * plane_blocks + near_blocks % plane_blocks,
        0,
    )
    blocks_own = wave_field.reshape(2, slab_planes * plane_blocks, block_cells)
    gathered = blocks_own[:, local_index] * inside[None, :, :, None].astype(jnp.bfloat16)
    partial_value = jnp.einsum(
        "ajsk,bask->abj", nearby, gathered, preferred_element_type=jnp.float32
    )
    summed = extended(partial_value, (("fft", 0),), atom_dev)
    projections_own = (
        summed[:atom_dev] + summed[2 * atom_dev : 3 * atom_dev] + summed[4 * atom_dev :]
    )
    energy_own = jnp.einsum(
        "ij,abj->abi", coupled, projections_own, precision=lax.Precision.HIGHEST
    )
    energy = extended(energy_own, (("fft", 0),), atom_dev)
    spread = jnp.einsum(
        "ajsk,abj->bask", nearby.astype(jnp.float32), energy, precision=lax.Precision.HIGHEST
    )
    spread = spread * inside[None, :, :, None].astype(jnp.float32)
    accumulated = (
        jnp.zeros((2, slab_planes * plane_blocks, block_cells), jnp.float32)
        .at[:, local_index]
        .add(spread)
    )
    nonlocal_term = accumulated.reshape(2, slab_planes, size_y, size_z)
    total_field = (
        potential.astype(jnp.float32)[None] * wave_field.astype(jnp.float32) + nonlocal_term
    ).astype(jnp.bfloat16)
    forward_z = dft_table(size_z, -1.0)
    forward_y = dft_table(size_y, -1.0)
    forward_x = dft_table(size_x, -1.0)
    back_z = jnp.einsum(
        "abzk,bxyk->axyz", forward_z, total_field, preferred_element_type=jnp.float32
    ).astype(jnp.bfloat16)
    back_y = jnp.einsum(
        "abyk,bxkz->axyz", forward_y, back_z, preferred_element_type=jnp.float32
    ).astype(jnp.bfloat16)
    transformed = jnp.einsum(
        "abxk,bkyz->axyz",
        forward_x,
        lax.all_to_all(back_y, "fft", split_axis=2, concat_axis=1, tiled=True),
        preferred_element_type=jnp.float32,
    )
    index_x = jnp.arange(size_x, dtype=jnp.int32)
    index_y = slab_index * columns + jnp.arange(columns, dtype=jnp.int32)
    index_z = jnp.arange(size_z, dtype=jnp.int32)
    kinetic = (
        wave_squares(index_x, size_x)[:, None, None]
        + wave_squares(index_y, size_y)[None, :, None]
        + wave_squares(index_z, size_z)[None, None, :]
    )
    applied = (transformed + kinetic[None] * coeffs.astype(jnp.float32)).astype(jnp.bfloat16)
    return (applied[None], density, projections_own[None])


def real_blocks(length, sign):
    index = np.arange(length)
    angles = 2.0 * np.pi / length * (index[:, None] * index[None, :] % length)
    cosine = np.cos(angles) / np.sqrt(length)
    sine = sign * np.sin(angles) / np.sqrt(length)
    blocks = np.empty((2, length, 2, length))
    blocks[0, :, 0, :] = cosine
    blocks[1, :, 1, :] = cosine
    blocks[0, :, 1, :] = -sine
    blocks[1, :, 0, :] = sine
    return blocks


def chunk_bases(slab_planes):
    inner = range(EDGE, slab_planes - EDGE, EDGE)
    return [0, slab_planes - EDGE] + list(inner)


def params(steps):
    return pltpu.CompilerParams(
        dimension_semantics=("arbitrary",) * steps, vmem_limit_bytes=VMEM_BYTES
    )


def whole(shape):
    return pl.BlockSpec(shape, lambda i: (0,) * len(shape))


SMEM_SPEC = pl.BlockSpec(memory_space=pltpu.SMEM)


def list_kernel(codes_ref, lists_ref, counts_ref, *, step):
    groups, length = codes_ref.shape
    for group in range(groups):

        def body(i, count):
            code = codes_ref[group, i]

            @pl.when(code >= 0)
            def _():
                lists_ref[group, count] = code + i * step

            return count + (code >= 0).astype(jnp.int32)

        counts_ref[group] = lax.fori_loop(0, length, body, jnp.int32(0))


def first_x_kernel(table_ref, coeffs_ref, *refs, chunks, pieces):
    outs, wide = refs[:chunks], refs[chunks]
    parts, size_x, columns, lanes = coeffs_ref.shape
    rows = parts * size_x
    part_rows = rows // chunks

    def widen(k, carry):
        for part in range(parts):
            start = pl.multiple_of((part * size_x + k * 8) * columns, 8)
            wide[pl.ds(start, 8 * columns), :] = (
                coeffs_ref[part, pl.ds(k * 8, 8)].astype(jnp.float32).reshape(8 * columns, lanes)
            )
        return carry

    lax.fori_loop(0, size_x // 8, widen, 0)

    def column_pair(g, carry):
        pair = [
            wide[pl.ds(2 * g + h, rows, stride=columns), :].astype(jnp.bfloat16) for h in range(2)
        ]
        result = jnp.dot(
            table_ref[...], jnp.concatenate(pair, axis=1), preferred_element_type=jnp.float32
        ).astype(jnp.bfloat16)
        for c in range(chunks):
            piece = result[c * part_rows : (c + 1) * part_rows]
            for h in range(2):
                outs[c][:, 2 * g + h] = piece[:, h * lanes : (h + 1) * lanes].reshape(
                    pieces, part_rows // pieces, lanes
                )
        return carry

    lax.fori_loop(0, columns // 2, column_pair, 0)


def first_x(table, coeffs, chunks, pieces):
    _, size_x, columns, size_z = coeffs.shape
    lanes = size_z // 2
    rows = 2 * EDGE
    return pl.pallas_call(
        functools.partial(first_x_kernel, chunks=chunks, pieces=pieces),
        grid=(2,),
        in_specs=[
            whole(table.shape),
            pl.BlockSpec((2, size_x, columns, lanes), lambda i: (0, 0, 0, i)),
        ],
        out_specs=[
            pl.BlockSpec((pieces, columns, rows, lanes), lambda i: (0, 0, 0, i))
            for _ in range(chunks)
        ],
        out_shape=[
            jax.ShapeDtypeStruct((pieces, columns, rows, size_z), jnp.bfloat16)
            for _ in range(chunks)
        ],
        scratch_shapes=[pltpu.VMEM((2 * size_x * columns, lanes), jnp.float32)],
        compiler_params=params(1),
        cost_estimate=pl.CostEstimate(
            flops=8 * size_x * size_x * columns * size_z,
            bytes_accessed=8 * size_x * columns * size_z,
            transcendentals=0,
        ),
        name="first_x",
    )(table, coeffs)


def unpack_entry(value, step, blocks):
    code = lax.rem(value, step)
    entry = lax.div(value, step)
    return code, entry, lax.div(entry, blocks)


def field_kernel(*refs, groups, step, blocks, aliased):
    counts, lists, weights, buf, table_y, table_z = refs[:6]
    projectors = refs[6 : 6 + len(groups)]
    position = 6 + len(groups) + (1 if aliased else 0)
    wave, density = refs[position : position + 2]
    sums = refs[position + 2 : position + 2 + len(groups)]
    wide, field = refs[position + 2 + len(groups) :]
    pieces, columns, rows, size_z = buf.shape
    planes = rows // 2
    size_y = pieces * columns
    step_planes = wave.shape[1]
    i = pl.program_id(0)

    @pl.when(i == 0)
    def _():
        def widen(src, carry):
            start = pl.multiple_of(src * columns * rows, 8)
            values = buf[src].astype(jnp.float32).reshape(columns * rows, size_z)
            for q in range(size_z // 128):
                wide[q, pl.ds(start, columns * rows), :] = values[:, q * 128 : (q + 1) * 128]
            return carry

        lax.fori_loop(0, pieces, widen, 0)

    loaded = []
    for h in range(step_planes):
        plane = i * step_planes + h
        loaded.append(
            jnp.concatenate(
                [
                    jnp.concatenate(
                        [
                            wide[q, pl.ds(part * planes + plane, size_y, stride=rows), :]
                            for q in range(size_z // 128)
                        ],
                        axis=1,
                    ).astype(jnp.bfloat16)
                    for part in range(2)
                ],
                axis=0,
            )
        )
    along_y = jnp.dot(
        table_y[...], jnp.concatenate(loaded, axis=1), preferred_element_type=jnp.float32
    ).astype(jnp.bfloat16)
    turned = jnp.concatenate(
        [
            jnp.concatenate(
                [
                    along_y[:size_y, h * size_z : (h + 1) * size_z],
                    along_y[size_y:, h * size_z : (h + 1) * size_z],
                ],
                axis=1,
            )
            for h in range(step_planes)
        ],
        axis=0,
    )
    result = jnp.dot(turned, table_z[...], preferred_element_type=jnp.float32).astype(jnp.bfloat16)
    lanes = 128
    for h in range(step_planes):
        plane = i * step_planes + h
        total = jnp.zeros((size_y, size_z), jnp.float32)
        for part in range(2):
            values = result[h * size_y : (h + 1) * size_y, part * size_z : (part + 1) * size_z]
            wave[part, h] = values
            values = values.astype(jnp.float32)
            total += weights[0, part] * values * values
            for q in range(size_z // lanes):
                start = pl.multiple_of((q * planes + plane) * size_y, 8)
                field[part, pl.ds(start, size_y), :] = values[:, q * lanes : (q + 1) * lanes]
        density[h] = total.astype(jnp.bfloat16)

    @pl.when(i == pl.num_programs(0) - 1)
    def _():
        for group, projector, total in zip(groups, projectors, sums):
            total[...] = jnp.zeros_like(total)

            def body(k, carry):
                code, entry, atom = unpack_entry(lists[group, k], step, blocks)
                tile = projector[entry]
                for part in range(2):
                    total[atom, part] += tile * field[part, pl.ds(code, 1), :]
                return carry

            lax.fori_loop(0, counts[group], body, 0)


def make_field(counts, lists, weights, buf, table_y, table_z, projectors, groups, step, blocks,
               density, base, slab_planes):
    pieces, columns, rows, size_z = buf.shape
    planes = rows // 2
    size_y = pieces * columns
    pair = 2
    offset = base // pair
    atoms = projectors[0].shape[0] // blocks
    nproj = projectors[0].shape[1]
    aliased = density is not None
    in_specs = [SMEM_SPEC, SMEM_SPEC, SMEM_SPEC, whole(buf.shape), whole(table_y.shape),
                whole(table_z.shape)]
    in_specs += [whole(p.shape) for p in projectors]
    args = [counts, lists, weights, buf, table_y, table_z, *projectors]
    aliases = {}
    if aliased:
        in_specs.append(pl.BlockSpec(memory_space=pl.ANY))
        aliases[len(args)] = 1
        args.append(density)
    return pl.pallas_call(
        functools.partial(field_kernel, groups=groups, step=step, blocks=blocks, aliased=aliased),
        grid=(planes // pair,),
        in_specs=in_specs,
        out_specs=[
            pl.BlockSpec((2, pair, size_y, size_z), lambda i: (0, i, 0, 0)),
            pl.BlockSpec((pair, size_y, size_z), lambda i: (i + offset, 0, 0)),
        ]
        + [whole((atoms, 2, nproj, 128)) for _ in groups],
        out_shape=[
            jax.ShapeDtypeStruct((2, planes, size_y, size_z), jnp.bfloat16),
            jax.ShapeDtypeStruct((slab_planes, size_y, size_z), jnp.bfloat16),
        ]
        + [jax.ShapeDtypeStruct((atoms, 2, nproj, 128), jnp.float32) for _ in groups],
        scratch_shapes=[
            pltpu.VMEM((size_z // 128, size_y * rows, 128), jnp.float32),
            pltpu.VMEM((2, planes * size_y * size_z // 128, 128), jnp.float32),
        ],
        input_output_aliases=aliases,
        compiler_params=params(1),
        cost_estimate=pl.CostEstimate(
            flops=8 * planes * size_y * size_z * (size_y + size_z),
            bytes_accessed=10 * planes * size_y * size_z,
            transcendentals=0,
        ),
        name="make_field",
    )(*args)


def energies_of(coupled, sums, atoms):
    projections, energies = [], []
    for atom in range(atoms):
        for part in range(2):
            tile = sum(s[atom, part] for s in sums)
            mixed = jnp.zeros_like(tile)
            for j in range(tile.shape[0]):
                mixed += coupled[j] * tile[j : j + 1]
            projections.append(jnp.broadcast_to(jnp.sum(tile, -1, keepdims=True), tile.shape))
            energies.append(jnp.broadcast_to(jnp.sum(mixed, -1, keepdims=True), tile.shape))
    return projections, energies


def back_kernel(*refs, groups, step, blocks, partials):
    counts, lists, wave, potential, table_z, table_y = refs[:6]
    position = 6
    projectors = refs[position : position + len(groups)]
    position += len(groups)
    if partials:
        coupled = refs[position]
        sums = refs[position + 1 : position + 1 + partials]
        position += 1 + partials
        out, projections_ref, energies_ref, nonlocal_ref = refs[position:]
        energies = [energies_ref]
    else:
        energies = refs[position : position + len(groups)]
        position += len(groups)
        out, nonlocal_ref = refs[position:]
    pair, size_y, size_z = potential.shape
    pieces, _, rows, _ = out.shape
    lanes = 128
    per_plane = size_y
    chunk_rows = nonlocal_ref.shape[1] // (size_z // lanes)
    i = pl.program_id(0)

    @pl.when(i == 0)
    def _():
        if partials:
            atoms = energies_ref.shape[0]
            projected, mixed = energies_of(coupled, sums, atoms)
            for atom in range(atoms):
                for part in range(2):
                    projections_ref[atom, part] = projected[2 * atom + part]
                    energies_ref[atom, part] = mixed[2 * atom + part]
        nonlocal_ref[...] = jnp.zeros_like(nonlocal_ref)
        for group, projector, energy in zip(groups, projectors, energies):

            def body(k, carry):
                code, entry, atom = unpack_entry(lists[group, k], step, blocks)
                tile = projector[entry]
                for part in range(2):
                    row = jnp.sum(tile * energy[atom, part], axis=0, keepdims=True)
                    nonlocal_ref[part, pl.ds(code, 1), :] += row
                return carry

            lax.fori_loop(0, counts[group], body, 0)

    fields = []
    for h in range(pair):
        local = potential[h].astype(jnp.float32)
        for part in range(2):
            start = pl.multiple_of((i * pair + h) * per_plane, 8)
            extra = jnp.concatenate(
                [
                    nonlocal_ref[part, pl.ds(q * chunk_rows + start, per_plane), :]
                    for q in range(size_z // lanes)
                ],
                axis=1,
            )
            fields.append((local * wave[part, h].astype(jnp.float32) + extra).astype(jnp.bfloat16))
    stacked = jnp.concatenate(
        [jnp.concatenate(fields[2 * h : 2 * h + 2], axis=1) for h in range(pair)], axis=0
    )
    back_z = jnp.dot(stacked, table_z[...], preferred_element_type=jnp.float32).astype(jnp.bfloat16)
    turned = jnp.concatenate(
        [
            jnp.concatenate(
                [
                    back_z[h * size_y : (h + 1) * size_y, :size_z],
                    back_z[h * size_y : (h + 1) * size_y, size_z:],
                ],
                axis=0,
            )
            for h in range(pair)
        ],
        axis=1,
    )
    back_y = jnp.dot(table_y[...], turned, preferred_element_type=jnp.float32).astype(jnp.bfloat16)
    for h in range(pair):
        out[:, h] = back_y[:, h * size_z : (h + 1) * size_z].reshape(pieces, rows, size_z)


def go_back(counts, lists, wave, potential, table_z, table_y, projectors, groups, step, blocks,
            base, pieces, coupled=None, sums=(), energies=()):
    _, planes, size_y, size_z = wave.shape
    rows = 2 * size_y // pieces
    pair = 2
    offset = base // pair
    atoms = projectors[0].shape[0] // blocks
    nproj = projectors[0].shape[1]
    in_specs = [
        SMEM_SPEC,
        SMEM_SPEC,
        pl.BlockSpec((2, pair, size_y, size_z), lambda i: (0, i, 0, 0)),
        pl.BlockSpec((pair, size_y, size_z), lambda i: (i + offset, 0, 0)),
        whole(table_z.shape),
        whole(table_y.shape),
    ]
    in_specs += [whole(p.shape) for p in projectors]
    args = [counts, lists, wave, potential, table_z, table_y, *projectors]
    small = (atoms, 2, nproj, 128)
    out_specs = [pl.BlockSpec((pieces, pair, rows, size_z), lambda i: (0, i, 0, 0))]
    out_shape = [jax.ShapeDtypeStruct((pieces, planes, rows, size_z), jnp.bfloat16)]
    if sums:
        args += [coupled, *sums]
        in_specs += [whole(coupled.shape)] + [whole(s.shape) for s in sums]
        out_specs += [whole(small), whole(small)]
        out_shape += [jax.ShapeDtypeStruct(small, jnp.float32)] * 2
    else:
        args += list(energies)
        in_specs += [whole(e.shape) for e in energies]
    return pl.pallas_call(
        functools.partial(
            back_kernel, groups=groups, step=step, blocks=blocks, partials=len(sums)
        ),
        grid=(planes // pair,),
        in_specs=in_specs,
        out_specs=out_specs,
        out_shape=out_shape,
        scratch_shapes=[pltpu.VMEM((2, planes * size_y * size_z // 128, 128), jnp.float32)],
        compiler_params=params(1),
        cost_estimate=pl.CostEstimate(
            flops=8 * planes * size_y * size_z * (size_y + size_z),
            bytes_accessed=10 * planes * size_y * size_z,
            transcendentals=0,
        ),
        name="go_back",
    )(*args)


def last_x_kernel(frequency_x, frequency_yz, table, coeffs, *refs, chunks):
    bufs = refs[:chunks]
    out, wide, tall = refs[chunks:]
    parts, size_x, columns, lanes = coeffs.shape
    pieces, planes, rows, _ = bufs[0].shape
    block = pieces * planes * rows

    for c in range(chunks):

        def widen(src, carry):
            start = pl.multiple_of(c * block + src * planes * rows, 8)
            wide[pl.ds(start, planes * rows), :] = (
                bufs[c][src].astype(jnp.float32).reshape(planes * rows, lanes)
            )
            return carry

        lax.fori_loop(0, pieces, widen, 0)

    def column_pair(g, carry):
        pair = []
        for h in range(2):
            column = 2 * g + h
            pair.append(
                jnp.concatenate(
                    [
                        wide[
                            pl.ds(c * block + part * columns + column, pieces * planes, stride=rows),
                            :,
                        ].astype(jnp.bfloat16)
                        for c in range(chunks)
                        for part in range(parts)
                    ],
                    axis=0,
                )
            )
        result = jnp.dot(
            table[...], jnp.concatenate(pair, axis=1), preferred_element_type=jnp.float32
        )
        for h in range(2):
            tall[pl.ds(2 * g + h, parts * size_x, stride=columns), :] = result[
                :, h * lanes : (h + 1) * lanes
            ]
        return carry

    lax.fori_loop(0, columns // 2, column_pair, 0)

    def finish(k, carry):
        kinetic = frequency_x[k] + frequency_yz[...]
        for part in range(parts):
            start = pl.multiple_of((part * size_x + k) * columns, 8)
            out[part, k] = (
                tall[pl.ds(start, columns), :] + kinetic * coeffs[part, k].astype(jnp.float32)
            ).astype(jnp.bfloat16)
        return carry

    lax.fori_loop(0, size_x, finish, 0, unroll=4)


def last_x(frequency_x, frequency_yz, table, coeffs, bufs):
    _, size_x, columns, size_z = coeffs.shape
    lanes = size_z // 2
    pieces, planes, rows, _ = bufs[0].shape
    spec = pl.BlockSpec((2, size_x, columns, lanes), lambda i: (0, 0, 0, i))
    return pl.pallas_call(
        functools.partial(last_x_kernel, chunks=len(bufs)),
        grid=(2,),
        in_specs=[
            SMEM_SPEC,
            pl.BlockSpec((columns, lanes), lambda i: (0, i)),
            whole(table.shape),
            spec,
        ]
        + [pl.BlockSpec((pieces, planes, rows, lanes), lambda i: (0, 0, 0, i)) for _ in bufs],
        out_specs=spec,
        out_shape=jax.ShapeDtypeStruct(coeffs.shape, jnp.bfloat16),
        scratch_shapes=[
            pltpu.VMEM((2 * size_x * columns, lanes), jnp.float32),
            pltpu.VMEM((2 * size_x * columns, lanes), jnp.float32),
        ],
        compiler_params=params(1),
        cost_estimate=pl.CostEstimate(
            flops=8 * size_x * size_x * columns * size_z,
            bytes_accessed=12 * size_x * columns * size_z,
            transcendentals=0,
        ),
        name="last_x",
    )(frequency_x, frequency_yz, table, coeffs, *bufs)


def per_device_chunked(wave_coeffs, occupation, potential, projectors, coupling, sphere_blocks):
    pieces = lax.axis_size("fft")
    bands = lax.axis_size("band")
    slab = lax.axis_index("fft")
    coeffs = wave_coeffs[0]
    _, size_x, columns, size_z = coeffs.shape
    slab_planes, size_y, _ = potential.shape
    atom_dev, nproj, blocks, cells = projectors.shape
    zblocks = size_z // cells
    bases = chunk_bases(slab_planes)
    chunks = len(bases)
    up = [(i, (i + 1) % pieces) for i in range(pieces)]
    down = [(j, i) for i, j in up]

    inverse_x, forward_x = (real_blocks(size_x, s) for s in (1.0, -1.0))
    inverse_y, forward_y = (real_blocks(size_y, s) for s in (1.0, -1.0))
    inverse_z, forward_z = (real_blocks(size_z, s) for s in (1.0, -1.0))
    planes_of = np.array(
        [[[d * slab_planes + b + p for p in range(EDGE)] for d in range(pieces)] for b in bases]
    )
    table_x = np.stack([inverse_x[r][planes_of] for r in range(2)], 2)
    table_x = table_x.reshape(2 * size_x, 2 * size_x)
    table_y = inverse_y.reshape(2 * size_y, 2 * size_y)
    table_z = inverse_z.transpose(2, 3, 0, 1).reshape(2 * size_z, 2 * size_z)
    table_back_z = forward_z.transpose(2, 3, 0, 1).reshape(2 * size_z, 2 * size_z)
    table_back_y = forward_y.reshape(2, pieces, columns, 2, size_y).transpose(1, 0, 2, 3, 4)
    table_back_y = table_back_y.reshape(2 * size_y, 2 * size_y)
    table_back_x = np.stack([forward_x[:, :, r][:, :, planes_of] for r in range(2)], 3)
    table_back_x = table_back_x.reshape(2 * size_x, 2 * size_x)
    table_x, table_y, table_z, table_back_z, table_back_y, table_back_x = (
        jnp.asarray(t.astype(jnp.bfloat16))
        for t in (table_x, table_y, table_z, table_back_z, table_back_y, table_back_x)
    )

    sections = first_x(table_x, coeffs, chunks, pieces)

    pairs = []
    for c in range(chunks):
        pairs.append((c, 0))
        if c == 0:
            pairs.append((c, -1))
        if c == 1:
            pairs.append((c, 1))
    group_of = {pair: k for k, pair in enumerate(pairs)}
    codes = []
    for c, shift in pairs:
        owner = (slab + shift + pieces) % pieces
        numbers = lax.dynamic_slice_in_dim(sphere_blocks, owner * atom_dev, atom_dev, 0)
        plane = numbers // (size_y * zblocks) - slab * slab_planes - bases[c]
        rest = numbers % (size_y * zblocks)
        code = (rest % zblocks * EDGE + plane) * size_y + rest // zblocks
        codes.append(jnp.where((plane >= 0) & (plane < EDGE), code, -1).reshape(-1))
    step = zblocks * EDGE * size_y
    lists, counts = pl.pallas_call(
        functools.partial(list_kernel, step=step),
        in_specs=[pl.BlockSpec(memory_space=pltpu.SMEM)],
        out_specs=[pl.BlockSpec(memory_space=pltpu.SMEM)] * 2,
        out_shape=[
            jax.ShapeDtypeStruct((len(pairs), atom_dev * blocks), jnp.int32),
            jax.ShapeDtypeStruct((len(pairs),), jnp.int32),
        ],
        name="block_lists",
    )(jnp.stack(codes))

    turned = projectors.transpose(0, 2, 1, 3)
    share = atom_dev // bands
    mine = lax.dynamic_slice_in_dim(turned, lax.axis_index("band") * share, share, 0)

    def flat(values):
        return values.astype(jnp.float32).reshape(atom_dev * blocks, nproj, cells)

    own = flat(turned)
    previous = flat(lax.all_gather(lax.ppermute(mine, "fft", up), "band", axis=0, tiled=True))
    following = flat(lax.all_gather(lax.ppermute(mine, "fft", down), "band", axis=0, tiled=True))
    near = {0: own, -1: previous, 1: following}

    waves, own_sums, outer = [], [], {}
    density = None
    for c in range(chunks):
        received = lax.all_to_all(sections[c], "fft", 0, 0, tiled=True)
        here = [shift for k, shift in pairs if k == c]
        wave, density, *sums = make_field(
            counts, lists, occupation, received, table_y, table_z, [near[s] for s in here],
            [group_of[c, s] for s in here], step, blocks, density, bases[c], slab_planes,
        )
        waves.append(wave)
        own_sums.append(sums[0])
        if c == 0:
            outer[0] = lax.ppermute(sums[1], "fft", down)
        if c == 1:
            outer[1] = lax.ppermute(sums[1], "fft", up)
    density = lax.psum(density, "band")

    strength = 3.0 * math.sqrt(cells * blocks) / nproj
    coupled = (coupling + coupling.T) * (0.5 * strength)
    coupled = jnp.broadcast_to(coupled.T[:, :, None], (nproj, nproj, 128))

    backs = [None] * chunks
    energy = {}
    for c in list(range(2, chunks)) + [0, 1]:
        here = [shift for k, shift in pairs if k == c]
        arguments = (
            counts, lists, waves[c], potential, table_back_z, table_back_y,
            [near[s] for s in here], [group_of[c, s] for s in here], step, blocks, bases[c], pieces,
        )
        if not energy:
            back, projected, energy[0] = go_back(
                *arguments, coupled=coupled, sums=[*own_sums, outer[0], outer[1]]
            )
            energy[-1] = lax.ppermute(energy[0], "fft", up)
            energy[1] = lax.ppermute(energy[0], "fft", down)
        else:
            (back,) = go_back(*arguments, energies=[energy[s] for s in here])
        backs[c] = lax.all_to_all(back, "fft", 0, 0, tiled=True)

    index_x = np.arange(size_x)
    frequency_x = jnp.asarray(
        (np.where(2 * index_x < size_x, index_x, index_x - size_x) / size_x) ** 2, jnp.float32
    )
    index_y = slab * columns + jnp.arange(columns, dtype=jnp.int32)
    index_z = jnp.arange(size_z, dtype=jnp.int32)
    frequency_yz = wave_squares(index_y, size_y)[:, None] + wave_squares(index_z, size_z)[None, :]
    applied = last_x(frequency_x, frequency_yz, table_back_x, coeffs, backs)
    return (applied[None], density, projected[None, :, :, :, 0])


def per_device(wave_coeffs, occupation, potential, projectors, coupling, sphere_blocks):
    pieces, bands = lax.axis_size("fft"), lax.axis_size("band")
    size_z = wave_coeffs.shape[4]
    columns = wave_coeffs.shape[3]
    slab_planes = potential.shape[0]
    chunked = (
        pieces >= 3
        and slab_planes % EDGE == 0
        and slab_planes >= 3 * EDGE
        and EDGE >= HALO
        and columns % 8 == 0
        and size_z % 256 == 0
        and projectors.shape[0] % bands == 0
        and projectors.shape[3] == 128
        and projectors.shape[1] == 8
    )
    chosen = per_device_chunked if chunked else per_device_plain
    return chosen(wave_coeffs, occupation, potential, projectors, coupling, sphere_blocks)


def solution(mesh):
    placed = (
        P("band", None, None, "fft", None),
        P("band", None),
        P("fft", None, None),
        P("fft", None, None, None),
        P(),
        P(),
    )
    return jax.shard_map(
        per_device,
        mesh=mesh,
        in_specs=placed,
        out_specs=(
            P("band", None, None, "fft", None),
            P("fft", None, None),
            P("band", "fft", None, None),
        ),
        check_vma=False,
    )
```

```python
import functools
import math

import jax
import jax.numpy as jnp
import numpy as np
from jax import lax
from jax.experimental import pallas as pl
from jax.experimental.pallas import tpu as pltpu
from jax.sharding import PartitionSpec as P

HALO = 6
EDGE = 8
PLANES = 4
COLUMNS = 8
VMEM_BYTES = 56 * 1024 * 1024


def extended(shard, sides, width):
    for axis, dim in sides:
        count, length = (lax.axis_size(axis), shard.shape[dim])
        up = [(i, (i + 1) % count) for i in range(count)]
        down = [(j, i) for i, j in up]
        last = lax.slice_in_dim(shard, length - width, length, axis=dim)
        first = lax.slice_in_dim(shard, 0, width, axis=dim)
        before = lax.ppermute(last, axis, up)
        after = lax.ppermute(first, axis, down)
        shard = jnp.concatenate([before, shard, after], axis=dim)
    return shard


def dft_table(length, sign_value):
    indices = jnp.arange(length, dtype=jnp.int32)
    phases = indices[:, None] * indices[None, :] % length
    angles = 2.0 * math.pi / length * phases.astype(jnp.float32)
    factor = 1.0 / math.sqrt(length)
    cosine = jnp.cos(angles) * factor
    sine_part = jnp.sin(angles) * (sign_value * factor)
    upper_rows = jnp.stack([cosine, -sine_part])
    bottom = jnp.stack([sine_part, cosine])
    return jnp.stack([upper_rows, bottom]).astype(jnp.bfloat16)


def wave_squares(indices, length):
    frequency = (
        jnp.where(2 * indices < length, indices, indices - length).astype(jnp.float32) / length
    )
    return frequency * frequency


def per_device_plain(wave_coeffs, occupation, potential, projectors, coupling, sphere_blocks):
    pieces = lax.axis_size("fft")
    slab_index = lax.axis_index("fft")
    coeffs = wave_coeffs[0]
    size_x = coeffs.shape[1]
    columns = coeffs.shape[2]
    size_z = coeffs.shape[3]
    slab_planes = potential.shape[0]
    size_y = potential.shape[1]
    atom_dev = projectors.shape[0]
    nproj_count = projectors.shape[1]
    block_cells = projectors.shape[3]
    zblocks = size_z // block_cells
    plane_blocks = size_y * zblocks
    total_atoms = atom_dev * pieces
    table_x = dft_table(size_x, 1.0).transpose(0, 2, 1, 3).reshape(2 * size_x, 2 * size_x)
    inverse_y = dft_table(size_y, 1.0)
    inverse_z = dft_table(size_z, 1.0)
    flattened = coeffs.reshape(2 * size_x, columns * size_z)
    along_x = jnp.dot(table_x, flattened, preferred_element_type=jnp.float32)
    along_x = along_x.reshape(2, size_x, columns, size_z).astype(jnp.bfloat16)
    along_y = jnp.einsum(
        "abyk,bxkz->axyz",
        inverse_y,
        lax.all_to_all(along_x, "fft", split_axis=1, concat_axis=2, tiled=True),
        preferred_element_type=jnp.float32,
    ).astype(jnp.bfloat16)
    wave_field = jnp.einsum(
        "abzk,bxyk->axyz", inverse_z, along_y, preferred_element_type=jnp.float32
    ).astype(jnp.bfloat16)
    weights = occupation[0]
    real_part = wave_field[0].astype(jnp.float32)
    imag_part = wave_field[1].astype(jnp.float32)
    partial_density = weights[0] * real_part * real_part + weights[1] * imag_part * imag_part
    density = lax.psum(partial_density.astype(jnp.bfloat16), "band")
    strength = 3.0 * math.sqrt(block_cells * projectors.shape[2]) / nproj_count
    coupled = (coupling + coupling.T) * (0.5 * strength)
    nearby = extended(projectors, (("fft", 0),), atom_dev)
    atom_rows = (
        slab_index * atom_dev - atom_dev + jnp.arange(3 * atom_dev, dtype=jnp.int32) + total_atoms
    ) % total_atoms
    near_blocks = sphere_blocks[atom_rows]
    plane_index = near_blocks // plane_blocks
    inside = plane_index // slab_planes == slab_index
    local_index = jnp.where(
        inside,
        (plane_index - slab_index * slab_planes) * plane_blocks + near_blocks % plane_blocks,
        0,
    )
    blocks_own = wave_field.reshape(2, slab_planes * plane_blocks, block_cells)
    gathered = blocks_own[:, local_index] * inside[None, :, :, None].astype(jnp.bfloat16)
    partial_value = jnp.einsum(
        "ajsk,bask->abj", nearby, gathered, preferred_element_type=jnp.float32
    )
    summed = extended(partial_value, (("fft", 0),), atom_dev)
    projections_own = (
        summed[:atom_dev] + summed[2 * atom_dev : 3 * atom_dev] + summed[4 * atom_dev :]
    )
    energy_own = jnp.einsum(
        "ij,abj->abi", coupled, projections_own, precision=lax.Precision.HIGHEST
    )
    energy = extended(energy_own, (("fft", 0),), atom_dev)
    spread = jnp.einsum(
        "ajsk,abj->bask", nearby.astype(jnp.float32), energy, precision=lax.Precision.HIGHEST
    )
    spread = spread * inside[None, :, :, None].astype(jnp.float32)
    accumulated = (
        jnp.zeros((2, slab_planes * plane_blocks, block_cells), jnp.float32)
        .at[:, local_index]
        .add(spread)
    )
    nonlocal_term = accumulated.reshape(2, slab_planes, size_y, size_z)
    total_field = (
        potential.astype(jnp.float32)[None] * wave_field.astype(jnp.float32) + nonlocal_term
    ).astype(jnp.bfloat16)
    forward_z = dft_table(size_z, -1.0)
    forward_y = dft_table(size_y, -1.0)
    forward_x = dft_table(size_x, -1.0)
    back_z = jnp.einsum(
        "abzk,bxyk->axyz", forward_z, total_field, preferred_element_type=jnp.float32
    ).astype(jnp.bfloat16)
    back_y = jnp.einsum(
        "abyk,bxkz->axyz", forward_y, back_z, preferred_element_type=jnp.float32
    ).astype(jnp.bfloat16)
    transformed = jnp.einsum(
        "abxk,bkyz->axyz",
        forward_x,
        lax.all_to_all(back_y, "fft", split_axis=2, concat_axis=1, tiled=True),
        preferred_element_type=jnp.float32,
    )
    index_x = jnp.arange(size_x, dtype=jnp.int32)
    index_y = slab_index * columns + jnp.arange(columns, dtype=jnp.int32)
    index_z = jnp.arange(size_z, dtype=jnp.int32)
    kinetic = (
        wave_squares(index_x, size_x)[:, None, None]
        + wave_squares(index_y, size_y)[None, :, None]
        + wave_squares(index_z, size_z)[None, None, :]
    )
    applied = (transformed + kinetic[None] * coeffs.astype(jnp.float32)).astype(jnp.bfloat16)
    return (applied[None], density, projections_own[None])


def real_blocks(length, sign):
    index = np.arange(length)
    angles = 2.0 * np.pi / length * (index[:, None] * index[None, :] % length)
    cosine = np.cos(angles) / np.sqrt(length)
    sine = sign * np.sin(angles) / np.sqrt(length)
    blocks = np.empty((2, length, 2, length))
    blocks[0, :, 0, :] = cosine
    blocks[1, :, 1, :] = cosine
    blocks[0, :, 1, :] = -sine
    blocks[1, :, 0, :] = sine
    return blocks


def chunk_planes(slab_planes):
    low, high = list(range(EDGE)), list(range(slab_planes - EDGE, slab_planes))
    return [low + high, list(range(EDGE, slab_planes - EDGE))]


def params(steps):
    return pltpu.CompilerParams(
        dimension_semantics=("arbitrary",) * steps, vmem_limit_bytes=VMEM_BYTES
    )


def whole(shape):
    return pl.BlockSpec(shape, lambda i: (0,) * len(shape))


SMEM_SPEC = pl.BlockSpec(memory_space=pltpu.SMEM)


def list_kernel(codes_ref, lists_ref, counts_ref, *, steps):
    groups, length = codes_ref.shape
    for group in range(groups):

        def body(i, count):
            code = codes_ref[group, i]
            lists_ref[group, count] = code + i * steps[group]
            return count + (code >= 0).astype(jnp.int32)

        counts_ref[group] = lax.fori_loop(0, length, body, jnp.int32(0), unroll=4)


def first_x_kernel(table_ref, coeffs_ref, out_ref, wide):
    parts, size_x, columns, lanes = coeffs_ref.shape
    pieces, _, part_rows, _ = out_ref.shape
    rows = parts * size_x

    def widen(k, carry):
        for part in range(parts):
            start = pl.multiple_of((part * size_x + k * 8) * columns, 8)
            wide[pl.ds(start, 8 * columns), :] = (
                coeffs_ref[part, pl.ds(k * 8, 8)].astype(jnp.float32).reshape(8 * columns, lanes)
            )
        return carry

    lax.fori_loop(0, size_x // 8, widen, 0, unroll=2)

    def some_columns(g, carry):
        loaded = [
            wide[pl.ds(COLUMNS * g + h, rows, stride=columns), :].astype(jnp.bfloat16)
            for h in range(COLUMNS)
        ]
        result = jnp.dot(
            table_ref[...], jnp.concatenate(loaded, axis=1), preferred_element_type=jnp.float32
        ).astype(jnp.bfloat16)
        for h in range(COLUMNS):
            out_ref[:, COLUMNS * g + h] = result[:, h * lanes : (h + 1) * lanes].reshape(
                pieces, part_rows, lanes
            )
        return carry

    lax.fori_loop(0, columns // COLUMNS, some_columns, 0)


def first_x(table, coeffs, planes, pieces):
    _, size_x, columns, size_z = coeffs.shape
    lanes = size_z // 2
    return pl.pallas_call(
        first_x_kernel,
        grid=(2,),
        in_specs=[
            whole(table.shape),
            pl.BlockSpec((2, size_x, columns, lanes), lambda i: (0, 0, 0, i)),
        ],
        out_specs=pl.BlockSpec((pieces, columns, 2 * planes, lanes), lambda i: (0, 0, 0, i)),
        out_shape=jax.ShapeDtypeStruct((pieces, columns, 2 * planes, size_z), jnp.bfloat16),
        scratch_shapes=[pltpu.VMEM((2 * size_x * columns, lanes), jnp.float32)],
        compiler_params=params(1),
        cost_estimate=pl.CostEstimate(
            flops=8 * size_x * pieces * planes * columns * size_z,
            bytes_accessed=4 * (size_x + pieces * planes) * columns * size_z,
            transcendentals=0,
        ),
        name="first_x",
    )(table, coeffs)


def unpack_entry(value, step, blocks):
    code = lax.rem(value, step)
    entry = lax.div(value, step)
    return code, entry, lax.div(entry, blocks)


def field_kernel(*refs, groups, step, blocks):
    counts, lists, weights, buf, table_y, table_z = refs[:6]
    projectors = refs[6 : 6 + len(groups)]
    position = 6 + len(groups)
    wave, density = refs[position : position + 2]
    sums = refs[position + 2 : position + 2 + len(groups)]
    wide, field = refs[position + 2 + len(groups) :]
    pieces, columns, rows, size_z = buf.shape
    planes = rows // 2
    size_y = pieces * columns
    step_planes = wave.shape[1]
    i = pl.program_id(0)

    @pl.when(i == 0)
    def _():
        def widen(src, carry):
            start = pl.multiple_of(src * columns * rows, 8)
            values = buf[src].astype(jnp.float32).reshape(columns * rows, size_z)
            for q in range(size_z // 128):
                wide[q, pl.ds(start, columns * rows), :] = values[:, q * 128 : (q + 1) * 128]
            return carry

        lax.fori_loop(0, pieces, widen, 0)

    loaded = []
    for h in range(step_planes):
        plane = i * step_planes + h
        loaded.append(
            jnp.concatenate(
                [
                    jnp.concatenate(
                        [
                            wide[q, pl.ds(part * planes + plane, size_y, stride=rows), :]
                            for q in range(size_z // 128)
                        ],
                        axis=1,
                    ).astype(jnp.bfloat16)
                    for part in range(2)
                ],
                axis=0,
            )
        )
    along_y = jnp.dot(
        table_y[...], jnp.concatenate(loaded, axis=1), preferred_element_type=jnp.float32
    ).astype(jnp.bfloat16)
    turned = jnp.concatenate(
        [
            jnp.concatenate(
                [
                    along_y[:size_y, h * size_z : (h + 1) * size_z],
                    along_y[size_y:, h * size_z : (h + 1) * size_z],
                ],
                axis=1,
            )
            for h in range(step_planes)
        ],
        axis=0,
    )
    result = jnp.dot(turned, table_z[...], preferred_element_type=jnp.float32).astype(jnp.bfloat16)
    lanes = 128
    for h in range(step_planes):
        plane = i * step_planes + h
        total = jnp.zeros((size_y, size_z), jnp.float32)
        for part in range(2):
            values = result[h * size_y : (h + 1) * size_y, part * size_z : (part + 1) * size_z]
            wave[part, h] = values
            values = values.astype(jnp.float32)
            total += weights[0, part] * values * values
            for q in range(size_z // lanes):
                start = pl.multiple_of((q * planes + plane) * size_y, 8)
                field[part, pl.ds(start, size_y), :] = values[:, q * lanes : (q + 1) * lanes]
        density[h] = total.astype(jnp.bfloat16)

    @pl.when(i == pl.num_programs(0) - 1)
    def _():
        for group, projector, total in zip(groups, projectors, sums):
            total[...] = jnp.zeros_like(total)

            def body(k, carry):
                code, entry, atom = unpack_entry(lists[group, k], step, blocks)
                tile = projector[entry]
                for part in range(2):
                    total[atom, part] += tile * field[part, pl.ds(code, 1), :]
                return carry

            lax.fori_loop(0, counts[group], body, 0)


def make_field(counts, lists, weights, buf, table_y, table_z, projectors, groups, step, blocks):
    pieces, columns, rows, size_z = buf.shape
    planes = rows // 2
    size_y = pieces * columns
    atoms = projectors[0].shape[0] // blocks
    nproj = projectors[0].shape[1]
    in_specs = [SMEM_SPEC, SMEM_SPEC, SMEM_SPEC, whole(buf.shape), whole(table_y.shape),
                whole(table_z.shape)]
    in_specs += [whole(p.shape) for p in projectors]
    return pl.pallas_call(
        functools.partial(field_kernel, groups=groups, step=step, blocks=blocks),
        grid=(planes // PLANES,),
        in_specs=in_specs,
        out_specs=[
            pl.BlockSpec((2, PLANES, size_y, size_z), lambda i: (0, i, 0, 0)),
            pl.BlockSpec((PLANES, size_y, size_z), lambda i: (i, 0, 0)),
        ]
        + [whole((atoms, 2, nproj, 128)) for _ in groups],
        out_shape=[
            jax.ShapeDtypeStruct((2, planes, size_y, size_z), jnp.bfloat16),
            jax.ShapeDtypeStruct((planes, size_y, size_z), jnp.bfloat16),
        ]
        + [jax.ShapeDtypeStruct((atoms, 2, nproj, 128), jnp.float32) for _ in groups],
        scratch_shapes=[
            pltpu.VMEM((size_z // 128, size_y * rows, 128), jnp.float32),
            pltpu.VMEM((2, planes * size_y * size_z // 128, 128), jnp.float32),
        ],
        compiler_params=params(1),
        cost_estimate=pl.CostEstimate(
            flops=8 * planes * size_y * size_z * (size_y + size_z),
            bytes_accessed=10 * planes * size_y * size_z,
            transcendentals=0,
        ),
        name="make_field",
    )(counts, lists, weights, buf, table_y, table_z, *projectors)


def energy_kernel(coupled, *refs):
    sums, (projections, energies) = refs[:-2], refs[-2:]
    for atom in range(energies.shape[0]):
        for part in range(2):
            tile = sum(s[atom, part] for s in sums)
            mixed = jnp.zeros_like(tile)
            for j in range(tile.shape[0]):
                mixed += coupled[j] * tile[j : j + 1]
            projections[atom, part] = jnp.broadcast_to(
                jnp.sum(tile, -1, keepdims=True), tile.shape
            )
            energies[atom, part] = jnp.broadcast_to(
                jnp.sum(mixed, -1, keepdims=True), tile.shape
            )


def make_energies(coupled, sums):
    shape = jax.ShapeDtypeStruct(sums[0].shape, jnp.float32)
    return pl.pallas_call(energy_kernel, out_shape=[shape, shape], name="energies")(coupled, *sums)


def back_kernel(*refs, groups, step, blocks):
    counts, lists, wave, potential, table_z, table_y = refs[:6]
    projectors = refs[6 : 6 + len(groups)]
    energies = refs[6 + len(groups) : 6 + 2 * len(groups)]
    out, nonlocal_ref, tall = refs[6 + 2 * len(groups) :]
    near, size_y, size_z = potential.shape
    pieces, columns, rows, _ = out.shape
    planes = rows // 2
    lanes = 128
    halves = size_z // lanes
    chunk_rows = planes * size_y
    i = pl.program_id(0)

    @pl.when(i == 0)
    def _():
        nonlocal_ref[...] = jnp.zeros_like(nonlocal_ref)
        for group, projector, energy in zip(groups, projectors, energies):

            def body(k, carry):
                code, entry, atom = unpack_entry(lists[group, k], step, blocks)
                tile = projector[entry]
                for part in range(2):
                    row = jnp.sum(tile * energy[atom, part], axis=0, keepdims=True)
                    nonlocal_ref[part, pl.ds(code, 1), :] += row
                return carry

            lax.fori_loop(0, counts[group], body, 0)

    fields = []
    for h in range(near):
        local = potential[h].astype(jnp.float32)
        start = pl.multiple_of((i * near + h) * size_y, 8)
        for part in range(2):
            extra = jnp.concatenate(
                [
                    nonlocal_ref[part, pl.ds(q * chunk_rows + start, size_y), :]
                    for q in range(halves)
                ],
                axis=1,
            )
            fields.append((local * wave[part, h].astype(jnp.float32) + extra).astype(jnp.bfloat16))
    stacked = jnp.concatenate(
        [jnp.concatenate(fields[2 * h : 2 * h + 2], axis=1) for h in range(near)], axis=0
    )
    back_z = jnp.dot(stacked, table_z[...], preferred_element_type=jnp.float32).astype(jnp.bfloat16)
    turned = jnp.concatenate(
        [
            jnp.concatenate(
                [
                    back_z[h * size_y : (h + 1) * size_y, :size_z],
                    back_z[h * size_y : (h + 1) * size_y, size_z:],
                ],
                axis=0,
            )
            for h in range(near)
        ],
        axis=1,
    )
    back_y = jnp.dot(table_y[...], turned, preferred_element_type=jnp.float32)
    for h in range(near):
        for part in range(2):
            for q in range(halves):
                start = h * size_z + q * lanes
                tall[q, pl.ds(part * planes + i * near + h, size_y, stride=rows), :] = back_y[
                    part * size_y : (part + 1) * size_y, start : start + lanes
                ]

    @pl.when(i == pl.num_programs(0) - 1)
    def _():
        def narrow(dst, carry):
            start = pl.multiple_of(dst * columns * rows, 8)
            values = [tall[q, pl.ds(start, columns * rows), :] for q in range(halves)]
            out[dst] = (
                jnp.concatenate(values, axis=1).astype(jnp.bfloat16).reshape(columns, rows, size_z)
            )
            return carry

        lax.fori_loop(0, pieces, narrow, 0)


def go_back(counts, lists, wave, potential, table_z, table_y, projectors, energies, groups, step,
            blocks, place, pieces):
    _, planes, size_y, size_z = wave.shape
    columns = size_y // pieces
    in_specs = [
        SMEM_SPEC,
        SMEM_SPEC,
        pl.BlockSpec((2, PLANES, size_y, size_z), lambda i: (0, i, 0, 0)),
        pl.BlockSpec((PLANES, size_y, size_z), lambda i: (place(i), 0, 0)),
        whole(table_z.shape),
        whole(table_y.shape),
    ]
    in_specs += [whole(p.shape) for p in projectors] + [whole(e.shape) for e in energies]
    shape = (pieces, columns, 2 * planes, size_z)
    return pl.pallas_call(
        functools.partial(back_kernel, groups=groups, step=step, blocks=blocks),
        grid=(planes // PLANES,),
        in_specs=in_specs,
        out_specs=whole(shape),
        out_shape=jax.ShapeDtypeStruct(shape, jnp.bfloat16),
        scratch_shapes=[
            pltpu.VMEM((2, planes * size_y * size_z // 128, 128), jnp.float32),
            pltpu.VMEM((size_z // 128, 2 * planes * size_y, 128), jnp.float32),
        ],
        compiler_params=params(1),
        cost_estimate=pl.CostEstimate(
            flops=8 * planes * size_y * size_z * (size_y + size_z),
            bytes_accessed=10 * planes * size_y * size_z,
            transcendentals=0,
        ),
        name="go_back",
    )(counts, lists, wave, potential, table_z, table_y, *projectors, *energies)


def last_x_kernel(frequency_x, frequency_yz, table, coeffs, *refs):
    bufs, (out, tall) = refs[:-2], refs[-2:]
    parts, size_x, columns, lanes = coeffs.shape

    def some_columns(g, carry):
        loaded = []
        for h in range(COLUMNS):
            pieces = [buf[:, COLUMNS * g + h] for buf in bufs]
            loaded.append(
                jnp.concatenate([p.reshape(p.shape[0] * p.shape[1], lanes) for p in pieces], axis=0)
            )
        result = jnp.dot(
            table[...], jnp.concatenate(loaded, axis=1), preferred_element_type=jnp.float32
        )
        for h in range(COLUMNS):
            tall[pl.ds(COLUMNS * g + h, parts * size_x, stride=columns), :] = result[
                :, h * lanes : (h + 1) * lanes
            ]
        return carry

    lax.fori_loop(0, columns // COLUMNS, some_columns, 0)

    def finish(k, carry):
        kinetic = frequency_x[k] + frequency_yz[...]
        for part in range(parts):
            start = pl.multiple_of((part * size_x + k) * columns, 8)
            out[part, k] = (
                tall[pl.ds(start, columns), :] + kinetic * coeffs[part, k].astype(jnp.float32)
            ).astype(jnp.bfloat16)
        return carry

    lax.fori_loop(0, size_x, finish, 0, unroll=8)


def last_x(frequency_x, frequency_yz, table, coeffs, bufs):
    _, size_x, columns, size_z = coeffs.shape
    lanes = size_z // 2
    spec = pl.BlockSpec((2, size_x, columns, lanes), lambda i: (0, 0, 0, i))
    return pl.pallas_call(
        last_x_kernel,
        grid=(2,),
        in_specs=[
            SMEM_SPEC,
            pl.BlockSpec((columns, lanes), lambda i: (0, i)),
            whole(table.shape),
            spec,
        ]
        + [pl.BlockSpec((*b.shape[:3], lanes), lambda i: (0, 0, 0, i)) for b in bufs],
        out_specs=spec,
        out_shape=jax.ShapeDtypeStruct(coeffs.shape, jnp.bfloat16),
        scratch_shapes=[pltpu.VMEM((2 * size_x * columns, lanes), jnp.float32)],
        compiler_params=params(1),
        cost_estimate=pl.CostEstimate(
            flops=8 * size_x * size_x * columns * size_z,
            bytes_accessed=12 * size_x * columns * size_z,
            transcendentals=0,
        ),
        name="last_x",
    )(frequency_x, frequency_yz, table, coeffs, *bufs)


def per_device_chunked(wave_coeffs, occupation, potential, projectors, coupling, sphere_blocks):
    pieces = lax.axis_size("fft")
    bands = lax.axis_size("band")
    slab = lax.axis_index("fft")
    coeffs = wave_coeffs[0]
    _, size_x, columns, size_z = coeffs.shape
    slab_planes, size_y, _ = potential.shape
    atom_dev, nproj, blocks, cells = projectors.shape
    zblocks = size_z // cells
    outer, inner = chunk_planes(slab_planes)
    up = [(i, (i + 1) % pieces) for i in range(pieces)]
    down = [(j, i) for i, j in up]

    inverse_x, forward_x = (real_blocks(size_x, s) for s in (1.0, -1.0))
    inverse_y, forward_y = (real_blocks(size_y, s) for s in (1.0, -1.0))
    inverse_z, forward_z = (real_blocks(size_z, s) for s in (1.0, -1.0))
    places = [
        np.arange(pieces)[:, None] * slab_planes + np.array(chunk)[None, :]
        for chunk in (outer, inner)
    ]
    tables_x = [
        np.stack([inverse_x[r][place] for r in range(2)], 1).reshape(-1, 2 * size_x)
        for place in places
    ]
    table_y = inverse_y.reshape(2 * size_y, 2 * size_y)
    table_z = inverse_z.transpose(2, 3, 0, 1).reshape(2 * size_z, 2 * size_z)
    table_back_z = forward_z.transpose(2, 3, 0, 1).reshape(2 * size_z, 2 * size_z)
    table_back_y = forward_y.reshape(2 * size_y, 2 * size_y)
    table_back_x = np.concatenate(
        [
            np.stack([forward_x[:, :, r][:, :, place] for r in range(2)], 3).reshape(2 * size_x, -1)
            for place in places
        ],
        axis=1,
    )
    *tables_x, table_y, table_z, table_back_z, table_back_y, table_back_x = (
        jnp.asarray(t.astype(jnp.bfloat16))
        for t in (*tables_x, table_y, table_z, table_back_z, table_back_y, table_back_x)
    )

    section_outer = first_x(tables_x[0], coeffs, len(outer), pieces)
    section_inner = first_x(tables_x[1], coeffs, len(inner), pieces)

    codes, steps = [], []
    for chunk, shift in ((outer, 0), (outer, -1), (outer, 1), (inner, 0)):
        owner = (slab + shift + pieces) % pieces
        numbers = lax.dynamic_slice_in_dim(sphere_blocks, owner * atom_dev, atom_dev, 0)
        plane = numbers // (size_y * zblocks) - slab * slab_planes
        rest = numbers % (size_y * zblocks)
        if chunk is outer:
            inside = ((plane >= 0) & (plane < EDGE)) | (
                (plane >= slab_planes - EDGE) & (plane < slab_planes)
            )
            plane = jnp.where(plane < EDGE, plane, plane - len(inner))
        else:
            inside = (plane >= EDGE) & (plane < slab_planes - EDGE)
            plane = plane - EDGE
        code = (rest % zblocks * len(chunk) + plane) * size_y + rest // zblocks
        codes.append(jnp.where(inside, code, -1).reshape(-1))
        steps.append(zblocks * len(chunk) * size_y)
    lists, counts = pl.pallas_call(
        functools.partial(list_kernel, steps=steps),
        in_specs=[SMEM_SPEC],
        out_specs=[SMEM_SPEC] * 2,
        out_shape=[
            jax.ShapeDtypeStruct((len(codes), atom_dev * blocks), jnp.int32),
            jax.ShapeDtypeStruct((len(codes),), jnp.int32),
        ],
        name="block_lists",
    )(jnp.stack(codes))

    turned = projectors.transpose(0, 2, 1, 3)
    share = atom_dev // bands
    mine = lax.dynamic_slice_in_dim(turned, lax.axis_index("band") * share, share, 0)

    def flat(values):
        return values.astype(jnp.float32).reshape(atom_dev * blocks, nproj, cells)

    own = flat(turned)
    previous = flat(lax.all_gather(lax.ppermute(mine, "fft", up), "band", axis=0, tiled=True))
    following = flat(lax.all_gather(lax.ppermute(mine, "fft", down), "band", axis=0, tiled=True))
    strength = 3.0 * math.sqrt(cells * blocks) / nproj
    coupled = (coupling + coupling.T) * (0.5 * strength)
    coupled = jnp.broadcast_to(coupled.T[:, :, None], (nproj, nproj, 128))

    def exchange(values):
        return lax.all_to_all(values, "fft", 0, 0, tiled=True)

    received_outer = exchange(section_outer)
    section_inner, lists, counts, own, previous, following, coupled = lax.optimization_barrier(
        (section_inner, lists, counts, own, previous, following, coupled)
    )
    received_inner = exchange(section_inner)
    near = [own, previous, following]
    wave_outer, density_outer, sums_outer, to_previous, to_following = make_field(
        counts, lists, occupation, received_outer, table_y, table_z, near, (0, 1, 2), steps[0],
        blocks,
    )
    from_following = lax.ppermute(to_previous, "fft", down)
    from_previous = lax.ppermute(to_following, "fft", up)
    density_outer = lax.psum(density_outer, "band")
    wave_inner, density_inner, sums_inner = make_field(
        counts, lists, occupation, received_inner, table_y, table_z, near[:1], (3,), steps[3],
        blocks,
    )
    density_inner = lax.psum(density_inner, "band")
    projected, energy = make_energies(
        coupled, [sums_outer, sums_inner, from_following, from_previous]
    )
    energies = [energy, lax.ppermute(energy, "fft", up), lax.ppermute(energy, "fft", down)]
    edge_steps = EDGE // PLANES
    inner_steps = len(inner) // PLANES
    back_inner = go_back(
        counts, lists, wave_inner, potential, table_back_z, table_back_y, near[:1], energies[:1],
        (3,), steps[3], blocks, lambda i: i + edge_steps, pieces,
    )
    back_inner, energies = lax.optimization_barrier((back_inner, energies))
    back_inner = exchange(back_inner)
    back_outer = go_back(
        counts, lists, wave_outer, potential, table_back_z, table_back_y, near, energies,
        (0, 1, 2), steps[0], blocks, lambda i: jnp.where(i < edge_steps, i, i + inner_steps),
        pieces,
    )
    back_outer = exchange(back_outer)
    density = jnp.concatenate([density_outer[:EDGE], density_inner, density_outer[EDGE:]], axis=0)

    index_x = np.arange(size_x)
    frequency_x = jnp.asarray(
        (np.where(2 * index_x < size_x, index_x, index_x - size_x) / size_x) ** 2, jnp.float32
    )
    index_y = slab * columns + jnp.arange(columns, dtype=jnp.int32)
    index_z = jnp.arange(size_z, dtype=jnp.int32)
    frequency_yz = wave_squares(index_y, size_y)[:, None] + wave_squares(index_z, size_z)[None, :]
    coeffs, density = lax.optimization_barrier((coeffs, density))
    applied = last_x(frequency_x, frequency_yz, table_back_x, coeffs, [back_outer, back_inner])
    return (applied[None], density, projected[None, :, :, :, 0])


def per_device(wave_coeffs, occupation, potential, projectors, coupling, sphere_blocks):
    pieces, bands = lax.axis_size("fft"), lax.axis_size("band")
    size_z = wave_coeffs.shape[4]
    columns = wave_coeffs.shape[3]
    slab_planes = potential.shape[0]
    chunked = (
        pieces >= 3
        and slab_planes % EDGE == 0
        and slab_planes >= 3 * EDGE
        and EDGE >= HALO
        and columns % 8 == 0
        and size_z % 256 == 0
        and projectors.shape[0] % bands == 0
        and projectors.shape[3] == 128
        and projectors.shape[1] == 8
    )
    chosen = per_device_chunked if chunked else per_device_plain
    return chosen(wave_coeffs, occupation, potential, projectors, coupling, sphere_blocks)


def solution(mesh):
    placed = (
        P("band", None, None, "fft", None),
        P("band", None),
        P("fft", None, None),
        P("fft", None, None, None),
        P(),
        P(),
    )
    return jax.shard_map(
        per_device,
        mesh=mesh,
        in_specs=placed,
        out_specs=(
            P("band", None, None, "fft", None),
            P("fft", None, None),
            P("band", "fft", None, None),
        ),
        check_vma=False,
    )
```

```python
import functools
import math

import jax
import jax.numpy as jnp
import numpy as np
from jax import lax
from jax.experimental import pallas as pl
from jax.experimental.pallas import tpu as pltpu
from jax.sharding import PartitionSpec as P

HALO = 6
EDGE = 8
PLANES = 4
COLUMNS = 8
VMEM_BYTES = 56 * 1024 * 1024


def extended(shard, sides, width):
    for axis, dim in sides:
        count, length = (lax.axis_size(axis), shard.shape[dim])
        up = [(i, (i + 1) % count) for i in range(count)]
        down = [(j, i) for i, j in up]
        last = lax.slice_in_dim(shard, length - width, length, axis=dim)
        first = lax.slice_in_dim(shard, 0, width, axis=dim)
        before = lax.ppermute(last, axis, up)
        after = lax.ppermute(first, axis, down)
        shard = jnp.concatenate([before, shard, after], axis=dim)
    return shard


def dft_table(length, sign_value):
    indices = jnp.arange(length, dtype=jnp.int32)
    phases = indices[:, None] * indices[None, :] % length
    angles = 2.0 * math.pi / length * phases.astype(jnp.float32)
    factor = 1.0 / math.sqrt(length)
    cosine = jnp.cos(angles) * factor
    sine_part = jnp.sin(angles) * (sign_value * factor)
    upper_rows = jnp.stack([cosine, -sine_part])
    bottom = jnp.stack([sine_part, cosine])
    return jnp.stack([upper_rows, bottom]).astype(jnp.bfloat16)


def wave_squares(indices, length):
    frequency = (
        jnp.where(2 * indices < length, indices, indices - length).astype(jnp.float32) / length
    )
    return frequency * frequency


def per_device_plain(wave_coeffs, occupation, potential, projectors, coupling, sphere_blocks):
    pieces = lax.axis_size("fft")
    slab_index = lax.axis_index("fft")
    coeffs = wave_coeffs[0]
    size_x = coeffs.shape[1]
    columns = coeffs.shape[2]
    size_z = coeffs.shape[3]
    slab_planes = potential.shape[0]
    size_y = potential.shape[1]
    atom_dev = projectors.shape[0]
    nproj_count = projectors.shape[1]
    block_cells = projectors.shape[3]
    zblocks = size_z // block_cells
    plane_blocks = size_y * zblocks
    total_atoms = atom_dev * pieces
    table_x = dft_table(size_x, 1.0).transpose(0, 2, 1, 3).reshape(2 * size_x, 2 * size_x)
    inverse_y = dft_table(size_y, 1.0)
    inverse_z = dft_table(size_z, 1.0)
    flattened = coeffs.reshape(2 * size_x, columns * size_z)
    along_x = jnp.dot(table_x, flattened, preferred_element_type=jnp.float32)
    along_x = along_x.reshape(2, size_x, columns, size_z).astype(jnp.bfloat16)
    along_y = jnp.einsum(
        "abyk,bxkz->axyz",
        inverse_y,
        lax.all_to_all(along_x, "fft", split_axis=1, concat_axis=2, tiled=True),
        preferred_element_type=jnp.float32,
    ).astype(jnp.bfloat16)
    wave_field = jnp.einsum(
        "abzk,bxyk->axyz", inverse_z, along_y, preferred_element_type=jnp.float32
    ).astype(jnp.bfloat16)
    weights = occupation[0]
    real_part = wave_field[0].astype(jnp.float32)
    imag_part = wave_field[1].astype(jnp.float32)
    partial_density = weights[0] * real_part * real_part + weights[1] * imag_part * imag_part
    density = lax.psum(partial_density.astype(jnp.bfloat16), "band")
    strength = 3.0 * math.sqrt(block_cells * projectors.shape[2]) / nproj_count
    coupled = (coupling + coupling.T) * (0.5 * strength)
    nearby = extended(projectors, (("fft", 0),), atom_dev)
    atom_rows = (
        slab_index * atom_dev - atom_dev + jnp.arange(3 * atom_dev, dtype=jnp.int32) + total_atoms
    ) % total_atoms
    near_blocks = sphere_blocks[atom_rows]
    plane_index = near_blocks // plane_blocks
    inside = plane_index // slab_planes == slab_index
    local_index = jnp.where(
        inside,
        (plane_index - slab_index * slab_planes) * plane_blocks + near_blocks % plane_blocks,
        0,
    )
    blocks_own = wave_field.reshape(2, slab_planes * plane_blocks, block_cells)
    gathered = blocks_own[:, local_index] * inside[None, :, :, None].astype(jnp.bfloat16)
    partial_value = jnp.einsum(
        "ajsk,bask->abj", nearby, gathered, preferred_element_type=jnp.float32
    )
    summed = extended(partial_value, (("fft", 0),), atom_dev)
    projections_own = (
        summed[:atom_dev] + summed[2 * atom_dev : 3 * atom_dev] + summed[4 * atom_dev :]
    )
    energy_own = jnp.einsum(
        "ij,abj->abi", coupled, projections_own, precision=lax.Precision.HIGHEST
    )
    energy = extended(energy_own, (("fft", 0),), atom_dev)
    spread = jnp.einsum(
        "ajsk,abj->bask", nearby.astype(jnp.float32), energy, precision=lax.Precision.HIGHEST
    )
    spread = spread * inside[None, :, :, None].astype(jnp.float32)
    accumulated = (
        jnp.zeros((2, slab_planes * plane_blocks, block_cells), jnp.float32)
        .at[:, local_index]
        .add(spread)
    )
    nonlocal_term = accumulated.reshape(2, slab_planes, size_y, size_z)
    total_field = (
        potential.astype(jnp.float32)[None] * wave_field.astype(jnp.float32) + nonlocal_term
    ).astype(jnp.bfloat16)
    forward_z = dft_table(size_z, -1.0)
    forward_y = dft_table(size_y, -1.0)
    forward_x = dft_table(size_x, -1.0)
    back_z = jnp.einsum(
        "abzk,bxyk->axyz", forward_z, total_field, preferred_element_type=jnp.float32
    ).astype(jnp.bfloat16)
    back_y = jnp.einsum(
        "abyk,bxkz->axyz", forward_y, back_z, preferred_element_type=jnp.float32
    ).astype(jnp.bfloat16)
    transformed = jnp.einsum(
        "abxk,bkyz->axyz",
        forward_x,
        lax.all_to_all(back_y, "fft", split_axis=2, concat_axis=1, tiled=True),
        preferred_element_type=jnp.float32,
    )
    index_x = jnp.arange(size_x, dtype=jnp.int32)
    index_y = slab_index * columns + jnp.arange(columns, dtype=jnp.int32)
    index_z = jnp.arange(size_z, dtype=jnp.int32)
    kinetic = (
        wave_squares(index_x, size_x)[:, None, None]
        + wave_squares(index_y, size_y)[None, :, None]
        + wave_squares(index_z, size_z)[None, None, :]
    )
    applied = (transformed + kinetic[None] * coeffs.astype(jnp.float32)).astype(jnp.bfloat16)
    return (applied[None], density, projections_own[None])


def real_blocks(length, sign):
    index = np.arange(length)
    angles = 2.0 * np.pi / length * (index[:, None] * index[None, :] % length)
    cosine = np.cos(angles) / np.sqrt(length)
    sine = sign * np.sin(angles) / np.sqrt(length)
    blocks = np.empty((2, length, 2, length))
    blocks[0, :, 0, :] = cosine
    blocks[1, :, 1, :] = cosine
    blocks[0, :, 1, :] = -sine
    blocks[1, :, 0, :] = sine
    return blocks


def chunk_planes(slab_planes):
    low, high = list(range(EDGE)), list(range(slab_planes - EDGE, slab_planes))
    return [low + high, list(range(EDGE, slab_planes - EDGE))]


def params(steps):
    return pltpu.CompilerParams(
        dimension_semantics=("arbitrary",) * steps, vmem_limit_bytes=VMEM_BYTES
    )


def whole(shape):
    return pl.BlockSpec(shape, lambda i: (0,) * len(shape))


SMEM_SPEC = pl.BlockSpec(memory_space=pltpu.SMEM)


def list_kernel(codes_ref, lists_ref, counts_ref, *, steps):
    groups, length = codes_ref.shape
    for group in range(groups):

        def body(i, count):
            code = codes_ref[group, i]
            lists_ref[group, count] = code + i * steps[group]
            return count + (code >= 0).astype(jnp.int32)

        counts_ref[group] = lax.fori_loop(0, length, body, jnp.int32(0), unroll=4)


def first_x_kernel(table_ref, coeffs_ref, out_ref, wide, *tall, natural):
    parts, size_x, columns, lanes = coeffs_ref.shape
    rows = parts * size_x

    def widen(k, carry):
        for part in range(parts):
            start = pl.multiple_of((part * size_x + k * 8) * columns, 8)
            wide[pl.ds(start, 8 * columns), :] = (
                coeffs_ref[part, pl.ds(k * 8, 8)].astype(jnp.float32).reshape(8 * columns, lanes)
            )
        return carry

    lax.fori_loop(0, size_x // 8, widen, 0, unroll=2)

    def some_columns(g, carry):
        loaded = [
            wide[pl.ds(COLUMNS * g + h, rows, stride=columns), :].astype(jnp.bfloat16)
            for h in range(COLUMNS)
        ]
        result = jnp.dot(
            table_ref[...], jnp.concatenate(loaded, axis=1), preferred_element_type=jnp.float32
        )
        for h in range(COLUMNS):
            piece = result[:, h * lanes : (h + 1) * lanes]
            if natural:
                tall[0][pl.ds(COLUMNS * g + h, piece.shape[0], stride=columns), :] = piece
            else:
                out_ref[:, COLUMNS * g + h] = piece.astype(jnp.bfloat16).reshape(
                    out_ref.shape[0], out_ref.shape[2], lanes
                )
        return carry

    lax.fori_loop(0, columns // COLUMNS, some_columns, 0)
    if natural:
        pieces, planes, height, _ = out_ref.shape

        def narrow(dst, carry):
            start = pl.multiple_of(dst * planes * height, 8)
            values = tall[0][pl.ds(start, planes * height), :]
            out_ref[dst] = values.astype(jnp.bfloat16).reshape(planes, height, lanes)
            return carry

        lax.fori_loop(0, pieces, narrow, 0)


def first_x(table, coeffs, planes, pieces, natural):
    _, size_x, columns, size_z = coeffs.shape
    lanes = size_z // 2
    shape = (pieces, planes, 2 * columns) if natural else (pieces, columns, 2 * planes)
    scratch = [pltpu.VMEM((2 * size_x * columns, lanes), jnp.float32)]
    if natural:
        scratch.append(pltpu.VMEM((2 * pieces * planes * columns, lanes), jnp.float32))
    return pl.pallas_call(
        functools.partial(first_x_kernel, natural=natural),
        grid=(2,),
        in_specs=[
            whole(table.shape),
            pl.BlockSpec((2, size_x, columns, lanes), lambda i: (0, 0, 0, i)),
        ],
        out_specs=pl.BlockSpec((*shape, lanes), lambda i: (0, 0, 0, i)),
        out_shape=jax.ShapeDtypeStruct((*shape, size_z), jnp.bfloat16),
        scratch_shapes=scratch,
        compiler_params=params(1),
        cost_estimate=pl.CostEstimate(
            flops=8 * size_x * pieces * planes * columns * size_z,
            bytes_accessed=4 * (size_x + pieces * planes) * columns * size_z,
            transcendentals=0,
        ),
        name="first_x",
    )(table, coeffs)


def unpack_entry(value, step):
    return lax.rem(value, step), lax.div(value, step)


def field_kernel(*refs, groups, step, natural):
    count = len(groups)
    counts, lists, weights, buf, table_y, table_z, wave, density = refs[:8]
    rows_out, rows_wide = refs[8 : 8 + count], refs[8 + count : 8 + 2 * count]
    field, *wide = refs[8 + 2 * count :]
    _, near, size_y, size_z = wave.shape
    lanes = 128
    halves = size_z // lanes
    planes = field.shape[1] // (size_y * halves)
    i = pl.program_id(0)
    loaded = []
    if natural:
        for h in range(near):
            loaded.append(buf[:, h].reshape(2 * size_y, size_z))
    else:
        pieces, columns, rows, _ = buf.shape

        @pl.when(i == 0)
        def _():
            def widen(src, carry):
                start = pl.multiple_of(src * columns * rows, 8)
                values = buf[src].astype(jnp.float32).reshape(columns * rows, size_z)
                for q in range(halves):
                    wide[0][q, pl.ds(start, columns * rows), :] = values[
                        :, q * lanes : (q + 1) * lanes
                    ]
                return carry

            lax.fori_loop(0, pieces, widen, 0)

        for h in range(near):
            plane = i * near + h
            both = [
                jnp.concatenate(
                    [
                        wide[0][q, pl.ds(part * planes + plane, size_y, stride=rows), :]
                        for q in range(halves)
                    ],
                    axis=1,
                ).astype(jnp.bfloat16)
                for part in range(2)
            ]
            loaded.append(jnp.concatenate(both, axis=0))
    along_y = jnp.dot(
        table_y[...], jnp.concatenate(loaded, axis=1), preferred_element_type=jnp.float32
    ).astype(jnp.bfloat16)
    turned = jnp.concatenate(
        [
            jnp.concatenate(
                [
                    along_y[:size_y, h * size_z : (h + 1) * size_z],
                    along_y[size_y:, h * size_z : (h + 1) * size_z],
                ],
                axis=1,
            )
            for h in range(near)
        ],
        axis=0,
    )
    result = jnp.dot(turned, table_z[...], preferred_element_type=jnp.float32).astype(jnp.bfloat16)
    for h in range(near):
        plane = i * near + h
        total = jnp.zeros((size_y, size_z), jnp.float32)
        for part in range(2):
            values = result[h * size_y : (h + 1) * size_y, part * size_z : (part + 1) * size_z]
            wave[part, h] = values
            values = values.astype(jnp.float32)
            total += weights[0, part] * values * values
            for q in range(halves):
                start = pl.multiple_of((q * planes + plane) * size_y, 8)
                field[part, pl.ds(start, size_y), :] = values[:, q * lanes : (q + 1) * lanes]
        density[h] = total.astype(jnp.bfloat16)

    @pl.when(i == pl.num_programs(0) - 1)
    def _():
        for group, out, rows in zip(groups, rows_out, rows_wide):
            rows[...] = jnp.zeros_like(rows)

            def body(k, carry):
                code, entry = unpack_entry(lists[group, k], step)
                for part in range(2):
                    rows[part, pl.ds(entry, 1), :] = field[part, pl.ds(code, 1), :]
                return carry

            lax.fori_loop(0, counts[group], body, 0)
            out[...] = rows[...].astype(jnp.bfloat16)


def make_field(counts, lists, weights, buf, table_y, table_z, groups, step, entries, natural):
    pieces, size_z = buf.shape[0], buf.shape[3]
    if natural:
        planes, size_y = buf.shape[1], pieces * buf.shape[2] // 2
        buf_spec = pl.BlockSpec((pieces, PLANES, *buf.shape[2:]), lambda i: (0, i, 0, 0))
    else:
        planes, size_y = buf.shape[2] // 2, pieces * buf.shape[1]
        buf_spec = whole(buf.shape)
    scratch = [pltpu.VMEM((2, entries, 128), jnp.float32) for _ in groups]
    scratch.append(pltpu.VMEM((2, planes * size_y * size_z // 128, 128), jnp.float32))
    if not natural:
        scratch.append(pltpu.VMEM((size_z // 128, 2 * planes * size_y, 128), jnp.float32))
    return pl.pallas_call(
        functools.partial(field_kernel, groups=groups, step=step, natural=natural),
        grid=(planes // PLANES,),
        in_specs=[SMEM_SPEC, SMEM_SPEC, SMEM_SPEC, buf_spec, whole(table_y.shape),
                  whole(table_z.shape)],
        out_specs=[
            pl.BlockSpec((2, PLANES, size_y, size_z), lambda i: (0, i, 0, 0)),
            pl.BlockSpec((PLANES, size_y, size_z), lambda i: (i, 0, 0)),
        ]
        + [whole((2, entries, 128)) for _ in groups],
        out_shape=[
            jax.ShapeDtypeStruct((2, planes, size_y, size_z), jnp.bfloat16),
            jax.ShapeDtypeStruct((planes, size_y, size_z), jnp.bfloat16),
        ]
        + [jax.ShapeDtypeStruct((2, entries, 128), jnp.bfloat16) for _ in groups],
        scratch_shapes=scratch,
        compiler_params=params(1),
        cost_estimate=pl.CostEstimate(
            flops=8 * planes * size_y * size_z * (size_y + size_z),
            bytes_accessed=10 * planes * size_y * size_z,
            transcendentals=0,
        ),
        name="make_field",
    )(counts, lists, weights, buf, table_y, table_z)


def nonlocal_kernel(coupled, projectors, *refs):
    parts, (projections, spread, spread_out) = refs[:-3], refs[-3:]
    atoms, nproj, blocks, cells = projectors.shape
    for atom in range(atoms):
        tables = [projectors[atom, j].astype(jnp.float32) for j in range(nproj)]
        place = pl.ds(atom * blocks, blocks)
        for part in range(2):
            rows = sum(p[part, place].astype(jnp.float32) for p in parts)
            tile = jnp.concatenate(
                [jnp.sum(t * rows, axis=0, keepdims=True) for t in tables], axis=0
            )
            mixed = jnp.zeros_like(tile)
            for j in range(nproj):
                mixed += coupled[j] * tile[j : j + 1]
            projections[atom, part] = jnp.broadcast_to(
                jnp.sum(tile, -1, keepdims=True), tile.shape
            )
            energy = jnp.broadcast_to(jnp.sum(mixed, -1, keepdims=True), tile.shape)
            result = sum(t * energy[j : j + 1] for j, t in enumerate(tables))
            spread[part, place] = result
            spread_out[part, place] = result.astype(jnp.bfloat16)


def make_nonlocal(coupled, projectors, parts):
    atoms, nproj, _, cells = projectors.shape
    return pl.pallas_call(
        nonlocal_kernel,
        out_shape=[
            jax.ShapeDtypeStruct((atoms, 2, nproj, cells), jnp.float32),
            jax.ShapeDtypeStruct(parts[0].shape, jnp.float32),
            jax.ShapeDtypeStruct(parts[0].shape, jnp.bfloat16),
        ],
        name="make_nonlocal",
    )(coupled, projectors, *parts)


def back_kernel(*refs, groups, step, natural):
    count = len(groups)
    counts, lists, wave, potential, table_z, table_y = refs[:6]
    sources = refs[6 : 6 + count]
    out, nonlocal_ref, spread, *tall = refs[6 + count :]
    near, size_y, size_z = potential.shape
    lanes = 128
    halves = size_z // lanes
    planes = nonlocal_ref.shape[1] // (size_y * halves)
    i = pl.program_id(0)

    @pl.when(i == 0)
    def _():
        nonlocal_ref[...] = jnp.zeros_like(nonlocal_ref)
        for group, source in zip(groups, sources):
            spread[...] = source[...].astype(jnp.float32)

            def body(k, carry):
                code, entry = unpack_entry(lists[group, k], step)
                for part in range(2):
                    nonlocal_ref[part, pl.ds(code, 1), :] += spread[part, pl.ds(entry, 1), :]
                return carry

            lax.fori_loop(0, counts[group], body, 0)

    fields = []
    for h in range(near):
        local = potential[h].astype(jnp.float32)
        for part in range(2):
            extra = jnp.concatenate(
                [
                    nonlocal_ref[
                        part,
                        pl.ds(pl.multiple_of((q * planes + i * near + h) * size_y, 8), size_y),
                        :,
                    ]
                    for q in range(halves)
                ],
                axis=1,
            )
            fields.append((local * wave[part, h].astype(jnp.float32) + extra).astype(jnp.bfloat16))
    stacked = jnp.concatenate(
        [jnp.concatenate(fields[2 * h : 2 * h + 2], axis=1) for h in range(near)], axis=0
    )
    back_z = jnp.dot(stacked, table_z[...], preferred_element_type=jnp.float32).astype(jnp.bfloat16)
    turned = jnp.concatenate(
        [
            jnp.concatenate(
                [
                    back_z[h * size_y : (h + 1) * size_y, :size_z],
                    back_z[h * size_y : (h + 1) * size_y, size_z:],
                ],
                axis=0,
            )
            for h in range(near)
        ],
        axis=1,
    )
    back_y = jnp.dot(table_y[...], turned, preferred_element_type=jnp.float32)
    if natural:
        back_y = back_y.astype(jnp.bfloat16)
        for h in range(near):
            out[:, h] = back_y[:, h * size_z : (h + 1) * size_z].reshape(
                out.shape[0], out.shape[2], size_z
            )
        return
    pieces, columns, rows, _ = out.shape
    for h in range(near):
        for part in range(2):
            for q in range(halves):
                start = h * size_z + q * lanes
                tall[0][q, pl.ds(part * planes + i * near + h, size_y, stride=rows), :] = back_y[
                    part * size_y : (part + 1) * size_y, start : start + lanes
                ]

    @pl.when(i == pl.num_programs(0) - 1)
    def _():
        def narrow(dst, carry):
            start = pl.multiple_of(dst * columns * rows, 8)
            values = [tall[0][q, pl.ds(start, columns * rows), :] for q in range(halves)]
            out[dst] = (
                jnp.concatenate(values, axis=1).astype(jnp.bfloat16).reshape(columns, rows, size_z)
            )
            return carry

        lax.fori_loop(0, pieces, narrow, 0)


def go_back(counts, lists, wave, potential, table_z, table_y, sources, groups, step, place, pieces,
            natural):
    _, planes, size_y, size_z = wave.shape
    columns = size_y // pieces
    scratch = [
        pltpu.VMEM((2, planes * size_y * size_z // 128, 128), jnp.float32),
        pltpu.VMEM(sources[0].shape, jnp.float32),
    ]
    if natural:
        shape = (pieces, planes, 2 * columns, size_z)
        out_spec = pl.BlockSpec((pieces, PLANES, 2 * columns, size_z), lambda i: (0, i, 0, 0))
    else:
        shape = (pieces, columns, 2 * planes, size_z)
        out_spec = whole(shape)
        scratch.append(pltpu.VMEM((size_z // 128, 2 * planes * size_y, 128), jnp.float32))
    return pl.pallas_call(
        functools.partial(back_kernel, groups=groups, step=step, natural=natural),
        grid=(planes // PLANES,),
        in_specs=[
            SMEM_SPEC,
            SMEM_SPEC,
            pl.BlockSpec((2, PLANES, size_y, size_z), lambda i: (0, i, 0, 0)),
            pl.BlockSpec((PLANES, size_y, size_z), lambda i: (place(i), 0, 0)),
            whole(table_z.shape),
            whole(table_y.shape),
        ]
        + [whole(s.shape) for s in sources],
        out_specs=out_spec,
        out_shape=jax.ShapeDtypeStruct(shape, jnp.bfloat16),
        scratch_shapes=scratch,
        compiler_params=params(1),
        cost_estimate=pl.CostEstimate(
            flops=8 * planes * size_y * size_z * (size_y + size_z),
            bytes_accessed=10 * planes * size_y * size_z,
            transcendentals=0,
        ),
        name="go_back",
    )(counts, lists, wave, potential, table_z, table_y, *sources)


def last_x_kernel(frequency_x, frequency_yz, table, coeffs, *refs):
    bufs, (out, tall) = refs[:-2], refs[-2:]
    parts, size_x, columns, lanes = coeffs.shape

    def some_columns(g, carry):
        loaded = []
        for h in range(COLUMNS):
            pieces = [buf[:, COLUMNS * g + h] for buf in bufs]
            loaded.append(
                jnp.concatenate([p.reshape(p.shape[0] * p.shape[1], lanes) for p in pieces], axis=0)
            )
        result = jnp.dot(
            table[...], jnp.concatenate(loaded, axis=1), preferred_element_type=jnp.float32
        )
        for h in range(COLUMNS):
            tall[pl.ds(COLUMNS * g + h, parts * size_x, stride=columns), :] = result[
                :, h * lanes : (h + 1) * lanes
            ]
        return carry

    lax.fori_loop(0, columns // COLUMNS, some_columns, 0)

    def finish(k, carry):
        kinetic = frequency_x[k] + frequency_yz[...]
        for part in range(parts):
            start = pl.multiple_of((part * size_x + k) * columns, 8)
            out[part, k] = (
                tall[pl.ds(start, columns), :] + kinetic * coeffs[part, k].astype(jnp.float32)
            ).astype(jnp.bfloat16)
        return carry

    lax.fori_loop(0, size_x, finish, 0, unroll=8)


def last_x(frequency_x, frequency_yz, table, coeffs, bufs):
    _, size_x, columns, size_z = coeffs.shape
    lanes = size_z // 2
    spec = pl.BlockSpec((2, size_x, columns, lanes), lambda i: (0, 0, 0, i))
    return pl.pallas_call(
        last_x_kernel,
        grid=(2,),
        in_specs=[
            SMEM_SPEC,
            pl.BlockSpec((columns, lanes), lambda i: (0, i)),
            whole(table.shape),
            spec,
        ]
        + [pl.BlockSpec((*b.shape[:3], lanes), lambda i: (0, 0, 0, i)) for b in bufs],
        out_specs=spec,
        out_shape=jax.ShapeDtypeStruct(coeffs.shape, jnp.bfloat16),
        scratch_shapes=[pltpu.VMEM((2 * size_x * columns, lanes), jnp.float32)],
        compiler_params=params(1),
        cost_estimate=pl.CostEstimate(
            flops=8 * size_x * size_x * columns * size_z,
            bytes_accessed=12 * size_x * columns * size_z,
            transcendentals=0,
        ),
        name="last_x",
    )(frequency_x, frequency_yz, table, coeffs, *bufs)


def per_device_chunked(wave_coeffs, occupation, potential, projectors, coupling, sphere_blocks):
    pieces = lax.axis_size("fft")
    bands = lax.axis_size("band")
    slab = lax.axis_index("fft")
    coeffs = wave_coeffs[0]
    _, size_x, columns, size_z = coeffs.shape
    slab_planes, size_y, _ = potential.shape
    atom_dev, nproj, blocks, cells = projectors.shape
    zblocks = size_z // cells
    outer, inner = chunk_planes(slab_planes)
    up = [(i, (i + 1) % pieces) for i in range(pieces)]
    down = [(j, i) for i, j in up]

    inverse_x, forward_x = (real_blocks(size_x, s) for s in (1.0, -1.0))
    inverse_y, forward_y = (real_blocks(size_y, s) for s in (1.0, -1.0))
    inverse_z, forward_z = (real_blocks(size_z, s) for s in (1.0, -1.0))
    place_outer, place_inner = (
        np.arange(pieces)[:, None] * slab_planes + np.array(chunk)[None, :]
        for chunk in (outer, inner)
    )
    table_x_outer = np.stack([inverse_x[r][place_outer] for r in range(2)], 1)
    table_x_inner = np.stack([inverse_x[r][place_inner] for r in range(2)], 2)
    table_back_x = np.concatenate(
        [
            np.stack([forward_x[:, :, r][:, :, place] for r in range(2)], 3).reshape(2 * size_x, -1)
            for place in (place_outer, place_inner)
        ],
        axis=1,
    )
    split_y = (2, size_y, 2, pieces, columns)
    tables = [
        table_x_outer.reshape(-1, 2 * size_x),
        table_x_inner.reshape(-1, 2 * size_x),
        inverse_y.reshape(2 * size_y, -1),
        inverse_y.reshape(split_y).transpose(0, 1, 3, 2, 4).reshape(2 * size_y, -1),
        inverse_z.transpose(2, 3, 0, 1).reshape(2 * size_z, -1),
        forward_z.transpose(2, 3, 0, 1).reshape(2 * size_z, -1),
        forward_y.reshape(2 * size_y, -1),
        forward_y.reshape(2, pieces, columns, -1).transpose(1, 0, 2, 3).reshape(2 * size_y, -1),
        table_back_x,
    ]
    (
        table_x_outer, table_x_inner, table_y_outer, table_y_inner, table_z,
        table_back_z, table_back_y_outer, table_back_y_inner, table_back_x,
    ) = (jnp.asarray(t.astype(jnp.bfloat16)) for t in tables)

    section_outer = first_x(table_x_outer, coeffs, len(outer), pieces, False)
    section_outer, table_x_inner, sphere_blocks = lax.optimization_barrier(
        (section_outer, table_x_inner, sphere_blocks)
    )
    section_inner = first_x(table_x_inner, coeffs, len(inner), pieces, True)

    codes, steps = [], []
    for chunk, shift in ((outer, 0), (outer, -1), (outer, 1), (inner, 0)):
        owner = (slab + shift + pieces) % pieces
        numbers = lax.dynamic_slice_in_dim(sphere_blocks, owner * atom_dev, atom_dev, 0)
        plane = numbers // (size_y * zblocks) - slab * slab_planes
        rest = numbers % (size_y * zblocks)
        if chunk is outer:
            inside = ((plane >= 0) & (plane < EDGE)) | (
                (plane >= slab_planes - EDGE) & (plane < slab_planes)
            )
            plane = jnp.where(plane < EDGE, plane, plane - len(inner))
        else:
            inside = (plane >= EDGE) & (plane < slab_planes - EDGE)
            plane = plane - EDGE
        code = (rest % zblocks * len(chunk) + plane) * size_y + rest // zblocks
        codes.append(jnp.where(inside, code, -1).reshape(-1))
        steps.append(zblocks * len(chunk) * size_y)
    lists, counts = pl.pallas_call(
        functools.partial(list_kernel, steps=steps),
        in_specs=[SMEM_SPEC],
        out_specs=[SMEM_SPEC] * 2,
        out_shape=[
            jax.ShapeDtypeStruct((len(codes), atom_dev * blocks), jnp.int32),
            jax.ShapeDtypeStruct((len(codes),), jnp.int32),
        ],
        name="block_lists",
    )(jnp.stack(codes))

    strength = 3.0 * math.sqrt(cells * blocks) / nproj
    coupled = (coupling + coupling.T) * (0.5 * strength)
    coupled = jnp.broadcast_to(coupled.T[:, :, None], (nproj, nproj, cells))

    def exchange(values):
        return lax.all_to_all(values, "fft", 0, 0, tiled=True)

    received_outer = exchange(section_outer)
    section_inner, lists, counts, coupled = lax.optimization_barrier(
        (section_inner, lists, counts, coupled)
    )
    received_inner = exchange(section_inner)
    entries = atom_dev * blocks
    wave_outer, density_outer, rows_outer, to_previous, to_following = make_field(
        counts, lists, occupation, received_outer, table_y_outer, table_z, (0, 1, 2), steps[0],
        entries, False,
    )
    from_following = lax.ppermute(to_previous, "fft", down)
    from_previous = lax.ppermute(to_following, "fft", up)
    density_outer = lax.psum(density_outer, "band")
    wave_inner, density_inner, rows_inner = make_field(
        counts, lists, occupation, received_inner, table_y_inner, table_z, (3,), steps[3],
        entries, True,
    )
    projected, spread, spread_out = make_nonlocal(
        coupled, projectors, [rows_outer, rows_inner, from_following, from_previous]
    )
    spread_previous = lax.ppermute(spread_out, "fft", up)
    spread_following = lax.ppermute(spread_out, "fft", down)
    edge_steps = EDGE // PLANES
    inner_steps = len(inner) // PLANES
    back_inner = go_back(
        counts, lists, wave_inner, potential, table_back_z, table_back_y_inner, [spread], (3,),
        steps[3], lambda i: i + edge_steps, pieces, True,
    )
    back_inner, spread_previous, spread_following = lax.optimization_barrier(
        (back_inner, spread_previous, spread_following)
    )
    back_inner = exchange(back_inner)
    back_outer = go_back(
        counts, lists, wave_outer, potential, table_back_z, table_back_y_outer,
        [spread, spread_previous, spread_following], (0, 1, 2), steps[0],
        lambda i: jnp.where(i < edge_steps, i, i + inner_steps), pieces, False,
    )
    density_inner, density_outer = lax.optimization_barrier((density_inner, density_outer))
    density_inner = lax.psum(density_inner, "band")
    back_outer, density_outer = lax.optimization_barrier((back_outer, density_outer))
    back_outer = exchange(back_outer)
    back_inner = back_inner.reshape(pieces, len(inner), 2, columns, size_z)
    back_inner = back_inner.transpose(0, 3, 2, 1, 4).reshape(pieces, columns, -1, size_z)
    density = jnp.concatenate([density_outer[:EDGE], density_inner, density_outer[EDGE:]], axis=0)

    index_x = np.arange(size_x)
    frequency_x = jnp.asarray(
        (np.where(2 * index_x < size_x, index_x, index_x - size_x) / size_x) ** 2, jnp.float32
    )
    index_y = slab * columns + jnp.arange(columns, dtype=jnp.int32)
    index_z = jnp.arange(size_z, dtype=jnp.int32)
    frequency_yz = wave_squares(index_y, size_y)[:, None] + wave_squares(index_z, size_z)[None, :]
    coeffs, density, back_inner = lax.optimization_barrier((coeffs, density, back_inner))
    applied = last_x(frequency_x, frequency_yz, table_back_x, coeffs, [back_outer, back_inner])
    return (applied[None], density, projected[None, :, :, :, 0])


def per_device(wave_coeffs, occupation, potential, projectors, coupling, sphere_blocks):
    pieces, bands = lax.axis_size("fft"), lax.axis_size("band")
    size_z = wave_coeffs.shape[4]
    columns = wave_coeffs.shape[3]
    slab_planes = potential.shape[0]
    chunked = (
        pieces >= 3
        and slab_planes % EDGE == 0
        and slab_planes >= 3 * EDGE
        and EDGE >= HALO
        and columns % 8 == 0
        and size_z % 256 == 0
        and projectors.shape[0] % bands == 0
        and projectors.shape[3] == 128
        and projectors.shape[1] == 8
    )
    chosen = per_device_chunked if chunked else per_device_plain
    return chosen(wave_coeffs, occupation, potential, projectors, coupling, sphere_blocks)


def solution(mesh):
    placed = (
        P("band", None, None, "fft", None),
        P("band", None),
        P("fft", None, None),
        P("fft", None, None, None),
        P(),
        P(),
    )
    return jax.shard_map(
        per_device,
        mesh=mesh,
        in_specs=placed,
        out_specs=(
            P("band", None, None, "fft", None),
            P("fft", None, None),
            P("band", "fft", None, None),
        ),
        check_vma=False,
    )
```

```python
import functools
import math

import jax
import jax.numpy as jnp
import numpy as np
from jax import lax
from jax.experimental import pallas as pl
from jax.experimental.pallas import tpu as pltpu
from jax.sharding import PartitionSpec as P

HALO = 6
EDGE = 8
PLANES = 4
COLUMNS = 8
VMEM_BYTES = 56 * 1024 * 1024


def extended(shard, sides, width):
    for axis, dim in sides:
        count, length = (lax.axis_size(axis), shard.shape[dim])
        up = [(i, (i + 1) % count) for i in range(count)]
        down = [(j, i) for i, j in up]
        last = lax.slice_in_dim(shard, length - width, length, axis=dim)
        first = lax.slice_in_dim(shard, 0, width, axis=dim)
        before = lax.ppermute(last, axis, up)
        after = lax.ppermute(first, axis, down)
        shard = jnp.concatenate([before, shard, after], axis=dim)
    return shard


def dft_table(length, sign_value):
    indices = jnp.arange(length, dtype=jnp.int32)
    phases = indices[:, None] * indices[None, :] % length
    angles = 2.0 * math.pi / length * phases.astype(jnp.float32)
    factor = 1.0 / math.sqrt(length)
    cosine = jnp.cos(angles) * factor
    sine_part = jnp.sin(angles) * (sign_value * factor)
    upper_rows = jnp.stack([cosine, -sine_part])
    bottom = jnp.stack([sine_part, cosine])
    return jnp.stack([upper_rows, bottom]).astype(jnp.bfloat16)


def wave_squares(indices, length):
    frequency = (
        jnp.where(2 * indices < length, indices, indices - length).astype(jnp.float32) / length
    )
    return frequency * frequency


def per_device_plain(wave_coeffs, occupation, potential, projectors, coupling, sphere_blocks):
    pieces = lax.axis_size("fft")
    slab_index = lax.axis_index("fft")
    coeffs = wave_coeffs[0]
    size_x = coeffs.shape[1]
    columns = coeffs.shape[2]
    size_z = coeffs.shape[3]
    slab_planes = potential.shape[0]
    size_y = potential.shape[1]
    atom_dev = projectors.shape[0]
    nproj_count = projectors.shape[1]
    block_cells = projectors.shape[3]
    zblocks = size_z // block_cells
    plane_blocks = size_y * zblocks
    total_atoms = atom_dev * pieces
    table_x = dft_table(size_x, 1.0).transpose(0, 2, 1, 3).reshape(2 * size_x, 2 * size_x)
    inverse_y = dft_table(size_y, 1.0)
    inverse_z = dft_table(size_z, 1.0)
    flattened = coeffs.reshape(2 * size_x, columns * size_z)
    along_x = jnp.dot(table_x, flattened, preferred_element_type=jnp.float32)
    along_x = along_x.reshape(2, size_x, columns, size_z).astype(jnp.bfloat16)
    along_y = jnp.einsum(
        "abyk,bxkz->axyz",
        inverse_y,
        lax.all_to_all(along_x, "fft", split_axis=1, concat_axis=2, tiled=True),
        preferred_element_type=jnp.float32,
    ).astype(jnp.bfloat16)
    wave_field = jnp.einsum(
        "abzk,bxyk->axyz", inverse_z, along_y, preferred_element_type=jnp.float32
    ).astype(jnp.bfloat16)
    weights = occupation[0]
    real_part = wave_field[0].astype(jnp.float32)
    imag_part = wave_field[1].astype(jnp.float32)
    partial_density = weights[0] * real_part * real_part + weights[1] * imag_part * imag_part
    density = lax.psum(partial_density.astype(jnp.bfloat16), "band")
    strength = 3.0 * math.sqrt(block_cells * projectors.shape[2]) / nproj_count
    coupled = (coupling + coupling.T) * (0.5 * strength)
    nearby = extended(projectors, (("fft", 0),), atom_dev)
    atom_rows = (
        slab_index * atom_dev - atom_dev + jnp.arange(3 * atom_dev, dtype=jnp.int32) + total_atoms
    ) % total_atoms
    near_blocks = sphere_blocks[atom_rows]
    plane_index = near_blocks // plane_blocks
    inside = plane_index // slab_planes == slab_index
    local_index = jnp.where(
        inside,
        (plane_index - slab_index * slab_planes) * plane_blocks + near_blocks % plane_blocks,
        0,
    )
    blocks_own = wave_field.reshape(2, slab_planes * plane_blocks, block_cells)
    gathered = blocks_own[:, local_index] * inside[None, :, :, None].astype(jnp.bfloat16)
    partial_value = jnp.einsum(
        "ajsk,bask->abj", nearby, gathered, preferred_element_type=jnp.float32
    )
    summed = extended(partial_value, (("fft", 0),), atom_dev)
    projections_own = (
        summed[:atom_dev] + summed[2 * atom_dev : 3 * atom_dev] + summed[4 * atom_dev :]
    )
    energy_own = jnp.einsum(
        "ij,abj->abi", coupled, projections_own, precision=lax.Precision.HIGHEST
    )
    energy = extended(energy_own, (("fft", 0),), atom_dev)
    spread = jnp.einsum(
        "ajsk,abj->bask", nearby.astype(jnp.float32), energy, precision=lax.Precision.HIGHEST
    )
    spread = spread * inside[None, :, :, None].astype(jnp.float32)
    accumulated = (
        jnp.zeros((2, slab_planes * plane_blocks, block_cells), jnp.float32)
        .at[:, local_index]
        .add(spread)
    )
    nonlocal_term = accumulated.reshape(2, slab_planes, size_y, size_z)
    total_field = (
        potential.astype(jnp.float32)[None] * wave_field.astype(jnp.float32) + nonlocal_term
    ).astype(jnp.bfloat16)
    forward_z = dft_table(size_z, -1.0)
    forward_y = dft_table(size_y, -1.0)
    forward_x = dft_table(size_x, -1.0)
    back_z = jnp.einsum(
        "abzk,bxyk->axyz", forward_z, total_field, preferred_element_type=jnp.float32
    ).astype(jnp.bfloat16)
    back_y = jnp.einsum(
        "abyk,bxkz->axyz", forward_y, back_z, preferred_element_type=jnp.float32
    ).astype(jnp.bfloat16)
    transformed = jnp.einsum(
        "abxk,bkyz->axyz",
        forward_x,
        lax.all_to_all(back_y, "fft", split_axis=2, concat_axis=1, tiled=True),
        preferred_element_type=jnp.float32,
    )
    index_x = jnp.arange(size_x, dtype=jnp.int32)
    index_y = slab_index * columns + jnp.arange(columns, dtype=jnp.int32)
    index_z = jnp.arange(size_z, dtype=jnp.int32)
    kinetic = (
        wave_squares(index_x, size_x)[:, None, None]
        + wave_squares(index_y, size_y)[None, :, None]
        + wave_squares(index_z, size_z)[None, None, :]
    )
    applied = (transformed + kinetic[None] * coeffs.astype(jnp.float32)).astype(jnp.bfloat16)
    return (applied[None], density, projections_own[None])


def real_blocks(length, sign):
    index = np.arange(length)
    angles = 2.0 * np.pi / length * (index[:, None] * index[None, :] % length)
    cosine = np.cos(angles) / np.sqrt(length)
    sine = sign * np.sin(angles) / np.sqrt(length)
    blocks = np.empty((2, length, 2, length))
    blocks[0, :, 0, :] = cosine
    blocks[1, :, 1, :] = cosine
    blocks[0, :, 1, :] = -sine
    blocks[1, :, 0, :] = sine
    return blocks


def chunk_planes(slab_planes):
    low, high = list(range(EDGE)), list(range(slab_planes - EDGE, slab_planes))
    return [low + high, list(range(EDGE, slab_planes - EDGE))]


def params(steps):
    return pltpu.CompilerParams(
        dimension_semantics=("arbitrary",) * steps, vmem_limit_bytes=VMEM_BYTES
    )


def whole(shape):
    return pl.BlockSpec(shape, lambda i: (0,) * len(shape))


SMEM_SPEC = pl.BlockSpec(memory_space=pltpu.SMEM)


def list_kernel(codes_ref, lists_ref, counts_ref, *, steps):
    groups, length = codes_ref.shape
    for group in range(groups):

        def body(i, count):
            code = codes_ref[group, i]
            lists_ref[group, count] = code + i * steps[group]
            return count + (code >= 0).astype(jnp.int32)

        counts_ref[group] = lax.fori_loop(0, length, body, jnp.int32(0), unroll=4)


def first_x_kernel(slab, table_ref, coeffs_ref, *refs, pieces, natural):
    outs, (turned, wide, *tall) = refs[:pieces], refs[pieces:]
    parts, size_x, columns, lanes = coeffs_ref.shape
    rows = parts * size_x
    height = table_ref.shape[0] // pieces

    for k in range(pieces):
        start = pl.multiple_of(lax.rem(slab[0] + k, pieces) * height, 16)
        turned[k * height : (k + 1) * height, :] = table_ref[pl.ds(start, height), :]

    def widen(k, carry):
        for part in range(parts):
            start = pl.multiple_of((part * size_x + k * 8) * columns, 8)
            wide[pl.ds(start, 8 * columns), :] = (
                coeffs_ref[part, pl.ds(k * 8, 8)].astype(jnp.float32).reshape(8 * columns, lanes)
            )
        return carry

    lax.fori_loop(0, size_x // 8, widen, 0, unroll=2)

    def some_columns(g, carry):
        loaded = [
            wide[pl.ds(COLUMNS * g + h, rows, stride=columns), :].astype(jnp.bfloat16)
            for h in range(COLUMNS)
        ]
        result = jnp.dot(
            turned[...], jnp.concatenate(loaded, axis=1), preferred_element_type=jnp.float32
        )
        for h in range(COLUMNS):
            piece = result[:, h * lanes : (h + 1) * lanes]
            if natural:
                tall[0][pl.ds(COLUMNS * g + h, piece.shape[0], stride=columns), :] = piece
            else:
                piece = piece.astype(jnp.bfloat16)
                for k in range(pieces):
                    outs[k][COLUMNS * g + h] = piece[k * height : (k + 1) * height]
        return carry

    lax.fori_loop(0, columns // COLUMNS, some_columns, 0)
    if natural:
        for k in range(pieces):
            values = tall[0][k * height * columns : (k + 1) * height * columns, :]
            outs[k][...] = values.astype(jnp.bfloat16).reshape(outs[k].shape)


def first_x(slab, table, coeffs, planes, pieces, natural):
    _, size_x, columns, size_z = coeffs.shape
    lanes = size_z // 2
    shape = (planes, 2 * columns) if natural else (columns, 2 * planes)
    scratch = [
        pltpu.VMEM(table.shape, jnp.bfloat16),
        pltpu.VMEM((2 * size_x * columns, lanes), jnp.float32),
    ]
    if natural:
        scratch.append(pltpu.VMEM((2 * pieces * planes * columns, lanes), jnp.float32))
    return pl.pallas_call(
        functools.partial(first_x_kernel, pieces=pieces, natural=natural),
        grid=(2,),
        in_specs=[
            SMEM_SPEC,
            whole(table.shape),
            pl.BlockSpec((2, size_x, columns, lanes), lambda i: (0, 0, 0, i)),
        ],
        out_specs=[pl.BlockSpec((*shape, lanes), lambda i: (0, 0, i)) for _ in range(pieces)],
        out_shape=[
            jax.ShapeDtypeStruct((*shape, size_z), jnp.bfloat16) for _ in range(pieces)
        ],
        scratch_shapes=scratch,
        compiler_params=params(1),
        cost_estimate=pl.CostEstimate(
            flops=8 * size_x * pieces * planes * columns * size_z,
            bytes_accessed=4 * (size_x + pieces * planes) * columns * size_z,
            transcendentals=0,
        ),
        name="first_x",
    )(slab, table, coeffs)


def unpack_entry(value, step):
    return lax.rem(value, step), lax.div(value, step)


def field_kernel(*refs, groups, step, pieces, natural):
    count = len(groups)
    slab, counts, lists, weights, table_y, table_z = refs[:6]
    bufs = refs[6 : 6 + pieces]
    wave, density = refs[6 + pieces : 8 + pieces]
    rows_out = refs[8 + pieces : 8 + pieces + count]
    rows_wide = refs[8 + pieces + count : 8 + pieces + 2 * count]
    field, wide = refs[8 + pieces + 2 * count :]
    sources = [lax.rem(slab[0] + (pieces - k), pieces) for k in range(pieces)]
    _, near, size_y, size_z = wave.shape
    lanes = 128
    halves = size_z // lanes
    planes = field.shape[1] // (size_y * halves)
    i = pl.program_id(0)
    loaded = []
    if natural:
        for source, buf in zip(sources, bufs):
            wide[source] = buf[...]
        for h in range(near):
            loaded.append(wide[:, h].reshape(2 * size_y, size_z))
    else:
        columns, rows, _ = bufs[0].shape

        @pl.when(i == 0)
        def _():
            for source, buf in zip(sources, bufs):
                start = pl.multiple_of(source * columns * rows, 8)
                values = buf[...].astype(jnp.float32).reshape(columns * rows, size_z)
                for q in range(halves):
                    wide[q, pl.ds(start, columns * rows), :] = values[
                        :, q * lanes : (q + 1) * lanes
                    ]

        for h in range(near):
            plane = i * near + h
            both = [
                jnp.concatenate(
                    [
                        wide[q, pl.ds(part * planes + plane, size_y, stride=rows), :]
                        for q in range(halves)
                    ],
                    axis=1,
                ).astype(jnp.bfloat16)
                for part in range(2)
            ]
            loaded.append(jnp.concatenate(both, axis=0))
    along_y = jnp.dot(
        table_y[...], jnp.concatenate(loaded, axis=1), preferred_element_type=jnp.float32
    ).astype(jnp.bfloat16)
    turned = jnp.concatenate(
        [
            jnp.concatenate(
                [
                    along_y[:size_y, h * size_z : (h + 1) * size_z],
                    along_y[size_y:, h * size_z : (h + 1) * size_z],
                ],
                axis=1,
            )
            for h in range(near)
        ],
        axis=0,
    )
    result = jnp.dot(turned, table_z[...], preferred_element_type=jnp.float32).astype(jnp.bfloat16)
    for h in range(near):
        plane = i * near + h
        total = jnp.zeros((size_y, size_z), jnp.float32)
        for part in range(2):
            values = result[h * size_y : (h + 1) * size_y, part * size_z : (part + 1) * size_z]
            wave[part, h] = values
            values = values.astype(jnp.float32)
            total += weights[0, part] * values * values
            for q in range(halves):
                start = pl.multiple_of((q * planes + plane) * size_y, 8)
                field[part, pl.ds(start, size_y), :] = values[:, q * lanes : (q + 1) * lanes]
        density[h] = total.astype(jnp.bfloat16)

    @pl.when(i == pl.num_programs(0) - 1)
    def _():
        for group, out, rows in zip(groups, rows_out, rows_wide):
            rows[...] = jnp.zeros_like(rows)

            def body(k, carry):
                code, entry = unpack_entry(lists[group, k], step)
                for part in range(2):
                    rows[part, pl.ds(entry, 1), :] = field[part, pl.ds(code, 1), :]
                return carry

            lax.fori_loop(0, counts[group], body, 0)
            out[...] = rows[...].astype(jnp.bfloat16)


def make_field(slab, counts, lists, weights, bufs, table_y, table_z, groups, step, entries, natural):
    pieces, (*_, size_z) = len(bufs), bufs[0].shape
    if natural:
        planes, size_y = bufs[0].shape[0], pieces * bufs[0].shape[1] // 2
        buf_spec = pl.BlockSpec((PLANES, *bufs[0].shape[1:]), lambda i: (i, 0, 0))
        held = pltpu.VMEM((pieces, PLANES, *bufs[0].shape[1:]), jnp.bfloat16)
    else:
        planes, size_y = bufs[0].shape[1] // 2, pieces * bufs[0].shape[0]
        buf_spec = whole(bufs[0].shape)
        held = pltpu.VMEM((size_z // 128, 2 * planes * size_y, 128), jnp.float32)
    scratch = [pltpu.VMEM((2, entries, 128), jnp.float32) for _ in groups]
    scratch += [pltpu.VMEM((2, planes * size_y * size_z // 128, 128), jnp.float32), held]
    return pl.pallas_call(
        functools.partial(field_kernel, groups=groups, step=step, pieces=pieces, natural=natural),
        grid=(planes // PLANES,),
        in_specs=[SMEM_SPEC] * 4
        + [whole(table_y.shape), whole(table_z.shape)]
        + [buf_spec] * pieces,
        out_specs=[
            pl.BlockSpec((2, PLANES, size_y, size_z), lambda i: (0, i, 0, 0)),
            pl.BlockSpec((PLANES, size_y, size_z), lambda i: (i, 0, 0)),
        ]
        + [whole((2, entries, 128)) for _ in groups],
        out_shape=[
            jax.ShapeDtypeStruct((2, planes, size_y, size_z), jnp.bfloat16),
            jax.ShapeDtypeStruct((planes, size_y, size_z), jnp.bfloat16),
        ]
        + [jax.ShapeDtypeStruct((2, entries, 128), jnp.bfloat16) for _ in groups],
        scratch_shapes=scratch,
        compiler_params=params(1),
        cost_estimate=pl.CostEstimate(
            flops=8 * planes * size_y * size_z * (size_y + size_z),
            bytes_accessed=10 * planes * size_y * size_z,
            transcendentals=0,
        ),
        name="make_field",
    )(slab, counts, lists, weights, table_y, table_z, *bufs)


def nonlocal_kernel(coupled, projectors, *refs):
    parts, (projections, spread, spread_out) = refs[:-3], refs[-3:]
    atoms, nproj, blocks, cells = projectors.shape
    for atom in range(atoms):
        tables = [projectors[atom, j].astype(jnp.float32) for j in range(nproj)]
        place = pl.ds(atom * blocks, blocks)
        for part in range(2):
            rows = sum(p[part, place].astype(jnp.float32) for p in parts)
            tile = jnp.concatenate(
                [jnp.sum(t * rows, axis=0, keepdims=True) for t in tables], axis=0
            )
            mixed = jnp.zeros_like(tile)
            for j in range(nproj):
                mixed += coupled[j] * tile[j : j + 1]
            projections[atom, part] = jnp.broadcast_to(
                jnp.sum(tile, -1, keepdims=True), tile.shape
            )
            energy = jnp.broadcast_to(jnp.sum(mixed, -1, keepdims=True), tile.shape)
            result = sum(t * energy[j : j + 1] for j, t in enumerate(tables))
            spread[part, place] = result
            spread_out[part, place] = result.astype(jnp.bfloat16)


def make_nonlocal(coupled, projectors, parts):
    atoms, nproj, _, cells = projectors.shape
    return pl.pallas_call(
        nonlocal_kernel,
        out_shape=[
            jax.ShapeDtypeStruct((atoms, 2, nproj, cells), jnp.float32),
            jax.ShapeDtypeStruct(parts[0].shape, jnp.float32),
            jax.ShapeDtypeStruct(parts[0].shape, jnp.bfloat16),
        ],
        name="make_nonlocal",
    )(coupled, projectors, *parts)


def back_kernel(*refs, groups, step, pieces, natural):
    count = len(groups)
    slab, counts, lists, wave, potential, table_z, table_y = refs[:7]
    sources = refs[7 : 7 + count]
    outs = refs[7 + count : 7 + count + pieces]
    nonlocal_ref, spread, tall = refs[7 + count + pieces :]
    targets = [lax.rem(slab[0] + k, pieces) for k in range(pieces)]
    near, size_y, size_z = potential.shape
    lanes = 128
    halves = size_z // lanes
    planes = nonlocal_ref.shape[1] // (size_y * halves)
    i = pl.program_id(0)

    @pl.when(i == 0)
    def _():
        nonlocal_ref[...] = jnp.zeros_like(nonlocal_ref)
        for group, source in zip(groups, sources):
            spread[...] = source[...].astype(jnp.float32)

            def body(k, carry):
                code, entry = unpack_entry(lists[group, k], step)
                for part in range(2):
                    nonlocal_ref[part, pl.ds(code, 1), :] += spread[part, pl.ds(entry, 1), :]
                return carry

            lax.fori_loop(0, counts[group], body, 0)

    fields = []
    for h in range(near):
        local = potential[h].astype(jnp.float32)
        for part in range(2):
            extra = jnp.concatenate(
                [
                    nonlocal_ref[
                        part,
                        pl.ds(pl.multiple_of((q * planes + i * near + h) * size_y, 8), size_y),
                        :,
                    ]
                    for q in range(halves)
                ],
                axis=1,
            )
            fields.append((local * wave[part, h].astype(jnp.float32) + extra).astype(jnp.bfloat16))
    stacked = jnp.concatenate(
        [jnp.concatenate(fields[2 * h : 2 * h + 2], axis=1) for h in range(near)], axis=0
    )
    back_z = jnp.dot(stacked, table_z[...], preferred_element_type=jnp.float32).astype(jnp.bfloat16)
    turned = jnp.concatenate(
        [
            jnp.concatenate(
                [
                    back_z[h * size_y : (h + 1) * size_y, :size_z],
                    back_z[h * size_y : (h + 1) * size_y, size_z:],
                ],
                axis=0,
            )
            for h in range(near)
        ],
        axis=1,
    )
    back_y = jnp.dot(table_y[...], turned, preferred_element_type=jnp.float32)
    if natural:
        back_y = back_y.astype(jnp.bfloat16)
        for h in range(near):
            tall[:, h] = back_y[:, h * size_z : (h + 1) * size_z].reshape(
                pieces, outs[0].shape[1], size_z
            )
        for target, out in zip(targets, outs):
            out[...] = tall[target]
        return
    columns, rows, _ = outs[0].shape
    for h in range(near):
        for part in range(2):
            for q in range(halves):
                start = h * size_z + q * lanes
                tall[q, pl.ds(part * planes + i * near + h, size_y, stride=rows), :] = back_y[
                    part * size_y : (part + 1) * size_y, start : start + lanes
                ]

    @pl.when(i == pl.num_programs(0) - 1)
    def _():
        for target, out in zip(targets, outs):
            start = pl.multiple_of(target * columns * rows, 8)
            values = [tall[q, pl.ds(start, columns * rows), :] for q in range(halves)]
            out[...] = (
                jnp.concatenate(values, axis=1).astype(jnp.bfloat16).reshape(columns, rows, size_z)
            )


def go_back(slab, counts, lists, wave, potential, table_z, table_y, sources, groups, step, place,
            pieces, natural):
    _, planes, size_y, size_z = wave.shape
    columns = size_y // pieces
    scratch = [
        pltpu.VMEM((2, planes * size_y * size_z // 128, 128), jnp.float32),
        pltpu.VMEM(sources[0].shape, jnp.float32),
    ]
    if natural:
        shape = (planes, 2 * columns, size_z)
        out_spec = pl.BlockSpec((PLANES, 2 * columns, size_z), lambda i: (i, 0, 0))
        scratch.append(pltpu.VMEM((pieces, PLANES, 2 * columns, size_z), jnp.bfloat16))
    else:
        shape = (columns, 2 * planes, size_z)
        out_spec = whole(shape)
        scratch.append(pltpu.VMEM((size_z // 128, 2 * planes * size_y, 128), jnp.float32))
    return pl.pallas_call(
        functools.partial(back_kernel, groups=groups, step=step, pieces=pieces, natural=natural),
        grid=(planes // PLANES,),
        in_specs=[SMEM_SPEC] * 3
        + [
            pl.BlockSpec((2, PLANES, size_y, size_z), lambda i: (0, i, 0, 0)),
            pl.BlockSpec((PLANES, size_y, size_z), lambda i: (place(i), 0, 0)),
            whole(table_z.shape),
            whole(table_y.shape),
        ]
        + [whole(s.shape) for s in sources],
        out_specs=[out_spec] * pieces,
        out_shape=[jax.ShapeDtypeStruct(shape, jnp.bfloat16)] * pieces,
        scratch_shapes=scratch,
        compiler_params=params(1),
        cost_estimate=pl.CostEstimate(
            flops=8 * planes * size_y * size_z * (size_y + size_z),
            bytes_accessed=10 * planes * size_y * size_z,
            transcendentals=0,
        ),
        name="go_back",
    )(slab, counts, lists, wave, potential, table_z, table_y, *sources)


def last_x_kernel(frequency_x, frequency_yz, table, coeffs, *refs):
    bufs, (out, tall) = refs[:-2], refs[-2:]
    parts, size_x, columns, lanes = coeffs.shape

    def some_columns(g, carry):
        loaded = []
        for h in range(COLUMNS):
            loaded.append(jnp.concatenate([buf[COLUMNS * g + h] for buf in bufs], axis=0))
        result = jnp.dot(
            table[...], jnp.concatenate(loaded, axis=1), preferred_element_type=jnp.float32
        )
        for h in range(COLUMNS):
            tall[pl.ds(COLUMNS * g + h, parts * size_x, stride=columns), :] = result[
                :, h * lanes : (h + 1) * lanes
            ]
        return carry

    lax.fori_loop(0, columns // COLUMNS, some_columns, 0)

    def finish(k, carry):
        kinetic = frequency_x[k] + frequency_yz[...]
        for part in range(parts):
            start = pl.multiple_of((part * size_x + k) * columns, 8)
            out[part, k] = (
                tall[pl.ds(start, columns), :] + kinetic * coeffs[part, k].astype(jnp.float32)
            ).astype(jnp.bfloat16)
        return carry

    lax.fori_loop(0, size_x, finish, 0, unroll=8)


def last_x(frequency_x, frequency_yz, table, coeffs, bufs):
    _, size_x, columns, size_z = coeffs.shape
    lanes = size_z // 2
    spec = pl.BlockSpec((2, size_x, columns, lanes), lambda i: (0, 0, 0, i))
    return pl.pallas_call(
        last_x_kernel,
        grid=(2,),
        in_specs=[
            SMEM_SPEC,
            pl.BlockSpec((columns, lanes), lambda i: (0, i)),
            whole(table.shape),
            spec,
        ]
        + [pl.BlockSpec((*b.shape[:2], lanes), lambda i: (0, 0, i)) for b in bufs],
        out_specs=spec,
        out_shape=jax.ShapeDtypeStruct(coeffs.shape, jnp.bfloat16),
        scratch_shapes=[pltpu.VMEM((2 * size_x * columns, lanes), jnp.float32)],
        compiler_params=params(1),
        cost_estimate=pl.CostEstimate(
            flops=8 * size_x * size_x * columns * size_z,
            bytes_accessed=12 * size_x * columns * size_z,
            transcendentals=0,
        ),
        name="last_x",
    )(frequency_x, frequency_yz, table, coeffs, *bufs)


def per_device_chunked(wave_coeffs, occupation, potential, projectors, coupling, sphere_blocks):
    pieces = lax.axis_size("fft")
    bands = lax.axis_size("band")
    slab = lax.axis_index("fft")
    coeffs = wave_coeffs[0]
    _, size_x, columns, size_z = coeffs.shape
    slab_planes, size_y, _ = potential.shape
    atom_dev, nproj, blocks, cells = projectors.shape
    zblocks = size_z // cells
    outer, inner = chunk_planes(slab_planes)
    up = [(i, (i + 1) % pieces) for i in range(pieces)]
    down = [(j, i) for i, j in up]

    inverse_x, forward_x = (real_blocks(size_x, s) for s in (1.0, -1.0))
    inverse_y, forward_y = (real_blocks(size_y, s) for s in (1.0, -1.0))
    inverse_z, forward_z = (real_blocks(size_z, s) for s in (1.0, -1.0))
    place_outer, place_inner = (
        np.arange(pieces)[:, None] * slab_planes + np.array(chunk)[None, :]
        for chunk in (outer, inner)
    )
    table_x_outer = np.stack([inverse_x[r][place_outer] for r in range(2)], 1)
    table_x_inner = np.stack([inverse_x[r][place_inner] for r in range(2)], 2)
    tables_back_x = [
        np.stack([forward_x[:, :, r][:, :, place] for r in range(2)], 3).reshape(
            2 * size_x, pieces, -1
        )
        for place in (place_outer, place_inner)
    ]
    split_y = (2, size_y, 2, pieces, columns)
    tables = [
        table_x_outer.reshape(-1, 2 * size_x),
        table_x_inner.reshape(-1, 2 * size_x),
        inverse_y.reshape(2 * size_y, -1),
        inverse_y.reshape(split_y).transpose(0, 1, 3, 2, 4).reshape(2 * size_y, -1),
        inverse_z.transpose(2, 3, 0, 1).reshape(2 * size_z, -1),
        forward_z.transpose(2, 3, 0, 1).reshape(2 * size_z, -1),
        forward_y.reshape(2 * size_y, -1),
        forward_y.reshape(2, pieces, columns, -1).transpose(1, 0, 2, 3).reshape(2 * size_y, -1),
        *(np.concatenate([t, t], 1)[:, ::-1] for t in tables_back_x),
    ]
    (
        table_x_outer, table_x_inner, table_y_outer, table_y_inner, table_z,
        table_back_z, table_back_y_outer, table_back_y_inner, *tables_back_x,
    ) = (jnp.asarray(t.astype(jnp.bfloat16)) for t in tables)

    tables_back_x = [
        lax.dynamic_slice_in_dim(t, pieces - 1 - slab, pieces, 1) for t in tables_back_x
    ]
    table_back_x = jnp.concatenate([t.reshape(2 * size_x, -1) for t in tables_back_x], axis=1)

    where = slab.reshape(1)
    section_outer = first_x(where, table_x_outer, coeffs, len(outer), pieces, False)
    section_outer, table_x_inner, sphere_blocks = lax.optimization_barrier(
        (section_outer, table_x_inner, sphere_blocks)
    )
    section_inner = first_x(where, table_x_inner, coeffs, len(inner), pieces, True)

    codes, steps = [], []
    for chunk, shift in ((outer, 0), (outer, -1), (outer, 1), (inner, 0)):
        owner = (slab + shift + pieces) % pieces
        numbers = lax.dynamic_slice_in_dim(sphere_blocks, owner * atom_dev, atom_dev, 0)
        plane = numbers // (size_y * zblocks) - slab * slab_planes
        rest = numbers % (size_y * zblocks)
        if chunk is outer:
            inside = ((plane >= 0) & (plane < EDGE)) | (
                (plane >= slab_planes - EDGE) & (plane < slab_planes)
            )
            plane = jnp.where(plane < EDGE, plane, plane - len(inner))
        else:
            inside = (plane >= EDGE) & (plane < slab_planes - EDGE)
            plane = plane - EDGE
        code = (rest % zblocks * len(chunk) + plane) * size_y + rest // zblocks
        codes.append(jnp.where(inside, code, -1).reshape(-1))
        steps.append(zblocks * len(chunk) * size_y)
    lists, counts = pl.pallas_call(
        functools.partial(list_kernel, steps=steps),
        in_specs=[SMEM_SPEC],
        out_specs=[SMEM_SPEC] * 2,
        out_shape=[
            jax.ShapeDtypeStruct((len(codes), atom_dev * blocks), jnp.int32),
            jax.ShapeDtypeStruct((len(codes),), jnp.int32),
        ],
        name="block_lists",
    )(jnp.stack(codes))

    strength = 3.0 * math.sqrt(cells * blocks) / nproj
    coupled = (coupling + coupling.T) * (0.5 * strength)
    coupled = jnp.broadcast_to(coupled.T[:, :, None], (nproj, nproj, cells))

    def exchange(values):
        received = [values[0]]
        for k in range(1, pieces):
            pairs = [(j, (j + k) % pieces) for j in range(pieces)]
            received.append(lax.ppermute(values[k], "fft", pairs))
        return received

    received_outer = exchange(section_outer)
    section_inner, lists, counts, coupled = lax.optimization_barrier(
        (section_inner, lists, counts, coupled)
    )
    received_inner = exchange(section_inner)
    entries = atom_dev * blocks
    wave_outer, density_outer, rows_outer, to_previous, to_following = make_field(
        where, counts, lists, occupation, received_outer, table_y_outer, table_z, (0, 1, 2), steps[0],
        entries, False,
    )
    from_following = lax.ppermute(to_previous, "fft", down)
    from_previous = lax.ppermute(to_following, "fft", up)
    density_outer = lax.psum(density_outer, "band")
    wave_inner, density_inner, rows_inner = make_field(
        where, counts, lists, occupation, received_inner, table_y_inner, table_z, (3,), steps[3],
        entries, True,
    )
    projected, spread, spread_out = make_nonlocal(
        coupled, projectors, [rows_outer, rows_inner, from_following, from_previous]
    )
    spread_previous = lax.ppermute(spread_out, "fft", up)
    spread_following = lax.ppermute(spread_out, "fft", down)
    edge_steps = EDGE // PLANES
    inner_steps = len(inner) // PLANES
    back_inner = go_back(
        where, counts, lists, wave_inner, potential, table_back_z, table_back_y_inner, [spread], (3,),
        steps[3], lambda i: i + edge_steps, pieces, True,
    )
    back_inner, spread_previous, spread_following = lax.optimization_barrier(
        (back_inner, spread_previous, spread_following)
    )
    back_inner = exchange(back_inner)
    back_outer = go_back(
        where, counts, lists, wave_outer, potential, table_back_z, table_back_y_outer,
        [spread, spread_previous, spread_following], (0, 1, 2), steps[0],
        lambda i: jnp.where(i < edge_steps, i, i + inner_steps), pieces, False,
    )
    density_inner, density_outer = lax.optimization_barrier((density_inner, density_outer))
    density_inner = lax.psum(density_inner, "band")
    back_outer, density_outer = lax.optimization_barrier((back_outer, density_outer))
    back_outer = exchange(back_outer)
    back_inner = [
        b.reshape(len(inner), 2, columns, size_z).transpose(2, 1, 0, 3).reshape(columns, -1, size_z)
        for b in back_inner
    ]
    density = jnp.concatenate([density_outer[:EDGE], density_inner, density_outer[EDGE:]], axis=0)

    index_x = np.arange(size_x)
    frequency_x = jnp.asarray(
        (np.where(2 * index_x < size_x, index_x, index_x - size_x) / size_x) ** 2, jnp.float32
    )
    index_y = slab * columns + jnp.arange(columns, dtype=jnp.int32)
    index_z = jnp.arange(size_z, dtype=jnp.int32)
    frequency_yz = wave_squares(index_y, size_y)[:, None] + wave_squares(index_z, size_z)[None, :]
    coeffs, density, back_inner = lax.optimization_barrier((coeffs, density, back_inner))
    applied = last_x(frequency_x, frequency_yz, table_back_x, coeffs, back_outer + back_inner)
    return (applied[None], density, projected[None, :, :, :, 0])


def per_device(wave_coeffs, occupation, potential, projectors, coupling, sphere_blocks):
    pieces, bands = lax.axis_size("fft"), lax.axis_size("band")
    size_z = wave_coeffs.shape[4]
    columns = wave_coeffs.shape[3]
    slab_planes = potential.shape[0]
    chunked = (
        pieces >= 3
        and slab_planes % EDGE == 0
        and slab_planes >= 3 * EDGE
        and EDGE >= HALO
        and columns % 8 == 0
        and size_z % 256 == 0
        and projectors.shape[0] % bands == 0
        and projectors.shape[3] == 128
        and projectors.shape[1] == 8
    )
    chosen = per_device_chunked if chunked else per_device_plain
    return chosen(wave_coeffs, occupation, potential, projectors, coupling, sphere_blocks)


def solution(mesh):
    placed = (
        P("band", None, None, "fft", None),
        P("band", None),
        P("fft", None, None),
        P("fft", None, None, None),
        P(),
        P(),
    )
    return jax.shard_map(
        per_device,
        mesh=mesh,
        in_specs=placed,
        out_specs=(
            P("band", None, None, "fft", None),
            P("fft", None, None),
            P("band", "fft", None, None),
        ),
        check_vma=False,
    )
```

```python
import functools
import math

import jax
import jax.numpy as jnp
import numpy as np
from jax import lax
from jax.experimental import pallas as pl
from jax.experimental.pallas import tpu as pltpu
from jax.sharding import PartitionSpec as P

HALO = 6
EDGE = 8
PLANES = 4
COLUMNS = 8
VMEM_BYTES = 56 * 1024 * 1024
COST = pl.CostEstimate(flops=1024, bytes_accessed=1024, transcendentals=0)


def extended(shard, sides, width):
    for axis, dim in sides:
        count, length = (lax.axis_size(axis), shard.shape[dim])
        up = [(i, (i + 1) % count) for i in range(count)]
        down = [(j, i) for i, j in up]
        last = lax.slice_in_dim(shard, length - width, length, axis=dim)
        first = lax.slice_in_dim(shard, 0, width, axis=dim)
        before = lax.ppermute(last, axis, up)
        after = lax.ppermute(first, axis, down)
        shard = jnp.concatenate([before, shard, after], axis=dim)
    return shard


def dft_table(length, sign_value):
    indices = jnp.arange(length, dtype=jnp.int32)
    phases = indices[:, None] * indices[None, :] % length
    angles = 2.0 * math.pi / length * phases.astype(jnp.float32)
    factor = 1.0 / math.sqrt(length)
    cosine = jnp.cos(angles) * factor
    sine_part = jnp.sin(angles) * (sign_value * factor)
    upper_rows = jnp.stack([cosine, -sine_part])
    bottom = jnp.stack([sine_part, cosine])
    return jnp.stack([upper_rows, bottom]).astype(jnp.bfloat16)


def wave_squares(indices, length):
    frequency = (
        jnp.where(2 * indices < length, indices, indices - length).astype(jnp.float32) / length
    )
    return frequency * frequency


def per_device_plain(wave_coeffs, occupation, potential, projectors, coupling, sphere_blocks):
    pieces = lax.axis_size("fft")
    slab_index = lax.axis_index("fft")
    coeffs = wave_coeffs[0]
    size_x = coeffs.shape[1]
    columns = coeffs.shape[2]
    size_z = coeffs.shape[3]
    slab_planes = potential.shape[0]
    size_y = potential.shape[1]
    atom_dev = projectors.shape[0]
    nproj_count = projectors.shape[1]
    block_cells = projectors.shape[3]
    zblocks = size_z // block_cells
    plane_blocks = size_y * zblocks
    total_atoms = atom_dev * pieces
    table_x = dft_table(size_x, 1.0).transpose(0, 2, 1, 3).reshape(2 * size_x, 2 * size_x)
    inverse_y = dft_table(size_y, 1.0)
    inverse_z = dft_table(size_z, 1.0)
    flattened = coeffs.reshape(2 * size_x, columns * size_z)
    along_x = jnp.dot(table_x, flattened, preferred_element_type=jnp.float32)
    along_x = along_x.reshape(2, size_x, columns, size_z).astype(jnp.bfloat16)
    along_y = jnp.einsum(
        "abyk,bxkz->axyz",
        inverse_y,
        lax.all_to_all(along_x, "fft", split_axis=1, concat_axis=2, tiled=True),
        preferred_element_type=jnp.float32,
    ).astype(jnp.bfloat16)
    wave_field = jnp.einsum(
        "abzk,bxyk->axyz", inverse_z, along_y, preferred_element_type=jnp.float32
    ).astype(jnp.bfloat16)
    weights = occupation[0]
    real_part = wave_field[0].astype(jnp.float32)
    imag_part = wave_field[1].astype(jnp.float32)
    partial_density = weights[0] * real_part * real_part + weights[1] * imag_part * imag_part
    density = lax.psum(partial_density.astype(jnp.bfloat16), "band")
    strength = 3.0 * math.sqrt(block_cells * projectors.shape[2]) / nproj_count
    coupled = (coupling + coupling.T) * (0.5 * strength)
    nearby = extended(projectors, (("fft", 0),), atom_dev)
    atom_rows = (
        slab_index * atom_dev - atom_dev + jnp.arange(3 * atom_dev, dtype=jnp.int32) + total_atoms
    ) % total_atoms
    near_blocks = sphere_blocks[atom_rows]
    plane_index = near_blocks // plane_blocks
    inside = plane_index // slab_planes == slab_index
    local_index = jnp.where(
        inside,
        (plane_index - slab_index * slab_planes) * plane_blocks + near_blocks % plane_blocks,
        0,
    )
    blocks_own = wave_field.reshape(2, slab_planes * plane_blocks, block_cells)
    gathered = blocks_own[:, local_index] * inside[None, :, :, None].astype(jnp.bfloat16)
    partial_value = jnp.einsum(
        "ajsk,bask->abj", nearby, gathered, preferred_element_type=jnp.float32
    )
    summed = extended(partial_value, (("fft", 0),), atom_dev)
    projections_own = (
        summed[:atom_dev] + summed[2 * atom_dev : 3 * atom_dev] + summed[4 * atom_dev :]
    )
    energy_own = jnp.einsum(
        "ij,abj->abi", coupled, projections_own, precision=lax.Precision.HIGHEST
    )
    energy = extended(energy_own, (("fft", 0),), atom_dev)
    spread = jnp.einsum(
        "ajsk,abj->bask", nearby.astype(jnp.float32), energy, precision=lax.Precision.HIGHEST
    )
    spread = spread * inside[None, :, :, None].astype(jnp.float32)
    accumulated = (
        jnp.zeros((2, slab_planes * plane_blocks, block_cells), jnp.float32)
        .at[:, local_index]
        .add(spread)
    )
    nonlocal_term = accumulated.reshape(2, slab_planes, size_y, size_z)
    total_field = (
        potential.astype(jnp.float32)[None] * wave_field.astype(jnp.float32) + nonlocal_term
    ).astype(jnp.bfloat16)
    forward_z = dft_table(size_z, -1.0)
    forward_y = dft_table(size_y, -1.0)
    forward_x = dft_table(size_x, -1.0)
    back_z = jnp.einsum(
        "abzk,bxyk->axyz", forward_z, total_field, preferred_element_type=jnp.float32
    ).astype(jnp.bfloat16)
    back_y = jnp.einsum(
        "abyk,bxkz->axyz", forward_y, back_z, preferred_element_type=jnp.float32
    ).astype(jnp.bfloat16)
    transformed = jnp.einsum(
        "abxk,bkyz->axyz",
        forward_x,
        lax.all_to_all(back_y, "fft", split_axis=2, concat_axis=1, tiled=True),
        preferred_element_type=jnp.float32,
    )
    index_x = jnp.arange(size_x, dtype=jnp.int32)
    index_y = slab_index * columns + jnp.arange(columns, dtype=jnp.int32)
    index_z = jnp.arange(size_z, dtype=jnp.int32)
    kinetic = (
        wave_squares(index_x, size_x)[:, None, None]
        + wave_squares(index_y, size_y)[None, :, None]
        + wave_squares(index_z, size_z)[None, None, :]
    )
    applied = (transformed + kinetic[None] * coeffs.astype(jnp.float32)).astype(jnp.bfloat16)
    return (applied[None], density, projections_own[None])


def real_blocks(length, sign):
    index = np.arange(length)
    angles = 2.0 * np.pi / length * (index[:, None] * index[None, :] % length)
    cosine = np.cos(angles) / np.sqrt(length)
    sine = sign * np.sin(angles) / np.sqrt(length)
    blocks = np.empty((2, length, 2, length))
    blocks[0, :, 0, :] = cosine
    blocks[1, :, 1, :] = cosine
    blocks[0, :, 1, :] = -sine
    blocks[1, :, 0, :] = sine
    return blocks


def chunk_planes(slab_planes):
    low, high = list(range(EDGE)), list(range(slab_planes - EDGE, slab_planes))
    return [low + high, list(range(EDGE, slab_planes - EDGE))]


def params(steps):
    return pltpu.CompilerParams(
        dimension_semantics=("arbitrary",) * steps, vmem_limit_bytes=VMEM_BYTES
    )


def whole(shape):
    return pl.BlockSpec(shape, lambda i: (0,) * len(shape))


SMEM_SPEC = pl.BlockSpec(memory_space=pltpu.SMEM)


def list_kernel(codes_ref, lists_ref, counts_ref, *, steps):
    groups, length = codes_ref.shape
    for group in range(groups):

        def body(i, count):
            code = codes_ref[group, i]
            lists_ref[group, count] = code + i * steps[group]
            return count + (code >= 0).astype(jnp.int32)

        counts_ref[group] = lax.fori_loop(0, length, body, jnp.int32(0), unroll=4)


def slots(near, far, slab):
    half = len(far)
    first = slab - lax.rem(slab, half)
    views = [near.at[j] for j in range(half)] + list(far)
    devices = [first + j for j in range(half)]
    devices += [lax.bitwise_xor(slab, jnp.int32(half + k)) for k in range(half)]
    return list(zip(devices, views))


def first_x_kernel(slab, table_ref, coeffs_ref, *refs, pieces, natural):
    half = pieces // 2
    near, far, (turned, wide, *tall) = refs[0], refs[1 : half + 1], refs[half + 1 :]
    outs = slots(near, far, slab[0])
    parts, size_x, columns, lanes = coeffs_ref.shape
    rows = parts * size_x
    height = table_ref.shape[0] // pieces

    for k, (device, _) in enumerate(outs):
        start = pl.multiple_of(device * height, 16)
        turned[k * height : (k + 1) * height, :] = table_ref[pl.ds(start, height), :]

    def widen(k, carry):
        for part in range(parts):
            start = pl.multiple_of((part * size_x + k * 8) * columns, 8)
            wide[pl.ds(start, 8 * columns), :] = (
                coeffs_ref[part, pl.ds(k * 8, 8)].astype(jnp.float32).reshape(8 * columns, lanes)
            )
        return carry

    lax.fori_loop(0, size_x // 8, widen, 0, unroll=2)

    def some_columns(g, carry):
        loaded = [
            wide[pl.ds(COLUMNS * g + h, rows, stride=columns), :].astype(jnp.bfloat16)
            for h in range(COLUMNS)
        ]
        result = jnp.dot(
            turned[...], jnp.concatenate(loaded, axis=1), preferred_element_type=jnp.float32
        )
        for h in range(COLUMNS):
            piece = result[:, h * lanes : (h + 1) * lanes]
            if natural:
                tall[0][pl.ds(COLUMNS * g + h, piece.shape[0], stride=columns), :] = piece
            else:
                piece = piece.astype(jnp.bfloat16)
                for k, (_, out) in enumerate(outs):
                    out[COLUMNS * g + h] = piece[k * height : (k + 1) * height]
        return carry

    lax.fori_loop(0, columns // COLUMNS, some_columns, 0)
    if natural:
        for k, (_, out) in enumerate(outs):
            values = tall[0][k * height * columns : (k + 1) * height * columns, :]
            out[...] = values.astype(jnp.bfloat16).reshape(out.shape)


def first_x(slab, table, coeffs, planes, pieces, natural):
    _, size_x, columns, size_z = coeffs.shape
    lanes, half = size_z // 2, pieces // 2
    shape = (planes, 2 * columns) if natural else (columns, 2 * planes)
    scratch = [
        pltpu.VMEM(table.shape, jnp.bfloat16),
        pltpu.VMEM((2 * size_x * columns, lanes), jnp.float32),
    ]
    if natural:
        scratch.append(pltpu.VMEM((2 * pieces * planes * columns, lanes), jnp.float32))
    return pl.pallas_call(
        functools.partial(first_x_kernel, pieces=pieces, natural=natural),
        grid=(2,),
        in_specs=[
            SMEM_SPEC,
            whole(table.shape),
            pl.BlockSpec((2, size_x, columns, lanes), lambda i: (0, 0, 0, i)),
        ],
        out_specs=[pl.BlockSpec((half, *shape, lanes), lambda i: (0, 0, 0, i))]
        + [pl.BlockSpec((*shape, lanes), lambda i: (0, 0, i))] * half,
        out_shape=[jax.ShapeDtypeStruct((half, *shape, size_z), jnp.bfloat16)]
        + [jax.ShapeDtypeStruct((*shape, size_z), jnp.bfloat16)] * half,
        scratch_shapes=scratch,
        compiler_params=params(1),
        cost_estimate=COST,
        name="first_x",
    )(slab, table, coeffs)


def unpack_entry(value, step):
    return lax.rem(value, step), lax.div(value, step)


def field_kernel(*refs, groups, step, pieces, natural):
    count = len(groups)
    slab, counts, lists, weights, table_y, table_z = refs[:6]
    half = pieces // 2
    bufs = slots(refs[6], refs[7 : 7 + half], slab[0])
    wave, density = refs[7 + half : 9 + half]
    rows_out = refs[9 + half : 9 + half + count]
    rows_wide = refs[9 + half + count : 9 + half + 2 * count]
    field, wide = refs[9 + half + 2 * count :]
    _, near, size_y, size_z = wave.shape
    lanes = 128
    halves = size_z // lanes
    planes = field.shape[1] // (size_y * halves)
    i = pl.program_id(0)
    loaded = []
    if natural:
        for source, buf in bufs:
            wide[source] = buf[...]
        for h in range(near):
            loaded.append(wide[:, h].reshape(2 * size_y, size_z))
    else:
        columns, rows, _ = bufs[0][1].shape

        @pl.when(i == 0)
        def _():
            for source, buf in bufs:
                start = pl.multiple_of(source * columns * rows, 8)
                values = buf[...].astype(jnp.float32).reshape(columns * rows, size_z)
                for q in range(halves):
                    wide[q, pl.ds(start, columns * rows), :] = values[
                        :, q * lanes : (q + 1) * lanes
                    ]

        for h in range(near):
            plane = i * near + h
            both = [
                jnp.concatenate(
                    [
                        wide[q, pl.ds(part * planes + plane, size_y, stride=rows), :]
                        for q in range(halves)
                    ],
                    axis=1,
                ).astype(jnp.bfloat16)
                for part in range(2)
            ]
            loaded.append(jnp.concatenate(both, axis=0))
    along_y = jnp.dot(
        table_y[...], jnp.concatenate(loaded, axis=1), preferred_element_type=jnp.float32
    ).astype(jnp.bfloat16)
    turned = jnp.concatenate(
        [
            jnp.concatenate(
                [
                    along_y[:size_y, h * size_z : (h + 1) * size_z],
                    along_y[size_y:, h * size_z : (h + 1) * size_z],
                ],
                axis=1,
            )
            for h in range(near)
        ],
        axis=0,
    )
    result = jnp.dot(turned, table_z[...], preferred_element_type=jnp.float32).astype(jnp.bfloat16)
    for h in range(near):
        plane = i * near + h
        total = jnp.zeros((size_y, size_z), jnp.float32)
        for part in range(2):
            values = result[h * size_y : (h + 1) * size_y, part * size_z : (part + 1) * size_z]
            wave[part, h] = values
            values = values.astype(jnp.float32)
            total += weights[0, part] * values * values
            for q in range(halves):
                start = pl.multiple_of((q * planes + plane) * size_y, 8)
                field[part, pl.ds(start, size_y), :] = values[:, q * lanes : (q + 1) * lanes]
        density[h] = total.astype(jnp.bfloat16)

    @pl.when(i == pl.num_programs(0) - 1)
    def _():
        for group, out, rows in zip(groups, rows_out, rows_wide):
            rows[...] = jnp.zeros_like(rows)

            def body(k, carry):
                code, entry = unpack_entry(lists[group, k], step)
                for part in range(2):
                    rows[part, pl.ds(entry, 1), :] = field[part, pl.ds(code, 1), :]
                return carry

            lax.fori_loop(0, counts[group], body, 0)
            out[...] = rows[...].astype(jnp.bfloat16)


def make_field(slab, counts, lists, weights, bufs, table_y, table_z, groups, step, entries, natural):
    half = len(bufs) - 1
    pieces, shape = 2 * half, bufs[1].shape
    size_z = shape[2]
    if natural:
        planes, size_y = shape[0], pieces * shape[1] // 2
        buf_specs = [pl.BlockSpec((half, PLANES, *shape[1:]), lambda i: (0, i, 0, 0))]
        buf_specs += [pl.BlockSpec((PLANES, *shape[1:]), lambda i: (i, 0, 0))] * half
        held = pltpu.VMEM((pieces, PLANES, *shape[1:]), jnp.bfloat16)
    else:
        planes, size_y = shape[1] // 2, pieces * shape[0]
        buf_specs = [whole(b.shape) for b in bufs]
        held = pltpu.VMEM((size_z // 128, 2 * planes * size_y, 128), jnp.float32)
    scratch = [pltpu.VMEM((2, entries, 128), jnp.float32) for _ in groups]
    scratch += [pltpu.VMEM((2, planes * size_y * size_z // 128, 128), jnp.float32), held]
    return pl.pallas_call(
        functools.partial(field_kernel, groups=groups, step=step, pieces=pieces, natural=natural),
        grid=(planes // PLANES,),
        in_specs=[SMEM_SPEC] * 4
        + [whole(table_y.shape), whole(table_z.shape)]
        + buf_specs,
        out_specs=[
            pl.BlockSpec((2, PLANES, size_y, size_z), lambda i: (0, i, 0, 0)),
            pl.BlockSpec((PLANES, size_y, size_z), lambda i: (i, 0, 0)),
        ]
        + [whole((2, entries, 128)) for _ in groups],
        out_shape=[
            jax.ShapeDtypeStruct((2, planes, size_y, size_z), jnp.bfloat16),
            jax.ShapeDtypeStruct((planes, size_y, size_z), jnp.bfloat16),
        ]
        + [jax.ShapeDtypeStruct((2, entries, 128), jnp.bfloat16) for _ in groups],
        scratch_shapes=scratch,
        compiler_params=params(1),
        cost_estimate=COST,
        name="make_field",
    )(slab, counts, lists, weights, table_y, table_z, *bufs)


def nonlocal_kernel(coupled, projectors, *refs):
    parts, (projections, spread, spread_out) = refs[:-3], refs[-3:]
    atoms, nproj, blocks, cells = projectors.shape
    for atom in range(atoms):
        tables = [projectors[atom, j].astype(jnp.float32) for j in range(nproj)]
        place = pl.ds(atom * blocks, blocks)
        for part in range(2):
            rows = sum(p[part, place].astype(jnp.float32) for p in parts)
            tile = jnp.concatenate(
                [jnp.sum(t * rows, axis=0, keepdims=True) for t in tables], axis=0
            )
            mixed = jnp.zeros_like(tile)
            for j in range(nproj):
                mixed += coupled[j] * tile[j : j + 1]
            projections[atom, part] = jnp.broadcast_to(
                jnp.sum(tile, -1, keepdims=True), tile.shape
            )
            energy = jnp.broadcast_to(jnp.sum(mixed, -1, keepdims=True), tile.shape)
            result = sum(t * energy[j : j + 1] for j, t in enumerate(tables))
            spread[part, place] = result
            spread_out[part, place] = result.astype(jnp.bfloat16)


def make_nonlocal(coupled, projectors, parts):
    atoms, nproj, _, cells = projectors.shape
    return pl.pallas_call(
        nonlocal_kernel,
        out_shape=[
            jax.ShapeDtypeStruct((atoms, 2, nproj, cells), jnp.float32),
            jax.ShapeDtypeStruct(parts[0].shape, jnp.float32),
            jax.ShapeDtypeStruct(parts[0].shape, jnp.bfloat16),
        ],
        cost_estimate=COST,
        name="make_nonlocal",
    )(coupled, projectors, *parts)


def back_kernel(*refs, groups, step, pieces, natural):
    count = len(groups)
    slab, counts, lists, wave, potential, table_z, table_y = refs[:7]
    sources = refs[7 : 7 + count]
    near_out, *far_outs = refs[7 + count : 8 + count + pieces // 2]
    nonlocal_ref, spread, tall = refs[8 + count + pieces // 2 :]
    outs = slots(near_out, far_outs, slab[0])
    near, size_y, size_z = potential.shape
    lanes = 128
    halves = size_z // lanes
    planes = nonlocal_ref.shape[1] // (size_y * halves)
    i = pl.program_id(0)

    @pl.when(i == 0)
    def _():
        nonlocal_ref[...] = jnp.zeros_like(nonlocal_ref)
        for group, source in zip(groups, sources):
            spread[...] = source[...].astype(jnp.float32)

            def body(k, carry):
                code, entry = unpack_entry(lists[group, k], step)
                for part in range(2):
                    nonlocal_ref[part, pl.ds(code, 1), :] += spread[part, pl.ds(entry, 1), :]
                return carry

            lax.fori_loop(0, counts[group], body, 0)

    fields = []
    for h in range(near):
        local = potential[h].astype(jnp.float32)
        for part in range(2):
            extra = jnp.concatenate(
                [
                    nonlocal_ref[
                        part,
                        pl.ds(pl.multiple_of((q * planes + i * near + h) * size_y, 8), size_y),
                        :,
                    ]
                    for q in range(halves)
                ],
                axis=1,
            )
            fields.append((local * wave[part, h].astype(jnp.float32) + extra).astype(jnp.bfloat16))
    stacked = jnp.concatenate(
        [jnp.concatenate(fields[2 * h : 2 * h + 2], axis=1) for h in range(near)], axis=0
    )
    back_z = jnp.dot(stacked, table_z[...], preferred_element_type=jnp.float32).astype(jnp.bfloat16)
    turned = jnp.concatenate(
        [
            jnp.concatenate(
                [
                    back_z[h * size_y : (h + 1) * size_y, :size_z],
                    back_z[h * size_y : (h + 1) * size_y, size_z:],
                ],
                axis=0,
            )
            for h in range(near)
        ],
        axis=1,
    )
    back_y = jnp.dot(table_y[...], turned, preferred_element_type=jnp.float32)
    if natural:
        back_y = back_y.astype(jnp.bfloat16)
        for h in range(near):
            tall[:, h] = back_y[:, h * size_z : (h + 1) * size_z].reshape(
                pieces, far_outs[0].shape[1], size_z
            )
        for target, out in outs:
            out[...] = tall[target]
        return
    columns, rows, _ = far_outs[0].shape
    for h in range(near):
        for part in range(2):
            for q in range(halves):
                start = h * size_z + q * lanes
                tall[q, pl.ds(part * planes + i * near + h, size_y, stride=rows), :] = back_y[
                    part * size_y : (part + 1) * size_y, start : start + lanes
                ]

    @pl.when(i == pl.num_programs(0) - 1)
    def _():
        for target, out in outs:
            start = pl.multiple_of(target * columns * rows, 8)
            values = [tall[q, pl.ds(start, columns * rows), :] for q in range(halves)]
            out[...] = (
                jnp.concatenate(values, axis=1).astype(jnp.bfloat16).reshape(columns, rows, size_z)
            )


def go_back(slab, counts, lists, wave, potential, table_z, table_y, sources, groups, step, place,
            pieces, natural):
    _, planes, size_y, size_z = wave.shape
    columns, half = size_y // pieces, pieces // 2
    scratch = [
        pltpu.VMEM((2, planes * size_y * size_z // 128, 128), jnp.float32),
        pltpu.VMEM(sources[0].shape, jnp.float32),
    ]
    if natural:
        shape = (planes, 2 * columns, size_z)
        out_specs = [pl.BlockSpec((half, PLANES, 2 * columns, size_z), lambda i: (0, i, 0, 0))]
        out_specs += [pl.BlockSpec((PLANES, 2 * columns, size_z), lambda i: (i, 0, 0))] * half
        scratch.append(pltpu.VMEM((pieces, PLANES, 2 * columns, size_z), jnp.bfloat16))
    else:
        shape = (columns, 2 * planes, size_z)
        out_specs = [whole((half, *shape))] + [whole(shape)] * half
        scratch.append(pltpu.VMEM((size_z // 128, 2 * planes * size_y, 128), jnp.float32))
    return pl.pallas_call(
        functools.partial(back_kernel, groups=groups, step=step, pieces=pieces, natural=natural),
        grid=(planes // PLANES,),
        in_specs=[SMEM_SPEC] * 3
        + [
            pl.BlockSpec((2, PLANES, size_y, size_z), lambda i: (0, i, 0, 0)),
            pl.BlockSpec((PLANES, size_y, size_z), lambda i: (place(i), 0, 0)),
            whole(table_z.shape),
            whole(table_y.shape),
        ]
        + [whole(s.shape) for s in sources],
        out_specs=out_specs,
        out_shape=[jax.ShapeDtypeStruct((half, *shape), jnp.bfloat16)]
        + [jax.ShapeDtypeStruct(shape, jnp.bfloat16)] * half,
        scratch_shapes=scratch,
        compiler_params=params(1),
        cost_estimate=COST,
        name="go_back",
    )(slab, counts, lists, wave, potential, table_z, table_y, *sources)


def last_x_kernel(frequency_x, frequency_yz, table, coeffs, *refs):
    bufs, (out, tall) = refs[:-2], refs[-2:]
    parts, size_x, columns, lanes = coeffs.shape

    def some_columns(g, carry):
        loaded = []
        for h in range(COLUMNS):
            column = COLUMNS * g + h
            blocks = []
            for buf in bufs:
                if len(buf.shape) == 4:
                    blocks += [buf[j, column] for j in range(buf.shape[0])]
                else:
                    blocks.append(buf[column])
            loaded.append(jnp.concatenate(blocks, axis=0))
        result = jnp.dot(
            table[...], jnp.concatenate(loaded, axis=1), preferred_element_type=jnp.float32
        )
        for h in range(COLUMNS):
            tall[pl.ds(COLUMNS * g + h, parts * size_x, stride=columns), :] = result[
                :, h * lanes : (h + 1) * lanes
            ]
        return carry

    lax.fori_loop(0, columns // COLUMNS, some_columns, 0)

    def finish(k, carry):
        kinetic = frequency_x[k] + frequency_yz[...]
        for part in range(parts):
            start = pl.multiple_of((part * size_x + k) * columns, 8)
            out[part, k] = (
                tall[pl.ds(start, columns), :] + kinetic * coeffs[part, k].astype(jnp.float32)
            ).astype(jnp.bfloat16)
        return carry

    lax.fori_loop(0, size_x, finish, 0, unroll=8)


def last_x(frequency_x, frequency_yz, table, coeffs, bufs):
    _, size_x, columns, size_z = coeffs.shape
    lanes = size_z // 2
    spec = pl.BlockSpec((2, size_x, columns, lanes), lambda i: (0, 0, 0, i))
    return pl.pallas_call(
        last_x_kernel,
        grid=(2,),
        in_specs=[
            SMEM_SPEC,
            pl.BlockSpec((columns, lanes), lambda i: (0, i)),
            whole(table.shape),
            spec,
        ]
        + [
            pl.BlockSpec((*b.shape[:-1], lanes), lambda i, b=b: (0,) * (b.ndim - 1) + (i,))
            for b in bufs
        ],
        out_specs=spec,
        out_shape=jax.ShapeDtypeStruct(coeffs.shape, jnp.bfloat16),
        scratch_shapes=[pltpu.VMEM((2 * size_x * columns, lanes), jnp.float32)],
        compiler_params=params(1),
        cost_estimate=COST,
        name="last_x",
    )(frequency_x, frequency_yz, table, coeffs, *bufs)


def per_device_chunked(wave_coeffs, occupation, potential, projectors, coupling, sphere_blocks):
    pieces = lax.axis_size("fft")
    bands = lax.axis_size("band")
    slab = lax.axis_index("fft")
    coeffs = wave_coeffs[0]
    _, size_x, columns, size_z = coeffs.shape
    slab_planes, size_y, _ = potential.shape
    atom_dev, nproj, blocks, cells = projectors.shape
    zblocks = size_z // cells
    outer, inner = chunk_planes(slab_planes)
    up = [(i, (i + 1) % pieces) for i in range(pieces)]
    down = [(j, i) for i, j in up]

    inverse_x, forward_x = (real_blocks(size_x, s) for s in (1.0, -1.0))
    inverse_y, forward_y = (real_blocks(size_y, s) for s in (1.0, -1.0))
    inverse_z, forward_z = (real_blocks(size_z, s) for s in (1.0, -1.0))
    place_outer, place_inner = (
        np.arange(pieces)[:, None] * slab_planes + np.array(chunk)[None, :]
        for chunk in (outer, inner)
    )
    table_x_outer = np.stack([inverse_x[r][place_outer] for r in range(2)], 1)
    table_x_inner = np.stack([inverse_x[r][place_inner] for r in range(2)], 2)
    tables_back_x = [
        np.stack([forward_x[:, :, r][:, :, place] for r in range(2)], 3).reshape(
            2 * size_x, pieces, -1
        )
        for place in (place_outer, place_inner)
    ]
    half = pieces // 2
    orders = [
        [d - d % half + j for j in range(half)] + [d ^ (half + k) for k in range(half)]
        for d in range(pieces)
    ]
    tables_back_x = np.stack(
        [
            np.concatenate([t[:, order].reshape(2 * size_x, -1) for t in tables_back_x], axis=1)
            for order in orders
        ]
    )
    split_y = (2, size_y, 2, pieces, columns)
    tables = [
        table_x_outer.reshape(-1, 2 * size_x),
        table_x_inner.reshape(-1, 2 * size_x),
        inverse_y.reshape(2 * size_y, -1),
        inverse_y.reshape(split_y).transpose(0, 1, 3, 2, 4).reshape(2 * size_y, -1),
        inverse_z.transpose(2, 3, 0, 1).reshape(2 * size_z, -1),
        forward_z.transpose(2, 3, 0, 1).reshape(2 * size_z, -1),
        forward_y.reshape(2 * size_y, -1),
        forward_y.reshape(2, pieces, columns, -1).transpose(1, 0, 2, 3).reshape(2 * size_y, -1),
        tables_back_x,
    ]
    (
        table_x_outer, table_x_inner, table_y_outer, table_y_inner, table_z,
        table_back_z, table_back_y_outer, table_back_y_inner, tables_back_x,
    ) = (jnp.asarray(t.astype(jnp.bfloat16)) for t in tables)

    table_back_x = lax.dynamic_index_in_dim(tables_back_x, slab, 0, keepdims=False)

    where = slab.reshape(1)
    section_outer = first_x(where, table_x_outer, coeffs, len(outer), pieces, False)
    def exchange(values):
        near, *far = values
        received = []
        for k, block in enumerate(far):
            pairs = [(j, j ^ (half + k)) for j in range(pieces)]
            received.append(lax.ppermute(block, "fft", pairs))
        halves = [list(range(half)), list(range(half, pieces))]
        near = lax.all_to_all(near, "fft", 0, 0, axis_index_groups=halves, tiled=True)
        return [near, *received]

    near, *far = exchange(section_outer)
    near, table_x_inner, sphere_blocks = lax.optimization_barrier(
        (near, table_x_inner, sphere_blocks)
    )
    received_outer = [near, *far]
    section_inner = first_x(where, table_x_inner, coeffs, len(inner), pieces, True)

    codes, steps = [], []
    for chunk, shift in ((outer, 0), (outer, -1), (outer, 1), (inner, 0)):
        owner = (slab + shift + pieces) % pieces
        numbers = lax.dynamic_slice_in_dim(sphere_blocks, owner * atom_dev, atom_dev, 0)
        plane = numbers // (size_y * zblocks) - slab * slab_planes
        rest = numbers % (size_y * zblocks)
        if chunk is outer:
            inside = ((plane >= 0) & (plane < EDGE)) | (
                (plane >= slab_planes - EDGE) & (plane < slab_planes)
            )
            plane = jnp.where(plane < EDGE, plane, plane - len(inner))
        else:
            inside = (plane >= EDGE) & (plane < slab_planes - EDGE)
            plane = plane - EDGE
        code = (rest % zblocks * len(chunk) + plane) * size_y + rest // zblocks
        codes.append(jnp.where(inside, code, -1).reshape(-1))
        steps.append(zblocks * len(chunk) * size_y)
    lists, counts = pl.pallas_call(
        functools.partial(list_kernel, steps=steps),
        in_specs=[SMEM_SPEC],
        out_specs=[SMEM_SPEC] * 2,
        out_shape=[
            jax.ShapeDtypeStruct((len(codes), atom_dev * blocks), jnp.int32),
            jax.ShapeDtypeStruct((len(codes),), jnp.int32),
        ],
        cost_estimate=COST,
        name="block_lists",
    )(jnp.stack(codes))

    strength = 3.0 * math.sqrt(cells * blocks) / nproj
    coupled = (coupling + coupling.T) * (0.5 * strength)
    coupled = jnp.broadcast_to(coupled.T[:, :, None], (nproj, nproj, cells))

    section_inner = list(section_inner)
    for k in range(1, half + 1):
        section_inner[k], received_outer[k] = lax.optimization_barrier(
            (section_inner[k], received_outer[k])
        )
    received_inner = exchange(section_inner)
    entries = atom_dev * blocks
    wave_outer, density_outer, rows_outer, to_previous, to_following = make_field(
        where, counts, lists, occupation, received_outer, table_y_outer, table_z, (0, 1, 2), steps[0],
        entries, False,
    )
    from_following = lax.ppermute(to_previous, "fft", down)
    from_previous = lax.ppermute(to_following, "fft", up)
    density_outer = lax.psum(density_outer, "band")
    wave_inner, density_inner, rows_inner = make_field(
        where, counts, lists, occupation, received_inner, table_y_inner, table_z, (3,), steps[3],
        entries, True,
    )
    projected, spread, spread_out = make_nonlocal(
        coupled, projectors, [rows_outer, rows_inner, from_following, from_previous]
    )
    spread_previous = lax.ppermute(spread_out, "fft", up)
    spread_following = lax.ppermute(spread_out, "fft", down)
    edge_steps = EDGE // PLANES
    inner_steps = len(inner) // PLANES
    back_inner = go_back(
        where, counts, lists, wave_inner, potential, table_back_z, table_back_y_inner, [spread], (3,),
        steps[3], lambda i: i + edge_steps, pieces, True,
    )
    back_inner, spread_previous, spread_following = lax.optimization_barrier(
        (back_inner, spread_previous, spread_following)
    )
    back_inner = exchange(back_inner)
    back_outer = go_back(
        where, counts, lists, wave_outer, potential, table_back_z, table_back_y_outer,
        [spread, spread_previous, spread_following], (0, 1, 2), steps[0],
        lambda i: jnp.where(i < edge_steps, i, i + inner_steps), pieces, False,
    )
    density_inner, density_outer = lax.optimization_barrier((density_inner, density_outer))
    density_inner = lax.psum(density_inner, "band")
    back_outer, density_outer = lax.optimization_barrier((back_outer, density_outer))
    back_outer = exchange(back_outer)
    back_inner = [
        jnp.swapaxes(b.reshape(*b.shape[:-2], 2, columns, size_z), -4, -2).reshape(
            *b.shape[:-3], columns, -1, size_z
        )
        for b in back_inner
    ]
    density = jnp.concatenate([density_outer[:EDGE], density_inner, density_outer[EDGE:]], axis=0)

    index_x = np.arange(size_x)
    frequency_x = jnp.asarray(
        (np.where(2 * index_x < size_x, index_x, index_x - size_x) / size_x) ** 2, jnp.float32
    )
    index_y = slab * columns + jnp.arange(columns, dtype=jnp.int32)
    index_z = jnp.arange(size_z, dtype=jnp.int32)
    frequency_yz = wave_squares(index_y, size_y)[:, None] + wave_squares(index_z, size_z)[None, :]
    coeffs, density, back_inner = lax.optimization_barrier((coeffs, density, back_inner))
    applied = last_x(frequency_x, frequency_yz, table_back_x, coeffs, back_outer + back_inner)
    return (applied[None], density, projected[None, :, :, :, 0])


def per_device(wave_coeffs, occupation, potential, projectors, coupling, sphere_blocks):
    pieces, bands = lax.axis_size("fft"), lax.axis_size("band")
    size_z = wave_coeffs.shape[4]
    columns = wave_coeffs.shape[3]
    slab_planes = potential.shape[0]
    chunked = (
        pieces >= 4
        and pieces & (pieces - 1) == 0
        and slab_planes % EDGE == 0
        and slab_planes >= 3 * EDGE
        and EDGE >= HALO
        and columns % 8 == 0
        and size_z % 256 == 0
        and projectors.shape[0] % bands == 0
        and projectors.shape[3] == 128
        and projectors.shape[1] == 8
    )
    chosen = per_device_chunked if chunked else per_device_plain
    return chosen(wave_coeffs, occupation, potential, projectors, coupling, sphere_blocks)


def solution(mesh):
    placed = (
        P("band", None, None, "fft", None),
        P("band", None),
        P("fft", None, None),
        P("fft", None, None, None),
        P(),
        P(),
    )
    return jax.shard_map(
        per_device,
        mesh=mesh,
        in_specs=placed,
        out_specs=(
            P("band", None, None, "fft", None),
            P("fft", None, None),
            P("band", "fft", None, None),
        ),
        check_vma=False,
    )
```

```python
import functools
import math

import jax
import jax.numpy as jnp
import numpy as np
from jax import lax
from jax.experimental import pallas as pl
from jax.experimental.pallas import tpu as pltpu
from jax.sharding import PartitionSpec as P

HALO = 6
EDGE = 8
PLANES = 4
COLUMNS = 8
VMEM_BYTES = 56 * 1024 * 1024
COST = pl.CostEstimate(flops=1024, bytes_accessed=1024, transcendentals=0)


def extended(shard, sides, width):
    for axis, dim in sides:
        count, length = (lax.axis_size(axis), shard.shape[dim])
        up = [(i, (i + 1) % count) for i in range(count)]
        down = [(j, i) for i, j in up]
        last = lax.slice_in_dim(shard, length - width, length, axis=dim)
        first = lax.slice_in_dim(shard, 0, width, axis=dim)
        before = lax.ppermute(last, axis, up)
        after = lax.ppermute(first, axis, down)
        shard = jnp.concatenate([before, shard, after], axis=dim)
    return shard


def dft_table(length, sign_value):
    indices = jnp.arange(length, dtype=jnp.int32)
    phases = indices[:, None] * indices[None, :] % length
    angles = 2.0 * math.pi / length * phases.astype(jnp.float32)
    factor = 1.0 / math.sqrt(length)
    cosine = jnp.cos(angles) * factor
    sine_part = jnp.sin(angles) * (sign_value * factor)
    upper_rows = jnp.stack([cosine, -sine_part])
    bottom = jnp.stack([sine_part, cosine])
    return jnp.stack([upper_rows, bottom]).astype(jnp.bfloat16)


def wave_squares(indices, length):
    frequency = (
        jnp.where(2 * indices < length, indices, indices - length).astype(jnp.float32) / length
    )
    return frequency * frequency


def per_device_plain(wave_coeffs, occupation, potential, projectors, coupling, sphere_blocks):
    pieces = lax.axis_size("fft")
    slab_index = lax.axis_index("fft")
    coeffs = wave_coeffs[0]
    size_x = coeffs.shape[1]
    columns = coeffs.shape[2]
    size_z = coeffs.shape[3]
    slab_planes = potential.shape[0]
    size_y = potential.shape[1]
    atom_dev = projectors.shape[0]
    nproj_count = projectors.shape[1]
    block_cells = projectors.shape[3]
    zblocks = size_z // block_cells
    plane_blocks = size_y * zblocks
    total_atoms = atom_dev * pieces
    table_x = dft_table(size_x, 1.0).transpose(0, 2, 1, 3).reshape(2 * size_x, 2 * size_x)
    inverse_y = dft_table(size_y, 1.0)
    inverse_z = dft_table(size_z, 1.0)
    flattened = coeffs.reshape(2 * size_x, columns * size_z)
    along_x = jnp.dot(table_x, flattened, preferred_element_type=jnp.float32)
    along_x = along_x.reshape(2, size_x, columns, size_z).astype(jnp.bfloat16)
    along_y = jnp.einsum(
        "abyk,bxkz->axyz",
        inverse_y,
        lax.all_to_all(along_x, "fft", split_axis=1, concat_axis=2, tiled=True),
        preferred_element_type=jnp.float32,
    ).astype(jnp.bfloat16)
    wave_field = jnp.einsum(
        "abzk,bxyk->axyz", inverse_z, along_y, preferred_element_type=jnp.float32
    ).astype(jnp.bfloat16)
    weights = occupation[0]
    real_part = wave_field[0].astype(jnp.float32)
    imag_part = wave_field[1].astype(jnp.float32)
    partial_density = weights[0] * real_part * real_part + weights[1] * imag_part * imag_part
    density = lax.psum(partial_density.astype(jnp.bfloat16), "band")
    strength = 3.0 * math.sqrt(block_cells * projectors.shape[2]) / nproj_count
    coupled = (coupling + coupling.T) * (0.5 * strength)
    nearby = extended(projectors, (("fft", 0),), atom_dev)
    atom_rows = (
        slab_index * atom_dev - atom_dev + jnp.arange(3 * atom_dev, dtype=jnp.int32) + total_atoms
    ) % total_atoms
    near_blocks = sphere_blocks[atom_rows]
    plane_index = near_blocks // plane_blocks
    inside = plane_index // slab_planes == slab_index
    local_index = jnp.where(
        inside,
        (plane_index - slab_index * slab_planes) * plane_blocks + near_blocks % plane_blocks,
        0,
    )
    blocks_own = wave_field.reshape(2, slab_planes * plane_blocks, block_cells)
    gathered = blocks_own[:, local_index] * inside[None, :, :, None].astype(jnp.bfloat16)
    partial_value = jnp.einsum(
        "ajsk,bask->abj", nearby, gathered, preferred_element_type=jnp.float32
    )
    summed = extended(partial_value, (("fft", 0),), atom_dev)
    projections_own = (
        summed[:atom_dev] + summed[2 * atom_dev : 3 * atom_dev] + summed[4 * atom_dev :]
    )
    energy_own = jnp.einsum(
        "ij,abj->abi", coupled, projections_own, precision=lax.Precision.HIGHEST
    )
    energy = extended(energy_own, (("fft", 0),), atom_dev)
    spread = jnp.einsum(
        "ajsk,abj->bask", nearby.astype(jnp.float32), energy, precision=lax.Precision.HIGHEST
    )
    spread = spread * inside[None, :, :, None].astype(jnp.float32)
    accumulated = (
        jnp.zeros((2, slab_planes * plane_blocks, block_cells), jnp.float32)
        .at[:, local_index]
        .add(spread)
    )
    nonlocal_term = accumulated.reshape(2, slab_planes, size_y, size_z)
    total_field = (
        potential.astype(jnp.float32)[None] * wave_field.astype(jnp.float32) + nonlocal_term
    ).astype(jnp.bfloat16)
    forward_z = dft_table(size_z, -1.0)
    forward_y = dft_table(size_y, -1.0)
    forward_x = dft_table(size_x, -1.0)
    back_z = jnp.einsum(
        "abzk,bxyk->axyz", forward_z, total_field, preferred_element_type=jnp.float32
    ).astype(jnp.bfloat16)
    back_y = jnp.einsum(
        "abyk,bxkz->axyz", forward_y, back_z, preferred_element_type=jnp.float32
    ).astype(jnp.bfloat16)
    transformed = jnp.einsum(
        "abxk,bkyz->axyz",
        forward_x,
        lax.all_to_all(back_y, "fft", split_axis=2, concat_axis=1, tiled=True),
        preferred_element_type=jnp.float32,
    )
    index_x = jnp.arange(size_x, dtype=jnp.int32)
    index_y = slab_index * columns + jnp.arange(columns, dtype=jnp.int32)
    index_z = jnp.arange(size_z, dtype=jnp.int32)
    kinetic = (
        wave_squares(index_x, size_x)[:, None, None]
        + wave_squares(index_y, size_y)[None, :, None]
        + wave_squares(index_z, size_z)[None, None, :]
    )
    applied = (transformed + kinetic[None] * coeffs.astype(jnp.float32)).astype(jnp.bfloat16)
    return (applied[None], density, projections_own[None])


def real_blocks(length, sign):
    index = np.arange(length)
    angles = 2.0 * np.pi / length * (index[:, None] * index[None, :] % length)
    cosine = np.cos(angles) / np.sqrt(length)
    sine = sign * np.sin(angles) / np.sqrt(length)
    blocks = np.empty((2, length, 2, length))
    blocks[0, :, 0, :] = cosine
    blocks[1, :, 1, :] = cosine
    blocks[0, :, 1, :] = -sine
    blocks[1, :, 0, :] = sine
    return blocks


def chunk_planes(slab_planes):
    low, high = list(range(EDGE)), list(range(slab_planes - EDGE, slab_planes))
    return [low + high, list(range(EDGE, slab_planes - EDGE))]


def params(steps):
    return pltpu.CompilerParams(
        dimension_semantics=("arbitrary",) * steps, vmem_limit_bytes=VMEM_BYTES
    )


def whole(shape):
    return pl.BlockSpec(shape, lambda i: (0,) * len(shape))


SMEM_SPEC = pl.BlockSpec(memory_space=pltpu.SMEM)


def list_kernel(codes_ref, lists_ref, counts_ref, *, steps):
    groups, length = codes_ref.shape
    for group in range(groups):

        def body(i, count):
            code = codes_ref[group, i]
            lists_ref[group, count] = code + i * steps[group]
            return count + (code >= 0).astype(jnp.int32)

        counts_ref[group] = lax.fori_loop(0, length, body, jnp.int32(0), unroll=4)


def first_x_kernel(slab, table_ref, coeffs_ref, *refs, pieces, natural):
    outs, (turned, wide, *tall) = refs[:pieces], refs[pieces:]
    parts, size_x, columns, lanes = coeffs_ref.shape
    rows = parts * size_x
    height = table_ref.shape[0] // pieces

    for k in range(pieces):
        start = pl.multiple_of(lax.bitwise_xor(slab[0], jnp.int32(k)) * height, 16)
        turned[k * height : (k + 1) * height, :] = table_ref[pl.ds(start, height), :]

    def widen(k, carry):
        for part in range(parts):
            start = pl.multiple_of((part * size_x + k * 8) * columns, 8)
            wide[pl.ds(start, 8 * columns), :] = (
                coeffs_ref[part, pl.ds(k * 8, 8)].astype(jnp.float32).reshape(8 * columns, lanes)
            )
        return carry

    lax.fori_loop(0, size_x // 8, widen, 0, unroll=2)

    def some_columns(g, carry):
        loaded = [
            wide[pl.ds(COLUMNS * g + h, rows, stride=columns), :].astype(jnp.bfloat16)
            for h in range(COLUMNS)
        ]
        result = jnp.dot(
            turned[...], jnp.concatenate(loaded, axis=1), preferred_element_type=jnp.float32
        )
        for h in range(COLUMNS):
            piece = result[:, h * lanes : (h + 1) * lanes]
            if natural:
                tall[0][pl.ds(COLUMNS * g + h, piece.shape[0], stride=columns), :] = piece
            else:
                piece = piece.astype(jnp.bfloat16)
                for k in range(pieces):
                    outs[k][COLUMNS * g + h] = piece[k * height : (k + 1) * height]
        return carry

    lax.fori_loop(0, columns // COLUMNS, some_columns, 0)
    if natural:
        for k in range(pieces):
            values = tall[0][k * height * columns : (k + 1) * height * columns, :]
            outs[k][...] = values.astype(jnp.bfloat16).reshape(outs[k].shape)


def first_x(slab, table, coeffs, planes, pieces, natural):
    _, size_x, columns, size_z = coeffs.shape
    lanes = size_z // 2
    shape = (planes, 2 * columns) if natural else (columns, 2 * planes)
    scratch = [
        pltpu.VMEM(table.shape, jnp.bfloat16),
        pltpu.VMEM((2 * size_x * columns, lanes), jnp.float32),
    ]
    if natural:
        scratch.append(pltpu.VMEM((2 * pieces * planes * columns, lanes), jnp.float32))
    return pl.pallas_call(
        functools.partial(first_x_kernel, pieces=pieces, natural=natural),
        grid=(2,),
        in_specs=[
            SMEM_SPEC,
            whole(table.shape),
            pl.BlockSpec((2, size_x, columns, lanes), lambda i: (0, 0, 0, i)),
        ],
        out_specs=[pl.BlockSpec((*shape, lanes), lambda i: (0, 0, i)) for _ in range(pieces)],
        out_shape=[
            jax.ShapeDtypeStruct((*shape, size_z), jnp.bfloat16) for _ in range(pieces)
        ],
        scratch_shapes=scratch,
        compiler_params=params(1),
        cost_estimate=pl.CostEstimate(
            flops=8 * size_x * pieces * planes * columns * size_z,
            bytes_accessed=4 * (size_x + pieces * planes) * columns * size_z,
            transcendentals=0,
        ),
        name="first_x",
    )(slab, table, coeffs)


def unpack_entry(value, step):
    return lax.rem(value, step), lax.div(value, step)


def field_kernel(*refs, groups, step, pieces, natural):
    count = len(groups)
    slab, counts, lists, weights, table_y, table_z = refs[:6]
    bufs = refs[6 : 6 + pieces]
    wave, density = refs[6 + pieces : 8 + pieces]
    rows_out = refs[8 + pieces : 8 + pieces + count]
    rows_wide = refs[8 + pieces + count : 8 + pieces + 2 * count]
    field, wide = refs[8 + pieces + 2 * count :]
    sources = [lax.bitwise_xor(slab[0], jnp.int32(k)) for k in range(pieces)]
    _, near, size_y, size_z = wave.shape
    lanes = 128
    halves = size_z // lanes
    planes = field.shape[1] // (size_y * halves)
    i = pl.program_id(0)
    loaded = []
    if natural:
        for source, buf in zip(sources, bufs):
            wide[source] = buf[...]
        for h in range(near):
            loaded.append(wide[:, h].reshape(2 * size_y, size_z))
    else:
        columns, rows, _ = bufs[0].shape

        @pl.when(i == 0)
        def _():
            for source, buf in zip(sources, bufs):
                start = pl.multiple_of(source * columns * rows, 8)
                values = buf[...].astype(jnp.float32).reshape(columns * rows, size_z)
                for q in range(halves):
                    wide[q, pl.ds(start, columns * rows), :] = values[
                        :, q * lanes : (q + 1) * lanes
                    ]

        for h in range(near):
            plane = i * near + h
            both = [
                jnp.concatenate(
                    [
                        wide[q, pl.ds(part * planes + plane, size_y, stride=rows), :]
                        for q in range(halves)
                    ],
                    axis=1,
                ).astype(jnp.bfloat16)
                for part in range(2)
            ]
            loaded.append(jnp.concatenate(both, axis=0))
    along_y = jnp.dot(
        table_y[...], jnp.concatenate(loaded, axis=1), preferred_element_type=jnp.float32
    ).astype(jnp.bfloat16)
    turned = jnp.concatenate(
        [
            jnp.concatenate(
                [
                    along_y[:size_y, h * size_z : (h + 1) * size_z],
                    along_y[size_y:, h * size_z : (h + 1) * size_z],
                ],
                axis=1,
            )
            for h in range(near)
        ],
        axis=0,
    )
    result = jnp.dot(turned, table_z[...], preferred_element_type=jnp.float32).astype(jnp.bfloat16)
    for h in range(near):
        plane = i * near + h
        total = jnp.zeros((size_y, size_z), jnp.float32)
        for part in range(2):
            values = result[h * size_y : (h + 1) * size_y, part * size_z : (part + 1) * size_z]
            wave[part, h] = values
            values = values.astype(jnp.float32)
            total += weights[0, part] * values * values
            for q in range(halves):
                start = pl.multiple_of((q * planes + plane) * size_y, 8)
                field[part, pl.ds(start, size_y), :] = values[:, q * lanes : (q + 1) * lanes]
        density[h] = total.astype(jnp.bfloat16)

    @pl.when(i == pl.num_programs(0) - 1)
    def _():
        for group, out, rows in zip(groups, rows_out, rows_wide):
            rows[...] = jnp.zeros_like(rows)

            def body(k, carry):
                code, entry = unpack_entry(lists[group, k], step)
                for part in range(2):
                    rows[part, pl.ds(entry, 1), :] = field[part, pl.ds(code, 1), :]
                return carry

            lax.fori_loop(0, counts[group], body, 0)
            out[...] = rows[...].astype(jnp.bfloat16)


def make_field(slab, counts, lists, weights, bufs, table_y, table_z, groups, step, entries, natural):
    pieces, (*_, size_z) = len(bufs), bufs[0].shape
    if natural:
        planes, size_y = bufs[0].shape[0], pieces * bufs[0].shape[1] // 2
        buf_spec = pl.BlockSpec((PLANES, *bufs[0].shape[1:]), lambda i: (i, 0, 0))
        held = pltpu.VMEM((pieces, PLANES, *bufs[0].shape[1:]), jnp.bfloat16)
    else:
        planes, size_y = bufs[0].shape[1] // 2, pieces * bufs[0].shape[0]
        buf_spec = whole(bufs[0].shape)
        held = pltpu.VMEM((size_z // 128, 2 * planes * size_y, 128), jnp.float32)
    scratch = [pltpu.VMEM((2, entries, 128), jnp.float32) for _ in groups]
    scratch += [pltpu.VMEM((2, planes * size_y * size_z // 128, 128), jnp.float32), held]
    return pl.pallas_call(
        functools.partial(field_kernel, groups=groups, step=step, pieces=pieces, natural=natural),
        grid=(planes // PLANES,),
        in_specs=[SMEM_SPEC] * 4
        + [whole(table_y.shape), whole(table_z.shape)]
        + [buf_spec] * pieces,
        out_specs=[
            pl.BlockSpec((2, PLANES, size_y, size_z), lambda i: (0, i, 0, 0)),
            pl.BlockSpec((PLANES, size_y, size_z), lambda i: (i, 0, 0)),
        ]
        + [whole((2, entries, 128)) for _ in groups],
        out_shape=[
            jax.ShapeDtypeStruct((2, planes, size_y, size_z), jnp.bfloat16),
            jax.ShapeDtypeStruct((planes, size_y, size_z), jnp.bfloat16),
        ]
        + [jax.ShapeDtypeStruct((2, entries, 128), jnp.bfloat16) for _ in groups],
        scratch_shapes=scratch,
        compiler_params=params(1),
        cost_estimate=pl.CostEstimate(
            flops=8 * planes * size_y * size_z * (size_y + size_z),
            bytes_accessed=10 * planes * size_y * size_z,
            transcendentals=0,
        ),
        name="make_field",
    )(slab, counts, lists, weights, table_y, table_z, *bufs)


def nonlocal_kernel(coupled, projectors, *refs):
    parts, (projections, spread, spread_out) = refs[:-3], refs[-3:]
    atoms, nproj, blocks, cells = projectors.shape
    for atom in range(atoms):
        tables = [projectors[atom, j].astype(jnp.float32) for j in range(nproj)]
        place = pl.ds(atom * blocks, blocks)
        for part in range(2):
            rows = sum(p[part, place].astype(jnp.float32) for p in parts)
            tile = jnp.concatenate(
                [jnp.sum(t * rows, axis=0, keepdims=True) for t in tables], axis=0
            )
            mixed = jnp.zeros_like(tile)
            for j in range(nproj):
                mixed += coupled[j] * tile[j : j + 1]
            projections[atom, part] = jnp.broadcast_to(
                jnp.sum(tile, -1, keepdims=True), tile.shape
            )
            energy = jnp.broadcast_to(jnp.sum(mixed, -1, keepdims=True), tile.shape)
            result = sum(t * energy[j : j + 1] for j, t in enumerate(tables))
            spread[part, place] = result
            spread_out[part, place] = result.astype(jnp.bfloat16)


def make_nonlocal(coupled, projectors, parts):
    atoms, nproj, _, cells = projectors.shape
    return pl.pallas_call(
        nonlocal_kernel,
        out_shape=[
            jax.ShapeDtypeStruct((atoms, 2, nproj, cells), jnp.float32),
            jax.ShapeDtypeStruct(parts[0].shape, jnp.float32),
            jax.ShapeDtypeStruct(parts[0].shape, jnp.bfloat16),
        ],
        name="make_nonlocal",
    )(coupled, projectors, *parts)


def back_kernel(*refs, groups, step, pieces, natural):
    count = len(groups)
    slab, counts, lists, wave, potential, table_z, table_y = refs[:7]
    sources = refs[7 : 7 + count]
    outs = refs[7 + count : 7 + count + pieces]
    nonlocal_ref, spread, tall = refs[7 + count + pieces :]
    targets = [lax.bitwise_xor(slab[0], jnp.int32(k)) for k in range(pieces)]
    near, size_y, size_z = potential.shape
    lanes = 128
    halves = size_z // lanes
    planes = nonlocal_ref.shape[1] // (size_y * halves)
    i = pl.program_id(0)

    @pl.when(i == 0)
    def _():
        nonlocal_ref[...] = jnp.zeros_like(nonlocal_ref)
        for group, source in zip(groups, sources):
            spread[...] = source[...].astype(jnp.float32)

            def body(k, carry):
                code, entry = unpack_entry(lists[group, k], step)
                for part in range(2):
                    nonlocal_ref[part, pl.ds(code, 1), :] += spread[part, pl.ds(entry, 1), :]
                return carry

            lax.fori_loop(0, counts[group], body, 0)

    fields = []
    for h in range(near):
        local = potential[h].astype(jnp.float32)
        for part in range(2):
            extra = jnp.concatenate(
                [
                    nonlocal_ref[
                        part,
                        pl.ds(pl.multiple_of((q * planes + i * near + h) * size_y, 8), size_y),
                        :,
                    ]
                    for q in range(halves)
                ],
                axis=1,
            )
            fields.append((local * wave[part, h].astype(jnp.float32) + extra).astype(jnp.bfloat16))
    stacked = jnp.concatenate(
        [jnp.concatenate(fields[2 * h : 2 * h + 2], axis=1) for h in range(near)], axis=0
    )
    back_z = jnp.dot(stacked, table_z[...], preferred_element_type=jnp.float32).astype(jnp.bfloat16)
    turned = jnp.concatenate(
        [
            jnp.concatenate(
                [
                    back_z[h * size_y : (h + 1) * size_y, :size_z],
                    back_z[h * size_y : (h + 1) * size_y, size_z:],
                ],
                axis=0,
            )
            for h in range(near)
        ],
        axis=1,
    )
    back_y = jnp.dot(table_y[...], turned, preferred_element_type=jnp.float32)
    if natural:
        back_y = back_y.astype(jnp.bfloat16)
        for h in range(near):
            tall[:, h] = back_y[:, h * size_z : (h + 1) * size_z].reshape(
                pieces, outs[0].shape[1], size_z
            )
        for target, out in zip(targets, outs):
            out[...] = tall[target]
        return
    columns, rows, _ = outs[0].shape
    for h in range(near):
        for part in range(2):
            for q in range(halves):
                start = h * size_z + q * lanes
                tall[q, pl.ds(part * planes + i * near + h, size_y, stride=rows), :] = back_y[
                    part * size_y : (part + 1) * size_y, start : start + lanes
                ]

    @pl.when(i == pl.num_programs(0) - 1)
    def _():
        for target, out in zip(targets, outs):
            start = pl.multiple_of(target * columns * rows, 8)
            values = [tall[q, pl.ds(start, columns * rows), :] for q in range(halves)]
            out[...] = (
                jnp.concatenate(values, axis=1).astype(jnp.bfloat16).reshape(columns, rows, size_z)
            )


def go_back(slab, counts, lists, wave, potential, table_z, table_y, sources, groups, step, place,
            pieces, natural):
    _, planes, size_y, size_z = wave.shape
    columns = size_y // pieces
    scratch = [
        pltpu.VMEM((2, planes * size_y * size_z // 128, 128), jnp.float32),
        pltpu.VMEM(sources[0].shape, jnp.float32),
    ]
    if natural:
        shape = (planes, 2 * columns, size_z)
        out_spec = pl.BlockSpec((PLANES, 2 * columns, size_z), lambda i: (i, 0, 0))
        scratch.append(pltpu.VMEM((pieces, PLANES, 2 * columns, size_z), jnp.bfloat16))
    else:
        shape = (columns, 2 * planes, size_z)
        out_spec = whole(shape)
        scratch.append(pltpu.VMEM((size_z // 128, 2 * planes * size_y, 128), jnp.float32))
    return pl.pallas_call(
        functools.partial(back_kernel, groups=groups, step=step, pieces=pieces, natural=natural),
        grid=(planes // PLANES,),
        in_specs=[SMEM_SPEC] * 3
        + [
            pl.BlockSpec((2, PLANES, size_y, size_z), lambda i: (0, i, 0, 0)),
            pl.BlockSpec((PLANES, size_y, size_z), lambda i: (place(i), 0, 0)),
            whole(table_z.shape),
            whole(table_y.shape),
        ]
        + [whole(s.shape) for s in sources],
        out_specs=[out_spec] * pieces,
        out_shape=[jax.ShapeDtypeStruct(shape, jnp.bfloat16)] * pieces,
        scratch_shapes=scratch,
        compiler_params=params(1),
        cost_estimate=pl.CostEstimate(
            flops=8 * planes * size_y * size_z * (size_y + size_z),
            bytes_accessed=10 * planes * size_y * size_z,
            transcendentals=0,
        ),
        name="go_back",
    )(slab, counts, lists, wave, potential, table_z, table_y, *sources)


def last_x_kernel(frequency_x, frequency_yz, table, coeffs, *refs):
    bufs, (out, tall) = refs[:-2], refs[-2:]
    parts, size_x, columns, lanes = coeffs.shape

    def some_columns(g, carry):
        loaded = []
        for h in range(COLUMNS):
            loaded.append(jnp.concatenate([buf[COLUMNS * g + h] for buf in bufs], axis=0))
        result = jnp.dot(
            table[...], jnp.concatenate(loaded, axis=1), preferred_element_type=jnp.float32
        )
        for h in range(COLUMNS):
            tall[pl.ds(COLUMNS * g + h, parts * size_x, stride=columns), :] = result[
                :, h * lanes : (h + 1) * lanes
            ]
        return carry

    lax.fori_loop(0, columns // COLUMNS, some_columns, 0)

    def finish(k, carry):
        kinetic = frequency_x[k] + frequency_yz[...]
        for part in range(parts):
            start = pl.multiple_of((part * size_x + k) * columns, 8)
            out[part, k] = (
                tall[pl.ds(start, columns), :] + kinetic * coeffs[part, k].astype(jnp.float32)
            ).astype(jnp.bfloat16)
        return carry

    lax.fori_loop(0, size_x, finish, 0, unroll=8)


def last_x(frequency_x, frequency_yz, table, coeffs, bufs):
    _, size_x, columns, size_z = coeffs.shape
    lanes = size_z // 2
    spec = pl.BlockSpec((2, size_x, columns, lanes), lambda i: (0, 0, 0, i))
    return pl.pallas_call(
        last_x_kernel,
        grid=(2,),
        in_specs=[
            SMEM_SPEC,
            pl.BlockSpec((columns, lanes), lambda i: (0, i)),
            whole(table.shape),
            spec,
        ]
        + [pl.BlockSpec((*b.shape[:2], lanes), lambda i: (0, 0, i)) for b in bufs],
        out_specs=spec,
        out_shape=jax.ShapeDtypeStruct(coeffs.shape, jnp.bfloat16),
        scratch_shapes=[pltpu.VMEM((2 * size_x * columns, lanes), jnp.float32)],
        compiler_params=params(1),
        cost_estimate=pl.CostEstimate(
            flops=8 * size_x * size_x * columns * size_z,
            bytes_accessed=12 * size_x * columns * size_z,
            transcendentals=0,
        ),
        name="last_x",
    )(frequency_x, frequency_yz, table, coeffs, *bufs)


def per_device_chunked(wave_coeffs, occupation, potential, projectors, coupling, sphere_blocks):
    pieces = lax.axis_size("fft")
    bands = lax.axis_size("band")
    slab = lax.axis_index("fft")
    coeffs = wave_coeffs[0]
    _, size_x, columns, size_z = coeffs.shape
    slab_planes, size_y, _ = potential.shape
    atom_dev, nproj, blocks, cells = projectors.shape
    zblocks = size_z // cells
    outer, inner = chunk_planes(slab_planes)
    up = [(i, (i + 1) % pieces) for i in range(pieces)]
    down = [(j, i) for i, j in up]

    inverse_x, forward_x = (real_blocks(size_x, s) for s in (1.0, -1.0))
    inverse_y, forward_y = (real_blocks(size_y, s) for s in (1.0, -1.0))
    inverse_z, forward_z = (real_blocks(size_z, s) for s in (1.0, -1.0))
    place_outer, place_inner = (
        np.arange(pieces)[:, None] * slab_planes + np.array(chunk)[None, :]
        for chunk in (outer, inner)
    )
    table_x_outer = np.stack([inverse_x[r][place_outer] for r in range(2)], 1)
    table_x_inner = np.stack([inverse_x[r][place_inner] for r in range(2)], 2)
    tables_back_x = [
        np.stack([forward_x[:, :, r][:, :, place] for r in range(2)], 3).reshape(
            2 * size_x, pieces, -1
        )
        for place in (place_outer, place_inner)
    ]
    tables_back_x = np.stack(
        [
            np.concatenate(
                [t[:, np.arange(pieces) ^ d].reshape(2 * size_x, -1) for t in tables_back_x], axis=1
            )
            for d in range(pieces)
        ]
    )
    split_y = (2, size_y, 2, pieces, columns)
    tables = [
        table_x_outer.reshape(-1, 2 * size_x),
        table_x_inner.reshape(-1, 2 * size_x),
        inverse_y.reshape(2 * size_y, -1),
        inverse_y.reshape(split_y).transpose(0, 1, 3, 2, 4).reshape(2 * size_y, -1),
        inverse_z.transpose(2, 3, 0, 1).reshape(2 * size_z, -1),
        forward_z.transpose(2, 3, 0, 1).reshape(2 * size_z, -1),
        forward_y.reshape(2 * size_y, -1),
        forward_y.reshape(2, pieces, columns, -1).transpose(1, 0, 2, 3).reshape(2 * size_y, -1),
        tables_back_x,
    ]
    (
        table_x_outer, table_x_inner, table_y_outer, table_y_inner, table_z,
        table_back_z, table_back_y_outer, table_back_y_inner, tables_back_x,
    ) = (jnp.asarray(t.astype(jnp.bfloat16)) for t in tables)

    table_back_x = lax.dynamic_index_in_dim(tables_back_x, slab, 0, keepdims=False)

    where = slab.reshape(1)
    section_outer = first_x(where, table_x_outer, coeffs, len(outer), pieces, False)
    section_outer, table_x_inner, sphere_blocks = lax.optimization_barrier(
        (section_outer, table_x_inner, sphere_blocks)
    )
    section_inner = first_x(where, table_x_inner, coeffs, len(inner), pieces, True)

    codes, steps = [], []
    for chunk, shift in ((outer, 0), (outer, -1), (outer, 1), (inner, 0)):
        owner = (slab + shift + pieces) % pieces
        numbers = lax.dynamic_slice_in_dim(sphere_blocks, owner * atom_dev, atom_dev, 0)
        plane = numbers // (size_y * zblocks) - slab * slab_planes
        rest = numbers % (size_y * zblocks)
        if chunk is outer:
            inside = ((plane >= 0) & (plane < EDGE)) | (
                (plane >= slab_planes - EDGE) & (plane < slab_planes)
            )
            plane = jnp.where(plane < EDGE, plane, plane - len(inner))
        else:
            inside = (plane >= EDGE) & (plane < slab_planes - EDGE)
            plane = plane - EDGE
        code = (rest % zblocks * len(chunk) + plane) * size_y + rest // zblocks
        codes.append(jnp.where(inside, code, -1).reshape(-1))
        steps.append(zblocks * len(chunk) * size_y)
    lists, counts = pl.pallas_call(
        functools.partial(list_kernel, steps=steps),
        in_specs=[SMEM_SPEC],
        out_specs=[SMEM_SPEC] * 2,
        out_shape=[
            jax.ShapeDtypeStruct((len(codes), atom_dev * blocks), jnp.int32),
            jax.ShapeDtypeStruct((len(codes),), jnp.int32),
        ],
        name="block_lists",
    )(jnp.stack(codes))

    strength = 3.0 * math.sqrt(cells * blocks) / nproj
    coupled = (coupling + coupling.T) * (0.5 * strength)
    coupled = jnp.broadcast_to(coupled.T[:, :, None], (nproj, nproj, cells))

    def send(block, k):
        return lax.ppermute(block, "fft", [(j, j ^ k) for j in range(pieces)])

    def tied(first, second):
        return lax.optimization_barrier((first, second))

    half = pieces // 2
    sides = (list(range(1, half)), list(range(half, pieces)))

    def exchange(values):
        received = [values[0]] + [None] * (pieces - 1)
        for k in sides[1] + sides[0]:
            received[k] = send(values[k], k)
        return received

    sections = [list(section_outer), list(section_inner)]
    received = [[s[0]] + [None] * (pieces - 1) for s in sections]
    for side in sides:
        queue = [(c, k) for c in range(2) for k in side]
        for place, (c, k) in enumerate(queue):
            block = sections[c][k]
            if place >= 2:
                d, m = queue[place - 2]
                block, received[d][m] = tied(block, received[d][m])
            received[c][k] = send(block, k)
    received_outer, received_inner = received
    entries = atom_dev * blocks
    wave_outer, density_outer, rows_outer, to_previous, to_following = make_field(
        where, counts, lists, occupation, received_outer, table_y_outer, table_z, (0, 1, 2), steps[0],
        entries, False,
    )
    from_following = lax.ppermute(to_previous, "fft", down)
    from_previous = lax.ppermute(to_following, "fft", up)
    density_outer = lax.psum(density_outer, "band")
    wave_inner, density_inner, rows_inner = make_field(
        where, counts, lists, occupation, received_inner, table_y_inner, table_z, (3,), steps[3],
        entries, True,
    )
    projected, spread, spread_out = make_nonlocal(
        coupled, projectors, [rows_outer, rows_inner, from_following, from_previous]
    )
    spread_previous = lax.ppermute(spread_out, "fft", up)
    spread_following = lax.ppermute(spread_out, "fft", down)
    edge_steps = EDGE // PLANES
    inner_steps = len(inner) // PLANES
    back_inner = go_back(
        where, counts, lists, wave_inner, potential, table_back_z, table_back_y_inner, [spread], (3,),
        steps[3], lambda i: i + edge_steps, pieces, True,
    )
    back_inner, spread_previous, spread_following = lax.optimization_barrier(
        (back_inner, spread_previous, spread_following)
    )
    back_inner = exchange(back_inner)
    back_outer = go_back(
        where, counts, lists, wave_outer, potential, table_back_z, table_back_y_outer,
        [spread, spread_previous, spread_following], (0, 1, 2), steps[0],
        lambda i: jnp.where(i < edge_steps, i, i + inner_steps), pieces, False,
    )
    density_inner, density_outer = lax.optimization_barrier((density_inner, density_outer))
    density_inner = lax.psum(density_inner, "band")
    back_outer, density_outer = lax.optimization_barrier((back_outer, density_outer))
    back_outer = exchange(back_outer)
    back_inner = [
        b.reshape(len(inner), 2, columns, size_z).transpose(2, 1, 0, 3).reshape(columns, -1, size_z)
        for b in back_inner
    ]
    density = jnp.concatenate([density_outer[:EDGE], density_inner, density_outer[EDGE:]], axis=0)

    index_x = np.arange(size_x)
    frequency_x = jnp.asarray(
        (np.where(2 * index_x < size_x, index_x, index_x - size_x) / size_x) ** 2, jnp.float32
    )
    index_y = slab * columns + jnp.arange(columns, dtype=jnp.int32)
    index_z = jnp.arange(size_z, dtype=jnp.int32)
    frequency_yz = wave_squares(index_y, size_y)[:, None] + wave_squares(index_z, size_z)[None, :]
    coeffs, density, back_inner = lax.optimization_barrier((coeffs, density, back_inner))
    applied = last_x(frequency_x, frequency_yz, table_back_x, coeffs, back_outer + back_inner)
    return (applied[None], density, projected[None, :, :, :, 0])


def per_device(wave_coeffs, occupation, potential, projectors, coupling, sphere_blocks):
    pieces, bands = lax.axis_size("fft"), lax.axis_size("band")
    size_z = wave_coeffs.shape[4]
    columns = wave_coeffs.shape[3]
    slab_planes = potential.shape[0]
    chunked = (
        pieces >= 4
        and pieces & (pieces - 1) == 0
        and slab_planes % EDGE == 0
        and slab_planes >= 3 * EDGE
        and EDGE >= HALO
        and columns % 8 == 0
        and size_z % 256 == 0
        and projectors.shape[0] % bands == 0
        and projectors.shape[3] == 128
        and projectors.shape[1] == 8
    )
    chosen = per_device_chunked if chunked else per_device_plain
    return chosen(wave_coeffs, occupation, potential, projectors, coupling, sphere_blocks)


def solution(mesh):
    placed = (
        P("band", None, None, "fft", None),
        P("band", None),
        P("fft", None, None),
        P("fft", None, None, None),
        P(),
        P(),
    )
    return jax.shard_map(
        per_device,
        mesh=mesh,
        in_specs=placed,
        out_specs=(
            P("band", None, None, "fft", None),
            P("fft", None, None),
            P("band", "fft", None, None),
        ),
        check_vma=False,
    )
```

```python
import functools
import math

import jax
import jax.numpy as jnp
import numpy as np
from jax import lax
from jax.experimental import pallas as pl
from jax.experimental.pallas import tpu as pltpu
from jax.sharding import PartitionSpec as P

HALO = 6
EDGE = 8
PLANES = 4
COLUMNS = 8
VMEM_BYTES = 56 * 1024 * 1024


def extended(shard, sides, width):
    for axis, dim in sides:
        count, length = (lax.axis_size(axis), shard.shape[dim])
        up = [(i, (i + 1) % count) for i in range(count)]
        down = [(j, i) for i, j in up]
        last = lax.slice_in_dim(shard, length - width, length, axis=dim)
        first = lax.slice_in_dim(shard, 0, width, axis=dim)
        before = lax.ppermute(last, axis, up)
        after = lax.ppermute(first, axis, down)
        shard = jnp.concatenate([before, shard, after], axis=dim)
    return shard


def dft_table(length, sign_value):
    indices = jnp.arange(length, dtype=jnp.int32)
    phases = indices[:, None] * indices[None, :] % length
    angles = 2.0 * math.pi / length * phases.astype(jnp.float32)
    factor = 1.0 / math.sqrt(length)
    cosine = jnp.cos(angles) * factor
    sine_part = jnp.sin(angles) * (sign_value * factor)
    upper_rows = jnp.stack([cosine, -sine_part])
    bottom = jnp.stack([sine_part, cosine])
    return jnp.stack([upper_rows, bottom]).astype(jnp.bfloat16)


def wave_squares(indices, length):
    frequency = (
        jnp.where(2 * indices < length, indices, indices - length).astype(jnp.float32) / length
    )
    return frequency * frequency


def per_device_plain(wave_coeffs, occupation, potential, projectors, coupling, sphere_blocks):
    pieces = lax.axis_size("fft")
    slab_index = lax.axis_index("fft")
    coeffs = wave_coeffs[0]
    size_x = coeffs.shape[1]
    columns = coeffs.shape[2]
    size_z = coeffs.shape[3]
    slab_planes = potential.shape[0]
    size_y = potential.shape[1]
    atom_dev = projectors.shape[0]
    nproj_count = projectors.shape[1]
    block_cells = projectors.shape[3]
    zblocks = size_z // block_cells
    plane_blocks = size_y * zblocks
    total_atoms = atom_dev * pieces
    table_x = dft_table(size_x, 1.0).transpose(0, 2, 1, 3).reshape(2 * size_x, 2 * size_x)
    inverse_y = dft_table(size_y, 1.0)
    inverse_z = dft_table(size_z, 1.0)
    flattened = coeffs.reshape(2 * size_x, columns * size_z)
    along_x = jnp.dot(table_x, flattened, preferred_element_type=jnp.float32)
    along_x = along_x.reshape(2, size_x, columns, size_z).astype(jnp.bfloat16)
    along_y = jnp.einsum(
        "abyk,bxkz->axyz",
        inverse_y,
        lax.all_to_all(along_x, "fft", split_axis=1, concat_axis=2, tiled=True),
        preferred_element_type=jnp.float32,
    ).astype(jnp.bfloat16)
    wave_field = jnp.einsum(
        "abzk,bxyk->axyz", inverse_z, along_y, preferred_element_type=jnp.float32
    ).astype(jnp.bfloat16)
    weights = occupation[0]
    real_part = wave_field[0].astype(jnp.float32)
    imag_part = wave_field[1].astype(jnp.float32)
    partial_density = weights[0] * real_part * real_part + weights[1] * imag_part * imag_part
    density = lax.psum(partial_density.astype(jnp.bfloat16), "band")
    strength = 3.0 * math.sqrt(block_cells * projectors.shape[2]) / nproj_count
    coupled = (coupling + coupling.T) * (0.5 * strength)
    nearby = extended(projectors, (("fft", 0),), atom_dev)
    atom_rows = (
        slab_index * atom_dev - atom_dev + jnp.arange(3 * atom_dev, dtype=jnp.int32) + total_atoms
    ) % total_atoms
    near_blocks = sphere_blocks[atom_rows]
    plane_index = near_blocks // plane_blocks
    inside = plane_index // slab_planes == slab_index
    local_index = jnp.where(
        inside,
        (plane_index - slab_index * slab_planes) * plane_blocks + near_blocks % plane_blocks,
        0,
    )
    blocks_own = wave_field.reshape(2, slab_planes * plane_blocks, block_cells)
    gathered = blocks_own[:, local_index] * inside[None, :, :, None].astype(jnp.bfloat16)
    partial_value = jnp.einsum(
        "ajsk,bask->abj", nearby, gathered, preferred_element_type=jnp.float32
    )
    summed = extended(partial_value, (("fft", 0),), atom_dev)
    projections_own = (
        summed[:atom_dev] + summed[2 * atom_dev : 3 * atom_dev] + summed[4 * atom_dev :]
    )
    energy_own = jnp.einsum(
        "ij,abj->abi", coupled, projections_own, precision=lax.Precision.HIGHEST
    )
    energy = extended(energy_own, (("fft", 0),), atom_dev)
    spread = jnp.einsum(
        "ajsk,abj->bask", nearby.astype(jnp.float32), energy, precision=lax.Precision.HIGHEST
    )
    spread = spread * inside[None, :, :, None].astype(jnp.float32)
    accumulated = (
        jnp.zeros((2, slab_planes * plane_blocks, block_cells), jnp.float32)
        .at[:, local_index]
        .add(spread)
    )
    nonlocal_term = accumulated.reshape(2, slab_planes, size_y, size_z)
    total_field = (
        potential.astype(jnp.float32)[None] * wave_field.astype(jnp.float32) + nonlocal_term
    ).astype(jnp.bfloat16)
    forward_z = dft_table(size_z, -1.0)
    forward_y = dft_table(size_y, -1.0)
    forward_x = dft_table(size_x, -1.0)
    back_z = jnp.einsum(
        "abzk,bxyk->axyz", forward_z, total_field, preferred_element_type=jnp.float32
    ).astype(jnp.bfloat16)
    back_y = jnp.einsum(
        "abyk,bxkz->axyz", forward_y, back_z, preferred_element_type=jnp.float32
    ).astype(jnp.bfloat16)
    transformed = jnp.einsum(
        "abxk,bkyz->axyz",
        forward_x,
        lax.all_to_all(back_y, "fft", split_axis=2, concat_axis=1, tiled=True),
        preferred_element_type=jnp.float32,
    )
    index_x = jnp.arange(size_x, dtype=jnp.int32)
    index_y = slab_index * columns + jnp.arange(columns, dtype=jnp.int32)
    index_z = jnp.arange(size_z, dtype=jnp.int32)
    kinetic = (
        wave_squares(index_x, size_x)[:, None, None]
        + wave_squares(index_y, size_y)[None, :, None]
        + wave_squares(index_z, size_z)[None, None, :]
    )
    applied = (transformed + kinetic[None] * coeffs.astype(jnp.float32)).astype(jnp.bfloat16)
    return (applied[None], density, projections_own[None])


def real_blocks(length, sign):
    index = np.arange(length)
    angles = 2.0 * np.pi / length * (index[:, None] * index[None, :] % length)
    cosine = np.cos(angles) / np.sqrt(length)
    sine = sign * np.sin(angles) / np.sqrt(length)
    blocks = np.empty((2, length, 2, length))
    blocks[0, :, 0, :] = cosine
    blocks[1, :, 1, :] = cosine
    blocks[0, :, 1, :] = -sine
    blocks[1, :, 0, :] = sine
    return blocks


def chunk_planes(slab_planes):
    low, high = list(range(EDGE)), list(range(slab_planes - EDGE, slab_planes))
    return [low + high, list(range(EDGE, slab_planes - EDGE))]


def params(steps):
    return pltpu.CompilerParams(
        dimension_semantics=("arbitrary",) * steps, vmem_limit_bytes=VMEM_BYTES
    )


def cost(microseconds):
    return pl.CostEstimate(
        flops=microseconds * 10**9, bytes_accessed=2**20, transcendentals=0
    )


def whole(shape):
    return pl.BlockSpec(shape, lambda i: (0,) * len(shape))


SMEM_SPEC = pl.BlockSpec(memory_space=pltpu.SMEM)


def list_kernel(codes_ref, lists_ref, counts_ref, *, steps):
    groups, length = codes_ref.shape
    for group in range(groups):

        def body(i, count):
            code = codes_ref[group, i]
            lists_ref[group, count] = code + i * steps[group]
            return count + (code >= 0).astype(jnp.int32)

        counts_ref[group] = lax.fori_loop(0, length, body, jnp.int32(0), unroll=4)


def slots(near, far, slab):
    half = len(far)
    first = slab - lax.rem(slab, half)
    views = [near.at[j] for j in range(half)] + list(far)
    devices = [first + j for j in range(half)]
    devices += [lax.bitwise_xor(slab, jnp.int32(half + k)) for k in range(half)]
    return list(zip(devices, views))


def first_x_kernel(slab, table_ref, coeffs_ref, *refs, pieces, natural):
    half = pieces // 2
    near, far, (turned, wide, *tall) = refs[0], refs[1 : half + 1], refs[half + 1 :]
    outs = slots(near, far, slab[0])
    parts, size_x, columns, lanes = coeffs_ref.shape
    rows = parts * size_x
    height = table_ref.shape[0] // pieces

    for k, (device, _) in enumerate(outs):
        start = pl.multiple_of(device * height, 16)
        turned[k * height : (k + 1) * height, :] = table_ref[pl.ds(start, height), :]

    def widen(k, carry):
        for part in range(parts):
            start = pl.multiple_of((part * size_x + k * 8) * columns, 8)
            wide[pl.ds(start, 8 * columns), :] = (
                coeffs_ref[part, pl.ds(k * 8, 8)].astype(jnp.float32).reshape(8 * columns, lanes)
            )
        return carry

    lax.fori_loop(0, size_x // 8, widen, 0, unroll=2)

    def some_columns(g, carry):
        loaded = [
            wide[pl.ds(COLUMNS * g + h, rows, stride=columns), :].astype(jnp.bfloat16)
            for h in range(COLUMNS)
        ]
        result = jnp.dot(
            turned[...], jnp.concatenate(loaded, axis=1), preferred_element_type=jnp.float32
        )
        for h in range(COLUMNS):
            piece = result[:, h * lanes : (h + 1) * lanes]
            if natural:
                tall[0][pl.ds(COLUMNS * g + h, piece.shape[0], stride=columns), :] = piece
            else:
                piece = piece.astype(jnp.bfloat16)
                for k, (_, out) in enumerate(outs):
                    out[COLUMNS * g + h] = piece[k * height : (k + 1) * height]
        return carry

    lax.fori_loop(0, columns // COLUMNS, some_columns, 0)
    if natural:
        for k, (_, out) in enumerate(outs):
            values = tall[0][k * height * columns : (k + 1) * height * columns, :]
            out[...] = values.astype(jnp.bfloat16).reshape(out.shape)


def first_x(slab, table, coeffs, planes, pieces, natural):
    _, size_x, columns, size_z = coeffs.shape
    lanes, half = size_z // 2, pieces // 2
    shape = (planes, 2 * columns) if natural else (columns, 2 * planes)
    scratch = [
        pltpu.VMEM(table.shape, jnp.bfloat16),
        pltpu.VMEM((2 * size_x * columns, lanes), jnp.float32),
    ]
    if natural:
        scratch.append(pltpu.VMEM((2 * pieces * planes * columns, lanes), jnp.float32))
    return pl.pallas_call(
        functools.partial(first_x_kernel, pieces=pieces, natural=natural),
        grid=(2,),
        in_specs=[
            SMEM_SPEC,
            whole(table.shape),
            pl.BlockSpec((2, size_x, columns, lanes), lambda i: (0, 0, 0, i)),
        ],
        out_specs=[pl.BlockSpec((half, *shape, lanes), lambda i: (0, 0, 0, i))]
        + [pl.BlockSpec((*shape, lanes), lambda i: (0, 0, i))] * half,
        out_shape=[jax.ShapeDtypeStruct((half, *shape, size_z), jnp.bfloat16)]
        + [jax.ShapeDtypeStruct((*shape, size_z), jnp.bfloat16)] * half,
        scratch_shapes=scratch,
        compiler_params=params(1),
        cost_estimate=cost(6),
        name="first_x",
    )(slab, table, coeffs)


def unpack_entry(value, step):
    return lax.rem(value, step), lax.div(value, step)


def field_kernel(*refs, groups, step, pieces, natural):
    count = len(groups)
    slab, counts, lists, weights, table_y, table_z = refs[:6]
    half = pieces // 2
    bufs = slots(refs[6], refs[7 : 7 + half], slab[0])
    wave, density = refs[7 + half : 9 + half]
    rows_out = refs[9 + half : 9 + half + count]
    rows_wide = refs[9 + half + count : 9 + half + 2 * count]
    field, wide = refs[9 + half + 2 * count :]
    _, near, size_y, size_z = wave.shape
    lanes = 128
    halves = size_z // lanes
    planes = field.shape[1] // (size_y * halves)
    i = pl.program_id(0)
    loaded = []
    if natural:
        for source, buf in bufs:
            wide[source] = buf[...]
        for h in range(near):
            loaded.append(wide[:, h].reshape(2 * size_y, size_z))
    else:
        columns, rows, _ = bufs[0][1].shape

        @pl.when(i == 0)
        def _():
            for source, buf in bufs:
                start = pl.multiple_of(source * columns * rows, 8)
                values = buf[...].astype(jnp.float32).reshape(columns * rows, size_z)
                for q in range(halves):
                    wide[q, pl.ds(start, columns * rows), :] = values[
                        :, q * lanes : (q + 1) * lanes
                    ]

        for h in range(near):
            plane = i * near + h
            both = [
                jnp.concatenate(
                    [
                        wide[q, pl.ds(part * planes + plane, size_y, stride=rows), :]
                        for q in range(halves)
                    ],
                    axis=1,
                ).astype(jnp.bfloat16)
                for part in range(2)
            ]
            loaded.append(jnp.concatenate(both, axis=0))
    along_y = jnp.dot(
        table_y[...], jnp.concatenate(loaded, axis=1), preferred_element_type=jnp.float32
    ).astype(jnp.bfloat16)
    turned = jnp.concatenate(
        [
            jnp.concatenate(
                [
                    along_y[:size_y, h * size_z : (h + 1) * size_z],
                    along_y[size_y:, h * size_z : (h + 1) * size_z],
                ],
                axis=1,
            )
            for h in range(near)
        ],
        axis=0,
    )
    result = jnp.dot(turned, table_z[...], preferred_element_type=jnp.float32).astype(jnp.bfloat16)
    for h in range(near):
        plane = i * near + h
        total = jnp.zeros((size_y, size_z), jnp.float32)
        for part in range(2):
            values = result[h * size_y : (h + 1) * size_y, part * size_z : (part + 1) * size_z]
            wave[part, h] = values
            values = values.astype(jnp.float32)
            total += weights[0, part] * values * values
            for q in range(halves):
                start = pl.multiple_of((q * planes + plane) * size_y, 8)
                field[part, pl.ds(start, size_y), :] = values[:, q * lanes : (q + 1) * lanes]
        density[h] = total.astype(jnp.bfloat16)

    @pl.when(i == pl.num_programs(0) - 1)
    def _():
        for group, out, rows in zip(groups, rows_out, rows_wide):
            rows[...] = jnp.zeros_like(rows)

            def body(k, carry):
                code, entry = unpack_entry(lists[group, k], step)
                for part in range(2):
                    rows[part, pl.ds(entry, 1), :] = field[part, pl.ds(code, 1), :]
                return carry

            lax.fori_loop(0, counts[group], body, 0)
            out[...] = rows[...].astype(jnp.bfloat16)


def make_field(slab, counts, lists, weights, bufs, table_y, table_z, groups, step, entries, natural):
    half = len(bufs) - 1
    pieces, shape = 2 * half, bufs[1].shape
    size_z = shape[2]
    if natural:
        planes, size_y = shape[0], pieces * shape[1] // 2
        buf_specs = [pl.BlockSpec((half, PLANES, *shape[1:]), lambda i: (0, i, 0, 0))]
        buf_specs += [pl.BlockSpec((PLANES, *shape[1:]), lambda i: (i, 0, 0))] * half
        held = pltpu.VMEM((pieces, PLANES, *shape[1:]), jnp.bfloat16)
    else:
        planes, size_y = shape[1] // 2, pieces * shape[0]
        buf_specs = [whole(b.shape) for b in bufs]
        held = pltpu.VMEM((size_z // 128, 2 * planes * size_y, 128), jnp.float32)
    scratch = [pltpu.VMEM((2, entries, 128), jnp.float32) for _ in groups]
    scratch += [pltpu.VMEM((2, planes * size_y * size_z // 128, 128), jnp.float32), held]
    return pl.pallas_call(
        functools.partial(field_kernel, groups=groups, step=step, pieces=pieces, natural=natural),
        grid=(planes // PLANES,),
        in_specs=[SMEM_SPEC] * 4
        + [whole(table_y.shape), whole(table_z.shape)]
        + buf_specs,
        out_specs=[
            pl.BlockSpec((2, PLANES, size_y, size_z), lambda i: (0, i, 0, 0)),
            pl.BlockSpec((PLANES, size_y, size_z), lambda i: (i, 0, 0)),
        ]
        + [whole((2, entries, 128)) for _ in groups],
        out_shape=[
            jax.ShapeDtypeStruct((2, planes, size_y, size_z), jnp.bfloat16),
            jax.ShapeDtypeStruct((planes, size_y, size_z), jnp.bfloat16),
        ]
        + [jax.ShapeDtypeStruct((2, entries, 128), jnp.bfloat16) for _ in groups],
        scratch_shapes=scratch,
        compiler_params=params(1),
        cost_estimate=cost(planes),
        name="make_field",
    )(slab, counts, lists, weights, table_y, table_z, *bufs)


def nonlocal_kernel(coupled, projectors, *refs):
    parts, (projections, spread, spread_out) = refs[:-3], refs[-3:]
    atoms, nproj, blocks, cells = projectors.shape
    for atom in range(atoms):
        tables = [projectors[atom, j].astype(jnp.float32) for j in range(nproj)]
        place = pl.ds(atom * blocks, blocks)
        for part in range(2):
            rows = sum(p[part, place].astype(jnp.float32) for p in parts)
            tile = jnp.concatenate(
                [jnp.sum(t * rows, axis=0, keepdims=True) for t in tables], axis=0
            )
            mixed = jnp.zeros_like(tile)
            for j in range(nproj):
                mixed += coupled[j] * tile[j : j + 1]
            projections[atom, part] = jnp.broadcast_to(
                jnp.sum(tile, -1, keepdims=True), tile.shape
            )
            energy = jnp.broadcast_to(jnp.sum(mixed, -1, keepdims=True), tile.shape)
            result = sum(t * energy[j : j + 1] for j, t in enumerate(tables))
            spread[part, place] = result
            spread_out[part, place] = result.astype(jnp.bfloat16)


def make_nonlocal(coupled, projectors, parts):
    atoms, nproj, _, cells = projectors.shape
    return pl.pallas_call(
        nonlocal_kernel,
        out_shape=[
            jax.ShapeDtypeStruct((atoms, 2, nproj, cells), jnp.float32),
            jax.ShapeDtypeStruct(parts[0].shape, jnp.float32),
            jax.ShapeDtypeStruct(parts[0].shape, jnp.bfloat16),
        ],
        cost_estimate=cost(2),
        name="make_nonlocal",
    )(coupled, projectors, *parts)


def back_kernel(*refs, groups, step, pieces, natural):
    count = len(groups)
    slab, counts, lists, wave, potential, table_z, table_y = refs[:7]
    sources = refs[7 : 7 + count]
    near_out, *far_outs = refs[7 + count : 8 + count + pieces // 2]
    nonlocal_ref, spread, tall = refs[8 + count + pieces // 2 :]
    outs = slots(near_out, far_outs, slab[0])
    near, size_y, size_z = potential.shape
    lanes = 128
    halves = size_z // lanes
    planes = nonlocal_ref.shape[1] // (size_y * halves)
    i = pl.program_id(0)

    @pl.when(i == 0)
    def _():
        nonlocal_ref[...] = jnp.zeros_like(nonlocal_ref)
        for group, source in zip(groups, sources):
            spread[...] = source[...].astype(jnp.float32)

            def body(k, carry):
                code, entry = unpack_entry(lists[group, k], step)
                for part in range(2):
                    nonlocal_ref[part, pl.ds(code, 1), :] += spread[part, pl.ds(entry, 1), :]
                return carry

            lax.fori_loop(0, counts[group], body, 0)

    fields = []
    for h in range(near):
        local = potential[h].astype(jnp.float32)
        for part in range(2):
            extra = jnp.concatenate(
                [
                    nonlocal_ref[
                        part,
                        pl.ds(pl.multiple_of((q * planes + i * near + h) * size_y, 8), size_y),
                        :,
                    ]
                    for q in range(halves)
                ],
                axis=1,
            )
            fields.append((local * wave[part, h].astype(jnp.float32) + extra).astype(jnp.bfloat16))
    stacked = jnp.concatenate(
        [jnp.concatenate(fields[2 * h : 2 * h + 2], axis=1) for h in range(near)], axis=0
    )
    back_z = jnp.dot(stacked, table_z[...], preferred_element_type=jnp.float32).astype(jnp.bfloat16)
    turned = jnp.concatenate(
        [
            jnp.concatenate(
                [
                    back_z[h * size_y : (h + 1) * size_y, :size_z],
                    back_z[h * size_y : (h + 1) * size_y, size_z:],
                ],
                axis=0,
            )
            for h in range(near)
        ],
        axis=1,
    )
    back_y = jnp.dot(table_y[...], turned, preferred_element_type=jnp.float32)
    if natural:
        back_y = back_y.astype(jnp.bfloat16)
        for h in range(near):
            tall[:, h] = back_y[:, h * size_z : (h + 1) * size_z].reshape(
                pieces, far_outs[0].shape[1], size_z
            )
        for target, out in outs:
            out[...] = tall[target]
        return
    columns, rows, _ = far_outs[0].shape
    for h in range(near):
        for part in range(2):
            for q in range(halves):
                start = h * size_z + q * lanes
                tall[q, pl.ds(part * planes + i * near + h, size_y, stride=rows), :] = back_y[
                    part * size_y : (part + 1) * size_y, start : start + lanes
                ]

    @pl.when(i == pl.num_programs(0) - 1)
    def _():
        for target, out in outs:
            start = pl.multiple_of(target * columns * rows, 8)
            values = [tall[q, pl.ds(start, columns * rows), :] for q in range(halves)]
            out[...] = (
                jnp.concatenate(values, axis=1).astype(jnp.bfloat16).reshape(columns, rows, size_z)
            )


def go_back(slab, counts, lists, wave, potential, table_z, table_y, sources, groups, step, place,
            pieces, natural):
    _, planes, size_y, size_z = wave.shape
    columns, half = size_y // pieces, pieces // 2
    scratch = [
        pltpu.VMEM((2, planes * size_y * size_z // 128, 128), jnp.float32),
        pltpu.VMEM(sources[0].shape, jnp.float32),
    ]
    if natural:
        shape = (planes, 2 * columns, size_z)
        out_specs = [pl.BlockSpec((half, PLANES, 2 * columns, size_z), lambda i: (0, i, 0, 0))]
        out_specs += [pl.BlockSpec((PLANES, 2 * columns, size_z), lambda i: (i, 0, 0))] * half
        scratch.append(pltpu.VMEM((pieces, PLANES, 2 * columns, size_z), jnp.bfloat16))
    else:
        shape = (columns, 2 * planes, size_z)
        out_specs = [whole((half, *shape))] + [whole(shape)] * half
        scratch.append(pltpu.VMEM((size_z // 128, 2 * planes * size_y, 128), jnp.float32))
    return pl.pallas_call(
        functools.partial(back_kernel, groups=groups, step=step, pieces=pieces, natural=natural),
        grid=(planes // PLANES,),
        in_specs=[SMEM_SPEC] * 3
        + [
            pl.BlockSpec((2, PLANES, size_y, size_z), lambda i: (0, i, 0, 0)),
            pl.BlockSpec((PLANES, size_y, size_z), lambda i: (place(i), 0, 0)),
            whole(table_z.shape),
            whole(table_y.shape),
        ]
        + [whole(s.shape) for s in sources],
        out_specs=out_specs,
        out_shape=[jax.ShapeDtypeStruct((half, *shape), jnp.bfloat16)]
        + [jax.ShapeDtypeStruct(shape, jnp.bfloat16)] * half,
        scratch_shapes=scratch,
        compiler_params=params(1),
        cost_estimate=cost(planes),
        name="go_back",
    )(slab, counts, lists, wave, potential, table_z, table_y, *sources)


def last_x_kernel(frequency_x, frequency_yz, table, coeffs, *refs):
    bufs, (out, tall) = refs[:-2], refs[-2:]
    parts, size_x, columns, lanes = coeffs.shape

    def some_columns(g, carry):
        loaded = []
        for h in range(COLUMNS):
            column = COLUMNS * g + h
            blocks = []
            for buf in bufs:
                if len(buf.shape) == 4:
                    blocks += [buf[j, column] for j in range(buf.shape[0])]
                else:
                    blocks.append(buf[column])
            loaded.append(jnp.concatenate(blocks, axis=0))
        result = jnp.dot(
            table[...], jnp.concatenate(loaded, axis=1), preferred_element_type=jnp.float32
        )
        for h in range(COLUMNS):
            tall[pl.ds(COLUMNS * g + h, parts * size_x, stride=columns), :] = result[
                :, h * lanes : (h + 1) * lanes
            ]
        return carry

    lax.fori_loop(0, columns // COLUMNS, some_columns, 0)

    def finish(k, carry):
        kinetic = frequency_x[k] + frequency_yz[...]
        for part in range(parts):
            start = pl.multiple_of((part * size_x + k) * columns, 8)
            out[part, k] = (
                tall[pl.ds(start, columns), :] + kinetic * coeffs[part, k].astype(jnp.float32)
            ).astype(jnp.bfloat16)
        return carry

    lax.fori_loop(0, size_x, finish, 0, unroll=8)


def last_x(frequency_x, frequency_yz, table, coeffs, bufs):
    _, size_x, columns, size_z = coeffs.shape
    lanes = size_z // 2
    spec = pl.BlockSpec((2, size_x, columns, lanes), lambda i: (0, 0, 0, i))
    return pl.pallas_call(
        last_x_kernel,
        grid=(2,),
        in_specs=[
            SMEM_SPEC,
            pl.BlockSpec((columns, lanes), lambda i: (0, i)),
            whole(table.shape),
            spec,
        ]
        + [
            pl.BlockSpec((*b.shape[:-1], lanes), lambda i, b=b: (0,) * (b.ndim - 1) + (i,))
            for b in bufs
        ],
        out_specs=spec,
        out_shape=jax.ShapeDtypeStruct(coeffs.shape, jnp.bfloat16),
        scratch_shapes=[pltpu.VMEM((2 * size_x * columns, lanes), jnp.float32)],
        compiler_params=params(1),
        cost_estimate=cost(9),
        name="last_x",
    )(frequency_x, frequency_yz, table, coeffs, *bufs)


def per_device_chunked(wave_coeffs, occupation, potential, projectors, coupling, sphere_blocks):
    pieces = lax.axis_size("fft")
    bands = lax.axis_size("band")
    slab = lax.axis_index("fft")
    coeffs = wave_coeffs[0]
    _, size_x, columns, size_z = coeffs.shape
    slab_planes, size_y, _ = potential.shape
    atom_dev, nproj, blocks, cells = projectors.shape
    zblocks = size_z // cells
    outer, inner = chunk_planes(slab_planes)
    up = [(i, (i + 1) % pieces) for i in range(pieces)]
    down = [(j, i) for i, j in up]

    inverse_x, forward_x = (real_blocks(size_x, s) for s in (1.0, -1.0))
    inverse_y, forward_y = (real_blocks(size_y, s) for s in (1.0, -1.0))
    inverse_z, forward_z = (real_blocks(size_z, s) for s in (1.0, -1.0))
    place_outer, place_inner = (
        np.arange(pieces)[:, None] * slab_planes + np.array(chunk)[None, :]
        for chunk in (outer, inner)
    )
    table_x_outer = np.stack([inverse_x[r][place_outer] for r in range(2)], 1)
    table_x_inner = np.stack([inverse_x[r][place_inner] for r in range(2)], 2)
    tables_back_x = [
        np.stack([forward_x[:, :, r][:, :, place] for r in range(2)], 3).reshape(
            2 * size_x, pieces, -1
        )
        for place in (place_outer, place_inner)
    ]
    half = pieces // 2
    orders = [
        [d - d % half + j for j in range(half)] + [d ^ (half + k) for k in range(half)]
        for d in range(pieces)
    ]
    tables_back_x = np.stack(
        [
            np.concatenate([t[:, order].reshape(2 * size_x, -1) for t in tables_back_x], axis=1)
            for order in orders
        ]
    )
    split_y = (2, size_y, 2, pieces, columns)
    tables = [
        table_x_outer.reshape(-1, 2 * size_x),
        table_x_inner.reshape(-1, 2 * size_x),
        inverse_y.reshape(2 * size_y, -1),
        inverse_y.reshape(split_y).transpose(0, 1, 3, 2, 4).reshape(2 * size_y, -1),
        inverse_z.transpose(2, 3, 0, 1).reshape(2 * size_z, -1),
        forward_z.transpose(2, 3, 0, 1).reshape(2 * size_z, -1),
        forward_y.reshape(2 * size_y, -1),
        forward_y.reshape(2, pieces, columns, -1).transpose(1, 0, 2, 3).reshape(2 * size_y, -1),
        tables_back_x,
    ]
    (
        table_x_outer, table_x_inner, table_y_outer, table_y_inner, table_z,
        table_back_z, table_back_y_outer, table_back_y_inner, tables_back_x,
    ) = (jnp.asarray(t.astype(jnp.bfloat16)) for t in tables)

    table_back_x = lax.dynamic_index_in_dim(tables_back_x, slab, 0, keepdims=False)

    where = slab.reshape(1)
    section_outer = first_x(where, table_x_outer, coeffs, len(outer), pieces, False)
    def exchange(values):
        near, *far = values
        received = []
        for k, block in enumerate(far):
            pairs = [(j, j ^ (half + k)) for j in range(pieces)]
            received.append(lax.ppermute(block, "fft", pairs))
        halves = [list(range(half)), list(range(half, pieces))]
        near = lax.all_to_all(near, "fft", 0, 0, axis_index_groups=halves, tiled=True)
        return [near, *received]

    section_outer, table_x_inner, sphere_blocks = lax.optimization_barrier(
        (section_outer, table_x_inner, sphere_blocks)
    )
    def exchange_after(values, others):
        values = list(values)
        for k in range(1, half + 1):
            values[k], others[k] = lax.optimization_barrier((values[k], others[k]))
        return exchange(values)

    received_outer = exchange(section_outer)
    section_inner = first_x(where, table_x_inner, coeffs, len(inner), pieces, True)

    codes, steps = [], []
    for chunk, shift in ((outer, 0), (outer, -1), (outer, 1), (inner, 0)):
        owner = (slab + shift + pieces) % pieces
        numbers = lax.dynamic_slice_in_dim(sphere_blocks, owner * atom_dev, atom_dev, 0)
        plane = numbers // (size_y * zblocks) - slab * slab_planes
        rest = numbers % (size_y * zblocks)
        if chunk is outer:
            inside = ((plane >= 0) & (plane < EDGE)) | (
                (plane >= slab_planes - EDGE) & (plane < slab_planes)
            )
            plane = jnp.where(plane < EDGE, plane, plane - len(inner))
        else:
            inside = (plane >= EDGE) & (plane < slab_planes - EDGE)
            plane = plane - EDGE
        code = (rest % zblocks * len(chunk) + plane) * size_y + rest // zblocks
        codes.append(jnp.where(inside, code, -1).reshape(-1))
        steps.append(zblocks * len(chunk) * size_y)
    lists, counts = pl.pallas_call(
        functools.partial(list_kernel, steps=steps),
        in_specs=[SMEM_SPEC],
        out_specs=[SMEM_SPEC] * 2,
        out_shape=[
            jax.ShapeDtypeStruct((len(codes), atom_dev * blocks), jnp.int32),
            jax.ShapeDtypeStruct((len(codes),), jnp.int32),
        ],
        cost_estimate=cost(7),
        name="block_lists",
    )(jnp.stack(codes))

    strength = 3.0 * math.sqrt(cells * blocks) / nproj
    coupled = (coupling + coupling.T) * (0.5 * strength)
    coupled = jnp.broadcast_to(coupled.T[:, :, None], (nproj, nproj, cells))

    received_inner = exchange_after(section_inner, received_outer)
    entries = atom_dev * blocks
    wave_outer, density_outer, rows_outer, to_previous, to_following = make_field(
        where, counts, lists, occupation, received_outer, table_y_outer, table_z, (0, 1, 2), steps[0],
        entries, False,
    )
    from_following = lax.ppermute(to_previous, "fft", down)
    from_previous = lax.ppermute(to_following, "fft", up)
    density_outer = lax.psum(density_outer, "band")
    wave_inner, density_inner, rows_inner = make_field(
        where, counts, lists, occupation, received_inner, table_y_inner, table_z, (3,), steps[3],
        entries, True,
    )
    projected, spread, spread_out = make_nonlocal(
        coupled, projectors, [rows_outer, rows_inner, from_following, from_previous]
    )
    spread_previous = lax.ppermute(spread_out, "fft", up)
    spread_following = lax.ppermute(spread_out, "fft", down)
    edge_steps = EDGE // PLANES
    inner_steps = len(inner) // PLANES
    back_inner = go_back(
        where, counts, lists, wave_inner, potential, table_back_z, table_back_y_inner, [spread], (3,),
        steps[3], lambda i: i + edge_steps, pieces, True,
    )
    back_inner, spread_previous, spread_following = lax.optimization_barrier(
        (back_inner, spread_previous, spread_following)
    )
    back_inner = exchange(back_inner)
    back_outer = go_back(
        where, counts, lists, wave_outer, potential, table_back_z, table_back_y_outer,
        [spread, spread_previous, spread_following], (0, 1, 2), steps[0],
        lambda i: jnp.where(i < edge_steps, i, i + inner_steps), pieces, False,
    )
    density_inner, density_outer = lax.optimization_barrier((density_inner, density_outer))
    density_inner = lax.psum(density_inner, "band")
    back_outer, density_outer = lax.optimization_barrier((back_outer, density_outer))
    back_outer = exchange_after(back_outer, back_inner)
    back_inner = [
        jnp.swapaxes(b.reshape(*b.shape[:-2], 2, columns, size_z), -4, -2).reshape(
            *b.shape[:-3], columns, -1, size_z
        )
        for b in back_inner
    ]
    density = jnp.concatenate([density_outer[:EDGE], density_inner, density_outer[EDGE:]], axis=0)

    index_x = np.arange(size_x)
    frequency_x = jnp.asarray(
        (np.where(2 * index_x < size_x, index_x, index_x - size_x) / size_x) ** 2, jnp.float32
    )
    index_y = slab * columns + jnp.arange(columns, dtype=jnp.int32)
    index_z = jnp.arange(size_z, dtype=jnp.int32)
    frequency_yz = wave_squares(index_y, size_y)[:, None] + wave_squares(index_z, size_z)[None, :]
    coeffs, density, back_inner = lax.optimization_barrier((coeffs, density, back_inner))
    applied = last_x(frequency_x, frequency_yz, table_back_x, coeffs, back_outer + back_inner)
    return (applied[None], density, projected[None, :, :, :, 0])


def per_device(wave_coeffs, occupation, potential, projectors, coupling, sphere_blocks):
    pieces, bands = lax.axis_size("fft"), lax.axis_size("band")
    size_z = wave_coeffs.shape[4]
    columns = wave_coeffs.shape[3]
    slab_planes = potential.shape[0]
    chunked = (
        pieces >= 4
        and pieces & (pieces - 1) == 0
        and slab_planes % EDGE == 0
        and slab_planes >= 3 * EDGE
        and EDGE >= HALO
        and columns % 8 == 0
        and size_z % 256 == 0
        and projectors.shape[0] % bands == 0
        and projectors.shape[3] == 128
        and projectors.shape[1] == 8
    )
    chosen = per_device_chunked if chunked else per_device_plain
    return chosen(wave_coeffs, occupation, potential, projectors, coupling, sphere_blocks)


def solution(mesh):
    placed = (
        P("band", None, None, "fft", None),
        P("band", None),
        P("fft", None, None),
        P("fft", None, None, None),
        P(),
        P(),
    )
    return jax.shard_map(
        per_device,
        mesh=mesh,
        in_specs=placed,
        out_specs=(
            P("band", None, None, "fft", None),
            P("fft", None, None),
            P("band", "fft", None, None),
        ),
        check_vma=False,
    )
```

```python
import functools
import math

import jax
import jax.numpy as jnp
import numpy as np
from jax import lax
from jax.experimental import pallas as pl
from jax.experimental.pallas import tpu as pltpu
from jax.sharding import PartitionSpec as P

HALO = 6
EDGE = 8
PLANES = 4
COLUMNS = 8
HELD = 4
VMEM_BYTES = 56 * 1024 * 1024


def extended(shard, sides, width):
    for axis, dim in sides:
        count, length = (lax.axis_size(axis), shard.shape[dim])
        up = [(i, (i + 1) % count) for i in range(count)]
        down = [(j, i) for i, j in up]
        last = lax.slice_in_dim(shard, length - width, length, axis=dim)
        first = lax.slice_in_dim(shard, 0, width, axis=dim)
        before = lax.ppermute(last, axis, up)
        after = lax.ppermute(first, axis, down)
        shard = jnp.concatenate([before, shard, after], axis=dim)
    return shard


def dft_table(length, sign_value):
    indices = jnp.arange(length, dtype=jnp.int32)
    phases = indices[:, None] * indices[None, :] % length
    angles = 2.0 * math.pi / length * phases.astype(jnp.float32)
    factor = 1.0 / math.sqrt(length)
    cosine = jnp.cos(angles) * factor
    sine_part = jnp.sin(angles) * (sign_value * factor)
    upper_rows = jnp.stack([cosine, -sine_part])
    bottom = jnp.stack([sine_part, cosine])
    return jnp.stack([upper_rows, bottom]).astype(jnp.bfloat16)


def wave_squares(indices, length):
    frequency = (
        jnp.where(2 * indices < length, indices, indices - length).astype(jnp.float32) / length
    )
    return frequency * frequency


def per_device_plain(wave_coeffs, occupation, potential, projectors, coupling, sphere_blocks):
    pieces = lax.axis_size("fft")
    slab_index = lax.axis_index("fft")
    coeffs = wave_coeffs[0]
    size_x = coeffs.shape[1]
    columns = coeffs.shape[2]
    size_z = coeffs.shape[3]
    slab_planes = potential.shape[0]
    size_y = potential.shape[1]
    atom_dev = projectors.shape[0]
    nproj_count = projectors.shape[1]
    block_cells = projectors.shape[3]
    zblocks = size_z // block_cells
    plane_blocks = size_y * zblocks
    total_atoms = atom_dev * pieces
    table_x = dft_table(size_x, 1.0).transpose(0, 2, 1, 3).reshape(2 * size_x, 2 * size_x)
    inverse_y = dft_table(size_y, 1.0)
    inverse_z = dft_table(size_z, 1.0)
    flattened = coeffs.reshape(2 * size_x, columns * size_z)
    along_x = jnp.dot(table_x, flattened, preferred_element_type=jnp.float32)
    along_x = along_x.reshape(2, size_x, columns, size_z).astype(jnp.bfloat16)
    along_y = jnp.einsum(
        "abyk,bxkz->axyz",
        inverse_y,
        lax.all_to_all(along_x, "fft", split_axis=1, concat_axis=2, tiled=True),
        preferred_element_type=jnp.float32,
    ).astype(jnp.bfloat16)
    wave_field = jnp.einsum(
        "abzk,bxyk->axyz", inverse_z, along_y, preferred_element_type=jnp.float32
    ).astype(jnp.bfloat16)
    weights = occupation[0]
    real_part = wave_field[0].astype(jnp.float32)
    imag_part = wave_field[1].astype(jnp.float32)
    partial_density = weights[0] * real_part * real_part + weights[1] * imag_part * imag_part
    density = lax.psum(partial_density.astype(jnp.bfloat16), "band")
    strength = 3.0 * math.sqrt(block_cells * projectors.shape[2]) / nproj_count
    coupled = (coupling + coupling.T) * (0.5 * strength)
    nearby = extended(projectors, (("fft", 0),), atom_dev)
    atom_rows = (
        slab_index * atom_dev - atom_dev + jnp.arange(3 * atom_dev, dtype=jnp.int32) + total_atoms
    ) % total_atoms
    near_blocks = sphere_blocks[atom_rows]
    plane_index = near_blocks // plane_blocks
    inside = plane_index // slab_planes == slab_index
    local_index = jnp.where(
        inside,
        (plane_index - slab_index * slab_planes) * plane_blocks + near_blocks % plane_blocks,
        0,
    )
    blocks_own = wave_field.reshape(2, slab_planes * plane_blocks, block_cells)
    gathered = blocks_own[:, local_index] * inside[None, :, :, None].astype(jnp.bfloat16)
    partial_value = jnp.einsum(
        "ajsk,bask->abj", nearby, gathered, preferred_element_type=jnp.float32
    )
    summed = extended(partial_value, (("fft", 0),), atom_dev)
    projections_own = (
        summed[:atom_dev] + summed[2 * atom_dev : 3 * atom_dev] + summed[4 * atom_dev :]
    )
    energy_own = jnp.einsum(
        "ij,abj->abi", coupled, projections_own, precision=lax.Precision.HIGHEST
    )
    energy = extended(energy_own, (("fft", 0),), atom_dev)
    spread = jnp.einsum(
        "ajsk,abj->bask", nearby.astype(jnp.float32), energy, precision=lax.Precision.HIGHEST
    )
    spread = spread * inside[None, :, :, None].astype(jnp.float32)
    accumulated = (
        jnp.zeros((2, slab_planes * plane_blocks, block_cells), jnp.float32)
        .at[:, local_index]
        .add(spread)
    )
    nonlocal_term = accumulated.reshape(2, slab_planes, size_y, size_z)
    total_field = (
        potential.astype(jnp.float32)[None] * wave_field.astype(jnp.float32) + nonlocal_term
    ).astype(jnp.bfloat16)
    forward_z = dft_table(size_z, -1.0)
    forward_y = dft_table(size_y, -1.0)
    forward_x = dft_table(size_x, -1.0)
    back_z = jnp.einsum(
        "abzk,bxyk->axyz", forward_z, total_field, preferred_element_type=jnp.float32
    ).astype(jnp.bfloat16)
    back_y = jnp.einsum(
        "abyk,bxkz->axyz", forward_y, back_z, preferred_element_type=jnp.float32
    ).astype(jnp.bfloat16)
    transformed = jnp.einsum(
        "abxk,bkyz->axyz",
        forward_x,
        lax.all_to_all(back_y, "fft", split_axis=2, concat_axis=1, tiled=True),
        preferred_element_type=jnp.float32,
    )
    index_x = jnp.arange(size_x, dtype=jnp.int32)
    index_y = slab_index * columns + jnp.arange(columns, dtype=jnp.int32)
    index_z = jnp.arange(size_z, dtype=jnp.int32)
    kinetic = (
        wave_squares(index_x, size_x)[:, None, None]
        + wave_squares(index_y, size_y)[None, :, None]
        + wave_squares(index_z, size_z)[None, None, :]
    )
    applied = (transformed + kinetic[None] * coeffs.astype(jnp.float32)).astype(jnp.bfloat16)
    return (applied[None], density, projections_own[None])


def real_blocks(length, sign):
    index = np.arange(length)
    angles = 2.0 * np.pi / length * (index[:, None] * index[None, :] % length)
    cosine = np.cos(angles) / np.sqrt(length)
    sine = sign * np.sin(angles) / np.sqrt(length)
    blocks = np.empty((2, length, 2, length))
    blocks[0, :, 0, :] = cosine
    blocks[1, :, 1, :] = cosine
    blocks[0, :, 1, :] = -sine
    blocks[1, :, 0, :] = sine
    return blocks


def chunk_planes(slab_planes):
    low, high = list(range(EDGE)), list(range(slab_planes - EDGE, slab_planes))
    return [low + high, list(range(EDGE, slab_planes - EDGE))]


def params(steps):
    return pltpu.CompilerParams(
        dimension_semantics=("arbitrary",) * steps, vmem_limit_bytes=VMEM_BYTES
    )


def cost(microseconds):
    return pl.CostEstimate(
        flops=microseconds * 10**9, bytes_accessed=2**20, transcendentals=0
    )


def whole(shape):
    return pl.BlockSpec(shape, lambda i: (0,) * len(shape))


SMEM_SPEC = pl.BlockSpec(memory_space=pltpu.SMEM)


def blocks_of(refs, slab, pieces, step):
    if len(refs) == 1:
        return [(d, refs[0].at[d]) for d in range(pieces)]
    return [(lax.rem(slab + (pieces + step * k), pieces), ref) for k, ref in enumerate(refs)]


def first_x_kernel(slab, table_ref, coeffs_ref, *refs, pieces, natural):
    scratch = 3 if natural else 2
    outs = blocks_of(refs[:-scratch], slab[0], pieces, 1)
    turned, wide, *tall = refs[-scratch:]
    parts, size_x, columns, lanes = coeffs_ref.shape
    rows = parts * size_x
    height = table_ref.shape[0] // pieces

    for k, (device, _) in enumerate(outs):
        start = pl.multiple_of(device * height, 16)
        turned[k * height : (k + 1) * height, :] = table_ref[pl.ds(start, height), :]

    def widen(k, carry):
        for part in range(parts):
            start = pl.multiple_of((part * size_x + k * 8) * columns, 8)
            wide[pl.ds(start, 8 * columns), :] = (
                coeffs_ref[part, pl.ds(k * 8, 8)].astype(jnp.float32).reshape(8 * columns, lanes)
            )
        return carry

    lax.fori_loop(0, size_x // 8, widen, 0, unroll=2)

    def some_columns(g, carry):
        loaded = [
            wide[pl.ds(COLUMNS * g + h, rows, stride=columns), :].astype(jnp.bfloat16)
            for h in range(COLUMNS)
        ]
        result = jnp.dot(
            turned[...], jnp.concatenate(loaded, axis=1), preferred_element_type=jnp.float32
        )
        for h in range(COLUMNS):
            piece = result[:, h * lanes : (h + 1) * lanes]
            if natural:
                tall[0][pl.ds(COLUMNS * g + h, piece.shape[0], stride=columns), :] = piece
            else:
                piece = piece.astype(jnp.bfloat16)
                for k, (_, out) in enumerate(outs):
                    out[COLUMNS * g + h] = piece[k * height : (k + 1) * height]
        return carry

    lax.fori_loop(0, columns // COLUMNS, some_columns, 0)
    if natural:
        for k, (_, out) in enumerate(outs):
            values = tall[0][k * height * columns : (k + 1) * height * columns, :]
            out[...] = values.astype(jnp.bfloat16).reshape(out.shape)


def first_x(slab, table, coeffs, planes, pieces, natural):
    _, size_x, columns, size_z = coeffs.shape
    lanes = size_z // 2
    shape = (planes, 2 * columns) if natural else (columns, 2 * planes)
    scratch = [
        pltpu.VMEM(table.shape, jnp.bfloat16),
        pltpu.VMEM((2 * size_x * columns, lanes), jnp.float32),
    ]
    if natural:
        scratch.append(pltpu.VMEM((2 * pieces * planes * columns, lanes), jnp.float32))
        out_specs = [pl.BlockSpec((pieces, *shape, lanes), lambda i: (0, 0, 0, i))]
        out_shape = [jax.ShapeDtypeStruct((pieces, *shape, size_z), jnp.bfloat16)]
    else:
        out_specs = [pl.BlockSpec((*shape, lanes), lambda i: (0, 0, i))] * pieces
        out_shape = [jax.ShapeDtypeStruct((*shape, size_z), jnp.bfloat16)] * pieces
    return pl.pallas_call(
        functools.partial(first_x_kernel, pieces=pieces, natural=natural),
        grid=(2,),
        in_specs=[
            SMEM_SPEC,
            whole(table.shape),
            pl.BlockSpec((2, size_x, columns, lanes), lambda i: (0, 0, 0, i)),
        ],
        out_specs=out_specs,
        out_shape=out_shape,
        scratch_shapes=scratch,
        compiler_params=params(1),
        cost_estimate=cost(6),
        name="first_x",
    )(slab, table, coeffs)


def ones_at(codes, count, axis):
    shape = (codes.shape[0], count) if axis == 1 else (count, codes.shape[1])
    places = lax.broadcasted_iota(jnp.int32, shape, axis)
    return jnp.where(codes == places, 1.0, 0.0).astype(jnp.bfloat16)


def field_kernel(slab, weights, table_y, table_z, codes, sides, *refs, pieces, count, natural):
    bufs = blocks_of(refs[:count], slab[0], pieces, -1)
    wave, density, rows_out, gathered, wide = refs[count:]
    _, near, size_y, size_z = wave.shape
    groups, entries, _ = codes.shape
    lanes = 128
    halves = size_z // lanes
    i, last = pl.program_id(0), pl.num_programs(0) - 1
    planes = near * (last + 1)

    @pl.when(i == 0)
    def _():
        gathered[...] = jnp.zeros_like(gathered)

    loaded = []
    if natural:
        for h in range(near):
            blocks = [buf[h] for _, buf in bufs]
            loaded.append(jnp.concatenate(blocks, axis=0))
    else:
        columns, rows, _ = bufs[0][1].shape

        @pl.when(i == 0)
        def _():
            for source, buf in bufs:
                start = pl.multiple_of(source * columns * rows, 8)
                values = buf[...].astype(jnp.float32).reshape(columns * rows, size_z)
                for q in range(halves):
                    wide[q, pl.ds(start, columns * rows), :] = values[
                        :, q * lanes : (q + 1) * lanes
                    ]

        for h in range(near):
            plane = i * near + h
            both = [
                jnp.concatenate(
                    [
                        wide[q, pl.ds(part * planes + plane, size_y, stride=rows), :]
                        for q in range(halves)
                    ],
                    axis=1,
                ).astype(jnp.bfloat16)
                for part in range(2)
            ]
            loaded.append(jnp.concatenate(both, axis=0))
    along_y = jnp.dot(
        table_y[...], jnp.concatenate(loaded, axis=1), preferred_element_type=jnp.float32
    ).astype(jnp.bfloat16)
    turned = jnp.concatenate(
        [
            jnp.concatenate(
                [
                    along_y[:size_y, h * size_z : (h + 1) * size_z],
                    along_y[size_y:, h * size_z : (h + 1) * size_z],
                ],
                axis=1,
            )
            for h in range(near)
        ],
        axis=0,
    )
    result = jnp.dot(turned, table_z[...], preferred_element_type=jnp.float32).astype(jnp.bfloat16)
    for h in range(near):
        total = jnp.zeros((size_y, size_z), jnp.float32)
        for part in range(2):
            values = result[h * size_y : (h + 1) * size_y, part * size_z : (part + 1) * size_z]
            wave[part, h] = values
            values = values.astype(jnp.float32)
            total += weights[0, part] * values * values
        density[h] = total.astype(jnp.bfloat16)

    used = [0] if groups == 1 else [0, 1 + (2 * i > last).astype(jnp.int32)]
    for group in used:
        places = ones_at(codes[group] - i * near * size_y, near * size_y, 1)
        gathered[group] += jnp.dot(places, result, preferred_element_type=jnp.float32)

    @pl.when(i == last)
    def _():
        for group in range(groups):
            for part in range(2):
                total = jnp.zeros((entries, lanes), jnp.float32)
                for q in range(halves):
                    start = part * size_z + q * lanes
                    total += jnp.where(
                        sides[group] == q, gathered[group, :, start : start + lanes], 0.0
                    )
                rows_out[group, part] = total.astype(jnp.bfloat16)


def make_field(slab, weights, bufs, table_y, table_z, codes, sides, planes, pieces, natural):
    size_z = bufs[0].shape[-1]
    size_y = table_y.shape[0] // 2
    columns = size_y // pieces
    groups, entries, _ = codes.shape
    if natural:
        buf_spec = pl.BlockSpec((pieces, PLANES, 2 * columns, size_z), lambda i: (0, i, 0, 0))
        wide = pltpu.VMEM((8, 128), jnp.float32)
    else:
        buf_spec = whole(bufs[0].shape)
        wide = pltpu.VMEM((size_z // 128, 2 * planes * size_y, 128), jnp.float32)
    return pl.pallas_call(
        functools.partial(field_kernel, pieces=pieces, count=len(bufs), natural=natural),
        grid=(planes // PLANES,),
        in_specs=[SMEM_SPEC, SMEM_SPEC]
        + [whole(a.shape) for a in (table_y, table_z, codes, sides)]
        + [buf_spec] * len(bufs),
        out_specs=[
            pl.BlockSpec((2, PLANES, size_y, size_z), lambda i: (0, i, 0, 0)),
            pl.BlockSpec((PLANES, size_y, size_z), lambda i: (i, 0, 0)),
            whole((groups, 2, entries, 128)),
        ],
        out_shape=[
            jax.ShapeDtypeStruct((2, planes, size_y, size_z), jnp.bfloat16),
            jax.ShapeDtypeStruct((planes, size_y, size_z), jnp.bfloat16),
            jax.ShapeDtypeStruct((groups, 2, entries, 128), jnp.bfloat16),
        ],
        scratch_shapes=[pltpu.VMEM((groups, entries, 2 * size_z), jnp.float32), wide],
        compiler_params=params(1),
        cost_estimate=cost(planes // 2),
        name="make_field",
    )(slab, weights, table_y, table_z, codes, sides, *bufs)


def nonlocal_kernel(coupled, projectors, *refs):
    parts, (projections, spread) = refs[:-2], refs[-2:]
    atoms, nproj, blocks, cells = projectors.shape
    for atom in range(atoms):
        tables = [projectors[atom, j].astype(jnp.float32) for j in range(nproj)]
        place = pl.ds(atom * blocks, blocks)
        for part in range(2):
            rows = sum(p[part, place].astype(jnp.float32) for p in parts)
            tile = jnp.concatenate(
                [jnp.sum(t * rows, axis=0, keepdims=True) for t in tables], axis=0
            )
            mixed = jnp.zeros_like(tile)
            for j in range(nproj):
                mixed += coupled[j] * tile[j : j + 1]
            projections[atom, part] = jnp.broadcast_to(
                jnp.sum(tile, -1, keepdims=True), tile.shape
            )
            energy = jnp.broadcast_to(jnp.sum(mixed, -1, keepdims=True), tile.shape)
            spread[part, place] = sum(
                t * energy[j : j + 1] for j, t in enumerate(tables)
            ).astype(jnp.bfloat16)


def make_nonlocal(coupled, projectors, parts):
    atoms, nproj, _, cells = projectors.shape
    return pl.pallas_call(
        nonlocal_kernel,
        out_shape=[
            jax.ShapeDtypeStruct((atoms, 2, nproj, cells), jnp.float32),
            jax.ShapeDtypeStruct(parts[0].shape, jnp.bfloat16),
        ],
        cost_estimate=cost(2),
        name="make_nonlocal",
    )(coupled, projectors, *parts)


def back_kernel(slab, wave, potential, table_z, table_y, codes, sides, *refs, pieces, natural):
    groups, _, entries = codes.shape
    sources, outs = refs[:groups], refs[groups:-2]
    spread, tall = refs[-2:]
    outs = blocks_of(outs, slab[0], pieces, 1)
    near, size_y, size_z = potential.shape
    lanes = 128
    halves = size_z // lanes
    i, last = pl.program_id(0), pl.num_programs(0) - 1
    planes = near * (last + 1)

    @pl.when(i == 0)
    def _():
        for group, source in enumerate(sources):
            for part in range(2):
                for q in range(halves):
                    start = part * size_z + q * lanes
                    spread[group, :, start : start + lanes] = jnp.where(
                        sides[group] == q, source[part].astype(jnp.float32), 0.0
                    ).astype(jnp.bfloat16)

    used = [0] if groups == 1 else [0, 1 + (2 * i > last).astype(jnp.int32)]
    extra = jnp.zeros((near * size_y, 2 * size_z), jnp.float32)
    for group in used:
        places = ones_at(codes[group] - i * near * size_y, near * size_y, 0)
        extra += jnp.dot(places, spread[group], preferred_element_type=jnp.float32)
    fields = []
    for h in range(near):
        local = potential[h].astype(jnp.float32)
        both = [
            local * wave[part, h].astype(jnp.float32)
            + extra[h * size_y : (h + 1) * size_y, part * size_z : (part + 1) * size_z]
            for part in range(2)
        ]
        fields.append(jnp.concatenate(both, axis=1).astype(jnp.bfloat16))
    stacked = jnp.concatenate(fields, axis=0)
    back_z = jnp.dot(stacked, table_z[...], preferred_element_type=jnp.float32).astype(jnp.bfloat16)
    turned = jnp.concatenate(
        [
            jnp.concatenate(
                [
                    back_z[h * size_y : (h + 1) * size_y, :size_z],
                    back_z[h * size_y : (h + 1) * size_y, size_z:],
                ],
                axis=0,
            )
            for h in range(near)
        ],
        axis=1,
    )
    back_y = jnp.dot(table_y[...], turned, preferred_element_type=jnp.float32)
    if natural:
        back_y = back_y.astype(jnp.bfloat16)
        for h in range(near):
            tall[:, h] = back_y[:, h * size_z : (h + 1) * size_z].reshape(
                pieces, outs[0][1].shape[1], size_z
            )
        for target, out in outs:
            out[...] = tall[target]
        return
    columns, rows, _ = outs[0][1].shape
    for h in range(near):
        for part in range(2):
            for q in range(halves):
                start = h * size_z + q * lanes
                tall[q, pl.ds(part * planes + i * near + h, size_y, stride=rows), :] = back_y[
                    part * size_y : (part + 1) * size_y, start : start + lanes
                ]

    @pl.when(i == last)
    def _():
        for target, out in outs:
            start = pl.multiple_of(target * columns * rows, 8)
            values = [tall[q, pl.ds(start, columns * rows), :] for q in range(halves)]
            out[...] = (
                jnp.concatenate(values, axis=1).astype(jnp.bfloat16).reshape(columns, rows, size_z)
            )


def go_back(slab, wave, potential, table_z, table_y, codes, sides, sources, place, pieces, natural):
    _, planes, size_y, size_z = wave.shape
    columns = size_y // pieces
    groups, _, entries = codes.shape
    scratch = [pltpu.VMEM((groups, entries, 2 * size_z), jnp.bfloat16)]
    if natural:
        shape = (planes, 2 * columns, size_z)
        out_specs = [pl.BlockSpec((PLANES, 2 * columns, size_z), lambda i: (i, 0, 0))] * pieces
        out_shape = [jax.ShapeDtypeStruct(shape, jnp.bfloat16)] * pieces
        scratch.append(pltpu.VMEM((pieces, PLANES, 2 * columns, size_z), jnp.bfloat16))
    else:
        shape = (pieces, columns, 2 * planes, size_z)
        out_specs = [whole(shape)]
        out_shape = [jax.ShapeDtypeStruct(shape, jnp.bfloat16)]
        scratch.append(pltpu.VMEM((size_z // 128, 2 * planes * size_y, 128), jnp.float32))
    return pl.pallas_call(
        functools.partial(back_kernel, pieces=pieces, natural=natural),
        grid=(planes // PLANES,),
        in_specs=[
            SMEM_SPEC,
            pl.BlockSpec((2, PLANES, size_y, size_z), lambda i: (0, i, 0, 0)),
            pl.BlockSpec((PLANES, size_y, size_z), lambda i: (place(i), 0, 0)),
        ]
        + [whole(a.shape) for a in (table_z, table_y, codes, sides, *sources)],
        out_specs=out_specs,
        out_shape=out_shape,
        scratch_shapes=scratch,
        compiler_params=params(1),
        cost_estimate=cost(planes // 2),
        name="go_back",
    )(slab, wave, potential, table_z, table_y, codes, sides, *sources)


def last_x_kernel(frequency_x, frequency_yz, table, coeffs, *refs):
    bufs, (out, tall) = refs[:-2], refs[-2:]
    parts, size_x, columns, lanes = coeffs.shape

    def some_columns(g, carry):
        loaded = []
        for h in range(COLUMNS):
            column = COLUMNS * g + h
            blocks = []
            for buf in bufs:
                if len(buf.shape) == 4:
                    blocks += [buf[d, column] for d in range(buf.shape[0])]
                else:
                    blocks.append(buf[column])
            loaded.append(jnp.concatenate(blocks, axis=0))
        result = jnp.dot(
            table[...], jnp.concatenate(loaded, axis=1), preferred_element_type=jnp.float32
        )
        for h in range(COLUMNS):
            tall[pl.ds(COLUMNS * g + h, parts * size_x, stride=columns), :] = result[
                :, h * lanes : (h + 1) * lanes
            ]
        return carry

    lax.fori_loop(0, columns // COLUMNS, some_columns, 0)

    def finish(k, carry):
        kinetic = frequency_x[k] + frequency_yz[...]
        for part in range(parts):
            start = pl.multiple_of((part * size_x + k) * columns, 8)
            out[part, k] = (
                tall[pl.ds(start, columns), :] + kinetic * coeffs[part, k].astype(jnp.float32)
            ).astype(jnp.bfloat16)
        return carry

    lax.fori_loop(0, size_x, finish, 0, unroll=8)


def last_x(frequency_x, frequency_yz, table, coeffs, bufs):
    _, size_x, columns, size_z = coeffs.shape
    lanes = size_z // 2
    spec = pl.BlockSpec((2, size_x, columns, lanes), lambda i: (0, 0, 0, i))
    return pl.pallas_call(
        last_x_kernel,
        grid=(2,),
        in_specs=[
            SMEM_SPEC,
            pl.BlockSpec((columns, lanes), lambda i: (0, i)),
            whole(table.shape),
            spec,
        ]
        + [
            pl.BlockSpec((*b.shape[:-1], lanes), lambda i, b=b: (0,) * (b.ndim - 1) + (i,))
            for b in bufs
        ],
        out_specs=spec,
        out_shape=jax.ShapeDtypeStruct(coeffs.shape, jnp.bfloat16),
        scratch_shapes=[pltpu.VMEM((2 * size_x * columns, lanes), jnp.float32)],
        compiler_params=params(1),
        cost_estimate=cost(9),
        name="last_x",
    )(frequency_x, frequency_yz, table, coeffs, *bufs)


def per_device_chunked(wave_coeffs, occupation, potential, projectors, coupling, sphere_blocks):
    pieces = lax.axis_size("fft")
    bands = lax.axis_size("band")
    slab = lax.axis_index("fft")
    coeffs = wave_coeffs[0]
    _, size_x, columns, size_z = coeffs.shape
    slab_planes, size_y, _ = potential.shape
    atom_dev, nproj, blocks, cells = projectors.shape
    zblocks = size_z // cells
    outer, inner = chunk_planes(slab_planes)
    up = [(i, (i + 1) % pieces) for i in range(pieces)]
    down = [(j, i) for i, j in up]

    inverse_x, forward_x = (real_blocks(size_x, s) for s in (1.0, -1.0))
    inverse_y, forward_y = (real_blocks(size_y, s) for s in (1.0, -1.0))
    inverse_z, forward_z = (real_blocks(size_z, s) for s in (1.0, -1.0))
    place_outer, place_inner = (
        np.arange(pieces)[:, None] * slab_planes + np.array(chunk)[None, :]
        for chunk in (outer, inner)
    )
    table_x_outer = np.stack([inverse_x[r][place_outer] for r in range(2)], 1)
    table_x_inner = np.stack([inverse_x[r][place_inner] for r in range(2)], 2)
    tables_back_x = [
        np.stack([forward_x[:, :, r][:, :, place] for r in range(2)], 3).reshape(
            2 * size_x, pieces, -1
        )
        for place in (place_outer, place_inner)
    ]
    split_y = (2, size_y, 2, pieces, columns)
    tables = [
        table_x_outer.reshape(-1, 2 * size_x),
        table_x_inner.reshape(-1, 2 * size_x),
        inverse_y.reshape(2 * size_y, -1),
        inverse_y.reshape(split_y).transpose(0, 1, 3, 2, 4).reshape(2 * size_y, -1),
        inverse_z.transpose(2, 3, 0, 1).reshape(2 * size_z, -1),
        forward_z.transpose(2, 3, 0, 1).reshape(2 * size_z, -1),
        forward_y.reshape(2 * size_y, -1),
        forward_y.reshape(2, pieces, columns, -1).transpose(1, 0, 2, 3).reshape(2 * size_y, -1),
        tables_back_x[0].reshape(2 * size_x, -1),
        np.concatenate([tables_back_x[1]] * 2, 1)[:, ::-1],
    ]
    (
        table_x_outer, table_x_inner, table_y_outer, table_y_inner, table_z,
        table_back_z, table_back_y_outer, table_back_y_inner, table_back_outer,
        table_back_inner,
    ) = (jnp.asarray(t.astype(jnp.bfloat16)) for t in tables)

    table_back_inner = lax.dynamic_slice_in_dim(table_back_inner, pieces - 1 - slab, pieces, 1)
    table_back_x = jnp.concatenate(
        [table_back_outer, table_back_inner.reshape(2 * size_x, -1)], axis=1
    )

    where = slab.reshape(1)
    section_outer = first_x(where, table_x_outer, coeffs, len(outer), pieces, False)
    section_outer, table_x_inner, sphere_blocks = lax.optimization_barrier(
        (section_outer, table_x_inner, sphere_blocks)
    )
    (section_inner,) = first_x(where, table_x_inner, coeffs, len(inner), pieces, True)

    entries = atom_dev * blocks

    def codes_of(chunk, shift):
        owner = (slab + shift + pieces) % pieces
        numbers = lax.dynamic_slice_in_dim(sphere_blocks, owner * atom_dev, atom_dev, 0)
        plane = numbers // (size_y * zblocks) - slab * slab_planes
        rest = numbers % (size_y * zblocks)
        if chunk is outer:
            inside = ((plane >= 0) & (plane < EDGE)) | (
                (plane >= slab_planes - EDGE) & (plane < slab_planes)
            )
            plane = jnp.where(plane < EDGE, plane, plane - len(inner))
        else:
            inside = (plane >= EDGE) & (plane < slab_planes - EDGE)
            plane = plane - EDGE
        code = jnp.where(inside, plane * size_y + rest // zblocks, -1)
        return code.reshape(entries), (rest % zblocks).reshape(entries)

    found = [codes_of(outer, shift) for shift in (0, -1, 1)]
    codes_outer, sides_outer = (jnp.stack(values) for values in zip(*found))
    codes_inner, sides_inner = (values[None] for values in codes_of(inner, 0))
    sides_outer, sides_inner = sides_outer[:, :, None], sides_inner[:, :, None]
    strength = 3.0 * math.sqrt(cells * blocks) / nproj
    coupled = (coupling + coupling.T) * (0.5 * strength)
    coupled = jnp.broadcast_to(coupled.T[:, :, None], (nproj, nproj, cells))

    def permute_all(values):
        received = [values[0]]
        for k in range(1, pieces):
            pairs = [(j, (j + k) % pieces) for j in range(pieces)]
            received.append(lax.ppermute(values[k], "fft", pairs))
        return received

    received_outer = permute_all(section_outer)
    section_inner, received_outer[1 : HELD + 1] = lax.optimization_barrier(
        (section_inner, received_outer[1 : HELD + 1])
    )
    received_inner = lax.all_to_all(section_inner, "fft", 0, 0, tiled=True)
    wave_outer, density_outer, rows_outer = make_field(
        where, occupation, received_outer, table_y_outer, table_z, codes_outer[:, :, None],
        sides_outer, len(outer), pieces, False,
    )
    from_following = lax.ppermute(rows_outer[1], "fft", down)
    from_previous = lax.ppermute(rows_outer[2], "fft", up)
    density_outer = lax.psum(density_outer, "band")
    wave_inner, density_inner, rows_inner = make_field(
        where, occupation, [received_inner], table_y_inner, table_z, codes_inner[:, :, None],
        sides_inner, len(inner), pieces, True,
    )
    projected, spread = make_nonlocal(
        coupled, projectors, [rows_outer[0], rows_inner[0], from_following, from_previous]
    )
    spread_previous = lax.ppermute(spread, "fft", up)
    spread_following = lax.ppermute(spread, "fft", down)
    edge_steps = EDGE // PLANES
    inner_steps = len(inner) // PLANES
    back_inner = go_back(
        where, wave_inner, potential, table_back_z, table_back_y_inner, codes_inner[:, None, :],
        sides_inner, [spread], lambda i: i + edge_steps, pieces, True,
    )
    back_inner, spread_previous, spread_following = lax.optimization_barrier(
        (back_inner, spread_previous, spread_following)
    )
    back_inner = permute_all(back_inner)
    (back_outer,) = go_back(
        where, wave_outer, potential, table_back_z, table_back_y_outer, codes_outer[:, None, :],
        sides_outer, [spread, spread_previous, spread_following],
        lambda i: jnp.where(i < edge_steps, i, i + inner_steps), pieces, False,
    )
    density_inner, density_outer = lax.optimization_barrier((density_inner, density_outer))
    density_inner = lax.psum(density_inner, "band")
    back_outer = lax.all_to_all(back_outer, "fft", 0, 0, tiled=True)
    back_inner = [
        b.reshape(len(inner), 2, columns, size_z).transpose(2, 1, 0, 3).reshape(columns, -1, size_z)
        for b in back_inner
    ]
    density = jnp.concatenate([density_outer[:EDGE], density_inner, density_outer[EDGE:]], axis=0)

    index_x = np.arange(size_x)
    frequency_x = jnp.asarray(
        (np.where(2 * index_x < size_x, index_x, index_x - size_x) / size_x) ** 2, jnp.float32
    )
    index_y = slab * columns + jnp.arange(columns, dtype=jnp.int32)
    index_z = jnp.arange(size_z, dtype=jnp.int32)
    frequency_yz = wave_squares(index_y, size_y)[:, None] + wave_squares(index_z, size_z)[None, :]
    coeffs, density, back_inner = lax.optimization_barrier((coeffs, density, back_inner))
    applied = last_x(frequency_x, frequency_yz, table_back_x, coeffs, [back_outer, *back_inner])
    return (applied[None], density, projected[None, :, :, :, 0])


def per_device(wave_coeffs, occupation, potential, projectors, coupling, sphere_blocks):
    pieces, bands = lax.axis_size("fft"), lax.axis_size("band")
    size_z = wave_coeffs.shape[4]
    columns = wave_coeffs.shape[3]
    slab_planes = potential.shape[0]
    chunked = (
        pieces >= 3
        and slab_planes % EDGE == 0
        and slab_planes >= 3 * EDGE
        and EDGE >= HALO
        and columns % 8 == 0
        and size_z % 256 == 0
        and projectors.shape[0] % bands == 0
        and projectors.shape[3] == 128
        and projectors.shape[1] == 8
    )
    chosen = per_device_chunked if chunked else per_device_plain
    return chosen(wave_coeffs, occupation, potential, projectors, coupling, sphere_blocks)


def solution(mesh):
    placed = (
        P("band", None, None, "fft", None),
        P("band", None),
        P("fft", None, None),
        P("fft", None, None, None),
        P(),
        P(),
    )
    return jax.shard_map(
        per_device,
        mesh=mesh,
        in_specs=placed,
        out_specs=(
            P("band", None, None, "fft", None),
            P("fft", None, None),
            P("band", "fft", None, None),
        ),
        check_vma=False,
    )
```

```python
import functools
import math

import jax
import jax.numpy as jnp
import numpy as np
from jax import lax
from jax.experimental import pallas as pl
from jax.experimental.pallas import tpu as pltpu
from jax.sharding import PartitionSpec as P

HALO = 6
EDGE = 8
PLANES = 4
COLUMNS = 8
VMEM_BYTES = 56 * 1024 * 1024


def extended(shard, sides, width):
    for axis, dim in sides:
        count, length = (lax.axis_size(axis), shard.shape[dim])
        up = [(i, (i + 1) % count) for i in range(count)]
        down = [(j, i) for i, j in up]
        last = lax.slice_in_dim(shard, length - width, length, axis=dim)
        first = lax.slice_in_dim(shard, 0, width, axis=dim)
        before = lax.ppermute(last, axis, up)
        after = lax.ppermute(first, axis, down)
        shard = jnp.concatenate([before, shard, after], axis=dim)
    return shard


def dft_table(length, sign_value):
    indices = jnp.arange(length, dtype=jnp.int32)
    phases = indices[:, None] * indices[None, :] % length
    angles = 2.0 * math.pi / length * phases.astype(jnp.float32)
    factor = 1.0 / math.sqrt(length)
    cosine = jnp.cos(angles) * factor
    sine_part = jnp.sin(angles) * (sign_value * factor)
    upper_rows = jnp.stack([cosine, -sine_part])
    bottom = jnp.stack([sine_part, cosine])
    return jnp.stack([upper_rows, bottom]).astype(jnp.bfloat16)


def wave_squares(indices, length):
    frequency = (
        jnp.where(2 * indices < length, indices, indices - length).astype(jnp.float32) / length
    )
    return frequency * frequency


def per_device_plain(wave_coeffs, occupation, potential, projectors, coupling, sphere_blocks):
    pieces = lax.axis_size("fft")
    slab_index = lax.axis_index("fft")
    coeffs = wave_coeffs[0]
    size_x = coeffs.shape[1]
    columns = coeffs.shape[2]
    size_z = coeffs.shape[3]
    slab_planes = potential.shape[0]
    size_y = potential.shape[1]
    atom_dev = projectors.shape[0]
    nproj_count = projectors.shape[1]
    block_cells = projectors.shape[3]
    zblocks = size_z // block_cells
    plane_blocks = size_y * zblocks
    total_atoms = atom_dev * pieces
    table_x = dft_table(size_x, 1.0).transpose(0, 2, 1, 3).reshape(2 * size_x, 2 * size_x)
    inverse_y = dft_table(size_y, 1.0)
    inverse_z = dft_table(size_z, 1.0)
    flattened = coeffs.reshape(2 * size_x, columns * size_z)
    along_x = jnp.dot(table_x, flattened, preferred_element_type=jnp.float32)
    along_x = along_x.reshape(2, size_x, columns, size_z).astype(jnp.bfloat16)
    along_y = jnp.einsum(
        "abyk,bxkz->axyz",
        inverse_y,
        lax.all_to_all(along_x, "fft", split_axis=1, concat_axis=2, tiled=True),
        preferred_element_type=jnp.float32,
    ).astype(jnp.bfloat16)
    wave_field = jnp.einsum(
        "abzk,bxyk->axyz", inverse_z, along_y, preferred_element_type=jnp.float32
    ).astype(jnp.bfloat16)
    weights = occupation[0]
    real_part = wave_field[0].astype(jnp.float32)
    imag_part = wave_field[1].astype(jnp.float32)
    partial_density = weights[0] * real_part * real_part + weights[1] * imag_part * imag_part
    density = lax.psum(partial_density.astype(jnp.bfloat16), "band")
    strength = 3.0 * math.sqrt(block_cells * projectors.shape[2]) / nproj_count
    coupled = (coupling + coupling.T) * (0.5 * strength)
    nearby = extended(projectors, (("fft", 0),), atom_dev)
    atom_rows = (
        slab_index * atom_dev - atom_dev + jnp.arange(3 * atom_dev, dtype=jnp.int32) + total_atoms
    ) % total_atoms
    near_blocks = sphere_blocks[atom_rows]
    plane_index = near_blocks // plane_blocks
    inside = plane_index // slab_planes == slab_index
    local_index = jnp.where(
        inside,
        (plane_index - slab_index * slab_planes) * plane_blocks + near_blocks % plane_blocks,
        0,
    )
    blocks_own = wave_field.reshape(2, slab_planes * plane_blocks, block_cells)
    gathered = blocks_own[:, local_index] * inside[None, :, :, None].astype(jnp.bfloat16)
    partial_value = jnp.einsum(
        "ajsk,bask->abj", nearby, gathered, preferred_element_type=jnp.float32
    )
    summed = extended(partial_value, (("fft", 0),), atom_dev)
    projections_own = (
        summed[:atom_dev] + summed[2 * atom_dev : 3 * atom_dev] + summed[4 * atom_dev :]
    )
    energy_own = jnp.einsum(
        "ij,abj->abi", coupled, projections_own, precision=lax.Precision.HIGHEST
    )
    energy = extended(energy_own, (("fft", 0),), atom_dev)
    spread = jnp.einsum(
        "ajsk,abj->bask", nearby.astype(jnp.float32), energy, precision=lax.Precision.HIGHEST
    )
    spread = spread * inside[None, :, :, None].astype(jnp.float32)
    accumulated = (
        jnp.zeros((2, slab_planes * plane_blocks, block_cells), jnp.float32)
        .at[:, local_index]
        .add(spread)
    )
    nonlocal_term = accumulated.reshape(2, slab_planes, size_y, size_z)
    total_field = (
        potential.astype(jnp.float32)[None] * wave_field.astype(jnp.float32) + nonlocal_term
    ).astype(jnp.bfloat16)
    forward_z = dft_table(size_z, -1.0)
    forward_y = dft_table(size_y, -1.0)
    forward_x = dft_table(size_x, -1.0)
    back_z = jnp.einsum(
        "abzk,bxyk->axyz", forward_z, total_field, preferred_element_type=jnp.float32
    ).astype(jnp.bfloat16)
    back_y = jnp.einsum(
        "abyk,bxkz->axyz", forward_y, back_z, preferred_element_type=jnp.float32
    ).astype(jnp.bfloat16)
    transformed = jnp.einsum(
        "abxk,bkyz->axyz",
        forward_x,
        lax.all_to_all(back_y, "fft", split_axis=2, concat_axis=1, tiled=True),
        preferred_element_type=jnp.float32,
    )
    index_x = jnp.arange(size_x, dtype=jnp.int32)
    index_y = slab_index * columns + jnp.arange(columns, dtype=jnp.int32)
    index_z = jnp.arange(size_z, dtype=jnp.int32)
    kinetic = (
        wave_squares(index_x, size_x)[:, None, None]
        + wave_squares(index_y, size_y)[None, :, None]
        + wave_squares(index_z, size_z)[None, None, :]
    )
    applied = (transformed + kinetic[None] * coeffs.astype(jnp.float32)).astype(jnp.bfloat16)
    return (applied[None], density, projections_own[None])


def real_blocks(length, sign):
    index = np.arange(length)
    angles = 2.0 * np.pi / length * (index[:, None] * index[None, :] % length)
    cosine = np.cos(angles) / np.sqrt(length)
    sine = sign * np.sin(angles) / np.sqrt(length)
    blocks = np.empty((2, length, 2, length))
    blocks[0, :, 0, :] = cosine
    blocks[1, :, 1, :] = cosine
    blocks[0, :, 1, :] = -sine
    blocks[1, :, 0, :] = sine
    return blocks


def chunk_planes(slab_planes):
    low, high = list(range(EDGE)), list(range(slab_planes - EDGE, slab_planes))
    return [low + high, list(range(EDGE, slab_planes - EDGE))]


def params(steps):
    return pltpu.CompilerParams(
        dimension_semantics=("arbitrary",) * steps, vmem_limit_bytes=VMEM_BYTES
    )


def cost(microseconds):
    return pl.CostEstimate(
        flops=microseconds * 10**9, bytes_accessed=2**20, transcendentals=0
    )


def whole(shape):
    return pl.BlockSpec(shape, lambda i: (0,) * len(shape))


SMEM_SPEC = pl.BlockSpec(memory_space=pltpu.SMEM)


def blocks_of(refs, slab):
    return [(lax.bitwise_xor(slab, jnp.int32(k)), ref) for k, ref in enumerate(refs)]


def first_x_kernel(slab, table_ref, coeffs_ref, *refs, pieces, natural):
    scratch = 3 if natural else 2
    outs = blocks_of(refs[:-scratch], slab[0])
    turned, wide, *tall = refs[-scratch:]
    parts, size_x, columns, lanes = coeffs_ref.shape
    rows = parts * size_x
    height = table_ref.shape[0] // pieces

    for k, (device, _) in enumerate(outs):
        start = pl.multiple_of(device * height, 16)
        turned[k * height : (k + 1) * height, :] = table_ref[pl.ds(start, height), :]

    def widen(k, carry):
        for part in range(parts):
            start = pl.multiple_of((part * size_x + k * 8) * columns, 8)
            wide[pl.ds(start, 8 * columns), :] = (
                coeffs_ref[part, pl.ds(k * 8, 8)].astype(jnp.float32).reshape(8 * columns, lanes)
            )
        return carry

    lax.fori_loop(0, size_x // 8, widen, 0, unroll=2)

    def some_columns(g, carry):
        loaded = [
            wide[pl.ds(COLUMNS * g + h, rows, stride=columns), :].astype(jnp.bfloat16)
            for h in range(COLUMNS)
        ]
        result = jnp.dot(
            turned[...], jnp.concatenate(loaded, axis=1), preferred_element_type=jnp.float32
        )
        for h in range(COLUMNS):
            piece = result[:, h * lanes : (h + 1) * lanes]
            if natural:
                tall[0][pl.ds(COLUMNS * g + h, piece.shape[0], stride=columns), :] = piece
            else:
                piece = piece.astype(jnp.bfloat16)
                for k, (_, out) in enumerate(outs):
                    out[COLUMNS * g + h] = piece[k * height : (k + 1) * height]
        return carry

    lax.fori_loop(0, columns // COLUMNS, some_columns, 0)
    if natural:
        for k, (_, out) in enumerate(outs):
            values = tall[0][k * height * columns : (k + 1) * height * columns, :]
            out[...] = values.astype(jnp.bfloat16).reshape(out.shape)


def first_x(slab, table, coeffs, planes, pieces, natural):
    _, size_x, columns, size_z = coeffs.shape
    lanes = size_z // 2
    shape = (planes, 2 * columns) if natural else (columns, 2 * planes)
    scratch = [
        pltpu.VMEM(table.shape, jnp.bfloat16),
        pltpu.VMEM((2 * size_x * columns, lanes), jnp.float32),
    ]
    if natural:
        scratch.append(pltpu.VMEM((2 * pieces * planes * columns, lanes), jnp.float32))
    out_specs = [pl.BlockSpec((*shape, lanes), lambda i: (0, 0, i))] * pieces
    out_shape = [jax.ShapeDtypeStruct((*shape, size_z), jnp.bfloat16)] * pieces
    return pl.pallas_call(
        functools.partial(first_x_kernel, pieces=pieces, natural=natural),
        grid=(2,),
        in_specs=[
            SMEM_SPEC,
            whole(table.shape),
            pl.BlockSpec((2, size_x, columns, lanes), lambda i: (0, 0, 0, i)),
        ],
        out_specs=out_specs,
        out_shape=out_shape,
        scratch_shapes=scratch,
        compiler_params=params(1),
        cost_estimate=cost(6),
        name="first_x",
    )(slab, table, coeffs)


def ones_at(codes, count, axis):
    shape = (codes.shape[0], count) if axis == 1 else (count, codes.shape[1])
    places = lax.broadcasted_iota(jnp.int32, shape, axis)
    return jnp.where(codes == places, 1.0, 0.0).astype(jnp.bfloat16)


def field_kernel(slab, weights, table_y, table_z, codes, sides, *refs, pieces, count, natural):
    bufs = blocks_of(refs[:count], slab[0])
    wave, density, rows_out, gathered, wide = refs[count:]
    _, near, size_y, size_z = wave.shape
    groups, entries, _ = codes.shape
    lanes = 128
    halves = size_z // lanes
    i, last = pl.program_id(0), pl.num_programs(0) - 1
    planes = near * (last + 1)

    @pl.when(i == 0)
    def _():
        gathered[...] = jnp.zeros_like(gathered)

    loaded = []
    if natural:
        for source, buf in bufs:
            wide[source] = buf[...]
        for h in range(near):
            loaded.append(wide[:, h].reshape(2 * size_y, size_z))
    else:
        columns, rows, _ = bufs[0][1].shape

        @pl.when(i == 0)
        def _():
            for source, buf in bufs:
                start = pl.multiple_of(source * columns * rows, 8)
                values = buf[...].astype(jnp.float32).reshape(columns * rows, size_z)
                for q in range(halves):
                    wide[q, pl.ds(start, columns * rows), :] = values[
                        :, q * lanes : (q + 1) * lanes
                    ]

        for h in range(near):
            plane = i * near + h
            both = [
                jnp.concatenate(
                    [
                        wide[q, pl.ds(part * planes + plane, size_y, stride=rows), :]
                        for q in range(halves)
                    ],
                    axis=1,
                ).astype(jnp.bfloat16)
                for part in range(2)
            ]
            loaded.append(jnp.concatenate(both, axis=0))
    along_y = jnp.dot(
        table_y[...], jnp.concatenate(loaded, axis=1), preferred_element_type=jnp.float32
    ).astype(jnp.bfloat16)
    turned = jnp.concatenate(
        [
            jnp.concatenate(
                [
                    along_y[:size_y, h * size_z : (h + 1) * size_z],
                    along_y[size_y:, h * size_z : (h + 1) * size_z],
                ],
                axis=1,
            )
            for h in range(near)
        ],
        axis=0,
    )
    result = jnp.dot(turned, table_z[...], preferred_element_type=jnp.float32).astype(jnp.bfloat16)
    for h in range(near):
        total = jnp.zeros((size_y, size_z), jnp.float32)
        for part in range(2):
            values = result[h * size_y : (h + 1) * size_y, part * size_z : (part + 1) * size_z]
            wave[part, h] = values
            values = values.astype(jnp.float32)
            total += weights[0, part] * values * values
        density[h] = total.astype(jnp.bfloat16)

    used = [0] if groups == 1 else [0, 1 + (2 * i > last).astype(jnp.int32)]
    for group in used:
        places = ones_at(codes[group] - i * near * size_y, near * size_y, 1)
        gathered[group] += jnp.dot(places, result, preferred_element_type=jnp.float32)

    @pl.when(i == last)
    def _():
        for group in range(groups):
            for part in range(2):
                total = jnp.zeros((entries, lanes), jnp.float32)
                for q in range(halves):
                    start = part * size_z + q * lanes
                    total += jnp.where(
                        sides[group] == q, gathered[group, :, start : start + lanes], 0.0
                    )
                rows_out[group, part] = total.astype(jnp.bfloat16)


def make_field(slab, weights, bufs, table_y, table_z, codes, sides, planes, pieces, natural):
    size_z = bufs[0].shape[-1]
    size_y = table_y.shape[0] // 2
    columns = size_y // pieces
    groups, entries, _ = codes.shape
    if natural:
        buf_spec = pl.BlockSpec((PLANES, 2 * columns, size_z), lambda i: (i, 0, 0))
        wide = pltpu.VMEM((pieces, PLANES, 2 * columns, size_z), jnp.bfloat16)
    else:
        buf_spec = whole(bufs[0].shape)
        wide = pltpu.VMEM((size_z // 128, 2 * planes * size_y, 128), jnp.float32)
    return pl.pallas_call(
        functools.partial(field_kernel, pieces=pieces, count=len(bufs), natural=natural),
        grid=(planes // PLANES,),
        in_specs=[SMEM_SPEC, SMEM_SPEC]
        + [whole(a.shape) for a in (table_y, table_z, codes, sides)]
        + [buf_spec] * len(bufs),
        out_specs=[
            pl.BlockSpec((2, PLANES, size_y, size_z), lambda i: (0, i, 0, 0)),
            pl.BlockSpec((PLANES, size_y, size_z), lambda i: (i, 0, 0)),
            whole((groups, 2, entries, 128)),
        ],
        out_shape=[
            jax.ShapeDtypeStruct((2, planes, size_y, size_z), jnp.bfloat16),
            jax.ShapeDtypeStruct((planes, size_y, size_z), jnp.bfloat16),
            jax.ShapeDtypeStruct((groups, 2, entries, 128), jnp.bfloat16),
        ],
        scratch_shapes=[pltpu.VMEM((groups, entries, 2 * size_z), jnp.float32), wide],
        compiler_params=params(1),
        cost_estimate=cost(planes),
        name="make_field",
    )(slab, weights, table_y, table_z, codes, sides, *bufs)


def nonlocal_kernel(coupled, projectors, *refs):
    parts, (projections, spread) = refs[:-2], refs[-2:]
    atoms, nproj, blocks, cells = projectors.shape
    for atom in range(atoms):
        tables = [projectors[atom, j].astype(jnp.float32) for j in range(nproj)]
        place = pl.ds(atom * blocks, blocks)
        for part in range(2):
            rows = sum(p[part, place].astype(jnp.float32) for p in parts)
            tile = jnp.concatenate(
                [jnp.sum(t * rows, axis=0, keepdims=True) for t in tables], axis=0
            )
            mixed = jnp.zeros_like(tile)
            for j in range(nproj):
                mixed += coupled[j] * tile[j : j + 1]
            projections[atom, part] = jnp.broadcast_to(
                jnp.sum(tile, -1, keepdims=True), tile.shape
            )
            energy = jnp.broadcast_to(jnp.sum(mixed, -1, keepdims=True), tile.shape)
            spread[part, place] = sum(
                t * energy[j : j + 1] for j, t in enumerate(tables)
            ).astype(jnp.bfloat16)


def make_nonlocal(coupled, projectors, parts):
    atoms, nproj, _, cells = projectors.shape
    return pl.pallas_call(
        nonlocal_kernel,
        out_shape=[
            jax.ShapeDtypeStruct((atoms, 2, nproj, cells), jnp.float32),
            jax.ShapeDtypeStruct(parts[0].shape, jnp.bfloat16),
        ],
        cost_estimate=cost(2),
        name="make_nonlocal",
    )(coupled, projectors, *parts)


def back_kernel(slab, wave, potential, table_z, table_y, codes, sides, *refs, pieces, natural):
    groups, _, entries = codes.shape
    sources, outs = refs[:groups], refs[groups:-2]
    spread, tall = refs[-2:]
    outs = blocks_of(outs, slab[0])
    near, size_y, size_z = potential.shape
    lanes = 128
    halves = size_z // lanes
    i, last = pl.program_id(0), pl.num_programs(0) - 1
    planes = near * (last + 1)

    @pl.when(i == 0)
    def _():
        for group, source in enumerate(sources):
            for part in range(2):
                for q in range(halves):
                    start = part * size_z + q * lanes
                    spread[group, :, start : start + lanes] = jnp.where(
                        sides[group] == q, source[part].astype(jnp.float32), 0.0
                    ).astype(jnp.bfloat16)

    used = [0] if groups == 1 else [0, 1 + (2 * i > last).astype(jnp.int32)]
    extra = jnp.zeros((near * size_y, 2 * size_z), jnp.float32)
    for group in used:
        places = ones_at(codes[group] - i * near * size_y, near * size_y, 0)
        extra += jnp.dot(places, spread[group], preferred_element_type=jnp.float32)
    fields = []
    for h in range(near):
        local = potential[h].astype(jnp.float32)
        both = [
            local * wave[part, h].astype(jnp.float32)
            + extra[h * size_y : (h + 1) * size_y, part * size_z : (part + 1) * size_z]
            for part in range(2)
        ]
        fields.append(jnp.concatenate(both, axis=1).astype(jnp.bfloat16))
    stacked = jnp.concatenate(fields, axis=0)
    back_z = jnp.dot(stacked, table_z[...], preferred_element_type=jnp.float32).astype(jnp.bfloat16)
    turned = jnp.concatenate(
        [
            jnp.concatenate(
                [
                    back_z[h * size_y : (h + 1) * size_y, :size_z],
                    back_z[h * size_y : (h + 1) * size_y, size_z:],
                ],
                axis=0,
            )
            for h in range(near)
        ],
        axis=1,
    )
    back_y = jnp.dot(table_y[...], turned, preferred_element_type=jnp.float32)
    if natural:
        back_y = back_y.astype(jnp.bfloat16)
        for h in range(near):
            tall[:, h] = back_y[:, h * size_z : (h + 1) * size_z].reshape(
                pieces, outs[0][1].shape[1], size_z
            )
        for target, out in outs:
            out[...] = tall[target]
        return
    columns, rows, _ = outs[0][1].shape
    for h in range(near):
        for part in range(2):
            for q in range(halves):
                start = h * size_z + q * lanes
                tall[q, pl.ds(part * planes + i * near + h, size_y, stride=rows), :] = back_y[
                    part * size_y : (part + 1) * size_y, start : start + lanes
                ]

    @pl.when(i == last)
    def _():
        for target, out in outs:
            start = pl.multiple_of(target * columns * rows, 8)
            values = [tall[q, pl.ds(start, columns * rows), :] for q in range(halves)]
            out[...] = (
                jnp.concatenate(values, axis=1).astype(jnp.bfloat16).reshape(columns, rows, size_z)
            )


def go_back(slab, wave, potential, table_z, table_y, codes, sides, sources, place, pieces, natural):
    _, planes, size_y, size_z = wave.shape
    columns = size_y // pieces
    groups, _, entries = codes.shape
    scratch = [pltpu.VMEM((groups, entries, 2 * size_z), jnp.bfloat16)]
    if natural:
        shape = (planes, 2 * columns, size_z)
        out_specs = [pl.BlockSpec((PLANES, 2 * columns, size_z), lambda i: (i, 0, 0))] * pieces
        scratch.append(pltpu.VMEM((pieces, PLANES, 2 * columns, size_z), jnp.bfloat16))
    else:
        shape = (columns, 2 * planes, size_z)
        out_specs = [whole(shape)] * pieces
        scratch.append(pltpu.VMEM((size_z // 128, 2 * planes * size_y, 128), jnp.float32))
    return pl.pallas_call(
        functools.partial(back_kernel, pieces=pieces, natural=natural),
        grid=(planes // PLANES,),
        in_specs=[
            SMEM_SPEC,
            pl.BlockSpec((2, PLANES, size_y, size_z), lambda i: (0, i, 0, 0)),
            pl.BlockSpec((PLANES, size_y, size_z), lambda i: (place(i), 0, 0)),
        ]
        + [whole(a.shape) for a in (table_z, table_y, codes, sides, *sources)],
        out_specs=out_specs,
        out_shape=[jax.ShapeDtypeStruct(shape, jnp.bfloat16)] * pieces,
        scratch_shapes=scratch,
        compiler_params=params(1),
        cost_estimate=cost(planes),
        name="go_back",
    )(slab, wave, potential, table_z, table_y, codes, sides, *sources)


def last_x_kernel(frequency_x, frequency_yz, table, coeffs, *refs):
    bufs, (out, tall) = refs[:-2], refs[-2:]
    parts, size_x, columns, lanes = coeffs.shape

    def some_columns(g, carry):
        loaded = []
        for h in range(COLUMNS):
            loaded.append(jnp.concatenate([buf[COLUMNS * g + h] for buf in bufs], axis=0))
        result = jnp.dot(
            table[...], jnp.concatenate(loaded, axis=1), preferred_element_type=jnp.float32
        )
        for h in range(COLUMNS):
            tall[pl.ds(COLUMNS * g + h, parts * size_x, stride=columns), :] = result[
                :, h * lanes : (h + 1) * lanes
            ]
        return carry

    lax.fori_loop(0, columns // COLUMNS, some_columns, 0)

    def finish(k, carry):
        kinetic = frequency_x[k] + frequency_yz[...]
        for part in range(parts):
            start = pl.multiple_of((part * size_x + k) * columns, 8)
            out[part, k] = (
                tall[pl.ds(start, columns), :] + kinetic * coeffs[part, k].astype(jnp.float32)
            ).astype(jnp.bfloat16)
        return carry

    lax.fori_loop(0, size_x, finish, 0, unroll=8)


def last_x(frequency_x, frequency_yz, table, coeffs, bufs):
    _, size_x, columns, size_z = coeffs.shape
    lanes = size_z // 2
    spec = pl.BlockSpec((2, size_x, columns, lanes), lambda i: (0, 0, 0, i))
    return pl.pallas_call(
        last_x_kernel,
        grid=(2,),
        in_specs=[
            SMEM_SPEC,
            pl.BlockSpec((columns, lanes), lambda i: (0, i)),
            whole(table.shape),
            spec,
        ]
        + [pl.BlockSpec((*b.shape[:2], lanes), lambda i: (0, 0, i)) for b in bufs],
        out_specs=spec,
        out_shape=jax.ShapeDtypeStruct(coeffs.shape, jnp.bfloat16),
        scratch_shapes=[pltpu.VMEM((2 * size_x * columns, lanes), jnp.float32)],
        compiler_params=params(1),
        cost_estimate=cost(9),
        name="last_x",
    )(frequency_x, frequency_yz, table, coeffs, *bufs)


def per_device_chunked(wave_coeffs, occupation, potential, projectors, coupling, sphere_blocks):
    pieces = lax.axis_size("fft")
    bands = lax.axis_size("band")
    slab = lax.axis_index("fft")
    coeffs = wave_coeffs[0]
    _, size_x, columns, size_z = coeffs.shape
    slab_planes, size_y, _ = potential.shape
    atom_dev, nproj, blocks, cells = projectors.shape
    zblocks = size_z // cells
    outer, inner = chunk_planes(slab_planes)
    up = [(i, (i + 1) % pieces) for i in range(pieces)]
    down = [(j, i) for i, j in up]

    inverse_x, forward_x = (real_blocks(size_x, s) for s in (1.0, -1.0))
    inverse_y, forward_y = (real_blocks(size_y, s) for s in (1.0, -1.0))
    inverse_z, forward_z = (real_blocks(size_z, s) for s in (1.0, -1.0))
    place_outer, place_inner = (
        np.arange(pieces)[:, None] * slab_planes + np.array(chunk)[None, :]
        for chunk in (outer, inner)
    )
    table_x_outer = np.stack([inverse_x[r][place_outer] for r in range(2)], 1)
    table_x_inner = np.stack([inverse_x[r][place_inner] for r in range(2)], 2)
    tables_back_x = [
        np.stack([forward_x[:, :, r][:, :, place] for r in range(2)], 3).reshape(
            2 * size_x, pieces, -1
        )
        for place in (place_outer, place_inner)
    ]
    split_y = (2, size_y, 2, pieces, columns)
    tables = [
        table_x_outer.reshape(-1, 2 * size_x),
        table_x_inner.reshape(-1, 2 * size_x),
        inverse_y.reshape(2 * size_y, -1),
        inverse_y.reshape(split_y).transpose(0, 1, 3, 2, 4).reshape(2 * size_y, -1),
        inverse_z.transpose(2, 3, 0, 1).reshape(2 * size_z, -1),
        forward_z.transpose(2, 3, 0, 1).reshape(2 * size_z, -1),
        forward_y.reshape(2 * size_y, -1),
        forward_y.reshape(2, pieces, columns, -1).transpose(1, 0, 2, 3).reshape(2 * size_y, -1),
        np.stack(
            [
                np.concatenate(
                    [t[:, np.arange(pieces) ^ d].reshape(2 * size_x, -1) for t in tables_back_x], 1
                )
                for d in range(pieces)
            ]
        ),
    ]
    (
        table_x_outer, table_x_inner, table_y_outer, table_y_inner, table_z,
        table_back_z, table_back_y_outer, table_back_y_inner, tables_back_x,
    ) = (jnp.asarray(t.astype(jnp.bfloat16)) for t in tables)

    table_back_x = lax.dynamic_index_in_dim(tables_back_x, slab, 0, keepdims=False)

    where = slab.reshape(1)
    section_outer = first_x(where, table_x_outer, coeffs, len(outer), pieces, False)
    section_outer, table_x_inner, sphere_blocks = lax.optimization_barrier(
        (section_outer, table_x_inner, sphere_blocks)
    )
    section_inner = first_x(where, table_x_inner, coeffs, len(inner), pieces, True)

    entries = atom_dev * blocks

    def codes_of(chunk, shift):
        owner = (slab + shift + pieces) % pieces
        numbers = lax.dynamic_slice_in_dim(sphere_blocks, owner * atom_dev, atom_dev, 0)
        plane = numbers // (size_y * zblocks) - slab * slab_planes
        rest = numbers % (size_y * zblocks)
        if chunk is outer:
            inside = ((plane >= 0) & (plane < EDGE)) | (
                (plane >= slab_planes - EDGE) & (plane < slab_planes)
            )
            plane = jnp.where(plane < EDGE, plane, plane - len(inner))
        else:
            inside = (plane >= EDGE) & (plane < slab_planes - EDGE)
            plane = plane - EDGE
        code = jnp.where(inside, plane * size_y + rest // zblocks, -1)
        return code.reshape(entries), (rest % zblocks).reshape(entries)

    found = [codes_of(outer, shift) for shift in (0, -1, 1)]
    codes_outer, sides_outer = (jnp.stack(values) for values in zip(*found))
    codes_inner, sides_inner = (values[None] for values in codes_of(inner, 0))
    sides_outer, sides_inner = sides_outer[:, :, None], sides_inner[:, :, None]
    strength = 3.0 * math.sqrt(cells * blocks) / nproj
    coupled = (coupling + coupling.T) * (0.5 * strength)
    coupled = jnp.broadcast_to(coupled.T[:, :, None], (nproj, nproj, cells))

    half = pieces // 2
    near, far = list(range(1, half)), list(range(half, pieces))

    class Queue:
        def __init__(self, window):
            self.window, self.sent = window, []

        def send(self, values, arrived, partners, gate=None):
            for k in partners:
                block = values[k]
                if gate is not None:
                    block, _ = lax.optimization_barrier((block, gate))
                if len(self.sent) >= self.window:
                    row, m = self.sent[-self.window]
                    block, row[m] = lax.optimization_barrier((block, row[m]))
                arrived[k] = lax.ppermute(block, "fft", [(j, j ^ k) for j in range(pieces)])
                self.sent.append((arrived, k))

    received_outer, received_inner = (
        [section[0]] + [None] * (pieces - 1) for section in (section_outer, section_inner)
    )
    for window, partners in ((2, near), (3, far)):
        queue = Queue(window)
        queue.send(section_outer, received_outer, partners)
        queue.send(section_inner, received_inner, partners)
    wave_outer, density_outer, rows_outer = make_field(
        where, occupation, received_outer, table_y_outer, table_z, codes_outer[:, :, None],
        sides_outer, len(outer), pieces, False,
    )
    from_following = lax.ppermute(rows_outer[1], "fft", down)
    from_previous = lax.ppermute(rows_outer[2], "fft", up)
    density_outer = lax.psum(density_outer, "band")
    wave_inner, density_inner, rows_inner = make_field(
        where, occupation, received_inner, table_y_inner, table_z, codes_inner[:, :, None],
        sides_inner, len(inner), pieces, True,
    )
    projected, spread = make_nonlocal(
        coupled, projectors, [rows_outer[0], rows_inner[0], from_following, from_previous]
    )
    spread_previous = lax.ppermute(spread, "fft", up)
    spread_following = lax.ppermute(spread, "fft", down)
    edge_steps = EDGE // PLANES
    inner_steps = len(inner) // PLANES
    back_inner = go_back(
        where, wave_inner, potential, table_back_z, table_back_y_inner, codes_inner[:, None, :],
        sides_inner, [spread], lambda i: i + edge_steps, pieces, True,
    )
    back_inner, spread_previous, spread_following = lax.optimization_barrier(
        (back_inner, spread_previous, spread_following)
    )
    near_queue, far_queue = Queue(1), Queue(half)
    arrived_inner = [back_inner[0]] + [None] * (pieces - 1)
    far_queue.send(back_inner, arrived_inner, far)
    near_queue.send(back_inner, arrived_inner, near[:1])
    wave_outer, density_outer = lax.optimization_barrier((wave_outer, density_outer))
    back_outer = go_back(
        where, wave_outer, potential, table_back_z, table_back_y_outer, codes_outer[:, None, :],
        sides_outer, [spread, spread_previous, spread_following],
        lambda i: jnp.where(i < edge_steps, i, i + inner_steps), pieces, False,
    )
    density_inner, density_outer = lax.optimization_barrier((density_inner, density_outer))
    density_inner = lax.psum(density_inner, "band")
    back_outer = list(back_outer)
    back_outer[-1], density_inner = lax.optimization_barrier((back_outer[-1], density_inner))
    near_queue.send(back_inner, arrived_inner, near[1:], back_outer[0])
    arrived_outer = [back_outer[0]] + [None] * (pieces - 1)
    far_queue.send(back_outer, arrived_outer, far)
    near_queue.send(back_outer, arrived_outer, near)
    back_inner = [
        b.reshape(len(inner), 2, columns, size_z).transpose(2, 1, 0, 3).reshape(columns, -1, size_z)
        for b in arrived_inner
    ]
    density = jnp.concatenate([density_outer[:EDGE], density_inner, density_outer[EDGE:]], axis=0)

    index_x = np.arange(size_x)
    frequency_x = jnp.asarray(
        (np.where(2 * index_x < size_x, index_x, index_x - size_x) / size_x) ** 2, jnp.float32
    )
    index_y = slab * columns + jnp.arange(columns, dtype=jnp.int32)
    index_z = jnp.arange(size_z, dtype=jnp.int32)
    frequency_yz = wave_squares(index_y, size_y)[:, None] + wave_squares(index_z, size_z)[None, :]
    coeffs, density, back_inner = lax.optimization_barrier((coeffs, density, back_inner))
    applied = last_x(frequency_x, frequency_yz, table_back_x, coeffs, arrived_outer + back_inner)
    return (applied[None], density, projected[None, :, :, :, 0])


def per_device(wave_coeffs, occupation, potential, projectors, coupling, sphere_blocks):
    pieces, bands = lax.axis_size("fft"), lax.axis_size("band")
    size_z = wave_coeffs.shape[4]
    columns = wave_coeffs.shape[3]
    slab_planes = potential.shape[0]
    chunked = (
        pieces >= 4
        and pieces & (pieces - 1) == 0
        and slab_planes % EDGE == 0
        and slab_planes >= 3 * EDGE
        and EDGE >= HALO
        and columns % 8 == 0
        and size_z % 256 == 0
        and projectors.shape[0] % bands == 0
        and projectors.shape[3] == 128
        and projectors.shape[1] == 8
    )
    chosen = per_device_chunked if chunked else per_device_plain
    return chosen(wave_coeffs, occupation, potential, projectors, coupling, sphere_blocks)


def solution(mesh):
    placed = (
        P("band", None, None, "fft", None),
        P("band", None),
        P("fft", None, None),
        P("fft", None, None, None),
        P(),
        P(),
    )
    return jax.shard_map(
        per_device,
        mesh=mesh,
        in_specs=placed,
        out_specs=(
            P("band", None, None, "fft", None),
            P("fft", None, None),
            P("band", "fft", None, None),
        ),
        check_vma=False,
    )
```

```python
import functools
import math

import jax
import jax.numpy as jnp
import numpy as np
from jax import lax
from jax.experimental import pallas as pl
from jax.experimental.pallas import tpu as pltpu
from jax.sharding import PartitionSpec as P

HALO = 6
EDGE = 8
PLANES = 4
COLUMNS = 8
VMEM_BYTES = 56 * 1024 * 1024


def extended(shard, sides, width):
    for axis, dim in sides:
        count, length = (lax.axis_size(axis), shard.shape[dim])
        up = [(i, (i + 1) % count) for i in range(count)]
        down = [(j, i) for i, j in up]
        last = lax.slice_in_dim(shard, length - width, length, axis=dim)
        first = lax.slice_in_dim(shard, 0, width, axis=dim)
        before = lax.ppermute(last, axis, up)
        after = lax.ppermute(first, axis, down)
        shard = jnp.concatenate([before, shard, after], axis=dim)
    return shard


def dft_table(length, sign_value):
    indices = jnp.arange(length, dtype=jnp.int32)
    phases = indices[:, None] * indices[None, :] % length
    angles = 2.0 * math.pi / length * phases.astype(jnp.float32)
    factor = 1.0 / math.sqrt(length)
    cosine = jnp.cos(angles) * factor
    sine_part = jnp.sin(angles) * (sign_value * factor)
    upper_rows = jnp.stack([cosine, -sine_part])
    bottom = jnp.stack([sine_part, cosine])
    return jnp.stack([upper_rows, bottom]).astype(jnp.bfloat16)


def wave_squares(indices, length):
    frequency = (
        jnp.where(2 * indices < length, indices, indices - length).astype(jnp.float32) / length
    )
    return frequency * frequency


def per_device_plain(wave_coeffs, occupation, potential, projectors, coupling, sphere_blocks):
    pieces = lax.axis_size("fft")
    slab_index = lax.axis_index("fft")
    coeffs = wave_coeffs[0]
    size_x = coeffs.shape[1]
    columns = coeffs.shape[2]
    size_z = coeffs.shape[3]
    slab_planes = potential.shape[0]
    size_y = potential.shape[1]
    atom_dev = projectors.shape[0]
    nproj_count = projectors.shape[1]
    block_cells = projectors.shape[3]
    zblocks = size_z // block_cells
    plane_blocks = size_y * zblocks
    total_atoms = atom_dev * pieces
    table_x = dft_table(size_x, 1.0).transpose(0, 2, 1, 3).reshape(2 * size_x, 2 * size_x)
    inverse_y = dft_table(size_y, 1.0)
    inverse_z = dft_table(size_z, 1.0)
    flattened = coeffs.reshape(2 * size_x, columns * size_z)
    along_x = jnp.dot(table_x, flattened, preferred_element_type=jnp.float32)
    along_x = along_x.reshape(2, size_x, columns, size_z).astype(jnp.bfloat16)
    along_y = jnp.einsum(
        "abyk,bxkz->axyz",
        inverse_y,
        lax.all_to_all(along_x, "fft", split_axis=1, concat_axis=2, tiled=True),
        preferred_element_type=jnp.float32,
    ).astype(jnp.bfloat16)
    wave_field = jnp.einsum(
        "abzk,bxyk->axyz", inverse_z, along_y, preferred_element_type=jnp.float32
    ).astype(jnp.bfloat16)
    weights = occupation[0]
    real_part = wave_field[0].astype(jnp.float32)
    imag_part = wave_field[1].astype(jnp.float32)
    partial_density = weights[0] * real_part * real_part + weights[1] * imag_part * imag_part
    density = lax.psum(partial_density.astype(jnp.bfloat16), "band")
    strength = 3.0 * math.sqrt(block_cells * projectors.shape[2]) / nproj_count
    coupled = (coupling + coupling.T) * (0.5 * strength)
    nearby = extended(projectors, (("fft", 0),), atom_dev)
    atom_rows = (
        slab_index * atom_dev - atom_dev + jnp.arange(3 * atom_dev, dtype=jnp.int32) + total_atoms
    ) % total_atoms
    near_blocks = sphere_blocks[atom_rows]
    plane_index = near_blocks // plane_blocks
    inside = plane_index // slab_planes == slab_index
    local_index = jnp.where(
        inside,
        (plane_index - slab_index * slab_planes) * plane_blocks + near_blocks % plane_blocks,
        0,
    )
    blocks_own = wave_field.reshape(2, slab_planes * plane_blocks, block_cells)
    gathered = blocks_own[:, local_index] * inside[None, :, :, None].astype(jnp.bfloat16)
    partial_value = jnp.einsum(
        "ajsk,bask->abj", nearby, gathered, preferred_element_type=jnp.float32
    )
    summed = extended(partial_value, (("fft", 0),), atom_dev)
    projections_own = (
        summed[:atom_dev] + summed[2 * atom_dev : 3 * atom_dev] + summed[4 * atom_dev :]
    )
    energy_own = jnp.einsum(
        "ij,abj->abi", coupled, projections_own, precision=lax.Precision.HIGHEST
    )
    energy = extended(energy_own, (("fft", 0),), atom_dev)
    spread = jnp.einsum(
        "ajsk,abj->bask", nearby.astype(jnp.float32), energy, precision=lax.Precision.HIGHEST
    )
    spread = spread * inside[None, :, :, None].astype(jnp.float32)
    accumulated = (
        jnp.zeros((2, slab_planes * plane_blocks, block_cells), jnp.float32)
        .at[:, local_index]
        .add(spread)
    )
    nonlocal_term = accumulated.reshape(2, slab_planes, size_y, size_z)
    total_field = (
        potential.astype(jnp.float32)[None] * wave_field.astype(jnp.float32) + nonlocal_term
    ).astype(jnp.bfloat16)
    forward_z = dft_table(size_z, -1.0)
    forward_y = dft_table(size_y, -1.0)
    forward_x = dft_table(size_x, -1.0)
    back_z = jnp.einsum(
        "abzk,bxyk->axyz", forward_z, total_field, preferred_element_type=jnp.float32
    ).astype(jnp.bfloat16)
    back_y = jnp.einsum(
        "abyk,bxkz->axyz", forward_y, back_z, preferred_element_type=jnp.float32
    ).astype(jnp.bfloat16)
    transformed = jnp.einsum(
        "abxk,bkyz->axyz",
        forward_x,
        lax.all_to_all(back_y, "fft", split_axis=2, concat_axis=1, tiled=True),
        preferred_element_type=jnp.float32,
    )
    index_x = jnp.arange(size_x, dtype=jnp.int32)
    index_y = slab_index * columns + jnp.arange(columns, dtype=jnp.int32)
    index_z = jnp.arange(size_z, dtype=jnp.int32)
    kinetic = (
        wave_squares(index_x, size_x)[:, None, None]
        + wave_squares(index_y, size_y)[None, :, None]
        + wave_squares(index_z, size_z)[None, None, :]
    )
    applied = (transformed + kinetic[None] * coeffs.astype(jnp.float32)).astype(jnp.bfloat16)
    return (applied[None], density, projections_own[None])


def real_blocks(length, sign):
    index = np.arange(length)
    angles = 2.0 * np.pi / length * (index[:, None] * index[None, :] % length)
    cosine = np.cos(angles) / np.sqrt(length)
    sine = sign * np.sin(angles) / np.sqrt(length)
    blocks = np.empty((2, length, 2, length))
    blocks[0, :, 0, :] = cosine
    blocks[1, :, 1, :] = cosine
    blocks[0, :, 1, :] = -sine
    blocks[1, :, 0, :] = sine
    return blocks


def chunk_planes(slab_planes):
    low, high = list(range(EDGE)), list(range(slab_planes - EDGE, slab_planes))
    return [low + high, list(range(EDGE, slab_planes - EDGE))]


def params(steps):
    return pltpu.CompilerParams(
        dimension_semantics=("arbitrary",) * steps, vmem_limit_bytes=VMEM_BYTES
    )


def cost(products, values):
    return pl.CostEstimate(flops=4 * products, bytes_accessed=4 * values, transcendentals=0)


def whole(shape):
    return pl.BlockSpec(shape, lambda i: (0,) * len(shape))


SMEM_SPEC = pl.BlockSpec(memory_space=pltpu.SMEM)


def paired(refs, slab):
    return [(lax.bitwise_xor(slab, jnp.int32(k)), ref) for k, ref in enumerate(refs)]


def shifted(refs, slab):
    return [(lax.rem(slab + k, len(refs)), ref) for k, ref in enumerate(refs)]


def first_x_kernel(slab, table_ref, coeffs_ref, *refs, pieces, natural):
    scratch = 3 if natural else 2
    outs = paired(refs[:-scratch], slab[0])
    turned, wide, *tall = refs[-scratch:]
    parts, size_x, columns, lanes = coeffs_ref.shape
    rows = parts * size_x
    height = table_ref.shape[0] // pieces

    for k, (device, _) in enumerate(outs):
        start = pl.multiple_of(device * height, 16)
        turned[k * height : (k + 1) * height, :] = table_ref[pl.ds(start, height), :]

    def widen(k, carry):
        for part in range(parts):
            start = pl.multiple_of((part * size_x + k * 8) * columns, 8)
            wide[pl.ds(start, 8 * columns), :] = (
                coeffs_ref[part, pl.ds(k * 8, 8)].astype(jnp.float32).reshape(8 * columns, lanes)
            )
        return carry

    lax.fori_loop(0, size_x // 8, widen, 0, unroll=2)

    def some_columns(g, carry):
        loaded = [
            wide[pl.ds(COLUMNS * g + h, rows, stride=columns), :].astype(jnp.bfloat16)
            for h in range(COLUMNS)
        ]
        result = jnp.dot(
            turned[...], jnp.concatenate(loaded, axis=1), preferred_element_type=jnp.float32
        )
        for h in range(COLUMNS):
            piece = result[:, h * lanes : (h + 1) * lanes]
            if natural:
                tall[0][pl.ds(COLUMNS * g + h, piece.shape[0], stride=columns), :] = piece
            else:
                piece = piece.astype(jnp.bfloat16)
                for k, (_, out) in enumerate(outs):
                    out[COLUMNS * g + h] = piece[k * height : (k + 1) * height]
        return carry

    lax.fori_loop(0, columns // COLUMNS, some_columns, 0)
    if natural:
        for k, (_, out) in enumerate(outs):
            values = tall[0][k * height * columns : (k + 1) * height * columns, :]
            out[...] = values.astype(jnp.bfloat16).reshape(out.shape)


def first_x(slab, table, coeffs, planes, pieces, natural):
    _, size_x, columns, size_z = coeffs.shape
    lanes = size_z // 2
    shape = (planes, 2 * columns) if natural else (columns, 2 * planes)
    scratch = [
        pltpu.VMEM(table.shape, jnp.bfloat16),
        pltpu.VMEM((2 * size_x * columns, lanes), jnp.float32),
    ]
    if natural:
        scratch.append(pltpu.VMEM((2 * pieces * planes * columns, lanes), jnp.float32))
    out_specs = [pl.BlockSpec((*shape, lanes), lambda i: (0, 0, i))] * pieces
    out_shape = [jax.ShapeDtypeStruct((*shape, size_z), jnp.bfloat16)] * pieces
    return pl.pallas_call(
        functools.partial(first_x_kernel, pieces=pieces, natural=natural),
        grid=(2,),
        in_specs=[
            SMEM_SPEC,
            whole(table.shape),
            pl.BlockSpec((2, size_x, columns, lanes), lambda i: (0, 0, 0, i)),
        ],
        out_specs=out_specs,
        out_shape=out_shape,
        scratch_shapes=scratch,
        compiler_params=params(1),
        cost_estimate=cost(2 * size_x * pieces * planes * columns * size_z, 2 * size_x * columns * size_z),
        name="first_x",
    )(slab, table, coeffs)


def ones_at(codes, count, axis):
    shape = (codes.shape[0], count) if axis == 1 else (count, codes.shape[1])
    places = lax.broadcasted_iota(jnp.int32, shape, axis)
    return jnp.where(codes == places, 1.0, 0.0).astype(jnp.bfloat16)


def field_kernel(slab, weights, table_y, table_z, codes, sides, *refs, pieces, count, natural):
    bufs = paired(refs[:count], slab[0])
    wave, density, rows_out, gathered, wide = refs[count:]
    _, near, size_y, size_z = wave.shape
    groups, entries, _ = codes.shape
    lanes = 128
    halves = size_z // lanes
    i, last = pl.program_id(0), pl.num_programs(0) - 1
    planes = near * (last + 1)

    @pl.when(i == 0)
    def _():
        gathered[...] = jnp.zeros_like(gathered)

    loaded = []
    if natural:
        for source, buf in bufs:
            wide[source] = buf[...]
        for h in range(near):
            loaded.append(wide[:, h].reshape(2 * size_y, size_z))
    else:
        columns, rows, _ = bufs[0][1].shape

        @pl.when(i == 0)
        def _():
            for source, buf in bufs:
                start = pl.multiple_of(source * columns * rows, 8)
                values = buf[...].astype(jnp.float32).reshape(columns * rows, size_z)
                for q in range(halves):
                    wide[q, pl.ds(start, columns * rows), :] = values[
                        :, q * lanes : (q + 1) * lanes
                    ]

        for h in range(near):
            plane = i * near + h
            both = [
                jnp.concatenate(
                    [
                        wide[q, pl.ds(part * planes + plane, size_y, stride=rows), :]
                        for q in range(halves)
                    ],
                    axis=1,
                ).astype(jnp.bfloat16)
                for part in range(2)
            ]
            loaded.append(jnp.concatenate(both, axis=0))
    along_y = jnp.dot(
        table_y[...], jnp.concatenate(loaded, axis=1), preferred_element_type=jnp.float32
    ).astype(jnp.bfloat16)
    turned = jnp.concatenate(
        [
            jnp.concatenate(
                [
                    along_y[:size_y, h * size_z : (h + 1) * size_z],
                    along_y[size_y:, h * size_z : (h + 1) * size_z],
                ],
                axis=1,
            )
            for h in range(near)
        ],
        axis=0,
    )
    result = jnp.dot(turned, table_z[...], preferred_element_type=jnp.float32).astype(jnp.bfloat16)
    for h in range(near):
        total = jnp.zeros((size_y, size_z), jnp.float32)
        for part in range(2):
            values = result[h * size_y : (h + 1) * size_y, part * size_z : (part + 1) * size_z]
            wave[part, h] = values
            values = values.astype(jnp.float32)
            total += weights[0, part] * values * values
        density[h] = total.astype(jnp.bfloat16)

    used = [0] if groups == 1 else [0, 1 + (2 * i > last).astype(jnp.int32)]
    for group in used:
        places = ones_at(codes[group] - i * near * size_y, near * size_y, 1)
        gathered[group] += jnp.dot(places, result, preferred_element_type=jnp.float32)

    @pl.when(i == last)
    def _():
        for group in range(groups):
            for part in range(2):
                total = jnp.zeros((entries, lanes), jnp.float32)
                for q in range(halves):
                    start = part * size_z + q * lanes
                    total += jnp.where(
                        sides[group] == q, gathered[group, :, start : start + lanes], 0.0
                    )
                rows_out[group, part] = total.astype(jnp.bfloat16)


def make_field(slab, weights, bufs, table_y, table_z, codes, sides, planes, pieces, natural):
    size_z = bufs[0].shape[-1]
    size_y = table_y.shape[0] // 2
    columns = size_y // pieces
    groups, entries, _ = codes.shape
    if natural:
        buf_spec = pl.BlockSpec((PLANES, 2 * columns, size_z), lambda i: (i, 0, 0))
        wide = pltpu.VMEM((pieces, PLANES, 2 * columns, size_z), jnp.bfloat16)
    else:
        buf_spec = whole(bufs[0].shape)
        wide = pltpu.VMEM((size_z // 128, 2 * planes * size_y, 128), jnp.float32)
    return pl.pallas_call(
        functools.partial(field_kernel, pieces=pieces, count=len(bufs), natural=natural),
        grid=(planes // PLANES,),
        in_specs=[SMEM_SPEC, SMEM_SPEC]
        + [whole(a.shape) for a in (table_y, table_z, codes, sides)]
        + [buf_spec] * len(bufs),
        out_specs=[
            pl.BlockSpec((2, PLANES, size_y, size_z), lambda i: (0, i, 0, 0)),
            pl.BlockSpec((PLANES, size_y, size_z), lambda i: (i, 0, 0)),
            whole((groups, 2, entries, 128)),
        ],
        out_shape=[
            jax.ShapeDtypeStruct((2, planes, size_y, size_z), jnp.bfloat16),
            jax.ShapeDtypeStruct((planes, size_y, size_z), jnp.bfloat16),
            jax.ShapeDtypeStruct((groups, 2, entries, 128), jnp.bfloat16),
        ],
        scratch_shapes=[pltpu.VMEM((groups, entries, 2 * size_z), jnp.float32), wide],
        compiler_params=params(1),
        cost_estimate=cost(
            2 * planes * size_y * size_z * (size_y + size_z), 2 * planes * size_y * size_z
        ),
        name="make_field",
    )(slab, weights, table_y, table_z, codes, sides, *bufs)


def nonlocal_kernel(coupled, projectors, *refs):
    parts, (projections, spread) = refs[:-2], refs[-2:]
    atoms, nproj, blocks, cells = projectors.shape
    for atom in range(atoms):
        tables = [projectors[atom, j].astype(jnp.float32) for j in range(nproj)]
        place = pl.ds(atom * blocks, blocks)
        for part in range(2):
            rows = sum(p[part, place].astype(jnp.float32) for p in parts)
            tile = jnp.concatenate(
                [jnp.sum(t * rows, axis=0, keepdims=True) for t in tables], axis=0
            )
            mixed = jnp.zeros_like(tile)
            for j in range(nproj):
                mixed += coupled[j] * tile[j : j + 1]
            projections[atom, part] = jnp.broadcast_to(
                jnp.sum(tile, -1, keepdims=True), tile.shape
            )
            energy = jnp.broadcast_to(jnp.sum(mixed, -1, keepdims=True), tile.shape)
            spread[part, place] = sum(
                t * energy[j : j + 1] for j, t in enumerate(tables)
            ).astype(jnp.bfloat16)


def make_nonlocal(coupled, projectors, parts):
    atoms, nproj, _, cells = projectors.shape
    return pl.pallas_call(
        nonlocal_kernel,
        out_shape=[
            jax.ShapeDtypeStruct((atoms, 2, nproj, cells), jnp.float32),
            jax.ShapeDtypeStruct(parts[0].shape, jnp.bfloat16),
        ],
        name="make_nonlocal",
    )(coupled, projectors, *parts)


def back_kernel(slab, wave, potential, table_z, table_y, codes, sides, *refs, pieces, natural):
    groups, _, entries = codes.shape
    sources, outs = refs[:groups], refs[groups:-2]
    spread, tall = refs[-2:]
    outs = shifted(outs, slab[0])
    near, size_y, size_z = potential.shape
    lanes = 128
    halves = size_z // lanes
    i, last = pl.program_id(0), pl.num_programs(0) - 1
    planes = near * (last + 1)

    @pl.when(i == 0)
    def _():
        for group, source in enumerate(sources):
            for part in range(2):
                for q in range(halves):
                    start = part * size_z + q * lanes
                    spread[group, :, start : start + lanes] = jnp.where(
                        sides[group] == q, source[part].astype(jnp.float32), 0.0
                    ).astype(jnp.bfloat16)

    used = [0] if groups == 1 else [0, 1 + (2 * i > last).astype(jnp.int32)]
    extra = jnp.zeros((near * size_y, 2 * size_z), jnp.float32)
    for group in used:
        places = ones_at(codes[group] - i * near * size_y, near * size_y, 0)
        extra += jnp.dot(places, spread[group], preferred_element_type=jnp.float32)
    fields = []
    for h in range(near):
        local = potential[h].astype(jnp.float32)
        both = [
            local * wave[part, h].astype(jnp.float32)
            + extra[h * size_y : (h + 1) * size_y, part * size_z : (part + 1) * size_z]
            for part in range(2)
        ]
        fields.append(jnp.concatenate(both, axis=1).astype(jnp.bfloat16))
    stacked = jnp.concatenate(fields, axis=0)
    back_z = jnp.dot(stacked, table_z[...], preferred_element_type=jnp.float32).astype(jnp.bfloat16)
    turned = jnp.concatenate(
        [
            jnp.concatenate(
                [
                    back_z[h * size_y : (h + 1) * size_y, :size_z],
                    back_z[h * size_y : (h + 1) * size_y, size_z:],
                ],
                axis=0,
            )
            for h in range(near)
        ],
        axis=1,
    )
    back_y = jnp.dot(table_y[...], turned, preferred_element_type=jnp.float32)
    if natural:
        back_y = back_y.astype(jnp.bfloat16)
        for h in range(near):
            tall[:, h] = back_y[:, h * size_z : (h + 1) * size_z].reshape(
                pieces, outs[0][1].shape[1], size_z
            )
        for target, out in outs:
            out[...] = tall[target]
        return
    columns, rows, _ = outs[0][1].shape
    for h in range(near):
        for part in range(2):
            for q in range(halves):
                start = h * size_z + q * lanes
                tall[q, pl.ds(part * planes + i * near + h, size_y, stride=rows), :] = back_y[
                    part * size_y : (part + 1) * size_y, start : start + lanes
                ]

    @pl.when(i == last)
    def _():
        for target, out in outs:
            start = pl.multiple_of(target * columns * rows, 8)
            values = [tall[q, pl.ds(start, columns * rows), :] for q in range(halves)]
            out[...] = (
                jnp.concatenate(values, axis=1).astype(jnp.bfloat16).reshape(columns, rows, size_z)
            )


def go_back(slab, wave, potential, table_z, table_y, codes, sides, sources, place, pieces, natural):
    _, planes, size_y, size_z = wave.shape
    columns = size_y // pieces
    groups, _, entries = codes.shape
    scratch = [pltpu.VMEM((groups, entries, 2 * size_z), jnp.bfloat16)]
    if natural:
        shape = (planes, 2 * columns, size_z)
        out_specs = [pl.BlockSpec((PLANES, 2 * columns, size_z), lambda i: (i, 0, 0))] * pieces
        scratch.append(pltpu.VMEM((pieces, PLANES, 2 * columns, size_z), jnp.bfloat16))
    else:
        shape = (columns, 2 * planes, size_z)
        out_specs = [whole(shape)] * pieces
        scratch.append(pltpu.VMEM((size_z // 128, 2 * planes * size_y, 128), jnp.float32))
    return pl.pallas_call(
        functools.partial(back_kernel, pieces=pieces, natural=natural),
        grid=(planes // PLANES,),
        in_specs=[
            SMEM_SPEC,
            pl.BlockSpec((2, PLANES, size_y, size_z), lambda i: (0, i, 0, 0)),
            pl.BlockSpec((PLANES, size_y, size_z), lambda i: (place(i), 0, 0)),
        ]
        + [whole(a.shape) for a in (table_z, table_y, codes, sides, *sources)],
        out_specs=out_specs,
        out_shape=[jax.ShapeDtypeStruct(shape, jnp.bfloat16)] * pieces,
        scratch_shapes=scratch,
        compiler_params=params(1),
        cost_estimate=cost(
            2 * planes * size_y * size_z * (size_y + size_z), 2 * planes * size_y * size_z
        ),
        name="go_back",
    )(slab, wave, potential, table_z, table_y, codes, sides, *sources)


def last_x_kernel(frequency_x, frequency_yz, table, coeffs, *refs):
    bufs, (out, tall) = refs[:-2], refs[-2:]
    parts, size_x, columns, lanes = coeffs.shape

    def some_columns(g, carry):
        loaded = []
        for h in range(COLUMNS):
            loaded.append(jnp.concatenate([buf[COLUMNS * g + h] for buf in bufs], axis=0))
        result = jnp.dot(
            table[...], jnp.concatenate(loaded, axis=1), preferred_element_type=jnp.float32
        )
        for h in range(COLUMNS):
            tall[pl.ds(COLUMNS * g + h, parts * size_x, stride=columns), :] = result[
                :, h * lanes : (h + 1) * lanes
            ]
        return carry

    lax.fori_loop(0, columns // COLUMNS, some_columns, 0)

    def finish(k, carry):
        kinetic = frequency_x[k] + frequency_yz[...]
        for part in range(parts):
            start = pl.multiple_of((part * size_x + k) * columns, 8)
            out[part, k] = (
                tall[pl.ds(start, columns), :] + kinetic * coeffs[part, k].astype(jnp.float32)
            ).astype(jnp.bfloat16)
        return carry

    lax.fori_loop(0, size_x, finish, 0, unroll=8)


def last_x(frequency_x, frequency_yz, table, coeffs, bufs):
    _, size_x, columns, size_z = coeffs.shape
    lanes = size_z // 2
    spec = pl.BlockSpec((2, size_x, columns, lanes), lambda i: (0, 0, 0, i))
    return pl.pallas_call(
        last_x_kernel,
        grid=(2,),
        in_specs=[
            SMEM_SPEC,
            pl.BlockSpec((columns, lanes), lambda i: (0, i)),
            whole(table.shape),
            spec,
        ]
        + [pl.BlockSpec((*b.shape[:2], lanes), lambda i: (0, 0, i)) for b in bufs],
        out_specs=spec,
        out_shape=jax.ShapeDtypeStruct(coeffs.shape, jnp.bfloat16),
        scratch_shapes=[pltpu.VMEM((2 * size_x * columns, lanes), jnp.float32)],
        compiler_params=params(1),
        cost_estimate=cost(2 * size_x * size_x * columns * size_z, 3 * size_x * columns * size_z),
        name="last_x",
    )(frequency_x, frequency_yz, table, coeffs, *bufs)


def per_device_chunked(wave_coeffs, occupation, potential, projectors, coupling, sphere_blocks):
    pieces = lax.axis_size("fft")
    bands = lax.axis_size("band")
    slab = lax.axis_index("fft")
    coeffs = wave_coeffs[0]
    _, size_x, columns, size_z = coeffs.shape
    slab_planes, size_y, _ = potential.shape
    atom_dev, nproj, blocks, cells = projectors.shape
    zblocks = size_z // cells
    outer, inner = chunk_planes(slab_planes)
    up = [(i, (i + 1) % pieces) for i in range(pieces)]
    down = [(j, i) for i, j in up]

    inverse_x, forward_x = (real_blocks(size_x, s) for s in (1.0, -1.0))
    inverse_y, forward_y = (real_blocks(size_y, s) for s in (1.0, -1.0))
    inverse_z, forward_z = (real_blocks(size_z, s) for s in (1.0, -1.0))
    place_outer, place_inner = (
        np.arange(pieces)[:, None] * slab_planes + np.array(chunk)[None, :]
        for chunk in (outer, inner)
    )
    table_x_outer = np.stack([inverse_x[r][place_outer] for r in range(2)], 1)
    table_x_inner = np.stack([inverse_x[r][place_inner] for r in range(2)], 2)
    tables_back_x = [
        np.stack([forward_x[:, :, r][:, :, place] for r in range(2)], 3).reshape(
            2 * size_x, pieces, -1
        )
        for place in (place_outer, place_inner)
    ]
    split_y = (2, size_y, 2, pieces, columns)
    tables = [
        table_x_outer.reshape(-1, 2 * size_x),
        table_x_inner.reshape(-1, 2 * size_x),
        inverse_y.reshape(2 * size_y, -1),
        inverse_y.reshape(split_y).transpose(0, 1, 3, 2, 4).reshape(2 * size_y, -1),
        inverse_z.transpose(2, 3, 0, 1).reshape(2 * size_z, -1),
        forward_z.transpose(2, 3, 0, 1).reshape(2 * size_z, -1),
        forward_y.reshape(2 * size_y, -1),
        forward_y.reshape(2, pieces, columns, -1).transpose(1, 0, 2, 3).reshape(2 * size_y, -1),
        np.stack(
            [
                np.concatenate(
                    [t[:, (d - np.arange(pieces)) % pieces].reshape(2 * size_x, -1) for t in tables_back_x],
                    axis=1,
                )
                for d in range(pieces)
            ]
        ),
    ]
    (
        table_x_outer, table_x_inner, table_y_outer, table_y_inner, table_z,
        table_back_z, table_back_y_outer, table_back_y_inner, tables_back_x,
    ) = (jnp.asarray(t.astype(jnp.bfloat16)) for t in tables)

    table_back_x = lax.dynamic_index_in_dim(tables_back_x, slab, 0, keepdims=False)

    where = slab.reshape(1)
    section_outer = first_x(where, table_x_outer, coeffs, len(outer), pieces, False)
    section_outer, table_x_inner, sphere_blocks = lax.optimization_barrier(
        (section_outer, table_x_inner, sphere_blocks)
    )
    section_inner = first_x(where, table_x_inner, coeffs, len(inner), pieces, True)

    entries = atom_dev * blocks

    def codes_of(chunk, shift):
        owner = (slab + shift + pieces) % pieces
        numbers = lax.dynamic_slice_in_dim(sphere_blocks, owner * atom_dev, atom_dev, 0)
        plane = numbers // (size_y * zblocks) - slab * slab_planes
        rest = numbers % (size_y * zblocks)
        if chunk is outer:
            inside = ((plane >= 0) & (plane < EDGE)) | (
                (plane >= slab_planes - EDGE) & (plane < slab_planes)
            )
            plane = jnp.where(plane < EDGE, plane, plane - len(inner))
        else:
            inside = (plane >= EDGE) & (plane < slab_planes - EDGE)
            plane = plane - EDGE
        code = jnp.where(inside, plane * size_y + rest // zblocks, -1)
        return code.reshape(entries), (rest % zblocks).reshape(entries)

    found = [codes_of(outer, shift) for shift in (0, -1, 1)]
    codes_outer, sides_outer = (jnp.stack(values) for values in zip(*found))
    codes_inner, sides_inner = (values[None] for values in codes_of(inner, 0))
    sides_outer, sides_inner = sides_outer[:, :, None], sides_inner[:, :, None]
    strength = 3.0 * math.sqrt(cells * blocks) / nproj
    coupled = (coupling + coupling.T) * (0.5 * strength)
    coupled = jnp.broadcast_to(coupled.T[:, :, None], (nproj, nproj, cells))

    half = pieces // 2
    near, far = list(range(1, half)), list(range(half, pieces))

    class Queue:
        def __init__(self, window):
            self.window, self.sent = window, []

        def send(self, values, arrived, partners):
            for k in partners:
                block = values[k]
                if len(self.sent) >= self.window:
                    row, m = self.sent[-self.window]
                    block, row[m] = lax.optimization_barrier((block, row[m]))
                arrived[k] = lax.ppermute(block, "fft", [(j, j ^ k) for j in range(pieces)])
                self.sent.append((arrived, k))

    received_outer, received_inner = (
        [section[0]] + [None] * (pieces - 1) for section in (section_outer, section_inner)
    )
    for partners in (near, far):
        queue = Queue(2)
        queue.send(section_outer, received_outer, partners)
        queue.send(section_inner, received_inner, partners)
    wave_outer, density_outer, rows_outer = make_field(
        where, occupation, received_outer, table_y_outer, table_z, codes_outer[:, :, None],
        sides_outer, len(outer), pieces, False,
    )
    from_following = lax.ppermute(rows_outer[1], "fft", down)
    from_previous = lax.ppermute(rows_outer[2], "fft", up)
    density_outer = lax.psum(density_outer, "band")
    wave_inner, density_inner, rows_inner = make_field(
        where, occupation, received_inner, table_y_inner, table_z, codes_inner[:, :, None],
        sides_inner, len(inner), pieces, True,
    )
    projected, spread = make_nonlocal(
        coupled, projectors, [rows_outer[0], rows_inner[0], from_following, from_previous]
    )
    spread_previous = lax.ppermute(spread, "fft", up)
    spread_following = lax.ppermute(spread, "fft", down)
    edge_steps = EDGE // PLANES
    inner_steps = len(inner) // PLANES
    back_inner = go_back(
        where, wave_inner, potential, table_back_z, table_back_y_inner, codes_inner[:, None, :],
        sides_inner, [spread], lambda i: i + edge_steps, pieces, True,
    )
    back_inner, spread_previous, spread_following = lax.optimization_barrier(
        (back_inner, spread_previous, spread_following)
    )
    def permute_all(values):
        received = [values[0]]
        for k in range(1, pieces):
            pairs = [(j, (j + k) % pieces) for j in range(pieces)]
            received.append(lax.ppermute(values[k], "fft", pairs))
        return received

    back_inner = permute_all(back_inner)
    back_outer = go_back(
        where, wave_outer, potential, table_back_z, table_back_y_outer, codes_outer[:, None, :],
        sides_outer, [spread, spread_previous, spread_following],
        lambda i: jnp.where(i < edge_steps, i, i + inner_steps), pieces, False,
    )
    density_inner, density_outer = lax.optimization_barrier((density_inner, density_outer))
    density_inner = lax.psum(density_inner, "band")
    back_outer, density_outer = lax.optimization_barrier((back_outer, density_outer))
    back_outer = permute_all(back_outer)
    back_inner = [
        b.reshape(len(inner), 2, columns, size_z).transpose(2, 1, 0, 3).reshape(columns, -1, size_z)
        for b in back_inner
    ]
    density = jnp.concatenate([density_outer[:EDGE], density_inner, density_outer[EDGE:]], axis=0)

    index_x = np.arange(size_x)
    frequency_x = jnp.asarray(
        (np.where(2 * index_x < size_x, index_x, index_x - size_x) / size_x) ** 2, jnp.float32
    )
    index_y = slab * columns + jnp.arange(columns, dtype=jnp.int32)
    index_z = jnp.arange(size_z, dtype=jnp.int32)
    frequency_yz = wave_squares(index_y, size_y)[:, None] + wave_squares(index_z, size_z)[None, :]
    coeffs, density, back_inner = lax.optimization_barrier((coeffs, density, back_inner))
    applied = last_x(frequency_x, frequency_yz, table_back_x, coeffs, back_outer + back_inner)
    return (applied[None], density, projected[None, :, :, :, 0])


def per_device(wave_coeffs, occupation, potential, projectors, coupling, sphere_blocks):
    pieces, bands = lax.axis_size("fft"), lax.axis_size("band")
    size_z = wave_coeffs.shape[4]
    columns = wave_coeffs.shape[3]
    slab_planes = potential.shape[0]
    chunked = (
        pieces >= 4
        and pieces & (pieces - 1) == 0
        and slab_planes % EDGE == 0
        and slab_planes >= 3 * EDGE
        and EDGE >= HALO
        and columns % 8 == 0
        and size_z % 256 == 0
        and projectors.shape[0] % bands == 0
        and projectors.shape[3] == 128
        and projectors.shape[1] == 8
    )
    chosen = per_device_chunked if chunked else per_device_plain
    return chosen(wave_coeffs, occupation, potential, projectors, coupling, sphere_blocks)


def solution(mesh):
    placed = (
        P("band", None, None, "fft", None),
        P("band", None),
        P("fft", None, None),
        P("fft", None, None, None),
        P(),
        P(),
    )
    return jax.shard_map(
        per_device,
        mesh=mesh,
        in_specs=placed,
        out_specs=(
            P("band", None, None, "fft", None),
            P("fft", None, None),
            P("band", "fft", None, None),
        ),
        check_vma=False,
    )
```

```python
import functools
import math

import jax
import jax.numpy as jnp
import numpy as np
from jax import lax
from jax.experimental import pallas as pl
from jax.experimental.pallas import tpu as pltpu
from jax.sharding import PartitionSpec as P

HALO = 6
EDGE = 8
PLANES = 4
COLUMNS = 8
PAIR = 2
FOUR = 4
VMEM_BYTES = 56 * 1024 * 1024


def extended(shard, sides, width):
    for axis, dim in sides:
        count, length = (lax.axis_size(axis), shard.shape[dim])
        up = [(i, (i + 1) % count) for i in range(count)]
        down = [(j, i) for i, j in up]
        last = lax.slice_in_dim(shard, length - width, length, axis=dim)
        first = lax.slice_in_dim(shard, 0, width, axis=dim)
        before = lax.ppermute(last, axis, up)
        after = lax.ppermute(first, axis, down)
        shard = jnp.concatenate([before, shard, after], axis=dim)
    return shard


def dft_table(length, sign_value):
    indices = jnp.arange(length, dtype=jnp.int32)
    phases = indices[:, None] * indices[None, :] % length
    angles = 2.0 * math.pi / length * phases.astype(jnp.float32)
    factor = 1.0 / math.sqrt(length)
    cosine = jnp.cos(angles) * factor
    sine_part = jnp.sin(angles) * (sign_value * factor)
    upper_rows = jnp.stack([cosine, -sine_part])
    bottom = jnp.stack([sine_part, cosine])
    return jnp.stack([upper_rows, bottom]).astype(jnp.bfloat16)


def wave_squares(indices, length):
    frequency = (
        jnp.where(2 * indices < length, indices, indices - length).astype(jnp.float32) / length
    )
    return frequency * frequency


def per_device_plain(wave_coeffs, occupation, potential, projectors, coupling, sphere_blocks):
    pieces = lax.axis_size("fft")
    slab_index = lax.axis_index("fft")
    coeffs = wave_coeffs[0]
    size_x = coeffs.shape[1]
    columns = coeffs.shape[2]
    size_z = coeffs.shape[3]
    slab_planes = potential.shape[0]
    size_y = potential.shape[1]
    atom_dev = projectors.shape[0]
    nproj_count = projectors.shape[1]
    block_cells = projectors.shape[3]
    zblocks = size_z // block_cells
    plane_blocks = size_y * zblocks
    total_atoms = atom_dev * pieces
    table_x = dft_table(size_x, 1.0).transpose(0, 2, 1, 3).reshape(2 * size_x, 2 * size_x)
    inverse_y = dft_table(size_y, 1.0)
    inverse_z = dft_table(size_z, 1.0)
    flattened = coeffs.reshape(2 * size_x, columns * size_z)
    along_x = jnp.dot(table_x, flattened, preferred_element_type=jnp.float32)
    along_x = along_x.reshape(2, size_x, columns, size_z).astype(jnp.bfloat16)
    along_y = jnp.einsum(
        "abyk,bxkz->axyz",
        inverse_y,
        lax.all_to_all(along_x, "fft", split_axis=1, concat_axis=2, tiled=True),
        preferred_element_type=jnp.float32,
    ).astype(jnp.bfloat16)
    wave_field = jnp.einsum(
        "abzk,bxyk->axyz", inverse_z, along_y, preferred_element_type=jnp.float32
    ).astype(jnp.bfloat16)
    weights = occupation[0]
    real_part = wave_field[0].astype(jnp.float32)
    imag_part = wave_field[1].astype(jnp.float32)
    partial_density = weights[0] * real_part * real_part + weights[1] * imag_part * imag_part
    density = lax.psum(partial_density.astype(jnp.bfloat16), "band")
    strength = 3.0 * math.sqrt(block_cells * projectors.shape[2]) / nproj_count
    coupled = (coupling + coupling.T) * (0.5 * strength)
    nearby = extended(projectors, (("fft", 0),), atom_dev)
    atom_rows = (
        slab_index * atom_dev - atom_dev + jnp.arange(3 * atom_dev, dtype=jnp.int32) + total_atoms
    ) % total_atoms
    near_blocks = sphere_blocks[atom_rows]
    plane_index = near_blocks // plane_blocks
    inside = plane_index // slab_planes == slab_index
    local_index = jnp.where(
        inside,
        (plane_index - slab_index * slab_planes) * plane_blocks + near_blocks % plane_blocks,
        0,
    )
    blocks_own = wave_field.reshape(2, slab_planes * plane_blocks, block_cells)
    gathered = blocks_own[:, local_index] * inside[None, :, :, None].astype(jnp.bfloat16)
    partial_value = jnp.einsum(
        "ajsk,bask->abj", nearby, gathered, preferred_element_type=jnp.float32
    )
    summed = extended(partial_value, (("fft", 0),), atom_dev)
    projections_own = (
        summed[:atom_dev] + summed[2 * atom_dev : 3 * atom_dev] + summed[4 * atom_dev :]
    )
    energy_own = jnp.einsum(
        "ij,abj->abi", coupled, projections_own, precision=lax.Precision.HIGHEST
    )
    energy = extended(energy_own, (("fft", 0),), atom_dev)
    spread = jnp.einsum(
        "ajsk,abj->bask", nearby.astype(jnp.float32), energy, precision=lax.Precision.HIGHEST
    )
    spread = spread * inside[None, :, :, None].astype(jnp.float32)
    accumulated = (
        jnp.zeros((2, slab_planes * plane_blocks, block_cells), jnp.float32)
        .at[:, local_index]
        .add(spread)
    )
    nonlocal_term = accumulated.reshape(2, slab_planes, size_y, size_z)
    total_field = (
        potential.astype(jnp.float32)[None] * wave_field.astype(jnp.float32) + nonlocal_term
    ).astype(jnp.bfloat16)
    forward_z = dft_table(size_z, -1.0)
    forward_y = dft_table(size_y, -1.0)
    forward_x = dft_table(size_x, -1.0)
    back_z = jnp.einsum(
        "abzk,bxyk->axyz", forward_z, total_field, preferred_element_type=jnp.float32
    ).astype(jnp.bfloat16)
    back_y = jnp.einsum(
        "abyk,bxkz->axyz", forward_y, back_z, preferred_element_type=jnp.float32
    ).astype(jnp.bfloat16)
    transformed = jnp.einsum(
        "abxk,bkyz->axyz",
        forward_x,
        lax.all_to_all(back_y, "fft", split_axis=2, concat_axis=1, tiled=True),
        preferred_element_type=jnp.float32,
    )
    index_x = jnp.arange(size_x, dtype=jnp.int32)
    index_y = slab_index * columns + jnp.arange(columns, dtype=jnp.int32)
    index_z = jnp.arange(size_z, dtype=jnp.int32)
    kinetic = (
        wave_squares(index_x, size_x)[:, None, None]
        + wave_squares(index_y, size_y)[None, :, None]
        + wave_squares(index_z, size_z)[None, None, :]
    )
    applied = (transformed + kinetic[None] * coeffs.astype(jnp.float32)).astype(jnp.bfloat16)
    return (applied[None], density, projections_own[None])


def real_blocks(length, sign):
    index = np.arange(length)
    angles = 2.0 * np.pi / length * (index[:, None] * index[None, :] % length)
    cosine = np.cos(angles) / np.sqrt(length)
    sine = sign * np.sin(angles) / np.sqrt(length)
    blocks = np.empty((2, length, 2, length))
    blocks[0, :, 0, :] = cosine
    blocks[1, :, 1, :] = cosine
    blocks[0, :, 1, :] = -sine
    blocks[1, :, 0, :] = sine
    return blocks


def chunk_planes(slab_planes):
    low, high = list(range(EDGE)), list(range(slab_planes - EDGE, slab_planes))
    return [low + high, list(range(EDGE, slab_planes - EDGE))]


def params(steps):
    return pltpu.CompilerParams(
        dimension_semantics=("arbitrary",) * steps, vmem_limit_bytes=VMEM_BYTES
    )


def cost(products, values):
    return pl.CostEstimate(flops=4 * products, bytes_accessed=4 * values, transcendentals=0)


def whole(shape):
    return pl.BlockSpec(shape, lambda i: (0,) * len(shape))


SMEM_SPEC = pl.BlockSpec(memory_space=pltpu.SMEM)


def paired(refs, slab):
    return [(lax.bitwise_xor(slab, jnp.int32(k)), ref) for k, ref in enumerate(refs)]


def shifted(refs, slab):
    return [(lax.rem(slab + k, len(refs)), ref) for k, ref in enumerate(refs)]


def first_x_kernel(slab, table_ref, coeffs_ref, *refs, pieces, natural):
    scratch = 3 if natural else 2
    outs = paired(refs[:-scratch], slab[0])
    turned, wide, *tall = refs[-scratch:]
    parts, size_x, columns, lanes = coeffs_ref.shape
    rows = parts * size_x
    height = table_ref.shape[0] // pieces

    for k, (device, _) in enumerate(outs):
        start = pl.multiple_of(device * height, 16)
        turned[k * height : (k + 1) * height, :] = table_ref[pl.ds(start, height), :]

    def widen(k, carry):
        for part in range(parts):
            start = pl.multiple_of((part * size_x + k * 8) * columns, 8)
            wide[pl.ds(start, 8 * columns), :] = (
                coeffs_ref[part, pl.ds(k * 8, 8)].astype(jnp.float32).reshape(8 * columns, lanes)
            )
        return carry

    lax.fori_loop(0, size_x // 8, widen, 0, unroll=2)

    def some_columns(g, carry):
        loaded = [
            wide[pl.ds(COLUMNS * g + h, rows, stride=columns), :].astype(jnp.bfloat16)
            for h in range(COLUMNS)
        ]
        for first in range(0, COLUMNS, FOUR):
            result = jnp.dot(
                turned[...],
                jnp.concatenate(loaded[first : first + FOUR], axis=1),
                preferred_element_type=jnp.float32,
            )
            for h in range(FOUR):
                column = COLUMNS * g + first + h
                piece = result[:, h * lanes : (h + 1) * lanes]
                if natural:
                    tall[0][pl.ds(column, piece.shape[0], stride=columns), :] = piece
                else:
                    piece = piece.astype(jnp.bfloat16)
                    for k, (_, out) in enumerate(outs):
                        out[column] = piece[k * height : (k + 1) * height]
        return carry

    lax.fori_loop(0, columns // COLUMNS, some_columns, 0)
    if natural:
        for k, (_, out) in enumerate(outs):
            values = tall[0][k * height * columns : (k + 1) * height * columns, :]
            out[...] = values.astype(jnp.bfloat16).reshape(out.shape)


def first_x(slab, table, coeffs, planes, pieces, natural):
    _, size_x, columns, size_z = coeffs.shape
    lanes = size_z // 2
    shape = (planes, 2 * columns) if natural else (columns, 2 * planes)
    scratch = [
        pltpu.VMEM(table.shape, jnp.bfloat16),
        pltpu.VMEM((2 * size_x * columns, lanes), jnp.float32),
    ]
    if natural:
        scratch.append(pltpu.VMEM((2 * pieces * planes * columns, lanes), jnp.float32))
    out_specs = [pl.BlockSpec((*shape, lanes), lambda i: (0, 0, i))] * pieces
    out_shape = [jax.ShapeDtypeStruct((*shape, size_z), jnp.bfloat16)] * pieces
    return pl.pallas_call(
        functools.partial(first_x_kernel, pieces=pieces, natural=natural),
        grid=(2,),
        in_specs=[
            SMEM_SPEC,
            whole(table.shape),
            pl.BlockSpec((2, size_x, columns, lanes), lambda i: (0, 0, 0, i)),
        ],
        out_specs=out_specs,
        out_shape=out_shape,
        scratch_shapes=scratch,
        compiler_params=params(1),
        cost_estimate=cost(2 * size_x * pieces * planes * columns * size_z, 2 * size_x * columns * size_z),
        name="first_x",
    )(slab, table, coeffs)


def ones_at(codes, count, axis):
    shape = (codes.shape[0], count) if axis == 1 else (count, codes.shape[1])
    places = lax.broadcasted_iota(jnp.int32, shape, axis)
    return jnp.where(codes == places, 1.0, 0.0).astype(jnp.bfloat16)


def field_kernel(slab, weights, table_y, table_z, codes, sides, *refs, pieces, count, natural):
    bufs = paired(refs[:count], slab[0])
    wave, density, rows_out, gathered, wide = refs[count:]
    _, near, size_y, size_z = wave.shape
    groups, entries, _ = codes.shape
    lanes = 128
    halves = size_z // lanes
    i, last = pl.program_id(0), pl.num_programs(0) - 1
    planes = near * (last + 1)

    @pl.when(i == 0)
    def _():
        gathered[...] = jnp.zeros_like(gathered)

    loaded = []
    if natural:
        for source, buf in bufs:
            wide[source] = buf[...]
        for h in range(near):
            loaded.append(wide[:, h].reshape(2 * size_y, size_z))
    else:
        columns, rows, _ = bufs[0][1].shape

        @pl.when(i == 0)
        def _():
            for source, buf in bufs:
                start = pl.multiple_of(source * columns * rows, 8)
                values = buf[...].astype(jnp.float32).reshape(columns * rows, size_z)
                for q in range(halves):
                    wide[q, pl.ds(start, columns * rows), :] = values[
                        :, q * lanes : (q + 1) * lanes
                    ]

        for h in range(near):
            plane = i * near + h
            both = [
                jnp.concatenate(
                    [
                        wide[q, pl.ds(part * planes + plane, size_y, stride=rows), :]
                        for q in range(halves)
                    ],
                    axis=1,
                ).astype(jnp.bfloat16)
                for part in range(2)
            ]
            loaded.append(jnp.concatenate(both, axis=0))
    results = []
    for first in range(0, near, PAIR):
        along_y = jnp.dot(
            table_y[...],
            jnp.concatenate(loaded[first : first + PAIR], axis=1),
            preferred_element_type=jnp.float32,
        ).astype(jnp.bfloat16)
        turned = jnp.concatenate(
            [
                jnp.concatenate(
                    [
                        along_y[:size_y, h * size_z : (h + 1) * size_z],
                        along_y[size_y:, h * size_z : (h + 1) * size_z],
                    ],
                    axis=1,
                )
                for h in range(PAIR)
            ],
            axis=0,
        )
        result = jnp.dot(
            turned, table_z[...], preferred_element_type=jnp.float32
        ).astype(jnp.bfloat16)
        results.append(result)
        for h in range(PAIR):
            total = jnp.zeros((size_y, size_z), jnp.float32)
            for part in range(2):
                values = result[h * size_y : (h + 1) * size_y, part * size_z : (part + 1) * size_z]
                wave[part, first + h] = values
                values = values.astype(jnp.float32)
                total += weights[0, part] * values * values
            density[first + h] = total.astype(jnp.bfloat16)
    result = jnp.concatenate(results, axis=0)

    used = [0] if groups == 1 else [0, 1 + (2 * i > last).astype(jnp.int32)]
    for group in used:
        places = ones_at(codes[group] - i * near * size_y, near * size_y, 1)
        gathered[group] += jnp.dot(places, result, preferred_element_type=jnp.float32)

    @pl.when(i == last)
    def _():
        for group in range(groups):
            for part in range(2):
                total = jnp.zeros((entries, lanes), jnp.float32)
                for q in range(halves):
                    start = part * size_z + q * lanes
                    total += jnp.where(
                        sides[group] == q, gathered[group, :, start : start + lanes], 0.0
                    )
                rows_out[group, part] = total.astype(jnp.bfloat16)


def make_field(slab, weights, bufs, table_y, table_z, codes, sides, planes, pieces, natural):
    size_z = bufs[0].shape[-1]
    size_y = table_y.shape[0] // 2
    columns = size_y // pieces
    groups, entries, _ = codes.shape
    if natural:
        buf_spec = pl.BlockSpec((PLANES, 2 * columns, size_z), lambda i: (i, 0, 0))
        wide = pltpu.VMEM((pieces, PLANES, 2 * columns, size_z), jnp.bfloat16)
    else:
        buf_spec = whole(bufs[0].shape)
        wide = pltpu.VMEM((size_z // 128, 2 * planes * size_y, 128), jnp.float32)
    return pl.pallas_call(
        functools.partial(field_kernel, pieces=pieces, count=len(bufs), natural=natural),
        grid=(planes // PLANES,),
        in_specs=[SMEM_SPEC, SMEM_SPEC]
        + [whole(a.shape) for a in (table_y, table_z, codes, sides)]
        + [buf_spec] * len(bufs),
        out_specs=[
            pl.BlockSpec((2, PLANES, size_y, size_z), lambda i: (0, i, 0, 0)),
            pl.BlockSpec((PLANES, size_y, size_z), lambda i: (i, 0, 0)),
            whole((groups, 2, entries, 128)),
        ],
        out_shape=[
            jax.ShapeDtypeStruct((2, planes, size_y, size_z), jnp.bfloat16),
            jax.ShapeDtypeStruct((planes, size_y, size_z), jnp.bfloat16),
            jax.ShapeDtypeStruct((groups, 2, entries, 128), jnp.bfloat16),
        ],
        scratch_shapes=[pltpu.VMEM((groups, entries, 2 * size_z), jnp.float32), wide],
        compiler_params=params(1),
        cost_estimate=cost(
            2 * planes * size_y * size_z * (size_y + size_z), 2 * planes * size_y * size_z
        ),
        name="make_field",
    )(slab, weights, table_y, table_z, codes, sides, *bufs)


def nonlocal_kernel(coupled, projectors, *refs):
    parts, (projections, spread) = refs[:-2], refs[-2:]
    atoms, nproj, blocks, cells = projectors.shape
    for atom in range(atoms):
        tables = [projectors[atom, j].astype(jnp.float32) for j in range(nproj)]
        place = pl.ds(atom * blocks, blocks)
        for part in range(2):
            rows = sum(p[part, place].astype(jnp.float32) for p in parts)
            tile = jnp.concatenate(
                [jnp.sum(t * rows, axis=0, keepdims=True) for t in tables], axis=0
            )
            mixed = jnp.zeros_like(tile)
            for j in range(nproj):
                mixed += coupled[j] * tile[j : j + 1]
            projections[atom, part] = jnp.broadcast_to(
                jnp.sum(tile, -1, keepdims=True), tile.shape
            )
            energy = jnp.broadcast_to(jnp.sum(mixed, -1, keepdims=True), tile.shape)
            spread[part, place] = sum(
                t * energy[j : j + 1] for j, t in enumerate(tables)
            ).astype(jnp.bfloat16)


def make_nonlocal(coupled, projectors, parts):
    atoms, nproj, _, cells = projectors.shape
    return pl.pallas_call(
        nonlocal_kernel,
        out_shape=[
            jax.ShapeDtypeStruct((atoms, 2, nproj, cells), jnp.float32),
            jax.ShapeDtypeStruct(parts[0].shape, jnp.bfloat16),
        ],
        name="make_nonlocal",
    )(coupled, projectors, *parts)


def back_kernel(slab, wave, potential, table_z, table_y, codes, sides, *refs, pieces, natural):
    groups, _, entries = codes.shape
    sources, outs = refs[:groups], refs[groups:-2]
    spread, tall = refs[-2:]
    outs = shifted(outs, slab[0])
    near, size_y, size_z = potential.shape
    lanes = 128
    halves = size_z // lanes
    i, last = pl.program_id(0), pl.num_programs(0) - 1
    planes = near * (last + 1)

    @pl.when(i == 0)
    def _():
        for group, source in enumerate(sources):
            for part in range(2):
                for q in range(halves):
                    start = part * size_z + q * lanes
                    spread[group, :, start : start + lanes] = jnp.where(
                        sides[group] == q, source[part].astype(jnp.float32), 0.0
                    ).astype(jnp.bfloat16)

    used = [0] if groups == 1 else [0, 1 + (2 * i > last).astype(jnp.int32)]
    for first in range(0, near, PAIR):
        extra = jnp.zeros((PAIR * size_y, 2 * size_z), jnp.float32)
        for group in used:
            places = ones_at(codes[group] - (i * near + first) * size_y, PAIR * size_y, 0)
            extra += jnp.dot(places, spread[group], preferred_element_type=jnp.float32)
        fields = []
        for h in range(PAIR):
            local = potential[first + h].astype(jnp.float32)
            both = [
                local * wave[part, first + h].astype(jnp.float32)
                + extra[h * size_y : (h + 1) * size_y, part * size_z : (part + 1) * size_z]
                for part in range(2)
            ]
            fields.append(jnp.concatenate(both, axis=1).astype(jnp.bfloat16))
        back_z = jnp.dot(
            jnp.concatenate(fields, axis=0), table_z[...], preferred_element_type=jnp.float32
        ).astype(jnp.bfloat16)
        turned = jnp.concatenate(
            [
                jnp.concatenate(
                    [
                        back_z[h * size_y : (h + 1) * size_y, :size_z],
                        back_z[h * size_y : (h + 1) * size_y, size_z:],
                    ],
                    axis=0,
                )
                for h in range(PAIR)
            ],
            axis=1,
        )
        back_y = jnp.dot(table_y[...], turned, preferred_element_type=jnp.float32)
        if natural:
            back_y = back_y.astype(jnp.bfloat16)
            for h in range(PAIR):
                tall[:, first + h] = back_y[:, h * size_z : (h + 1) * size_z].reshape(
                    pieces, outs[0][1].shape[1], size_z
                )
            continue
        rows = outs[0][1].shape[1]
        for h in range(PAIR):
            plane = i * near + first + h
            for part in range(2):
                for q in range(halves):
                    start = h * size_z + q * lanes
                    tall[q, pl.ds(part * planes + plane, size_y, stride=rows), :] = back_y[
                        part * size_y : (part + 1) * size_y, start : start + lanes
                    ]

    if natural:
        for target, out in outs:
            out[...] = tall[target]
        return
    columns, rows, _ = outs[0][1].shape

    @pl.when(i == last)
    def _():
        for target, out in outs:
            start = pl.multiple_of(target * columns * rows, 8)
            values = [tall[q, pl.ds(start, columns * rows), :] for q in range(halves)]
            out[...] = (
                jnp.concatenate(values, axis=1).astype(jnp.bfloat16).reshape(columns, rows, size_z)
            )


def go_back(slab, wave, potential, table_z, table_y, codes, sides, sources, place, pieces, natural):
    _, planes, size_y, size_z = wave.shape
    columns = size_y // pieces
    groups, _, entries = codes.shape
    scratch = [pltpu.VMEM((groups, entries, 2 * size_z), jnp.bfloat16)]
    if natural:
        shape = (planes, 2 * columns, size_z)
        out_specs = [pl.BlockSpec((PLANES, 2 * columns, size_z), lambda i: (i, 0, 0))] * pieces
        scratch.append(pltpu.VMEM((pieces, PLANES, 2 * columns, size_z), jnp.bfloat16))
    else:
        shape = (columns, 2 * planes, size_z)
        out_specs = [whole(shape)] * pieces
        scratch.append(pltpu.VMEM((size_z // 128, 2 * planes * size_y, 128), jnp.float32))
    return pl.pallas_call(
        functools.partial(back_kernel, pieces=pieces, natural=natural),
        grid=(planes // PLANES,),
        in_specs=[
            SMEM_SPEC,
            pl.BlockSpec((2, PLANES, size_y, size_z), lambda i: (0, i, 0, 0)),
            pl.BlockSpec((PLANES, size_y, size_z), lambda i: (place(i), 0, 0)),
        ]
        + [whole(a.shape) for a in (table_z, table_y, codes, sides, *sources)],
        out_specs=out_specs,
        out_shape=[jax.ShapeDtypeStruct(shape, jnp.bfloat16)] * pieces,
        scratch_shapes=scratch,
        compiler_params=params(1),
        cost_estimate=cost(
            2 * planes * size_y * size_z * (size_y + size_z), 2 * planes * size_y * size_z
        ),
        name="go_back",
    )(slab, wave, potential, table_z, table_y, codes, sides, *sources)


def last_x_kernel(frequency_x, frequency_yz, table, coeffs, *refs):
    bufs, (out, tall) = refs[:-2], refs[-2:]
    parts, size_x, columns, lanes = coeffs.shape

    def some_columns(g, carry):
        loaded = []
        for h in range(COLUMNS):
            loaded.append(jnp.concatenate([buf[COLUMNS * g + h] for buf in bufs], axis=0))
        for first in range(0, COLUMNS, FOUR):
            result = jnp.dot(
                table[...],
                jnp.concatenate(loaded[first : first + FOUR], axis=1),
                preferred_element_type=jnp.float32,
            )
            for h in range(FOUR):
                tall[pl.ds(COLUMNS * g + first + h, parts * size_x, stride=columns), :] = result[
                    :, h * lanes : (h + 1) * lanes
                ]
        return carry

    lax.fori_loop(0, columns // COLUMNS, some_columns, 0)

    def finish(k, carry):
        kinetic = frequency_x[k] + frequency_yz[...]
        for part in range(parts):
            start = pl.multiple_of((part * size_x + k) * columns, 8)
            out[part, k] = (
                tall[pl.ds(start, columns), :] + kinetic * coeffs[part, k].astype(jnp.float32)
            ).astype(jnp.bfloat16)
        return carry

    lax.fori_loop(0, size_x, finish, 0, unroll=8)


def last_x(frequency_x, frequency_yz, table, coeffs, bufs):
    _, size_x, columns, size_z = coeffs.shape
    lanes = size_z // 2
    spec = pl.BlockSpec((2, size_x, columns, lanes), lambda i: (0, 0, 0, i))
    return pl.pallas_call(
        last_x_kernel,
        grid=(2,),
        in_specs=[
            SMEM_SPEC,
            pl.BlockSpec((columns, lanes), lambda i: (0, i)),
            whole(table.shape),
            spec,
        ]
        + [pl.BlockSpec((*b.shape[:2], lanes), lambda i: (0, 0, i)) for b in bufs],
        out_specs=spec,
        out_shape=jax.ShapeDtypeStruct(coeffs.shape, jnp.bfloat16),
        scratch_shapes=[pltpu.VMEM((2 * size_x * columns, lanes), jnp.float32)],
        compiler_params=params(1),
        cost_estimate=cost(2 * size_x * size_x * columns * size_z, 3 * size_x * columns * size_z),
        name="last_x",
    )(frequency_x, frequency_yz, table, coeffs, *bufs)


def per_device_chunked(wave_coeffs, occupation, potential, projectors, coupling, sphere_blocks):
    pieces = lax.axis_size("fft")
    bands = lax.axis_size("band")
    slab = lax.axis_index("fft")
    coeffs = wave_coeffs[0]
    _, size_x, columns, size_z = coeffs.shape
    slab_planes, size_y, _ = potential.shape
    atom_dev, nproj, blocks, cells = projectors.shape
    zblocks = size_z // cells
    outer, inner = chunk_planes(slab_planes)
    up = [(i, (i + 1) % pieces) for i in range(pieces)]
    down = [(j, i) for i, j in up]

    inverse_x, forward_x = (real_blocks(size_x, s) for s in (1.0, -1.0))
    inverse_y, forward_y = (real_blocks(size_y, s) for s in (1.0, -1.0))
    inverse_z, forward_z = (real_blocks(size_z, s) for s in (1.0, -1.0))
    place_outer, place_inner = (
        np.arange(pieces)[:, None] * slab_planes + np.array(chunk)[None, :]
        for chunk in (outer, inner)
    )
    table_x_outer = np.stack([inverse_x[r][place_outer] for r in range(2)], 1)
    table_x_inner = np.stack([inverse_x[r][place_inner] for r in range(2)], 2)
    tables_back_x = [
        np.stack([forward_x[:, :, r][:, :, place] for r in range(2)], 3).reshape(
            2 * size_x, pieces, -1
        )
        for place in (place_outer, place_inner)
    ]
    split_y = (2, size_y, 2, pieces, columns)
    tables = [
        table_x_outer.reshape(-1, 2 * size_x),
        table_x_inner.reshape(-1, 2 * size_x),
        inverse_y.reshape(2 * size_y, -1),
        inverse_y.reshape(split_y).transpose(0, 1, 3, 2, 4).reshape(2 * size_y, -1),
        inverse_z.transpose(2, 3, 0, 1).reshape(2 * size_z, -1),
        forward_z.transpose(2, 3, 0, 1).reshape(2 * size_z, -1),
        forward_y.reshape(2 * size_y, -1),
        forward_y.reshape(2, pieces, columns, -1).transpose(1, 0, 2, 3).reshape(2 * size_y, -1),
        np.stack(
            [
                np.concatenate(
                    [t[:, (d - np.arange(pieces)) % pieces].reshape(2 * size_x, -1) for t in tables_back_x],
                    axis=1,
                )
                for d in range(pieces)
            ]
        ),
    ]
    (
        table_x_outer, table_x_inner, table_y_outer, table_y_inner, table_z,
        table_back_z, table_back_y_outer, table_back_y_inner, tables_back_x,
    ) = (jnp.asarray(t.astype(jnp.bfloat16)) for t in tables)

    table_back_x = lax.dynamic_index_in_dim(tables_back_x, slab, 0, keepdims=False)

    where = slab.reshape(1)
    section_outer = first_x(where, table_x_outer, coeffs, len(outer), pieces, False)
    section_outer, table_x_inner, sphere_blocks = lax.optimization_barrier(
        (section_outer, table_x_inner, sphere_blocks)
    )
    section_inner = first_x(where, table_x_inner, coeffs, len(inner), pieces, True)

    entries = atom_dev * blocks

    def codes_of(chunk, shift):
        owner = (slab + shift + pieces) % pieces
        numbers = lax.dynamic_slice_in_dim(sphere_blocks, owner * atom_dev, atom_dev, 0)
        plane = numbers // (size_y * zblocks) - slab * slab_planes
        rest = numbers % (size_y * zblocks)
        if chunk is outer:
            inside = ((plane >= 0) & (plane < EDGE)) | (
                (plane >= slab_planes - EDGE) & (plane < slab_planes)
            )
            plane = jnp.where(plane < EDGE, plane, plane - len(inner))
        else:
            inside = (plane >= EDGE) & (plane < slab_planes - EDGE)
            plane = plane - EDGE
        code = jnp.where(inside, plane * size_y + rest // zblocks, -1)
        return code.reshape(entries), (rest % zblocks).reshape(entries)

    found = [codes_of(outer, shift) for shift in (0, -1, 1)]
    codes_outer, sides_outer = (jnp.stack(values) for values in zip(*found))
    codes_inner, sides_inner = (values[None] for values in codes_of(inner, 0))
    sides_outer, sides_inner = sides_outer[:, :, None], sides_inner[:, :, None]
    rows_codes = [codes_outer[:, :, None], codes_inner[:, :, None]]
    strength = 3.0 * math.sqrt(cells * blocks) / nproj
    coupled = (coupling + coupling.T) * (0.5 * strength)
    coupled = jnp.broadcast_to(coupled.T[:, :, None], (nproj, nproj, cells))
    section_inner, rows_codes, sides_outer, sides_inner, coupled = lax.optimization_barrier(
        (section_inner, rows_codes, sides_outer, sides_inner, coupled)
    )

    half = pieces // 2
    near, far = list(range(1, half)), list(range(half, pieces))

    def send(block, k, *awaited):
        for row, m in awaited:
            block, row[m] = lax.optimization_barrier((block, row[m]))
        return lax.ppermute(block, "fft", [(j, j ^ k) for j in range(pieces)])

    received_outer, received_inner = (
        [section[0]] + [None] * (pieces - 1) for section in (section_outer, section_inner)
    )
    for partners in (near, far):
        queue = [(section_outer, received_outer, k) for k in partners]
        queue += [(section_inner, received_inner, k) for k in partners]
        for place, (section, received, k) in enumerate(queue):
            awaited = [queue[place - 2][1:]] if place >= 2 else []
            received[k] = send(section[k], k, *awaited)
    wave_outer, density_outer, rows_outer = make_field(
        where, occupation, received_outer, table_y_outer, table_z, rows_codes[0],
        sides_outer, len(outer), pieces, False,
    )
    from_following = lax.ppermute(rows_outer[1], "fft", down)
    from_previous = lax.ppermute(rows_outer[2], "fft", up)
    density_outer = lax.psum(density_outer, "band")
    wave_inner, density_inner, rows_inner = make_field(
        where, occupation, received_inner, table_y_inner, table_z, rows_codes[1],
        sides_inner, len(inner), pieces, True,
    )
    projected, spread = make_nonlocal(
        coupled, projectors, [rows_outer[0], rows_inner[0], from_following, from_previous]
    )
    spread_previous = lax.ppermute(spread, "fft", up)
    spread_following = lax.ppermute(spread, "fft", down)
    edge_steps = EDGE // PLANES
    inner_steps = len(inner) // PLANES
    back_inner = go_back(
        where, wave_inner, potential, table_back_z, table_back_y_inner, codes_inner[:, None, :],
        sides_inner, [spread], lambda i: i + edge_steps, pieces, True,
    )
    back_inner, spread_previous, spread_following = lax.optimization_barrier(
        (back_inner, spread_previous, spread_following)
    )
    def permute_all(values):
        received = [values[0]]
        for k in range(1, pieces):
            pairs = [(j, (j + k) % pieces) for j in range(pieces)]
            received.append(lax.ppermute(values[k], "fft", pairs))
        return received

    back_inner = permute_all(back_inner)
    back_outer = go_back(
        where, wave_outer, potential, table_back_z, table_back_y_outer, codes_outer[:, None, :],
        sides_outer, [spread, spread_previous, spread_following],
        lambda i: jnp.where(i < edge_steps, i, i + inner_steps), pieces, False,
    )
    density_inner, density_outer = lax.optimization_barrier((density_inner, density_outer))
    density_inner = lax.psum(density_inner, "band")
    back_outer, density_outer = lax.optimization_barrier((back_outer, density_outer))
    back_outer = permute_all(back_outer)
    back_inner = [
        b.reshape(len(inner), 2, columns, size_z).transpose(2, 1, 0, 3).reshape(columns, -1, size_z)
        for b in back_inner
    ]
    density = jnp.concatenate([density_outer[:EDGE], density_inner, density_outer[EDGE:]], axis=0)

    index_x = np.arange(size_x)
    frequency_x = jnp.asarray(
        (np.where(2 * index_x < size_x, index_x, index_x - size_x) / size_x) ** 2, jnp.float32
    )
    index_y = slab * columns + jnp.arange(columns, dtype=jnp.int32)
    index_z = jnp.arange(size_z, dtype=jnp.int32)
    frequency_yz = wave_squares(index_y, size_y)[:, None] + wave_squares(index_z, size_z)[None, :]
    coeffs, density, back_inner = lax.optimization_barrier((coeffs, density, back_inner))
    applied = last_x(frequency_x, frequency_yz, table_back_x, coeffs, back_outer + back_inner)
    return (applied[None], density, projected[None, :, :, :, 0])


def per_device(wave_coeffs, occupation, potential, projectors, coupling, sphere_blocks):
    pieces, bands = lax.axis_size("fft"), lax.axis_size("band")
    size_z = wave_coeffs.shape[4]
    columns = wave_coeffs.shape[3]
    slab_planes = potential.shape[0]
    chunked = (
        pieces >= 4
        and pieces & (pieces - 1) == 0
        and slab_planes % EDGE == 0
        and slab_planes >= 3 * EDGE
        and EDGE >= HALO
        and columns % 8 == 0
        and size_z % 256 == 0
        and projectors.shape[0] % bands == 0
        and projectors.shape[3] == 128
        and projectors.shape[1] == 8
    )
    chosen = per_device_chunked if chunked else per_device_plain
    return chosen(wave_coeffs, occupation, potential, projectors, coupling, sphere_blocks)


def solution(mesh):
    placed = (
        P("band", None, None, "fft", None),
        P("band", None),
        P("fft", None, None),
        P("fft", None, None, None),
        P(),
        P(),
    )
    return jax.shard_map(
        per_device,
        mesh=mesh,
        in_specs=placed,
        out_specs=(
            P("band", None, None, "fft", None),
            P("fft", None, None),
            P("band", "fft", None, None),
        ),
        check_vma=False,
    )
```

```python
import functools
import math

import jax
import jax.numpy as jnp
import numpy as np
from jax import lax
from jax.experimental import pallas as pl
from jax.experimental.pallas import tpu as pltpu
from jax.sharding import PartitionSpec as P

HALO = 6
EDGE = 8
PLANES = 4
COLUMNS = 8
PAIR = 4
FOUR = 8
HELD = 3
VMEM_BYTES = 56 * 1024 * 1024


def extended(shard, sides, width):
    for axis, dim in sides:
        count, length = (lax.axis_size(axis), shard.shape[dim])
        up = [(i, (i + 1) % count) for i in range(count)]
        down = [(j, i) for i, j in up]
        last = lax.slice_in_dim(shard, length - width, length, axis=dim)
        first = lax.slice_in_dim(shard, 0, width, axis=dim)
        before = lax.ppermute(last, axis, up)
        after = lax.ppermute(first, axis, down)
        shard = jnp.concatenate([before, shard, after], axis=dim)
    return shard


def dft_table(length, sign_value):
    indices = jnp.arange(length, dtype=jnp.int32)
    phases = indices[:, None] * indices[None, :] % length
    angles = 2.0 * math.pi / length * phases.astype(jnp.float32)
    factor = 1.0 / math.sqrt(length)
    cosine = jnp.cos(angles) * factor
    sine_part = jnp.sin(angles) * (sign_value * factor)
    upper_rows = jnp.stack([cosine, -sine_part])
    bottom = jnp.stack([sine_part, cosine])
    return jnp.stack([upper_rows, bottom]).astype(jnp.bfloat16)


def wave_squares(indices, length):
    frequency = (
        jnp.where(2 * indices < length, indices, indices - length).astype(jnp.float32) / length
    )
    return frequency * frequency


def per_device_plain(wave_coeffs, occupation, potential, projectors, coupling, sphere_blocks):
    pieces = lax.axis_size("fft")
    slab_index = lax.axis_index("fft")
    coeffs = wave_coeffs[0]
    size_x = coeffs.shape[1]
    columns = coeffs.shape[2]
    size_z = coeffs.shape[3]
    slab_planes = potential.shape[0]
    size_y = potential.shape[1]
    atom_dev = projectors.shape[0]
    nproj_count = projectors.shape[1]
    block_cells = projectors.shape[3]
    zblocks = size_z // block_cells
    plane_blocks = size_y * zblocks
    total_atoms = atom_dev * pieces
    table_x = dft_table(size_x, 1.0).transpose(0, 2, 1, 3).reshape(2 * size_x, 2 * size_x)
    inverse_y = dft_table(size_y, 1.0)
    inverse_z = dft_table(size_z, 1.0)
    flattened = coeffs.reshape(2 * size_x, columns * size_z)
    along_x = jnp.dot(table_x, flattened, preferred_element_type=jnp.float32)
    along_x = along_x.reshape(2, size_x, columns, size_z).astype(jnp.bfloat16)
    along_y = jnp.einsum(
        "abyk,bxkz->axyz",
        inverse_y,
        lax.all_to_all(along_x, "fft", split_axis=1, concat_axis=2, tiled=True),
        preferred_element_type=jnp.float32,
    ).astype(jnp.bfloat16)
    wave_field = jnp.einsum(
        "abzk,bxyk->axyz", inverse_z, along_y, preferred_element_type=jnp.float32
    ).astype(jnp.bfloat16)
    weights = occupation[0]
    real_part = wave_field[0].astype(jnp.float32)
    imag_part = wave_field[1].astype(jnp.float32)
    partial_density = weights[0] * real_part * real_part + weights[1] * imag_part * imag_part
    density = lax.psum(partial_density.astype(jnp.bfloat16), "band")
    strength = 3.0 * math.sqrt(block_cells * projectors.shape[2]) / nproj_count
    coupled = (coupling + coupling.T) * (0.5 * strength)
    nearby = extended(projectors, (("fft", 0),), atom_dev)
    atom_rows = (
        slab_index * atom_dev - atom_dev + jnp.arange(3 * atom_dev, dtype=jnp.int32) + total_atoms
    ) % total_atoms
    near_blocks = sphere_blocks[atom_rows]
    plane_index = near_blocks // plane_blocks
    inside = plane_index // slab_planes == slab_index
    local_index = jnp.where(
        inside,
        (plane_index - slab_index * slab_planes) * plane_blocks + near_blocks % plane_blocks,
        0,
    )
    blocks_own = wave_field.reshape(2, slab_planes * plane_blocks, block_cells)
    gathered = blocks_own[:, local_index] * inside[None, :, :, None].astype(jnp.bfloat16)
    partial_value = jnp.einsum(
        "ajsk,bask->abj", nearby, gathered, preferred_element_type=jnp.float32
    )
    summed = extended(partial_value, (("fft", 0),), atom_dev)
    projections_own = (
        summed[:atom_dev] + summed[2 * atom_dev : 3 * atom_dev] + summed[4 * atom_dev :]
    )
    energy_own = jnp.einsum(
        "ij,abj->abi", coupled, projections_own, precision=lax.Precision.HIGHEST
    )
    energy = extended(energy_own, (("fft", 0),), atom_dev)
    spread = jnp.einsum(
        "ajsk,abj->bask", nearby.astype(jnp.float32), energy, precision=lax.Precision.HIGHEST
    )
    spread = spread * inside[None, :, :, None].astype(jnp.float32)
    accumulated = (
        jnp.zeros((2, slab_planes * plane_blocks, block_cells), jnp.float32)
        .at[:, local_index]
        .add(spread)
    )
    nonlocal_term = accumulated.reshape(2, slab_planes, size_y, size_z)
    total_field = (
        potential.astype(jnp.float32)[None] * wave_field.astype(jnp.float32) + nonlocal_term
    ).astype(jnp.bfloat16)
    forward_z = dft_table(size_z, -1.0)
    forward_y = dft_table(size_y, -1.0)
    forward_x = dft_table(size_x, -1.0)
    back_z = jnp.einsum(
        "abzk,bxyk->axyz", forward_z, total_field, preferred_element_type=jnp.float32
    ).astype(jnp.bfloat16)
    back_y = jnp.einsum(
        "abyk,bxkz->axyz", forward_y, back_z, preferred_element_type=jnp.float32
    ).astype(jnp.bfloat16)
    transformed = jnp.einsum(
        "abxk,bkyz->axyz",
        forward_x,
        lax.all_to_all(back_y, "fft", split_axis=2, concat_axis=1, tiled=True),
        preferred_element_type=jnp.float32,
    )
    index_x = jnp.arange(size_x, dtype=jnp.int32)
    index_y = slab_index * columns + jnp.arange(columns, dtype=jnp.int32)
    index_z = jnp.arange(size_z, dtype=jnp.int32)
    kinetic = (
        wave_squares(index_x, size_x)[:, None, None]
        + wave_squares(index_y, size_y)[None, :, None]
        + wave_squares(index_z, size_z)[None, None, :]
    )
    applied = (transformed + kinetic[None] * coeffs.astype(jnp.float32)).astype(jnp.bfloat16)
    return (applied[None], density, projections_own[None])


def real_blocks(length, sign):
    index = np.arange(length)
    angles = 2.0 * np.pi / length * (index[:, None] * index[None, :] % length)
    cosine = np.cos(angles) / np.sqrt(length)
    sine = sign * np.sin(angles) / np.sqrt(length)
    blocks = np.empty((2, length, 2, length))
    blocks[0, :, 0, :] = cosine
    blocks[1, :, 1, :] = cosine
    blocks[0, :, 1, :] = -sine
    blocks[1, :, 0, :] = sine
    return blocks


def chunk_planes(slab_planes):
    low, high = list(range(EDGE)), list(range(slab_planes - EDGE, slab_planes))
    return [low + high, list(range(EDGE, slab_planes - EDGE))]


def params(steps):
    return pltpu.CompilerParams(
        dimension_semantics=("arbitrary",) * steps, vmem_limit_bytes=VMEM_BYTES
    )


def cost(products, values):
    return pl.CostEstimate(flops=4 * products, bytes_accessed=4 * values, transcendentals=0)


def whole(shape):
    return pl.BlockSpec(shape, lambda i: (0,) * len(shape))


SMEM_SPEC = pl.BlockSpec(memory_space=pltpu.SMEM)


def shifted(refs, slab):
    return [(lax.rem(slab + k, len(refs)), ref) for k, ref in enumerate(refs)]


def shifted_back(refs, slab):
    return [(lax.rem(slab + len(refs) - k, len(refs)), ref) for k, ref in enumerate(refs)]


def first_x_kernel(slab, table_ref, coeffs_ref, *refs, pieces, natural):
    scratch = 3 if natural else 2
    outs = shifted(refs[:-scratch], slab[0])
    turned, wide, *tall = refs[-scratch:]
    parts, size_x, columns, lanes = coeffs_ref.shape
    rows = parts * size_x
    height = table_ref.shape[0] // pieces

    for k, (device, _) in enumerate(outs):
        start = pl.multiple_of(device * height, 16)
        turned[k * height : (k + 1) * height, :] = table_ref[pl.ds(start, height), :]

    def widen(k, carry):
        for part in range(parts):
            start = pl.multiple_of((part * size_x + k * 8) * columns, 8)
            wide[pl.ds(start, 8 * columns), :] = (
                coeffs_ref[part, pl.ds(k * 8, 8)].astype(jnp.float32).reshape(8 * columns, lanes)
            )
        return carry

    lax.fori_loop(0, size_x // 8, widen, 0, unroll=2)

    def some_columns(g, carry):
        loaded = [
            wide[pl.ds(COLUMNS * g + h, rows, stride=columns), :].astype(jnp.bfloat16)
            for h in range(COLUMNS)
        ]
        for first in range(0, COLUMNS, FOUR):
            result = jnp.dot(
                turned[...],
                jnp.concatenate(loaded[first : first + FOUR], axis=1),
                preferred_element_type=jnp.float32,
            )
            for h in range(FOUR):
                column = COLUMNS * g + first + h
                piece = result[:, h * lanes : (h + 1) * lanes]
                if natural:
                    tall[0][pl.ds(column, piece.shape[0], stride=columns), :] = piece
                else:
                    piece = piece.astype(jnp.bfloat16)
                    for k, (_, out) in enumerate(outs):
                        out[column] = piece[k * height : (k + 1) * height]
        return carry

    lax.fori_loop(0, columns // COLUMNS, some_columns, 0)
    if natural:
        for k, (_, out) in enumerate(outs):
            values = tall[0][k * height * columns : (k + 1) * height * columns, :]
            out[...] = values.astype(jnp.bfloat16).reshape(out.shape)


def first_x(slab, table, coeffs, planes, pieces, natural):
    _, size_x, columns, size_z = coeffs.shape
    lanes = size_z // 2
    shape = (planes, 2 * columns) if natural else (columns, 2 * planes)
    scratch = [
        pltpu.VMEM(table.shape, jnp.bfloat16),
        pltpu.VMEM((2 * size_x * columns, lanes), jnp.float32),
    ]
    if natural:
        scratch.append(pltpu.VMEM((2 * pieces * planes * columns, lanes), jnp.float32))
    out_specs = [pl.BlockSpec((*shape, lanes), lambda i: (0, 0, i))] * pieces
    out_shape = [jax.ShapeDtypeStruct((*shape, size_z), jnp.bfloat16)] * pieces
    return pl.pallas_call(
        functools.partial(first_x_kernel, pieces=pieces, natural=natural),
        grid=(2,),
        in_specs=[
            SMEM_SPEC,
            whole(table.shape),
            pl.BlockSpec((2, size_x, columns, lanes), lambda i: (0, 0, 0, i)),
        ],
        out_specs=out_specs,
        out_shape=out_shape,
        scratch_shapes=scratch,
        compiler_params=params(1),
        cost_estimate=cost(2 * size_x * pieces * planes * columns * size_z, 2 * size_x * columns * size_z),
        name="first_x",
    )(slab, table, coeffs)


def ones_at(codes, count, axis):
    shape = (codes.shape[0], count) if axis == 1 else (count, codes.shape[1])
    places = lax.broadcasted_iota(jnp.int32, shape, axis)
    return jnp.where(codes == places, 1.0, 0.0).astype(jnp.bfloat16)


def field_kernel(slab, weights, table_y, table_z, codes, sides, *refs, pieces, count, natural):
    bufs = shifted_back(refs[:count], slab[0])
    wave, density, rows_out, gathered, wide = refs[count:]
    _, near, size_y, size_z = wave.shape
    groups, entries, _ = codes.shape
    lanes = 128
    halves = size_z // lanes
    i, last = pl.program_id(0), pl.num_programs(0) - 1
    planes = near * (last + 1)

    @pl.when(i == 0)
    def _():
        gathered[...] = jnp.zeros_like(gathered)

    loaded = []
    if natural:
        for source, buf in bufs:
            wide[source] = buf[...]
        for h in range(near):
            loaded.append(wide[:, h].reshape(2 * size_y, size_z))
    else:
        columns, rows, _ = bufs[0][1].shape

        @pl.when(i == 0)
        def _():
            for source, buf in bufs:
                start = pl.multiple_of(source * columns * rows, 8)
                values = buf[...].astype(jnp.float32).reshape(columns * rows, size_z)
                for q in range(halves):
                    wide[q, pl.ds(start, columns * rows), :] = values[
                        :, q * lanes : (q + 1) * lanes
                    ]

        for h in range(near):
            plane = i * near + h
            both = [
                jnp.concatenate(
                    [
                        wide[q, pl.ds(part * planes + plane, size_y, stride=rows), :]
                        for q in range(halves)
                    ],
                    axis=1,
                ).astype(jnp.bfloat16)
                for part in range(2)
            ]
            loaded.append(jnp.concatenate(both, axis=0))
    results = []
    for first in range(0, near, PAIR):
        along_y = jnp.dot(
            table_y[...],
            jnp.concatenate(loaded[first : first + PAIR], axis=1),
            preferred_element_type=jnp.float32,
        ).astype(jnp.bfloat16)
        turned = jnp.concatenate(
            [
                jnp.concatenate(
                    [
                        along_y[:size_y, h * size_z : (h + 1) * size_z],
                        along_y[size_y:, h * size_z : (h + 1) * size_z],
                    ],
                    axis=1,
                )
                for h in range(PAIR)
            ],
            axis=0,
        )
        result = jnp.dot(
            turned, table_z[...], preferred_element_type=jnp.float32
        ).astype(jnp.bfloat16)
        results.append(result)
        for h in range(PAIR):
            total = jnp.zeros((size_y, size_z), jnp.float32)
            for part in range(2):
                values = result[h * size_y : (h + 1) * size_y, part * size_z : (part + 1) * size_z]
                wave[part, first + h] = values
                values = values.astype(jnp.float32)
                total += weights[0, part] * values * values
            density[first + h] = total.astype(jnp.bfloat16)
    result = jnp.concatenate(results, axis=0)

    used = [0] if groups == 1 else [0, 1 + (2 * i > last).astype(jnp.int32)]
    for group in used:
        places = ones_at(codes[group] - i * near * size_y, near * size_y, 1)
        gathered[group] += jnp.dot(places, result, preferred_element_type=jnp.float32)

    @pl.when(i == last)
    def _():
        for group in range(groups):
            for part in range(2):
                total = jnp.zeros((entries, lanes), jnp.float32)
                for q in range(halves):
                    start = part * size_z + q * lanes
                    total += jnp.where(
                        sides[group] == q, gathered[group, :, start : start + lanes], 0.0
                    )
                rows_out[group, part] = total.astype(jnp.bfloat16)


def make_field(slab, weights, bufs, table_y, table_z, codes, sides, planes, pieces, natural):
    size_z = bufs[0].shape[-1]
    size_y = table_y.shape[0] // 2
    columns = size_y // pieces
    groups, entries, _ = codes.shape
    if natural:
        buf_spec = pl.BlockSpec((PLANES, 2 * columns, size_z), lambda i: (i, 0, 0))
        wide = pltpu.VMEM((pieces, PLANES, 2 * columns, size_z), jnp.bfloat16)
    else:
        buf_spec = whole(bufs[0].shape)
        wide = pltpu.VMEM((size_z // 128, 2 * planes * size_y, 128), jnp.float32)
    return pl.pallas_call(
        functools.partial(field_kernel, pieces=pieces, count=len(bufs), natural=natural),
        grid=(planes // PLANES,),
        in_specs=[SMEM_SPEC, SMEM_SPEC]
        + [whole(a.shape) for a in (table_y, table_z, codes, sides)]
        + [buf_spec] * len(bufs),
        out_specs=[
            pl.BlockSpec((2, PLANES, size_y, size_z), lambda i: (0, i, 0, 0)),
            pl.BlockSpec((PLANES, size_y, size_z), lambda i: (i, 0, 0)),
            whole((groups, 2, entries, 128)),
        ],
        out_shape=[
            jax.ShapeDtypeStruct((2, planes, size_y, size_z), jnp.bfloat16),
            jax.ShapeDtypeStruct((planes, size_y, size_z), jnp.bfloat16),
            jax.ShapeDtypeStruct((groups, 2, entries, 128), jnp.bfloat16),
        ],
        scratch_shapes=[pltpu.VMEM((groups, entries, 2 * size_z), jnp.float32), wide],
        compiler_params=params(1),
        cost_estimate=cost(
            2 * planes * size_y * size_z * (size_y + size_z), 2 * planes * size_y * size_z
        ),
        name="make_field",
    )(slab, weights, table_y, table_z, codes, sides, *bufs)


def nonlocal_kernel(coupled, projectors, *refs):
    parts, (projections, spread) = refs[:-2], refs[-2:]
    atoms, nproj, blocks, cells = projectors.shape
    for atom in range(atoms):
        tables = [projectors[atom, j].astype(jnp.float32) for j in range(nproj)]
        place = pl.ds(atom * blocks, blocks)
        for part in range(2):
            rows = sum(p[part, place].astype(jnp.float32) for p in parts)
            tile = jnp.concatenate(
                [jnp.sum(t * rows, axis=0, keepdims=True) for t in tables], axis=0
            )
            mixed = jnp.zeros_like(tile)
            for j in range(nproj):
                mixed += coupled[j] * tile[j : j + 1]
            projections[atom, part] = jnp.broadcast_to(
                jnp.sum(tile, -1, keepdims=True), tile.shape
            )
            energy = jnp.broadcast_to(jnp.sum(mixed, -1, keepdims=True), tile.shape)
            spread[part, place] = sum(
                t * energy[j : j + 1] for j, t in enumerate(tables)
            ).astype(jnp.bfloat16)


def make_nonlocal(coupled, projectors, parts):
    atoms, nproj, _, cells = projectors.shape
    return pl.pallas_call(
        nonlocal_kernel,
        out_shape=[
            jax.ShapeDtypeStruct((atoms, 2, nproj, cells), jnp.float32),
            jax.ShapeDtypeStruct(parts[0].shape, jnp.bfloat16),
        ],
        name="make_nonlocal",
    )(coupled, projectors, *parts)


def back_kernel(slab, wave, potential, table_z, table_y, codes, sides, *refs, pieces, natural):
    groups, _, entries = codes.shape
    sources, outs = refs[:groups], refs[groups:-2]
    spread, tall = refs[-2:]
    outs = shifted(outs, slab[0])
    near, size_y, size_z = potential.shape
    lanes = 128
    halves = size_z // lanes
    i, last = pl.program_id(0), pl.num_programs(0) - 1
    planes = near * (last + 1)

    @pl.when(i == 0)
    def _():
        for group, source in enumerate(sources):
            for part in range(2):
                for q in range(halves):
                    start = part * size_z + q * lanes
                    spread[group, :, start : start + lanes] = jnp.where(
                        sides[group] == q, source[part].astype(jnp.float32), 0.0
                    ).astype(jnp.bfloat16)

    used = [0] if groups == 1 else [0, 1 + (2 * i > last).astype(jnp.int32)]
    for first in range(0, near, PAIR):
        extra = jnp.zeros((PAIR * size_y, 2 * size_z), jnp.float32)
        for group in used:
            places = ones_at(codes[group] - (i * near + first) * size_y, PAIR * size_y, 0)
            extra += jnp.dot(places, spread[group], preferred_element_type=jnp.float32)
        fields = []
        for h in range(PAIR):
            local = potential[first + h].astype(jnp.float32)
            both = [
                local * wave[part, first + h].astype(jnp.float32)
                + extra[h * size_y : (h + 1) * size_y, part * size_z : (part + 1) * size_z]
                for part in range(2)
            ]
            fields.append(jnp.concatenate(both, axis=1).astype(jnp.bfloat16))
        back_z = jnp.dot(
            jnp.concatenate(fields, axis=0), table_z[...], preferred_element_type=jnp.float32
        ).astype(jnp.bfloat16)
        turned = jnp.concatenate(
            [
                jnp.concatenate(
                    [
                        back_z[h * size_y : (h + 1) * size_y, :size_z],
                        back_z[h * size_y : (h + 1) * size_y, size_z:],
                    ],
                    axis=0,
                )
                for h in range(PAIR)
            ],
            axis=1,
        )
        back_y = jnp.dot(table_y[...], turned, preferred_element_type=jnp.float32)
        if natural:
            back_y = back_y.astype(jnp.bfloat16)
            for h in range(PAIR):
                tall[:, first + h] = back_y[:, h * size_z : (h + 1) * size_z].reshape(
                    pieces, outs[0][1].shape[1], size_z
                )
            continue
        rows = outs[0][1].shape[1]
        for h in range(PAIR):
            plane = i * near + first + h
            for part in range(2):
                for q in range(halves):
                    start = h * size_z + q * lanes
                    tall[q, pl.ds(part * planes + plane, size_y, stride=rows), :] = back_y[
                        part * size_y : (part + 1) * size_y, start : start + lanes
                    ]

    if natural:
        for target, out in outs:
            out[...] = tall[target]
        return
    columns, rows, _ = outs[0][1].shape

    @pl.when(i == last)
    def _():
        for target, out in outs:
            start = pl.multiple_of(target * columns * rows, 8)
            values = [tall[q, pl.ds(start, columns * rows), :] for q in range(halves)]
            out[...] = (
                jnp.concatenate(values, axis=1).astype(jnp.bfloat16).reshape(columns, rows, size_z)
            )


def go_back(slab, wave, potential, table_z, table_y, codes, sides, sources, place, pieces, natural):
    _, planes, size_y, size_z = wave.shape
    columns = size_y // pieces
    groups, _, entries = codes.shape
    scratch = [pltpu.VMEM((groups, entries, 2 * size_z), jnp.bfloat16)]
    if natural:
        shape = (planes, 2 * columns, size_z)
        out_specs = [pl.BlockSpec((PLANES, 2 * columns, size_z), lambda i: (i, 0, 0))] * pieces
        scratch.append(pltpu.VMEM((pieces, PLANES, 2 * columns, size_z), jnp.bfloat16))
    else:
        shape = (columns, 2 * planes, size_z)
        out_specs = [whole(shape)] * pieces
        scratch.append(pltpu.VMEM((size_z // 128, 2 * planes * size_y, 128), jnp.float32))
    return pl.pallas_call(
        functools.partial(back_kernel, pieces=pieces, natural=natural),
        grid=(planes // PLANES,),
        in_specs=[
            SMEM_SPEC,
            pl.BlockSpec((2, PLANES, size_y, size_z), lambda i: (0, i, 0, 0)),
            pl.BlockSpec((PLANES, size_y, size_z), lambda i: (place(i), 0, 0)),
        ]
        + [whole(a.shape) for a in (table_z, table_y, codes, sides, *sources)],
        out_specs=out_specs,
        out_shape=[jax.ShapeDtypeStruct(shape, jnp.bfloat16)] * pieces,
        scratch_shapes=scratch,
        compiler_params=params(1),
        cost_estimate=cost(
            2 * planes * size_y * size_z * (size_y + size_z), 2 * planes * size_y * size_z
        ),
        name="go_back",
    )(slab, wave, potential, table_z, table_y, codes, sides, *sources)


def last_x_kernel(frequency_x, frequency_yz, table, coeffs, *refs):
    bufs, (out, tall) = refs[:-2], refs[-2:]
    parts, size_x, columns, lanes = coeffs.shape

    def some_columns(g, carry):
        loaded = []
        for h in range(COLUMNS):
            loaded.append(jnp.concatenate([buf[COLUMNS * g + h] for buf in bufs], axis=0))
        for first in range(0, COLUMNS, FOUR):
            result = jnp.dot(
                table[...],
                jnp.concatenate(loaded[first : first + FOUR], axis=1),
                preferred_element_type=jnp.float32,
            )
            for h in range(FOUR):
                tall[pl.ds(COLUMNS * g + first + h, parts * size_x, stride=columns), :] = result[
                    :, h * lanes : (h + 1) * lanes
                ]
        return carry

    lax.fori_loop(0, columns // COLUMNS, some_columns, 0)

    def finish(k, carry):
        kinetic = frequency_x[k] + frequency_yz[...]
        for part in range(parts):
            start = pl.multiple_of((part * size_x + k) * columns, 8)
            out[part, k] = (
                tall[pl.ds(start, columns), :] + kinetic * coeffs[part, k].astype(jnp.float32)
            ).astype(jnp.bfloat16)
        return carry

    lax.fori_loop(0, size_x, finish, 0, unroll=8)


def last_x(frequency_x, frequency_yz, table, coeffs, bufs):
    _, size_x, columns, size_z = coeffs.shape
    lanes = size_z // 2
    spec = pl.BlockSpec((2, size_x, columns, lanes), lambda i: (0, 0, 0, i))
    return pl.pallas_call(
        last_x_kernel,
        grid=(2,),
        in_specs=[
            SMEM_SPEC,
            pl.BlockSpec((columns, lanes), lambda i: (0, i)),
            whole(table.shape),
            spec,
        ]
        + [pl.BlockSpec((*b.shape[:2], lanes), lambda i: (0, 0, i)) for b in bufs],
        out_specs=spec,
        out_shape=jax.ShapeDtypeStruct(coeffs.shape, jnp.bfloat16),
        scratch_shapes=[pltpu.VMEM((2 * size_x * columns, lanes), jnp.float32)],
        compiler_params=params(1),
        cost_estimate=cost(2 * size_x * size_x * columns * size_z, 3 * size_x * columns * size_z),
        name="last_x",
    )(frequency_x, frequency_yz, table, coeffs, *bufs)


def per_device_chunked(wave_coeffs, occupation, potential, projectors, coupling, sphere_blocks):
    pieces = lax.axis_size("fft")
    bands = lax.axis_size("band")
    slab = lax.axis_index("fft")
    coeffs = wave_coeffs[0]
    _, size_x, columns, size_z = coeffs.shape
    slab_planes, size_y, _ = potential.shape
    atom_dev, nproj, blocks, cells = projectors.shape
    zblocks = size_z // cells
    outer, inner = chunk_planes(slab_planes)
    up = [(i, (i + 1) % pieces) for i in range(pieces)]
    down = [(j, i) for i, j in up]

    inverse_x, forward_x = (real_blocks(size_x, s) for s in (1.0, -1.0))
    inverse_y, forward_y = (real_blocks(size_y, s) for s in (1.0, -1.0))
    inverse_z, forward_z = (real_blocks(size_z, s) for s in (1.0, -1.0))
    place_outer, place_inner = (
        np.arange(pieces)[:, None] * slab_planes + np.array(chunk)[None, :]
        for chunk in (outer, inner)
    )
    table_x_outer = np.stack([inverse_x[r][place_outer] for r in range(2)], 1)
    table_x_inner = np.stack([inverse_x[r][place_inner] for r in range(2)], 2)
    tables_back_x = [
        np.stack([forward_x[:, :, r][:, :, place] for r in range(2)], 3).reshape(
            2 * size_x, pieces, -1
        )
        for place in (place_outer, place_inner)
    ]
    split_y = (2, size_y, 2, pieces, columns)
    tables = [
        table_x_outer.reshape(-1, 2 * size_x),
        table_x_inner.reshape(-1, 2 * size_x),
        inverse_y.reshape(2 * size_y, -1),
        inverse_y.reshape(split_y).transpose(0, 1, 3, 2, 4).reshape(2 * size_y, -1),
        inverse_z.transpose(2, 3, 0, 1).reshape(2 * size_z, -1),
        forward_z.transpose(2, 3, 0, 1).reshape(2 * size_z, -1),
        forward_y.reshape(2 * size_y, -1),
        forward_y.reshape(2, pieces, columns, -1).transpose(1, 0, 2, 3).reshape(2 * size_y, -1),
        np.stack(
            [
                np.concatenate(
                    [t[:, (d - np.arange(pieces)) % pieces].reshape(2 * size_x, -1) for t in tables_back_x],
                    axis=1,
                )
                for d in range(pieces)
            ]
        ),
    ]
    (
        table_x_outer, table_x_inner, table_y_outer, table_y_inner, table_z,
        table_back_z, table_back_y_outer, table_back_y_inner, tables_back_x,
    ) = (jnp.asarray(t.astype(jnp.bfloat16)) for t in tables)

    table_back_x = lax.dynamic_index_in_dim(tables_back_x, slab, 0, keepdims=False)

    where = slab.reshape(1)
    section_outer = first_x(where, table_x_outer, coeffs, len(outer), pieces, False)
    section_outer, table_x_inner, sphere_blocks = lax.optimization_barrier(
        (section_outer, table_x_inner, sphere_blocks)
    )
    section_inner = first_x(where, table_x_inner, coeffs, len(inner), pieces, True)

    entries = atom_dev * blocks

    def codes_of(chunk, shift):
        owner = (slab + shift + pieces) % pieces
        numbers = lax.dynamic_slice_in_dim(sphere_blocks, owner * atom_dev, atom_dev, 0)
        plane = numbers // (size_y * zblocks) - slab * slab_planes
        rest = numbers % (size_y * zblocks)
        if chunk is outer:
            inside = ((plane >= 0) & (plane < EDGE)) | (
                (plane >= slab_planes - EDGE) & (plane < slab_planes)
            )
            plane = jnp.where(plane < EDGE, plane, plane - len(inner))
        else:
            inside = (plane >= EDGE) & (plane < slab_planes - EDGE)
            plane = plane - EDGE
        code = jnp.where(inside, plane * size_y + rest // zblocks, -1)
        return code.reshape(entries), (rest % zblocks).reshape(entries)

    found = [codes_of(outer, shift) for shift in (0, -1, 1)]
    codes_outer, sides_outer = (jnp.stack(values) for values in zip(*found))
    codes_inner, sides_inner = (values[None] for values in codes_of(inner, 0))
    sides_outer, sides_inner = sides_outer[:, :, None], sides_inner[:, :, None]
    rows_codes = [codes_outer[:, :, None], codes_inner[:, :, None]]
    strength = 3.0 * math.sqrt(cells * blocks) / nproj
    coupled = (coupling + coupling.T) * (0.5 * strength)
    coupled = jnp.broadcast_to(coupled.T[:, :, None], (nproj, nproj, cells))
    section_inner, rows_codes, sides_outer, sides_inner, coupled = lax.optimization_barrier(
        (section_inner, rows_codes, sides_outer, sides_inner, coupled)
    )

    def permute_all(values):
        received = [values[0]]
        for k in range(1, pieces):
            pairs = [(j, (j + k) % pieces) for j in range(pieces)]
            received.append(lax.ppermute(values[k], "fft", pairs))
        return received

    received_outer = permute_all(section_outer)
    received_inner = permute_all(section_inner)
    received_outer[0], received_inner[1:HELD] = lax.optimization_barrier(
        (received_outer[0], received_inner[1:HELD])
    )
    wave_outer, density_outer, rows_outer = make_field(
        where, occupation, received_outer, table_y_outer, table_z, rows_codes[0],
        sides_outer, len(outer), pieces, False,
    )
    from_following = lax.ppermute(rows_outer[1], "fft", down)
    from_previous = lax.ppermute(rows_outer[2], "fft", up)
    density_outer = lax.psum(density_outer, "band")
    wave_inner, density_inner, rows_inner = make_field(
        where, occupation, received_inner, table_y_inner, table_z, rows_codes[1],
        sides_inner, len(inner), pieces, True,
    )
    projected, spread = make_nonlocal(
        coupled, projectors, [rows_outer[0], rows_inner[0], from_following, from_previous]
    )
    spread_previous = lax.ppermute(spread, "fft", up)
    spread_following = lax.ppermute(spread, "fft", down)
    edge_steps = EDGE // PLANES
    inner_steps = len(inner) // PLANES
    back_inner = go_back(
        where, wave_inner, potential, table_back_z, table_back_y_inner, codes_inner[:, None, :],
        sides_inner, [spread], lambda i: i + edge_steps, pieces, True,
    )
    back_inner, spread_previous, spread_following = lax.optimization_barrier(
        (back_inner, spread_previous, spread_following)
    )
    back_inner = permute_all(back_inner)
    back_outer = go_back(
        where, wave_outer, potential, table_back_z, table_back_y_outer, codes_outer[:, None, :],
        sides_outer, [spread, spread_previous, spread_following],
        lambda i: jnp.where(i < edge_steps, i, i + inner_steps), pieces, False,
    )
    density_inner, density_outer = lax.optimization_barrier((density_inner, density_outer))
    density_inner = lax.psum(density_inner, "band")
    back_outer, density_outer = lax.optimization_barrier((back_outer, density_outer))
    back_outer = permute_all(back_outer)
    back_inner = [
        b.reshape(len(inner), 2, columns, size_z).transpose(2, 1, 0, 3).reshape(columns, -1, size_z)
        for b in back_inner
    ]
    density = jnp.concatenate([density_outer[:EDGE], density_inner, density_outer[EDGE:]], axis=0)

    index_x = np.arange(size_x)
    frequency_x = jnp.asarray(
        (np.where(2 * index_x < size_x, index_x, index_x - size_x) / size_x) ** 2, jnp.float32
    )
    index_y = slab * columns + jnp.arange(columns, dtype=jnp.int32)
    index_z = jnp.arange(size_z, dtype=jnp.int32)
    frequency_yz = wave_squares(index_y, size_y)[:, None] + wave_squares(index_z, size_z)[None, :]
    coeffs, density, back_inner = lax.optimization_barrier((coeffs, density, back_inner))
    applied = last_x(frequency_x, frequency_yz, table_back_x, coeffs, back_outer + back_inner)
    return (applied[None], density, projected[None, :, :, :, 0])


def per_device(wave_coeffs, occupation, potential, projectors, coupling, sphere_blocks):
    pieces, bands = lax.axis_size("fft"), lax.axis_size("band")
    size_z = wave_coeffs.shape[4]
    columns = wave_coeffs.shape[3]
    slab_planes = potential.shape[0]
    chunked = (
        pieces >= 4
        and slab_planes % EDGE == 0
        and slab_planes >= 3 * EDGE
        and EDGE >= HALO
        and columns % 8 == 0
        and size_z % 256 == 0
        and projectors.shape[0] % bands == 0
        and projectors.shape[3] == 128
        and projectors.shape[1] == 8
    )
    chosen = per_device_chunked if chunked else per_device_plain
    return chosen(wave_coeffs, occupation, potential, projectors, coupling, sphere_blocks)


def solution(mesh):
    placed = (
        P("band", None, None, "fft", None),
        P("band", None),
        P("fft", None, None),
        P("fft", None, None, None),
        P(),
        P(),
    )
    return jax.shard_map(
        per_device,
        mesh=mesh,
        in_specs=placed,
        out_specs=(
            P("band", None, None, "fft", None),
            P("fft", None, None),
            P("band", "fft", None, None),
        ),
        check_vma=False,
    )
```

```python
import functools
import math

import jax
import jax.numpy as jnp
import numpy as np
from jax import lax
from jax.experimental import pallas as pl
from jax.experimental.pallas import tpu as pltpu
from jax.sharding import PartitionSpec as P

HALO = 6
EDGE = 8
PLANES = 4
COLUMNS = 8
FOUR = 4
VMEM_BYTES = 56 * 1024 * 1024


def extended(shard, sides, width):
    for axis, dim in sides:
        count, length = (lax.axis_size(axis), shard.shape[dim])
        up = [(i, (i + 1) % count) for i in range(count)]
        down = [(j, i) for i, j in up]
        last = lax.slice_in_dim(shard, length - width, length, axis=dim)
        first = lax.slice_in_dim(shard, 0, width, axis=dim)
        before = lax.ppermute(last, axis, up)
        after = lax.ppermute(first, axis, down)
        shard = jnp.concatenate([before, shard, after], axis=dim)
    return shard


def dft_table(length, sign_value):
    indices = jnp.arange(length, dtype=jnp.int32)
    phases = indices[:, None] * indices[None, :] % length
    angles = 2.0 * math.pi / length * phases.astype(jnp.float32)
    factor = 1.0 / math.sqrt(length)
    cosine = jnp.cos(angles) * factor
    sine_part = jnp.sin(angles) * (sign_value * factor)
    upper_rows = jnp.stack([cosine, -sine_part])
    bottom = jnp.stack([sine_part, cosine])
    return jnp.stack([upper_rows, bottom]).astype(jnp.bfloat16)


def wave_squares(indices, length):
    frequency = (
        jnp.where(2 * indices < length, indices, indices - length).astype(jnp.float32) / length
    )
    return frequency * frequency


def per_device_plain(wave_coeffs, occupation, potential, projectors, coupling, sphere_blocks):
    pieces = lax.axis_size("fft")
    slab_index = lax.axis_index("fft")
    coeffs = wave_coeffs[0]
    size_x = coeffs.shape[1]
    columns = coeffs.shape[2]
    size_z = coeffs.shape[3]
    slab_planes = potential.shape[0]
    size_y = potential.shape[1]
    atom_dev = projectors.shape[0]
    nproj_count = projectors.shape[1]
    block_cells = projectors.shape[3]
    zblocks = size_z // block_cells
    plane_blocks = size_y * zblocks
    total_atoms = atom_dev * pieces
    table_x = dft_table(size_x, 1.0).transpose(0, 2, 1, 3).reshape(2 * size_x, 2 * size_x)
    inverse_y = dft_table(size_y, 1.0)
    inverse_z = dft_table(size_z, 1.0)
    flattened = coeffs.reshape(2 * size_x, columns * size_z)
    along_x = jnp.dot(table_x, flattened, preferred_element_type=jnp.float32)
    along_x = along_x.reshape(2, size_x, columns, size_z).astype(jnp.bfloat16)
    along_y = jnp.einsum(
        "abyk,bxkz->axyz",
        inverse_y,
        lax.all_to_all(along_x, "fft", split_axis=1, concat_axis=2, tiled=True),
        preferred_element_type=jnp.float32,
    ).astype(jnp.bfloat16)
    wave_field = jnp.einsum(
        "abzk,bxyk->axyz", inverse_z, along_y, preferred_element_type=jnp.float32
    ).astype(jnp.bfloat16)
    weights = occupation[0]
    real_part = wave_field[0].astype(jnp.float32)
    imag_part = wave_field[1].astype(jnp.float32)
    partial_density = weights[0] * real_part * real_part + weights[1] * imag_part * imag_part
    density = lax.psum(partial_density.astype(jnp.bfloat16), "band")
    strength = 3.0 * math.sqrt(block_cells * projectors.shape[2]) / nproj_count
    coupled = (coupling + coupling.T) * (0.5 * strength)
    nearby = extended(projectors, (("fft", 0),), atom_dev)
    atom_rows = (
        slab_index * atom_dev - atom_dev + jnp.arange(3 * atom_dev, dtype=jnp.int32) + total_atoms
    ) % total_atoms
    near_blocks = sphere_blocks[atom_rows]
    plane_index = near_blocks // plane_blocks
    inside = plane_index // slab_planes == slab_index
    local_index = jnp.where(
        inside,
        (plane_index - slab_index * slab_planes) * plane_blocks + near_blocks % plane_blocks,
        0,
    )
    blocks_own = wave_field.reshape(2, slab_planes * plane_blocks, block_cells)
    gathered = blocks_own[:, local_index] * inside[None, :, :, None].astype(jnp.bfloat16)
    partial_value = jnp.einsum(
        "ajsk,bask->abj", nearby, gathered, preferred_element_type=jnp.float32
    )
    summed = extended(partial_value, (("fft", 0),), atom_dev)
    projections_own = (
        summed[:atom_dev] + summed[2 * atom_dev : 3 * atom_dev] + summed[4 * atom_dev :]
    )
    energy_own = jnp.einsum(
        "ij,abj->abi", coupled, projections_own, precision=lax.Precision.HIGHEST
    )
    energy = extended(energy_own, (("fft", 0),), atom_dev)
    spread = jnp.einsum(
        "ajsk,abj->bask", nearby.astype(jnp.float32), energy, precision=lax.Precision.HIGHEST
    )
    spread = spread * inside[None, :, :, None].astype(jnp.float32)
    accumulated = (
        jnp.zeros((2, slab_planes * plane_blocks, block_cells), jnp.float32)
        .at[:, local_index]
        .add(spread)
    )
    nonlocal_term = accumulated.reshape(2, slab_planes, size_y, size_z)
    total_field = (
        potential.astype(jnp.float32)[None] * wave_field.astype(jnp.float32) + nonlocal_term
    ).astype(jnp.bfloat16)
    forward_z = dft_table(size_z, -1.0)
    forward_y = dft_table(size_y, -1.0)
    forward_x = dft_table(size_x, -1.0)
    back_z = jnp.einsum(
        "abzk,bxyk->axyz", forward_z, total_field, preferred_element_type=jnp.float32
    ).astype(jnp.bfloat16)
    back_y = jnp.einsum(
        "abyk,bxkz->axyz", forward_y, back_z, preferred_element_type=jnp.float32
    ).astype(jnp.bfloat16)
    transformed = jnp.einsum(
        "abxk,bkyz->axyz",
        forward_x,
        lax.all_to_all(back_y, "fft", split_axis=2, concat_axis=1, tiled=True),
        preferred_element_type=jnp.float32,
    )
    index_x = jnp.arange(size_x, dtype=jnp.int32)
    index_y = slab_index * columns + jnp.arange(columns, dtype=jnp.int32)
    index_z = jnp.arange(size_z, dtype=jnp.int32)
    kinetic = (
        wave_squares(index_x, size_x)[:, None, None]
        + wave_squares(index_y, size_y)[None, :, None]
        + wave_squares(index_z, size_z)[None, None, :]
    )
    applied = (transformed + kinetic[None] * coeffs.astype(jnp.float32)).astype(jnp.bfloat16)
    return (applied[None], density, projections_own[None])


def real_blocks(length, sign):
    index = np.arange(length)
    angles = 2.0 * np.pi / length * (index[:, None] * index[None, :] % length)
    cosine = np.cos(angles) / np.sqrt(length)
    sine = sign * np.sin(angles) / np.sqrt(length)
    blocks = np.empty((2, length, 2, length))
    blocks[0, :, 0, :] = cosine
    blocks[1, :, 1, :] = cosine
    blocks[0, :, 1, :] = -sine
    blocks[1, :, 0, :] = sine
    return blocks


def chunk_planes(slab_planes):
    low, high = list(range(EDGE)), list(range(slab_planes - EDGE, slab_planes))
    return [low + high, list(range(EDGE, slab_planes - EDGE))]


def params(steps):
    return pltpu.CompilerParams(
        dimension_semantics=("arbitrary",) * steps, vmem_limit_bytes=VMEM_BYTES
    )


def cost(products, values):
    return pl.CostEstimate(flops=4 * products, bytes_accessed=4 * values, transcendentals=0)


def whole(shape):
    return pl.BlockSpec(shape, lambda i: (0,) * len(shape))


SMEM_SPEC = pl.BlockSpec(memory_space=pltpu.SMEM)


def paired(refs, slab):
    return [(lax.bitwise_xor(slab, jnp.int32(k)), ref) for k, ref in enumerate(refs)]


def shifted(refs, slab):
    return [(lax.rem(slab + k, len(refs)), ref) for k, ref in enumerate(refs)]


def first_x_kernel(slab, table_ref, coeffs_ref, *refs, pieces, natural):
    scratch = 3 if natural else 2
    outs = paired(refs[:-scratch], slab[0])
    turned, wide, *tall = refs[-scratch:]
    parts, size_x, columns, lanes = coeffs_ref.shape
    rows = parts * size_x
    height = table_ref.shape[0] // pieces

    for k, (device, _) in enumerate(outs):
        start = pl.multiple_of(device * height, 16)
        turned[k * height : (k + 1) * height, :] = table_ref[pl.ds(start, height), :]

    def widen(k, carry):
        for part in range(parts):
            start = pl.multiple_of((part * size_x + k * 8) * columns, 8)
            wide[pl.ds(start, 8 * columns), :] = (
                coeffs_ref[part, pl.ds(k * 8, 8)].astype(jnp.float32).reshape(8 * columns, lanes)
            )
        return carry

    lax.fori_loop(0, size_x // 8, widen, 0, unroll=2)

    def some_columns(g, carry):
        loaded = [
            wide[pl.ds(COLUMNS * g + h, rows, stride=columns), :].astype(jnp.bfloat16)
            for h in range(COLUMNS)
        ]
        for first in range(0, COLUMNS, FOUR):
            result = jnp.dot(
                turned[...],
                jnp.concatenate(loaded[first : first + FOUR], axis=1),
                preferred_element_type=jnp.float32,
            )
            for h in range(FOUR):
                column = COLUMNS * g + first + h
                piece = result[:, h * lanes : (h + 1) * lanes]
                if natural:
                    place = (first + h) % 2 * columns + COLUMNS // 2 * g + (first + h) // 2
                    planes = height // 2
                    for k in range(pieces):
                        for part in range(2):
                            start = k * height * columns + part * (columns // 2) + place
                            row = k * height + part * planes
                            tall[0][pl.ds(start, planes, stride=2 * columns), :] = piece[
                                row : row + planes
                            ]
                else:
                    piece = piece.astype(jnp.bfloat16)
                    for k, (_, out) in enumerate(outs):
                        out[column] = piece[k * height : (k + 1) * height]
        return carry

    lax.fori_loop(0, columns // COLUMNS, some_columns, 0)
    if natural:
        for k, (_, out) in enumerate(outs):
            values = tall[0][k * height * columns : (k + 1) * height * columns, :]
            out[...] = values.astype(jnp.bfloat16).reshape(out.shape)


def first_x(slab, table, coeffs, planes, pieces, natural):
    _, size_x, columns, size_z = coeffs.shape
    lanes = size_z // 2
    shape = (planes, 2 * columns) if natural else (columns, 2 * planes)
    scratch = [
        pltpu.VMEM(table.shape, jnp.bfloat16),
        pltpu.VMEM((2 * size_x * columns, lanes), jnp.float32),
    ]
    if natural:
        scratch.append(pltpu.VMEM((2 * pieces * planes * columns, lanes), jnp.float32))
    out_specs = [pl.BlockSpec((*shape, lanes), lambda i: (0, 0, i))] * pieces
    out_shape = [jax.ShapeDtypeStruct((*shape, size_z), jnp.bfloat16)] * pieces
    return pl.pallas_call(
        functools.partial(first_x_kernel, pieces=pieces, natural=natural),
        grid=(2,),
        in_specs=[
            SMEM_SPEC,
            whole(table.shape),
            pl.BlockSpec((2, size_x, columns, lanes), lambda i: (0, 0, 0, i)),
        ],
        out_specs=out_specs,
        out_shape=out_shape,
        scratch_shapes=scratch,
        compiler_params=params(1),
        cost_estimate=cost(2 * size_x * pieces * planes * columns * size_z, 2 * size_x * columns * size_z),
        name="first_x",
    )(slab, table, coeffs)


def ones_at(codes, count, axis):
    shape = (codes.shape[0], count) if axis == 1 else (count, codes.shape[1])
    places = lax.broadcasted_iota(jnp.int32, shape, axis)
    return jnp.where(codes == places, 1.0, 0.0).astype(jnp.bfloat16)


def field_kernel(slab, weights, table_y, table_z, codes, sides, *refs, pieces, count, natural):
    bufs = paired(refs[:count], slab[0])
    wave, density, *rows_out, gathered, wide = refs[count:]
    _, near, size_y, size_z = wave.shape
    columns = size_y // pieces
    groups, entries, _ = codes.shape
    lanes = 128
    halves = size_z // lanes
    i, last = pl.program_id(0), pl.num_programs(0) - 1
    planes = near * (last + 1)

    @pl.when(i == 0)
    def _():
        gathered[...] = jnp.zeros_like(gathered)

    loaded = []
    if natural:
        for source, buf in bufs:
            wide[source] = buf[...]
        for h in range(near):
            loaded.append(
                [wide[:, h, s * columns : (s + 1) * columns].reshape(size_y, size_z) for s in (0, 1)]
            )
    else:
        rows = bufs[0][1].shape[1]

        @pl.when(i == 0)
        def _():
            for source, buf in bufs:
                start = pl.multiple_of(source * columns * rows, 8)
                values = buf[...].astype(jnp.float32).reshape(columns * rows, size_z)
                for q in range(halves):
                    wide[q, pl.ds(start, columns * rows), :] = values[
                        :, q * lanes : (q + 1) * lanes
                    ]

        def strided(start):
            return jnp.concatenate(
                [
                    wide[q, pl.ds(start, size_y // 2, stride=2 * rows), :]
                    for q in range(halves)
                ],
                axis=1,
            ).astype(jnp.bfloat16)

        for h in range(near):
            plane = i * near + h
            loaded.append(
                [
                    jnp.concatenate(
                        [strided(s * rows + part * planes + plane) for part in range(2)], axis=0
                    )
                    for s in (0, 1)
                ]
            )
    even, odd = (
        jnp.dot(
            table_y[s],
            jnp.concatenate([pair[s] for pair in loaded], axis=1),
            preferred_element_type=jnp.float32,
        )
        for s in (0, 1)
    )
    low, high = (even + odd).astype(jnp.bfloat16), (even - odd).astype(jnp.bfloat16)
    middle = size_y // 2
    turned = []
    for h in range(near):
        span = slice(h * size_z, (h + 1) * size_z)
        both = [
            jnp.concatenate(
                [values[part * middle : (part + 1) * middle, span] for values in (low, high)], axis=0
            )
            for part in range(2)
        ]
        turned.append(jnp.concatenate(both, axis=1))
    result = jnp.dot(
        jnp.concatenate(turned, axis=0), table_z[...], preferred_element_type=jnp.float32
    ).astype(jnp.bfloat16)
    for h in range(near):
        total = jnp.zeros((size_y, size_z), jnp.float32)
        for part in range(2):
            values = result[h * size_y : (h + 1) * size_y, part * size_z : (part + 1) * size_z]
            wave[part, h] = values
            values = values.astype(jnp.float32)
            total += weights[0, part] * values * values
        density[h] = total.astype(jnp.bfloat16)

    used = [0] if groups == 1 else [0, 1 + (2 * i > last).astype(jnp.int32)]
    for group in used:
        places = ones_at(codes[group] - i * near * size_y, near * size_y, 1)
        gathered[group] += jnp.dot(places, result, preferred_element_type=jnp.float32)

    @pl.when(i == last)
    def _():
        for group in range(groups):
            for part in range(2):
                total = jnp.zeros((entries, lanes), jnp.float32)
                for q in range(halves):
                    start = part * size_z + q * lanes
                    total += jnp.where(
                        sides[group] == q, gathered[group, :, start : start + lanes], 0.0
                    )
                rows_out[group][part] = total.astype(jnp.bfloat16)


def make_field(slab, weights, bufs, table_y, table_z, codes, sides, planes, pieces, natural):
    size_z = bufs[0].shape[-1]
    size_y = table_y.shape[1]
    columns = size_y // pieces
    groups, entries, _ = codes.shape
    if natural:
        buf_spec = pl.BlockSpec((PLANES, 2 * columns, size_z), lambda i: (i, 0, 0))
        wide = pltpu.VMEM((pieces, PLANES, 2 * columns, size_z), jnp.bfloat16)
    else:
        buf_spec = whole(bufs[0].shape)
        wide = pltpu.VMEM((size_z // 128, 2 * planes * size_y, 128), jnp.float32)
    return pl.pallas_call(
        functools.partial(field_kernel, pieces=pieces, count=len(bufs), natural=natural),
        grid=(planes // PLANES,),
        in_specs=[SMEM_SPEC, SMEM_SPEC]
        + [whole(a.shape) for a in (table_y, table_z, codes, sides)]
        + [buf_spec] * len(bufs),
        out_specs=[
            pl.BlockSpec((2, PLANES, size_y, size_z), lambda i: (0, i, 0, 0)),
            pl.BlockSpec((PLANES, size_y, size_z), lambda i: (i, 0, 0)),
        ]
        + [whole((2, entries, 128))] * groups,
        out_shape=[
            jax.ShapeDtypeStruct((2, planes, size_y, size_z), jnp.bfloat16),
            jax.ShapeDtypeStruct((planes, size_y, size_z), jnp.bfloat16),
        ]
        + [jax.ShapeDtypeStruct((2, entries, 128), jnp.bfloat16)] * groups,
        scratch_shapes=[pltpu.VMEM((groups, entries, 2 * size_z), jnp.float32), wide],
        compiler_params=params(1),
        cost_estimate=cost(
            2 * planes * size_y * size_z * (size_y + size_z), 2 * planes * size_y * size_z
        ),
        name="make_field",
    )(slab, weights, table_y, table_z, codes, sides, *bufs)


def nonlocal_kernel(coupled, projectors, *refs):
    parts, (projections, spread) = refs[:-2], refs[-2:]
    atoms, nproj, blocks, cells = projectors.shape
    for atom in range(atoms):
        tables = [projectors[atom, j].astype(jnp.float32) for j in range(nproj)]
        place = pl.ds(atom * blocks, blocks)
        for part in range(2):
            rows = sum(p[part, place].astype(jnp.float32) for p in parts)
            tile = jnp.concatenate(
                [jnp.sum(t * rows, axis=0, keepdims=True) for t in tables], axis=0
            )
            mixed = jnp.zeros_like(tile)
            for j in range(nproj):
                mixed += coupled[j] * tile[j : j + 1]
            projections[atom, part] = jnp.broadcast_to(
                jnp.sum(tile, -1, keepdims=True), tile.shape
            )
            energy = jnp.broadcast_to(jnp.sum(mixed, -1, keepdims=True), tile.shape)
            spread[part, place] = sum(
                t * energy[j : j + 1] for j, t in enumerate(tables)
            ).astype(jnp.bfloat16)


def make_nonlocal(coupled, projectors, parts):
    atoms, nproj, _, cells = projectors.shape
    return pl.pallas_call(
        nonlocal_kernel,
        out_shape=[
            jax.ShapeDtypeStruct((atoms, 2, nproj, cells), jnp.float32),
            jax.ShapeDtypeStruct(parts[0].shape, jnp.bfloat16),
        ],
        name="make_nonlocal",
    )(coupled, projectors, *parts)


def back_kernel(slab, wave, potential, table_z, table_y, codes, sides, *refs, pieces, natural):
    groups, _, entries = codes.shape
    sources, outs = refs[:groups], refs[groups:-2]
    spread, tall = refs[-2:]
    outs = shifted(outs, slab[0])
    near, size_y, size_z = potential.shape
    lanes = 128
    halves = size_z // lanes
    i, last = pl.program_id(0), pl.num_programs(0) - 1
    planes = near * (last + 1)

    @pl.when(i == 0)
    def _():
        for group, source in enumerate(sources):
            for part in range(2):
                for q in range(halves):
                    start = part * size_z + q * lanes
                    spread[group, :, start : start + lanes] = jnp.where(
                        sides[group] == q, source[part].astype(jnp.float32), 0.0
                    ).astype(jnp.bfloat16)

    used = [0] if groups == 1 else [0, 1 + (2 * i > last).astype(jnp.int32)]
    extra = jnp.zeros((near * size_y, 2 * size_z), jnp.float32)
    for group in used:
        places = ones_at(codes[group] - i * near * size_y, near * size_y, 0)
        extra += jnp.dot(places, spread[group], preferred_element_type=jnp.float32)
    fields = []
    for h in range(near):
        local = potential[h].astype(jnp.float32)
        both = [
            local * wave[part, h].astype(jnp.float32)
            + extra[h * size_y : (h + 1) * size_y, part * size_z : (part + 1) * size_z]
            for part in range(2)
        ]
        fields.append(jnp.concatenate(both, axis=1).astype(jnp.bfloat16))
    back_z = jnp.dot(
        jnp.concatenate(fields, axis=0), table_z[...], preferred_element_type=jnp.float32
    )
    middle = size_y // 2
    folded = [[], []]
    for h in range(near):
        low = back_z[h * size_y : h * size_y + middle]
        high = back_z[h * size_y + middle : (h + 1) * size_y]
        for kept, values in zip(folded, (low + high, low - high)):
            values = values.astype(jnp.bfloat16)
            kept.append(jnp.concatenate([values[:, :size_z], values[:, size_z:]], axis=0))
    columns = size_y // pieces
    for s, kept in enumerate(folded):
        back_y = jnp.dot(
            table_y[s], jnp.concatenate(kept, axis=1), preferred_element_type=jnp.float32
        )
        if natural:
            back_y = back_y.astype(jnp.bfloat16)
            for h in range(near):
                tall[:, h, s * columns : (s + 1) * columns] = back_y[
                    :, h * size_z : (h + 1) * size_z
                ].reshape(pieces, columns, size_z)
            continue
        rows = outs[0][1].shape[1]
        for h in range(near):
            for part in range(2):
                for q in range(halves):
                    start = s * rows + part * planes + i * near + h
                    lane = h * size_z + q * lanes
                    tall[q, pl.ds(start, middle, stride=2 * rows), :] = back_y[
                        part * middle : (part + 1) * middle, lane : lane + lanes
                    ]

    if natural:
        for target, out in outs:
            out[...] = tall[target]
        return
    columns, rows, _ = outs[0][1].shape

    @pl.when(i == last)
    def _():
        for target, out in outs:
            start = pl.multiple_of(target * columns * rows, 8)
            values = [tall[q, pl.ds(start, columns * rows), :] for q in range(halves)]
            out[...] = (
                jnp.concatenate(values, axis=1).astype(jnp.bfloat16).reshape(columns, rows, size_z)
            )


def go_back(slab, wave, potential, table_z, table_y, codes, sides, sources, place, pieces, natural):
    _, planes, size_y, size_z = wave.shape
    columns = size_y // pieces
    groups, _, entries = codes.shape
    scratch = [pltpu.VMEM((groups, entries, 2 * size_z), jnp.bfloat16)]
    if natural:
        shape = (planes, 2 * columns, size_z)
        out_specs = [pl.BlockSpec((PLANES, 2 * columns, size_z), lambda i: (i, 0, 0))] * pieces
        scratch.append(pltpu.VMEM((pieces, PLANES, 2 * columns, size_z), jnp.bfloat16))
    else:
        shape = (columns, 2 * planes, size_z)
        out_specs = [whole(shape)] * pieces
        scratch.append(pltpu.VMEM((size_z // 128, 2 * planes * size_y, 128), jnp.float32))
    return pl.pallas_call(
        functools.partial(back_kernel, pieces=pieces, natural=natural),
        grid=(planes // PLANES,),
        in_specs=[
            SMEM_SPEC,
            pl.BlockSpec((2, PLANES, size_y, size_z), lambda i: (0, i, 0, 0)),
            pl.BlockSpec((PLANES, size_y, size_z), lambda i: (place(i), 0, 0)),
        ]
        + [whole(a.shape) for a in (table_z, table_y, codes, sides, *sources)],
        out_specs=out_specs,
        out_shape=[jax.ShapeDtypeStruct(shape, jnp.bfloat16)] * pieces,
        scratch_shapes=scratch,
        compiler_params=params(1),
        cost_estimate=cost(
            2 * planes * size_y * size_z * (size_y + size_z), 2 * planes * size_y * size_z
        ),
        name="go_back",
    )(slab, wave, potential, table_z, table_y, codes, sides, *sources)


def last_x_kernel(frequency_x, frequency_yz, table, coeffs, *refs):
    bufs, (out, tall) = refs[:-2], refs[-2:]
    parts, size_x, columns, lanes = coeffs.shape

    def some_columns(g, carry):
        loaded = []
        for h in range(COLUMNS):
            loaded.append(jnp.concatenate([buf[COLUMNS * g + h] for buf in bufs], axis=0))
        for first in range(0, COLUMNS, FOUR):
            result = jnp.dot(
                table[...],
                jnp.concatenate(loaded[first : first + FOUR], axis=1),
                preferred_element_type=jnp.float32,
            )
            for h in range(FOUR):
                tall[pl.ds(COLUMNS * g + first + h, parts * size_x, stride=columns), :] = result[
                    :, h * lanes : (h + 1) * lanes
                ]
        return carry

    lax.fori_loop(0, columns // COLUMNS, some_columns, 0)

    def finish(k, carry):
        kinetic = frequency_x[k] + frequency_yz[...]
        for part in range(parts):
            start = pl.multiple_of((part * size_x + k) * columns, 8)
            out[part, k] = (
                tall[pl.ds(start, columns), :] + kinetic * coeffs[part, k].astype(jnp.float32)
            ).astype(jnp.bfloat16)
        return carry

    lax.fori_loop(0, size_x, finish, 0, unroll=8)


def last_x(frequency_x, frequency_yz, table, coeffs, bufs):
    _, size_x, columns, size_z = coeffs.shape
    lanes = size_z // 2
    spec = pl.BlockSpec((2, size_x, columns, lanes), lambda i: (0, 0, 0, i))
    return pl.pallas_call(
        last_x_kernel,
        grid=(2,),
        in_specs=[
            SMEM_SPEC,
            pl.BlockSpec((columns, lanes), lambda i: (0, i)),
            whole(table.shape),
            spec,
        ]
        + [pl.BlockSpec((*b.shape[:2], lanes), lambda i: (0, 0, i)) for b in bufs],
        out_specs=spec,
        out_shape=jax.ShapeDtypeStruct(coeffs.shape, jnp.bfloat16),
        scratch_shapes=[pltpu.VMEM((2 * size_x * columns, lanes), jnp.float32)],
        compiler_params=params(1),
        cost_estimate=cost(2 * size_x * size_x * columns * size_z, 3 * size_x * columns * size_z),
        name="last_x",
    )(frequency_x, frequency_yz, table, coeffs, *bufs)


def per_device_chunked(wave_coeffs, occupation, potential, projectors, coupling, sphere_blocks):
    pieces = lax.axis_size("fft")
    bands = lax.axis_size("band")
    slab = lax.axis_index("fft")
    coeffs = wave_coeffs[0]
    _, size_x, columns, size_z = coeffs.shape
    slab_planes, size_y, _ = potential.shape
    atom_dev, nproj, blocks, cells = projectors.shape
    zblocks = size_z // cells
    outer, inner = chunk_planes(slab_planes)
    up = [(i, (i + 1) % pieces) for i in range(pieces)]
    down = [(j, i) for i, j in up]

    inverse_x, forward_x = (real_blocks(size_x, s) for s in (1.0, -1.0))
    inverse_y, forward_y = (real_blocks(size_y, s) for s in (1.0, -1.0))
    inverse_z, forward_z = (real_blocks(size_z, s) for s in (1.0, -1.0))
    place_outer, place_inner = (
        np.arange(pieces)[:, None] * slab_planes + np.array(chunk)[None, :]
        for chunk in (outer, inner)
    )
    table_x_outer = np.stack([inverse_x[r][place_outer] for r in range(2)], 1)
    table_x_inner = np.stack([inverse_x[r][place_inner] for r in range(2)], 1)
    tables_back_x = [
        np.stack([forward_x[:, :, r][:, :, place] for r in range(2)], 3).reshape(
            2 * size_x, pieces, -1
        )
        for place in (place_outer, place_inner)
    ]
    middle = size_y // 2
    down_y = [inverse_y[:, :middle, :, s::2] for s in (0, 1)]
    back_y = [forward_y[:, s::2, :, :middle] for s in (0, 1)]
    split = (pieces, columns // 2)
    tables = [
        table_x_outer.reshape(-1, 2 * size_x),
        table_x_inner.reshape(-1, 2 * size_x),
        np.stack([t.reshape(size_y, -1) for t in down_y]),
        np.stack(
            [t.reshape(2, middle, 2, *split).swapaxes(2, 3).reshape(size_y, -1) for t in down_y]
        ),
        inverse_z.transpose(2, 3, 0, 1).reshape(2 * size_z, -1),
        forward_z.transpose(2, 3, 0, 1).reshape(2 * size_z, -1),
        np.stack([t.reshape(size_y, -1) for t in back_y]),
        np.stack([t.reshape(2, *split, -1).swapaxes(0, 1).reshape(size_y, -1) for t in back_y]),
        np.stack(
            [
                np.concatenate(
                    [t[:, (d - np.arange(pieces)) % pieces].reshape(2 * size_x, -1) for t in tables_back_x],
                    axis=1,
                )
                for d in range(pieces)
            ]
        ),
    ]
    (
        table_x_outer, table_x_inner, table_y_outer, table_y_inner, table_z,
        table_back_z, table_back_y_outer, table_back_y_inner, tables_back_x,
    ) = (jnp.asarray(t.astype(jnp.bfloat16)) for t in tables)

    table_back_x = lax.dynamic_index_in_dim(tables_back_x, slab, 0, keepdims=False)

    where = slab.reshape(1)
    section_outer = first_x(where, table_x_outer, coeffs, len(outer), pieces, False)
    section_outer, table_x_inner, sphere_blocks = lax.optimization_barrier(
        (section_outer, table_x_inner, sphere_blocks)
    )
    section_inner = first_x(where, table_x_inner, coeffs, len(inner), pieces, True)

    entries = atom_dev * blocks

    def codes_of(chunk, shift):
        owner = (slab + shift + pieces) % pieces
        numbers = lax.dynamic_slice_in_dim(sphere_blocks, owner * atom_dev, atom_dev, 0)
        plane = numbers // (size_y * zblocks) - slab * slab_planes
        rest = numbers % (size_y * zblocks)
        if chunk is outer:
            inside = ((plane >= 0) & (plane < EDGE)) | (
                (plane >= slab_planes - EDGE) & (plane < slab_planes)
            )
            plane = jnp.where(plane < EDGE, plane, plane - len(inner))
        else:
            inside = (plane >= EDGE) & (plane < slab_planes - EDGE)
            plane = plane - EDGE
        code = jnp.where(inside, plane * size_y + rest // zblocks, -1)
        return code.reshape(entries), (rest % zblocks).reshape(entries)

    found = [codes_of(outer, shift) for shift in (0, -1, 1)]
    codes_outer, sides_outer = (jnp.stack(values) for values in zip(*found))
    codes_inner, sides_inner = (values[None] for values in codes_of(inner, 0))
    sides_outer, sides_inner = sides_outer[:, :, None], sides_inner[:, :, None]
    rows_codes = [codes_outer[:, :, None], codes_inner[:, :, None]]
    lane_codes = [codes_outer[:, None, :], codes_inner[:, None, :]]
    strength = 3.0 * math.sqrt(cells * blocks) / nproj
    coupled = (coupling + coupling.T) * (0.5 * strength)
    coupled = jnp.broadcast_to(coupled.T[:, :, None], (nproj, nproj, cells))
    section_inner, rows_codes, lane_codes, sides_outer, sides_inner, coupled = (
        lax.optimization_barrier(
            (section_inner, rows_codes, lane_codes, sides_outer, sides_inner, coupled)
        )
    )

    half = pieces // 2
    near, far = list(range(1, half)), list(range(half, pieces))

    def send(block, k, *awaited):
        for row, m in awaited:
            block, row[m] = lax.optimization_barrier((block, row[m]))
        return lax.ppermute(block, "fft", [(j, j ^ k) for j in range(pieces)])

    received_outer, received_inner = (
        [section[0]] + [None] * (pieces - 1) for section in (section_outer, section_inner)
    )
    for partners in (near, far):
        queue = [(section_outer, received_outer, k) for k in partners]
        queue += [(section_inner, received_inner, k) for k in partners]
        for place, (section, received, k) in enumerate(queue):
            awaited = [queue[place - 2][1:]] if place >= 2 else []
            received[k] = send(section[k], k, *awaited)
    wave_outer, density_outer, rows_outer, to_previous, to_following = make_field(
        where, occupation, received_outer, table_y_outer, table_z, rows_codes[0],
        sides_outer, len(outer), pieces, False,
    )
    from_following = lax.ppermute(to_previous, "fft", down)
    from_previous = lax.ppermute(to_following, "fft", up)
    density_outer = lax.psum(density_outer, "band")
    wave_inner, density_inner, rows_inner = make_field(
        where, occupation, received_inner, table_y_inner, table_z, rows_codes[1],
        sides_inner, len(inner), pieces, True,
    )
    projected, spread = make_nonlocal(
        coupled, projectors, [rows_outer, rows_inner, from_following, from_previous]
    )
    spread_previous = lax.ppermute(spread, "fft", up)
    spread_following = lax.ppermute(spread, "fft", down)
    edge_steps = EDGE // PLANES
    inner_steps = len(inner) // PLANES
    back_inner = go_back(
        where, wave_inner, potential, table_back_z, table_back_y_inner, lane_codes[1],
        sides_inner, [spread], lambda i: i + edge_steps, pieces, True,
    )
    def permute_all(values):
        received = [values[0]]
        for k in range(1, pieces):
            pairs = [(j, (j + k) % pieces) for j in range(pieces)]
            received.append(lax.ppermute(values[k], "fft", pairs))
        return received

    back_inner = permute_all(back_inner)
    back_outer = go_back(
        where, wave_outer, potential, table_back_z, table_back_y_outer, lane_codes[0],
        sides_outer, [spread, spread_previous, spread_following],
        lambda i: jnp.where(i < edge_steps, i, i + inner_steps), pieces, False,
    )
    density_inner, density_outer = lax.optimization_barrier((density_inner, density_outer))
    density_inner = lax.psum(density_inner, "band")
    back_outer, density_outer = lax.optimization_barrier((back_outer, density_outer))
    back_outer = permute_all(back_outer)
    back_inner = [
        b.reshape(len(inner), 2, 2, columns // 2, size_z)
        .transpose(3, 1, 2, 0, 4)
        .reshape(columns, -1, size_z)
        for b in back_inner
    ]
    density = jnp.concatenate([density_outer[:EDGE], density_inner, density_outer[EDGE:]], axis=0)

    index_x = np.arange(size_x)
    frequency_x = jnp.asarray(
        (np.where(2 * index_x < size_x, index_x, index_x - size_x) / size_x) ** 2, jnp.float32
    )
    index_y = slab * columns + jnp.arange(columns, dtype=jnp.int32)
    index_z = jnp.arange(size_z, dtype=jnp.int32)
    frequency_yz = wave_squares(index_y, size_y)[:, None] + wave_squares(index_z, size_z)[None, :]
    coeffs, density, back_inner = lax.optimization_barrier((coeffs, density, back_inner))
    applied = last_x(frequency_x, frequency_yz, table_back_x, coeffs, back_outer + back_inner)
    return (applied[None], density, projected[None, :, :, :, 0])


def per_device(wave_coeffs, occupation, potential, projectors, coupling, sphere_blocks):
    pieces, bands = lax.axis_size("fft"), lax.axis_size("band")
    size_z = wave_coeffs.shape[4]
    columns = wave_coeffs.shape[3]
    slab_planes = potential.shape[0]
    chunked = (
        pieces >= 4
        and pieces & (pieces - 1) == 0
        and slab_planes % EDGE == 0
        and slab_planes >= 3 * EDGE
        and EDGE >= HALO
        and columns % 8 == 0
        and size_z % 256 == 0
        and projectors.shape[0] % bands == 0
        and projectors.shape[3] == 128
        and projectors.shape[1] == 8
    )
    chosen = per_device_chunked if chunked else per_device_plain
    return chosen(wave_coeffs, occupation, potential, projectors, coupling, sphere_blocks)


def solution(mesh):
    placed = (
        P("band", None, None, "fft", None),
        P("band", None),
        P("fft", None, None),
        P("fft", None, None, None),
        P(),
        P(),
    )
    return jax.shard_map(
        per_device,
        mesh=mesh,
        in_specs=placed,
        out_specs=(
            P("band", None, None, "fft", None),
            P("fft", None, None),
            P("band", "fft", None, None),
        ),
        check_vma=False,
    )
```

```python
import functools
import math

import jax
import jax.numpy as jnp
import numpy as np
from jax import lax
from jax.experimental import pallas as pl
from jax.experimental.pallas import tpu as pltpu
from jax.sharding import PartitionSpec as P

HALO = 6
EDGE = 8
PLANES = 4
COLUMNS = 8
FOUR = 4
VMEM_BYTES = 56 * 1024 * 1024


def extended(shard, sides, width):
    for axis, dim in sides:
        count, length = (lax.axis_size(axis), shard.shape[dim])
        up = [(i, (i + 1) % count) for i in range(count)]
        down = [(j, i) for i, j in up]
        last = lax.slice_in_dim(shard, length - width, length, axis=dim)
        first = lax.slice_in_dim(shard, 0, width, axis=dim)
        before = lax.ppermute(last, axis, up)
        after = lax.ppermute(first, axis, down)
        shard = jnp.concatenate([before, shard, after], axis=dim)
    return shard


def dft_table(length, sign_value):
    indices = jnp.arange(length, dtype=jnp.int32)
    phases = indices[:, None] * indices[None, :] % length
    angles = 2.0 * math.pi / length * phases.astype(jnp.float32)
    factor = 1.0 / math.sqrt(length)
    cosine = jnp.cos(angles) * factor
    sine_part = jnp.sin(angles) * (sign_value * factor)
    upper_rows = jnp.stack([cosine, -sine_part])
    bottom = jnp.stack([sine_part, cosine])
    return jnp.stack([upper_rows, bottom]).astype(jnp.bfloat16)


def wave_squares(indices, length):
    frequency = (
        jnp.where(2 * indices < length, indices, indices - length).astype(jnp.float32) / length
    )
    return frequency * frequency


def per_device_plain(wave_coeffs, occupation, potential, projectors, coupling, sphere_blocks):
    pieces = lax.axis_size("fft")
    slab_index = lax.axis_index("fft")
    coeffs = wave_coeffs[0]
    size_x = coeffs.shape[1]
    columns = coeffs.shape[2]
    size_z = coeffs.shape[3]
    slab_planes = potential.shape[0]
    size_y = potential.shape[1]
    atom_dev = projectors.shape[0]
    nproj_count = projectors.shape[1]
    block_cells = projectors.shape[3]
    zblocks = size_z // block_cells
    plane_blocks = size_y * zblocks
    total_atoms = atom_dev * pieces
    table_x = dft_table(size_x, 1.0).transpose(0, 2, 1, 3).reshape(2 * size_x, 2 * size_x)
    inverse_y = dft_table(size_y, 1.0)
    inverse_z = dft_table(size_z, 1.0)
    flattened = coeffs.reshape(2 * size_x, columns * size_z)
    along_x = jnp.dot(table_x, flattened, preferred_element_type=jnp.float32)
    along_x = along_x.reshape(2, size_x, columns, size_z).astype(jnp.bfloat16)
    along_y = jnp.einsum(
        "abyk,bxkz->axyz",
        inverse_y,
        lax.all_to_all(along_x, "fft", split_axis=1, concat_axis=2, tiled=True),
        preferred_element_type=jnp.float32,
    ).astype(jnp.bfloat16)
    wave_field = jnp.einsum(
        "abzk,bxyk->axyz", inverse_z, along_y, preferred_element_type=jnp.float32
    ).astype(jnp.bfloat16)
    weights = occupation[0]
    real_part = wave_field[0].astype(jnp.float32)
    imag_part = wave_field[1].astype(jnp.float32)
    partial_density = weights[0] * real_part * real_part + weights[1] * imag_part * imag_part
    density = lax.psum(partial_density.astype(jnp.bfloat16), "band")
    strength = 3.0 * math.sqrt(block_cells * projectors.shape[2]) / nproj_count
    coupled = (coupling + coupling.T) * (0.5 * strength)
    nearby = extended(projectors, (("fft", 0),), atom_dev)
    atom_rows = (
        slab_index * atom_dev - atom_dev + jnp.arange(3 * atom_dev, dtype=jnp.int32) + total_atoms
    ) % total_atoms
    near_blocks = sphere_blocks[atom_rows]
    plane_index = near_blocks // plane_blocks
    inside = plane_index // slab_planes == slab_index
    local_index = jnp.where(
        inside,
        (plane_index - slab_index * slab_planes) * plane_blocks + near_blocks % plane_blocks,
        0,
    )
    blocks_own = wave_field.reshape(2, slab_planes * plane_blocks, block_cells)
    gathered = blocks_own[:, local_index] * inside[None, :, :, None].astype(jnp.bfloat16)
    partial_value = jnp.einsum(
        "ajsk,bask->abj", nearby, gathered, preferred_element_type=jnp.float32
    )
    summed = extended(partial_value, (("fft", 0),), atom_dev)
    projections_own = (
        summed[:atom_dev] + summed[2 * atom_dev : 3 * atom_dev] + summed[4 * atom_dev :]
    )
    energy_own = jnp.einsum(
        "ij,abj->abi", coupled, projections_own, precision=lax.Precision.HIGHEST
    )
    energy = extended(energy_own, (("fft", 0),), atom_dev)
    spread = jnp.einsum(
        "ajsk,abj->bask", nearby.astype(jnp.float32), energy, precision=lax.Precision.HIGHEST
    )
    spread = spread * inside[None, :, :, None].astype(jnp.float32)
    accumulated = (
        jnp.zeros((2, slab_planes * plane_blocks, block_cells), jnp.float32)
        .at[:, local_index]
        .add(spread)
    )
    nonlocal_term = accumulated.reshape(2, slab_planes, size_y, size_z)
    total_field = (
        potential.astype(jnp.float32)[None] * wave_field.astype(jnp.float32) + nonlocal_term
    ).astype(jnp.bfloat16)
    forward_z = dft_table(size_z, -1.0)
    forward_y = dft_table(size_y, -1.0)
    forward_x = dft_table(size_x, -1.0)
    back_z = jnp.einsum(
        "abzk,bxyk->axyz", forward_z, total_field, preferred_element_type=jnp.float32
    ).astype(jnp.bfloat16)
    back_y = jnp.einsum(
        "abyk,bxkz->axyz", forward_y, back_z, preferred_element_type=jnp.float32
    ).astype(jnp.bfloat16)
    transformed = jnp.einsum(
        "abxk,bkyz->axyz",
        forward_x,
        lax.all_to_all(back_y, "fft", split_axis=2, concat_axis=1, tiled=True),
        preferred_element_type=jnp.float32,
    )
    index_x = jnp.arange(size_x, dtype=jnp.int32)
    index_y = slab_index * columns + jnp.arange(columns, dtype=jnp.int32)
    index_z = jnp.arange(size_z, dtype=jnp.int32)
    kinetic = (
        wave_squares(index_x, size_x)[:, None, None]
        + wave_squares(index_y, size_y)[None, :, None]
        + wave_squares(index_z, size_z)[None, None, :]
    )
    applied = (transformed + kinetic[None] * coeffs.astype(jnp.float32)).astype(jnp.bfloat16)
    return (applied[None], density, projections_own[None])


def real_blocks(length, sign):
    index = np.arange(length)
    angles = 2.0 * np.pi / length * (index[:, None] * index[None, :] % length)
    cosine = np.cos(angles) / np.sqrt(length)
    sine = sign * np.sin(angles) / np.sqrt(length)
    blocks = np.empty((2, length, 2, length))
    blocks[0, :, 0, :] = cosine
    blocks[1, :, 1, :] = cosine
    blocks[0, :, 1, :] = -sine
    blocks[1, :, 0, :] = sine
    return blocks


def chunk_planes(slab_planes):
    low, high = list(range(EDGE)), list(range(slab_planes - EDGE, slab_planes))
    return [low + high, list(range(EDGE, slab_planes - EDGE))]


def params(steps):
    return pltpu.CompilerParams(
        dimension_semantics=("arbitrary",) * steps, vmem_limit_bytes=VMEM_BYTES
    )


def cost(products, values):
    return pl.CostEstimate(flops=4 * products, bytes_accessed=4 * values, transcendentals=0)


def whole(shape):
    return pl.BlockSpec(shape, lambda i: (0,) * len(shape))


SMEM_SPEC = pl.BlockSpec(memory_space=pltpu.SMEM)


def paired(refs, slab):
    return [(lax.bitwise_xor(slab, jnp.int32(k)), ref) for k, ref in enumerate(refs)]


def shifted(refs, slab):
    return [(lax.rem(slab + k, len(refs)), ref) for k, ref in enumerate(refs)]


def first_x_kernel(slab, table_ref, coeffs_ref, *refs, pieces, natural):
    scratch = 3 if natural else 2
    outs = paired(refs[:-scratch], slab[0])
    turned, wide, *tall = refs[-scratch:]
    parts, size_x, columns, lanes = coeffs_ref.shape
    rows = parts * size_x
    height = table_ref.shape[0] // pieces

    for k, (device, _) in enumerate(outs):
        start = pl.multiple_of(device * height, 16)
        turned[k * height : (k + 1) * height, :] = table_ref[pl.ds(start, height), :]

    def widen(k, carry):
        for part in range(parts):
            start = pl.multiple_of((part * size_x + k * 8) * columns, 8)
            wide[pl.ds(start, 8 * columns), :] = (
                coeffs_ref[part, pl.ds(k * 8, 8)].astype(jnp.float32).reshape(8 * columns, lanes)
            )
        return carry

    lax.fori_loop(0, size_x // 8, widen, 0, unroll=2)

    def some_columns(g, carry):
        loaded = [
            wide[pl.ds(COLUMNS * g + h, rows, stride=columns), :].astype(jnp.bfloat16)
            for h in range(COLUMNS)
        ]
        for first in range(0, COLUMNS, FOUR):
            result = jnp.dot(
                turned[...],
                jnp.concatenate(loaded[first : first + FOUR], axis=1),
                preferred_element_type=jnp.float32,
            )
            for h in range(FOUR):
                column = COLUMNS * g + first + h
                piece = result[:, h * lanes : (h + 1) * lanes]
                if natural:
                    place = (first + h) % 2 * columns + COLUMNS // 2 * g + (first + h) // 2
                    planes = height // 2
                    for k in range(pieces):
                        for part in range(2):
                            start = k * height * columns + part * (columns // 2) + place
                            row = k * height + part * planes
                            tall[0][pl.ds(start, planes, stride=2 * columns), :] = piece[
                                row : row + planes
                            ]
                else:
                    piece = piece.astype(jnp.bfloat16)
                    for k, (_, out) in enumerate(outs):
                        out[column] = piece[k * height : (k + 1) * height]
        return carry

    lax.fori_loop(0, columns // COLUMNS, some_columns, 0)
    if natural:
        for k, (_, out) in enumerate(outs):
            values = tall[0][k * height * columns : (k + 1) * height * columns, :]
            out[...] = values.astype(jnp.bfloat16).reshape(out.shape)


def first_x(slab, table, coeffs, planes, pieces, natural):
    _, size_x, columns, size_z = coeffs.shape
    lanes = size_z // 2
    shape = (planes, 2 * columns) if natural else (columns, 2 * planes)
    scratch = [
        pltpu.VMEM(table.shape, jnp.bfloat16),
        pltpu.VMEM((2 * size_x * columns, lanes), jnp.float32),
    ]
    if natural:
        scratch.append(pltpu.VMEM((2 * pieces * planes * columns, lanes), jnp.float32))
    out_specs = [pl.BlockSpec((*shape, lanes), lambda i: (0, 0, i))] * pieces
    out_shape = [jax.ShapeDtypeStruct((*shape, size_z), jnp.bfloat16)] * pieces
    return pl.pallas_call(
        functools.partial(first_x_kernel, pieces=pieces, natural=natural),
        grid=(2,),
        in_specs=[
            SMEM_SPEC,
            whole(table.shape),
            pl.BlockSpec((2, size_x, columns, lanes), lambda i: (0, 0, 0, i)),
        ],
        out_specs=out_specs,
        out_shape=out_shape,
        scratch_shapes=scratch,
        compiler_params=params(1),
        cost_estimate=cost(2 * size_x * pieces * planes * columns * size_z, 2 * size_x * columns * size_z),
        name="first_x",
    )(slab, table, coeffs)


def ones_at(codes, count, axis):
    shape = (codes.shape[0], count) if axis == 1 else (count, codes.shape[1])
    places = lax.broadcasted_iota(jnp.int32, shape, axis)
    return jnp.where(codes == places, 1.0, 0.0).astype(jnp.bfloat16)


def field_kernel(slab, weights, table_y, table_z, codes, sides, *refs, pieces, count, natural):
    bufs = paired(refs[:count], slab[0])
    wave, density, *rows_out, gathered, wide = refs[count:]
    _, near, size_y, size_z = wave.shape
    columns = size_y // pieces
    groups, entries, _ = codes.shape
    lanes = 128
    halves = size_z // lanes
    i, last = pl.program_id(0), pl.num_programs(0) - 1
    planes = near * (last + 1)

    @pl.when(i == 0)
    def _():
        gathered[...] = jnp.zeros_like(gathered)

    loaded = []
    if natural:
        for source, buf in bufs:
            wide[source] = buf[...]
        for h in range(near):
            loaded.append(
                [wide[:, h, s * columns : (s + 1) * columns].reshape(size_y, size_z) for s in (0, 1)]
            )
    else:
        rows = bufs[0][1].shape[1]

        @pl.when(i == 0)
        def _():
            for source, buf in bufs:
                start = pl.multiple_of(source * columns * rows, 8)
                values = buf[...].astype(jnp.float32).reshape(columns * rows, size_z)
                for q in range(halves):
                    wide[q, pl.ds(start, columns * rows), :] = values[
                        :, q * lanes : (q + 1) * lanes
                    ]

        def strided(start):
            return jnp.concatenate(
                [
                    wide[q, pl.ds(start, size_y // 2, stride=2 * rows), :]
                    for q in range(halves)
                ],
                axis=1,
            ).astype(jnp.bfloat16)

        for h in range(near):
            plane = i * near + h
            loaded.append(
                [
                    jnp.concatenate(
                        [strided(s * rows + part * planes + plane) for part in range(2)], axis=0
                    )
                    for s in (0, 1)
                ]
            )
    even, odd = (
        jnp.dot(
            table_y[s],
            jnp.concatenate([pair[s] for pair in loaded], axis=1),
            preferred_element_type=jnp.float32,
        )
        for s in (0, 1)
    )
    low, high = (even + odd).astype(jnp.bfloat16), (even - odd).astype(jnp.bfloat16)
    middle = size_y // 2
    turned = []
    for h in range(near):
        span = slice(h * size_z, (h + 1) * size_z)
        both = [
            jnp.concatenate(
                [values[part * middle : (part + 1) * middle, span] for values in (low, high)], axis=0
            )
            for part in range(2)
        ]
        turned.append(jnp.concatenate(both, axis=1))
    result = jnp.dot(
        jnp.concatenate(turned, axis=0), table_z[...], preferred_element_type=jnp.float32
    ).astype(jnp.bfloat16)
    for h in range(near):
        total = jnp.zeros((size_y, size_z), jnp.float32)
        for part in range(2):
            values = result[h * size_y : (h + 1) * size_y, part * size_z : (part + 1) * size_z]
            wave[part, h] = values
            values = values.astype(jnp.float32)
            total += weights[0, part] * values * values
        density[h] = total.astype(jnp.bfloat16)

    used = [0] if groups == 1 else [0, 1 + (2 * i > last).astype(jnp.int32)]
    for group in used:
        places = ones_at(codes[group] - i * near * size_y, near * size_y, 1)
        gathered[group] += jnp.dot(places, result, preferred_element_type=jnp.float32)

    @pl.when(i == last)
    def _():
        for group in range(groups):
            for part in range(2):
                total = jnp.zeros((entries, lanes), jnp.float32)
                for q in range(halves):
                    start = part * size_z + q * lanes
                    total += jnp.where(
                        sides[group] == q, gathered[group, :, start : start + lanes], 0.0
                    )
                rows_out[group][part] = total.astype(jnp.bfloat16)


def make_field(slab, weights, bufs, table_y, table_z, codes, sides, planes, pieces, natural):
    size_z = bufs[0].shape[-1]
    size_y = table_y.shape[1]
    columns = size_y // pieces
    groups, entries, _ = codes.shape
    if natural:
        buf_spec = pl.BlockSpec((PLANES, 2 * columns, size_z), lambda i: (i, 0, 0))
        wide = pltpu.VMEM((pieces, PLANES, 2 * columns, size_z), jnp.bfloat16)
    else:
        buf_spec = whole(bufs[0].shape)
        wide = pltpu.VMEM((size_z // 128, 2 * planes * size_y, 128), jnp.float32)
    return pl.pallas_call(
        functools.partial(field_kernel, pieces=pieces, count=len(bufs), natural=natural),
        grid=(planes // PLANES,),
        in_specs=[SMEM_SPEC, SMEM_SPEC]
        + [whole(a.shape) for a in (table_y, table_z, codes, sides)]
        + [buf_spec] * len(bufs),
        out_specs=[
            pl.BlockSpec((2, PLANES, size_y, size_z), lambda i: (0, i, 0, 0)),
            pl.BlockSpec((PLANES, size_y, size_z), lambda i: (i, 0, 0)),
        ]
        + [whole((2, entries, 128))] * groups,
        out_shape=[
            jax.ShapeDtypeStruct((2, planes, size_y, size_z), jnp.bfloat16),
            jax.ShapeDtypeStruct((planes, size_y, size_z), jnp.bfloat16),
        ]
        + [jax.ShapeDtypeStruct((2, entries, 128), jnp.bfloat16)] * groups,
        scratch_shapes=[pltpu.VMEM((groups, entries, 2 * size_z), jnp.float32), wide],
        compiler_params=params(1),
        cost_estimate=cost(
            2 * planes * size_y * size_z * (size_y + size_z), 2 * planes * size_y * size_z
        ),
        name="make_field",
    )(slab, weights, table_y, table_z, codes, sides, *bufs)


def nonlocal_kernel(coupled, projectors, *refs):
    parts, (projections, spread) = refs[:-2], refs[-2:]
    atoms, nproj, blocks, cells = projectors.shape
    for atom in range(atoms):
        tables = [projectors[atom, j].astype(jnp.float32) for j in range(nproj)]
        place = pl.ds(atom * blocks, blocks)
        for part in range(2):
            rows = sum(p[part, place].astype(jnp.float32) for p in parts)
            tile = jnp.concatenate(
                [jnp.sum(t * rows, axis=0, keepdims=True) for t in tables], axis=0
            )
            mixed = jnp.zeros_like(tile)
            for j in range(nproj):
                mixed += coupled[j] * tile[j : j + 1]
            projections[atom, part] = jnp.broadcast_to(
                jnp.sum(tile, -1, keepdims=True), tile.shape
            )
            energy = jnp.broadcast_to(jnp.sum(mixed, -1, keepdims=True), tile.shape)
            spread[part, place] = sum(
                t * energy[j : j + 1] for j, t in enumerate(tables)
            ).astype(jnp.bfloat16)


def make_nonlocal(coupled, projectors, parts):
    atoms, nproj, _, cells = projectors.shape
    return pl.pallas_call(
        nonlocal_kernel,
        out_shape=[
            jax.ShapeDtypeStruct((atoms, 2, nproj, cells), jnp.float32),
            jax.ShapeDtypeStruct(parts[0].shape, jnp.bfloat16),
        ],
        name="make_nonlocal",
    )(coupled, projectors, *parts)


def back_kernel(slab, wave, potential, table_z, table_y, codes, sides, *refs, pieces, natural):
    groups, _, entries = codes.shape
    sources, outs = refs[:groups], refs[groups:-2]
    spread, tall = refs[-2:]
    outs = shifted(outs, slab[0])
    near, size_y, size_z = potential.shape
    lanes = 128
    halves = size_z // lanes
    i, last = pl.program_id(0), pl.num_programs(0) - 1
    planes = near * (last + 1)

    @pl.when(i == 0)
    def _():
        for group, source in enumerate(sources):
            for part in range(2):
                for q in range(halves):
                    start = part * size_z + q * lanes
                    spread[group, :, start : start + lanes] = jnp.where(
                        sides[group] == q, source[part].astype(jnp.float32), 0.0
                    ).astype(jnp.bfloat16)

    used = [0] if groups == 1 else [0, 1 + (2 * i > last).astype(jnp.int32)]
    extra = jnp.zeros((near * size_y, 2 * size_z), jnp.float32)
    for group in used:
        places = ones_at(codes[group] - i * near * size_y, near * size_y, 0)
        extra += jnp.dot(places, spread[group], preferred_element_type=jnp.float32)
    fields = []
    for h in range(near):
        local = potential[h].astype(jnp.float32)
        both = [
            local * wave[part, h].astype(jnp.float32)
            + extra[h * size_y : (h + 1) * size_y, part * size_z : (part + 1) * size_z]
            for part in range(2)
        ]
        fields.append(jnp.concatenate(both, axis=1).astype(jnp.bfloat16))
    back_z = jnp.dot(
        jnp.concatenate(fields, axis=0), table_z[...], preferred_element_type=jnp.float32
    )
    middle = size_y // 2
    folded = [[], []]
    for h in range(near):
        low = back_z[h * size_y : h * size_y + middle]
        high = back_z[h * size_y + middle : (h + 1) * size_y]
        for kept, values in zip(folded, (low + high, low - high)):
            values = values.astype(jnp.bfloat16)
            kept.append(jnp.concatenate([values[:, :size_z], values[:, size_z:]], axis=0))
    columns = size_y // pieces
    for s, kept in enumerate(folded):
        back_y = jnp.dot(
            table_y[s], jnp.concatenate(kept, axis=1), preferred_element_type=jnp.float32
        )
        if natural:
            back_y = back_y.astype(jnp.bfloat16)
            for h in range(near):
                tall[:, h, s * columns : (s + 1) * columns] = back_y[
                    :, h * size_z : (h + 1) * size_z
                ].reshape(pieces, columns, size_z)
            continue
        rows = outs[0][1].shape[1]
        for h in range(near):
            for part in range(2):
                for q in range(halves):
                    start = s * rows + part * planes + i * near + h
                    lane = h * size_z + q * lanes
                    tall[q, pl.ds(start, middle, stride=2 * rows), :] = back_y[
                        part * middle : (part + 1) * middle, lane : lane + lanes
                    ]

    if natural:
        for target, out in outs:
            out[...] = tall[target]
        return
    columns, rows, _ = outs[0][1].shape

    @pl.when(i == last)
    def _():
        for target, out in outs:
            start = pl.multiple_of(target * columns * rows, 8)
            values = [tall[q, pl.ds(start, columns * rows), :] for q in range(halves)]
            out[...] = (
                jnp.concatenate(values, axis=1).astype(jnp.bfloat16).reshape(columns, rows, size_z)
            )


def go_back(slab, wave, potential, table_z, table_y, codes, sides, sources, place, pieces, natural):
    _, planes, size_y, size_z = wave.shape
    columns = size_y // pieces
    groups, _, entries = codes.shape
    scratch = [pltpu.VMEM((groups, entries, 2 * size_z), jnp.bfloat16)]
    if natural:
        shape = (planes, 2 * columns, size_z)
        out_specs = [pl.BlockSpec((PLANES, 2 * columns, size_z), lambda i: (i, 0, 0))] * pieces
        scratch.append(pltpu.VMEM((pieces, PLANES, 2 * columns, size_z), jnp.bfloat16))
    else:
        shape = (columns, 2 * planes, size_z)
        out_specs = [whole(shape)] * pieces
        scratch.append(pltpu.VMEM((size_z // 128, 2 * planes * size_y, 128), jnp.float32))
    return pl.pallas_call(
        functools.partial(back_kernel, pieces=pieces, natural=natural),
        grid=(planes // PLANES,),
        in_specs=[
            SMEM_SPEC,
            pl.BlockSpec((2, PLANES, size_y, size_z), lambda i: (0, i, 0, 0)),
            pl.BlockSpec((PLANES, size_y, size_z), lambda i: (place(i), 0, 0)),
        ]
        + [whole(a.shape) for a in (table_z, table_y, codes, sides, *sources)],
        out_specs=out_specs,
        out_shape=[jax.ShapeDtypeStruct(shape, jnp.bfloat16)] * pieces,
        scratch_shapes=scratch,
        compiler_params=params(1),
        cost_estimate=cost(
            2 * planes * size_y * size_z * (size_y + size_z), 2 * planes * size_y * size_z
        ),
        name="go_back",
    )(slab, wave, potential, table_z, table_y, codes, sides, *sources)


def last_x_kernel(frequency_x, frequency_yz, table, coeffs, *refs):
    bufs, (out, tall) = refs[:-2], refs[-2:]
    parts, size_x, columns, lanes = coeffs.shape

    def some_columns(g, carry):
        loaded = []
        for h in range(COLUMNS):
            loaded.append(jnp.concatenate([buf[COLUMNS * g + h] for buf in bufs], axis=0))
        for first in range(0, COLUMNS, FOUR):
            result = jnp.dot(
                table[...],
                jnp.concatenate(loaded[first : first + FOUR], axis=1),
                preferred_element_type=jnp.float32,
            )
            for h in range(FOUR):
                tall[pl.ds(COLUMNS * g + first + h, parts * size_x, stride=columns), :] = result[
                    :, h * lanes : (h + 1) * lanes
                ]
        return carry

    lax.fori_loop(0, columns // COLUMNS, some_columns, 0)

    def finish(k, carry):
        kinetic = frequency_x[k] + frequency_yz[...]
        for part in range(parts):
            start = pl.multiple_of((part * size_x + k) * columns, 8)
            out[part, k] = (
                tall[pl.ds(start, columns), :] + kinetic * coeffs[part, k].astype(jnp.float32)
            ).astype(jnp.bfloat16)
        return carry

    lax.fori_loop(0, size_x, finish, 0, unroll=8)


def last_x(frequency_x, frequency_yz, table, coeffs, bufs):
    _, size_x, columns, size_z = coeffs.shape
    lanes = size_z // 2
    spec = pl.BlockSpec((2, size_x, columns, lanes), lambda i: (0, 0, 0, i))
    return pl.pallas_call(
        last_x_kernel,
        grid=(2,),
        in_specs=[
            SMEM_SPEC,
            pl.BlockSpec((columns, lanes), lambda i: (0, i)),
            whole(table.shape),
            spec,
        ]
        + [pl.BlockSpec((*b.shape[:2], lanes), lambda i: (0, 0, i)) for b in bufs],
        out_specs=spec,
        out_shape=jax.ShapeDtypeStruct(coeffs.shape, jnp.bfloat16),
        scratch_shapes=[pltpu.VMEM((2 * size_x * columns, lanes), jnp.float32)],
        compiler_params=params(1),
        cost_estimate=cost(2 * size_x * size_x * columns * size_z, 3 * size_x * columns * size_z),
        name="last_x",
    )(frequency_x, frequency_yz, table, coeffs, *bufs)


def per_device_chunked(wave_coeffs, occupation, potential, projectors, coupling, sphere_blocks):
    pieces = lax.axis_size("fft")
    bands = lax.axis_size("band")
    slab = lax.axis_index("fft")
    coeffs = wave_coeffs[0]
    _, size_x, columns, size_z = coeffs.shape
    slab_planes, size_y, _ = potential.shape
    atom_dev, nproj, blocks, cells = projectors.shape
    zblocks = size_z // cells
    outer, inner = chunk_planes(slab_planes)
    up = [(i, (i + 1) % pieces) for i in range(pieces)]
    down = [(j, i) for i, j in up]

    inverse_x, forward_x = (real_blocks(size_x, s) for s in (1.0, -1.0))
    inverse_y, forward_y = (real_blocks(size_y, s) for s in (1.0, -1.0))
    inverse_z, forward_z = (real_blocks(size_z, s) for s in (1.0, -1.0))
    place_outer, place_inner = (
        np.arange(pieces)[:, None] * slab_planes + np.array(chunk)[None, :]
        for chunk in (outer, inner)
    )
    table_x_outer = np.stack([inverse_x[r][place_outer] for r in range(2)], 1)
    table_x_inner = np.stack([inverse_x[r][place_inner] for r in range(2)], 1)
    tables_back_x = [
        np.stack([forward_x[:, :, r][:, :, place] for r in range(2)], 3).reshape(
            2 * size_x, pieces, -1
        )
        for place in (place_outer, place_inner)
    ]
    middle = size_y // 2
    down_y = [inverse_y[:, :middle, :, s::2] for s in (0, 1)]
    back_y = [forward_y[:, s::2, :, :middle] for s in (0, 1)]
    split = (pieces, columns // 2)
    tables = [
        table_x_outer.reshape(-1, 2 * size_x),
        table_x_inner.reshape(-1, 2 * size_x),
        np.stack([t.reshape(size_y, -1) for t in down_y]),
        np.stack(
            [t.reshape(2, middle, 2, *split).swapaxes(2, 3).reshape(size_y, -1) for t in down_y]
        ),
        inverse_z.transpose(2, 3, 0, 1).reshape(2 * size_z, -1),
        forward_z.transpose(2, 3, 0, 1).reshape(2 * size_z, -1),
        np.stack([t.reshape(size_y, -1) for t in back_y]),
        np.stack([t.reshape(2, *split, -1).swapaxes(0, 1).reshape(size_y, -1) for t in back_y]),
        np.stack(
            [
                np.concatenate(
                    [t[:, (d - np.arange(pieces)) % pieces].reshape(2 * size_x, -1) for t in tables_back_x],
                    axis=1,
                )
                for d in range(pieces)
            ]
        ),
    ]
    (
        table_x_outer, table_x_inner, table_y_outer, table_y_inner, table_z,
        table_back_z, table_back_y_outer, table_back_y_inner, tables_back_x,
    ) = (jnp.asarray(t.astype(jnp.bfloat16)) for t in tables)

    table_back_x = lax.dynamic_index_in_dim(tables_back_x, slab, 0, keepdims=False)

    where = slab.reshape(1)
    section_outer = first_x(where, table_x_outer, coeffs, len(outer), pieces, False)
    section_outer, table_x_inner, sphere_blocks = lax.optimization_barrier(
        (section_outer, table_x_inner, sphere_blocks)
    )
    section_inner = first_x(where, table_x_inner, coeffs, len(inner), pieces, True)

    entries = atom_dev * blocks

    def codes_of(chunk, shift):
        owner = (slab + shift + pieces) % pieces
        numbers = lax.dynamic_slice_in_dim(sphere_blocks, owner * atom_dev, atom_dev, 0)
        plane = numbers // (size_y * zblocks) - slab * slab_planes
        rest = numbers % (size_y * zblocks)
        if chunk is outer:
            inside = ((plane >= 0) & (plane < EDGE)) | (
                (plane >= slab_planes - EDGE) & (plane < slab_planes)
            )
            plane = jnp.where(plane < EDGE, plane, plane - len(inner))
        else:
            inside = (plane >= EDGE) & (plane < slab_planes - EDGE)
            plane = plane - EDGE
        code = jnp.where(inside, plane * size_y + rest // zblocks, -1)
        return code.reshape(entries), (rest % zblocks).reshape(entries)

    found = [codes_of(outer, shift) for shift in (0, -1, 1)]
    codes_outer, sides_outer = (jnp.stack(values) for values in zip(*found))
    codes_inner, sides_inner = (values[None] for values in codes_of(inner, 0))
    sides_outer, sides_inner = sides_outer[:, :, None], sides_inner[:, :, None]
    rows_codes = [codes_outer[:, :, None], codes_inner[:, :, None]]
    lane_codes = [codes_outer[:, None, :], codes_inner[:, None, :]]
    strength = 3.0 * math.sqrt(cells * blocks) / nproj
    coupled = (coupling + coupling.T) * (0.5 * strength)
    coupled = jnp.broadcast_to(coupled.T[:, :, None], (nproj, nproj, cells))
    section_inner, rows_codes, lane_codes, sides_outer, sides_inner, coupled = (
        lax.optimization_barrier(
            (section_inner, rows_codes, lane_codes, sides_outer, sides_inner, coupled)
        )
    )

    half = pieces // 2
    near, far = list(range(1, half)), list(range(half, pieces))

    def send(block, k, *awaited):
        for row, m in awaited:
            block, row[m] = lax.optimization_barrier((block, row[m]))
        return lax.ppermute(block, "fft", [(j, j ^ k) for j in range(pieces)])

    received_outer, received_inner = (
        [section[0]] + [None] * (pieces - 1) for section in (section_outer, section_inner)
    )
    for partners, early in ((near, 0), (far, 1)):
        queue = [(section_outer, received_outer, k) for k in partners]
        queue += [(section_inner, received_inner, k) for k in partners]
        for place, (section, received, k) in enumerate(queue):
            behind = 2 + early * (place == len(partners) + 1)
            awaited = [queue[place - behind][1:]] if place >= behind else []
            received[k] = send(section[k], k, *awaited)
    wave_outer, density_outer, rows_outer, to_previous, to_following = make_field(
        where, occupation, received_outer, table_y_outer, table_z, rows_codes[0],
        sides_outer, len(outer), pieces, False,
    )
    from_following = lax.ppermute(to_previous, "fft", down)
    from_previous = lax.ppermute(to_following, "fft", up)
    density_outer = lax.psum(density_outer, "band")
    wave_inner, density_inner, rows_inner = make_field(
        where, occupation, received_inner, table_y_inner, table_z, rows_codes[1],
        sides_inner, len(inner), pieces, True,
    )
    projected, spread = make_nonlocal(
        coupled, projectors, [rows_outer, rows_inner, from_following, from_previous]
    )
    spread_previous = lax.ppermute(spread, "fft", up)
    spread_following = lax.ppermute(spread, "fft", down)
    edge_steps = EDGE // PLANES
    inner_steps = len(inner) // PLANES
    back_inner = go_back(
        where, wave_inner, potential, table_back_z, table_back_y_inner, lane_codes[1],
        sides_inner, [spread], lambda i: i + edge_steps, pieces, True,
    )
    def permute_all(values):
        received = [values[0]]
        for k in range(1, pieces):
            pairs = [(j, (j + k) % pieces) for j in range(pieces)]
            received.append(lax.ppermute(values[k], "fft", pairs))
        return received

    back_inner = permute_all(back_inner)
    back_outer = go_back(
        where, wave_outer, potential, table_back_z, table_back_y_outer, lane_codes[0],
        sides_outer, [spread, spread_previous, spread_following],
        lambda i: jnp.where(i < edge_steps, i, i + inner_steps), pieces, False,
    )
    density_inner, density_outer = lax.optimization_barrier((density_inner, density_outer))
    density_inner = lax.psum(density_inner, "band")
    back_outer, density_outer = lax.optimization_barrier((back_outer, density_outer))
    back_outer = permute_all(back_outer)
    back_inner = [
        b.reshape(len(inner), 2, 2, columns // 2, size_z)
        .transpose(3, 1, 2, 0, 4)
        .reshape(columns, -1, size_z)
        for b in back_inner
    ]
    density = jnp.concatenate([density_outer[:EDGE], density_inner, density_outer[EDGE:]], axis=0)

    index_x = np.arange(size_x)
    frequency_x = jnp.asarray(
        (np.where(2 * index_x < size_x, index_x, index_x - size_x) / size_x) ** 2, jnp.float32
    )
    index_y = slab * columns + jnp.arange(columns, dtype=jnp.int32)
    index_z = jnp.arange(size_z, dtype=jnp.int32)
    frequency_yz = wave_squares(index_y, size_y)[:, None] + wave_squares(index_z, size_z)[None, :]
    coeffs, density, back_inner = lax.optimization_barrier((coeffs, density, back_inner))
    applied = last_x(frequency_x, frequency_yz, table_back_x, coeffs, back_outer + back_inner)
    return (applied[None], density, projected[None, :, :, :, 0])


def per_device(wave_coeffs, occupation, potential, projectors, coupling, sphere_blocks):
    pieces, bands = lax.axis_size("fft"), lax.axis_size("band")
    size_z = wave_coeffs.shape[4]
    columns = wave_coeffs.shape[3]
    slab_planes = potential.shape[0]
    chunked = (
        pieces >= 4
        and pieces & (pieces - 1) == 0
        and slab_planes % EDGE == 0
        and slab_planes >= 3 * EDGE
        and EDGE >= HALO
        and columns % 8 == 0
        and size_z % 256 == 0
        and projectors.shape[0] % bands == 0
        and projectors.shape[3] == 128
        and projectors.shape[1] == 8
    )
    chosen = per_device_chunked if chunked else per_device_plain
    return chosen(wave_coeffs, occupation, potential, projectors, coupling, sphere_blocks)


def solution(mesh):
    placed = (
        P("band", None, None, "fft", None),
        P("band", None),
        P("fft", None, None),
        P("fft", None, None, None),
        P(),
        P(),
    )
    return jax.shard_map(
        per_device,
        mesh=mesh,
        in_specs=placed,
        out_specs=(
            P("band", None, None, "fft", None),
            P("fft", None, None),
            P("band", "fft", None, None),
        ),
        check_vma=False,
    )
```

```python
import functools
import math

import jax
import jax.numpy as jnp
import numpy as np
from jax import lax
from jax.experimental import pallas as pl
from jax.experimental.pallas import tpu as pltpu
from jax.sharding import PartitionSpec as P

HALO = 6
EDGE = 8
PLANES = 4
COLUMNS = 8
FOUR = 4
VMEM_BYTES = 56 * 1024 * 1024


def extended(shard, sides, width):
    for axis, dim in sides:
        count, length = (lax.axis_size(axis), shard.shape[dim])
        up = [(i, (i + 1) % count) for i in range(count)]
        down = [(j, i) for i, j in up]
        last = lax.slice_in_dim(shard, length - width, length, axis=dim)
        first = lax.slice_in_dim(shard, 0, width, axis=dim)
        before = lax.ppermute(last, axis, up)
        after = lax.ppermute(first, axis, down)
        shard = jnp.concatenate([before, shard, after], axis=dim)
    return shard


def dft_table(length, sign_value):
    indices = jnp.arange(length, dtype=jnp.int32)
    phases = indices[:, None] * indices[None, :] % length
    angles = 2.0 * math.pi / length * phases.astype(jnp.float32)
    factor = 1.0 / math.sqrt(length)
    cosine = jnp.cos(angles) * factor
    sine_part = jnp.sin(angles) * (sign_value * factor)
    upper_rows = jnp.stack([cosine, -sine_part])
    bottom = jnp.stack([sine_part, cosine])
    return jnp.stack([upper_rows, bottom]).astype(jnp.bfloat16)


def wave_squares(indices, length):
    frequency = (
        jnp.where(2 * indices < length, indices, indices - length).astype(jnp.float32) / length
    )
    return frequency * frequency


def per_device_plain(wave_coeffs, occupation, potential, projectors, coupling, sphere_blocks):
    pieces = lax.axis_size("fft")
    slab_index = lax.axis_index("fft")
    coeffs = wave_coeffs[0]
    size_x = coeffs.shape[1]
    columns = coeffs.shape[2]
    size_z = coeffs.shape[3]
    slab_planes = potential.shape[0]
    size_y = potential.shape[1]
    atom_dev = projectors.shape[0]
    nproj_count = projectors.shape[1]
    block_cells = projectors.shape[3]
    zblocks = size_z // block_cells
    plane_blocks = size_y * zblocks
    total_atoms = atom_dev * pieces
    table_x = dft_table(size_x, 1.0).transpose(0, 2, 1, 3).reshape(2 * size_x, 2 * size_x)
    inverse_y = dft_table(size_y, 1.0)
    inverse_z = dft_table(size_z, 1.0)
    flattened = coeffs.reshape(2 * size_x, columns * size_z)
    along_x = jnp.dot(table_x, flattened, preferred_element_type=jnp.float32)
    along_x = along_x.reshape(2, size_x, columns, size_z).astype(jnp.bfloat16)
    along_y = jnp.einsum(
        "abyk,bxkz->axyz",
        inverse_y,
        lax.all_to_all(along_x, "fft", split_axis=1, concat_axis=2, tiled=True),
        preferred_element_type=jnp.float32,
    ).astype(jnp.bfloat16)
    wave_field = jnp.einsum(
        "abzk,bxyk->axyz", inverse_z, along_y, preferred_element_type=jnp.float32
    ).astype(jnp.bfloat16)
    weights = occupation[0]
    real_part = wave_field[0].astype(jnp.float32)
    imag_part = wave_field[1].astype(jnp.float32)
    partial_density = weights[0] * real_part * real_part + weights[1] * imag_part * imag_part
    density = lax.psum(partial_density.astype(jnp.bfloat16), "band")
    strength = 3.0 * math.sqrt(block_cells * projectors.shape[2]) / nproj_count
    coupled = (coupling + coupling.T) * (0.5 * strength)
    nearby = extended(projectors, (("fft", 0),), atom_dev)
    atom_rows = (
        slab_index * atom_dev - atom_dev + jnp.arange(3 * atom_dev, dtype=jnp.int32) + total_atoms
    ) % total_atoms
    near_blocks = sphere_blocks[atom_rows]
    plane_index = near_blocks // plane_blocks
    inside = plane_index // slab_planes == slab_index
    local_index = jnp.where(
        inside,
        (plane_index - slab_index * slab_planes) * plane_blocks + near_blocks % plane_blocks,
        0,
    )
    blocks_own = wave_field.reshape(2, slab_planes * plane_blocks, block_cells)
    gathered = blocks_own[:, local_index] * inside[None, :, :, None].astype(jnp.bfloat16)
    partial_value = jnp.einsum(
        "ajsk,bask->abj", nearby, gathered, preferred_element_type=jnp.float32
    )
    summed = extended(partial_value, (("fft", 0),), atom_dev)
    projections_own = (
        summed[:atom_dev] + summed[2 * atom_dev : 3 * atom_dev] + summed[4 * atom_dev :]
    )
    energy_own = jnp.einsum(
        "ij,abj->abi", coupled, projections_own, precision=lax.Precision.HIGHEST
    )
    energy = extended(energy_own, (("fft", 0),), atom_dev)
    spread = jnp.einsum(
        "ajsk,abj->bask", nearby.astype(jnp.float32), energy, precision=lax.Precision.HIGHEST
    )
    spread = spread * inside[None, :, :, None].astype(jnp.float32)
    accumulated = (
        jnp.zeros((2, slab_planes * plane_blocks, block_cells), jnp.float32)
        .at[:, local_index]
        .add(spread)
    )
    nonlocal_term = accumulated.reshape(2, slab_planes, size_y, size_z)
    total_field = (
        potential.astype(jnp.float32)[None] * wave_field.astype(jnp.float32) + nonlocal_term
    ).astype(jnp.bfloat16)
    forward_z = dft_table(size_z, -1.0)
    forward_y = dft_table(size_y, -1.0)
    forward_x = dft_table(size_x, -1.0)
    back_z = jnp.einsum(
        "abzk,bxyk->axyz", forward_z, total_field, preferred_element_type=jnp.float32
    ).astype(jnp.bfloat16)
    back_y = jnp.einsum(
        "abyk,bxkz->axyz", forward_y, back_z, preferred_element_type=jnp.float32
    ).astype(jnp.bfloat16)
    transformed = jnp.einsum(
        "abxk,bkyz->axyz",
        forward_x,
        lax.all_to_all(back_y, "fft", split_axis=2, concat_axis=1, tiled=True),
        preferred_element_type=jnp.float32,
    )
    index_x = jnp.arange(size_x, dtype=jnp.int32)
    index_y = slab_index * columns + jnp.arange(columns, dtype=jnp.int32)
    index_z = jnp.arange(size_z, dtype=jnp.int32)
    kinetic = (
        wave_squares(index_x, size_x)[:, None, None]
        + wave_squares(index_y, size_y)[None, :, None]
        + wave_squares(index_z, size_z)[None, None, :]
    )
    applied = (transformed + kinetic[None] * coeffs.astype(jnp.float32)).astype(jnp.bfloat16)
    return (applied[None], density, projections_own[None])


def real_blocks(length, sign):
    index = np.arange(length)
    angles = 2.0 * np.pi / length * (index[:, None] * index[None, :] % length)
    cosine = np.cos(angles) / np.sqrt(length)
    sine = sign * np.sin(angles) / np.sqrt(length)
    blocks = np.empty((2, length, 2, length))
    blocks[0, :, 0, :] = cosine
    blocks[1, :, 1, :] = cosine
    blocks[0, :, 1, :] = -sine
    blocks[1, :, 0, :] = sine
    return blocks


def chunk_planes(slab_planes):
    low, high = list(range(EDGE)), list(range(slab_planes - EDGE, slab_planes))
    return [low + high, list(range(EDGE, slab_planes - EDGE))]


def params(steps):
    return pltpu.CompilerParams(
        dimension_semantics=("arbitrary",) * steps, vmem_limit_bytes=VMEM_BYTES
    )


def cost(products, values):
    return pl.CostEstimate(flops=4 * products, bytes_accessed=4 * values, transcendentals=0)


def whole(shape):
    return pl.BlockSpec(shape, lambda i: (0,) * len(shape))


SMEM_SPEC = pl.BlockSpec(memory_space=pltpu.SMEM)


def paired(refs, slab):
    return [(lax.bitwise_xor(slab, jnp.int32(k)), ref) for k, ref in enumerate(refs)]


def shifted(refs, slab):
    return [(lax.rem(slab + k, len(refs)), ref) for k, ref in enumerate(refs)]


def first_x_kernel(slab, table_ref, coeffs_ref, *refs, pieces, natural):
    scratch = 3 if natural else 2
    outs = paired(refs[:-scratch], slab[0])
    turned, wide, *tall = refs[-scratch:]
    parts, size_x, columns, lanes = coeffs_ref.shape
    rows = parts * size_x
    height = table_ref.shape[0] // pieces

    for k, (device, _) in enumerate(outs):
        start = pl.multiple_of(device * height, 16)
        turned[k * height : (k + 1) * height, :] = table_ref[pl.ds(start, height), :]

    pitch = columns + 1

    def widen(k, carry):
        for part in range(parts):
            wide[pl.ds((part * size_x + k) * pitch, columns), :] = coeffs_ref[part, k].astype(
                jnp.float32
            )
        return carry

    lax.fori_loop(0, size_x, widen, 0, unroll=8)

    def some_columns(g, carry):
        loaded = [
            wide[pl.ds(COLUMNS * g + h, rows, stride=pitch), :].astype(jnp.bfloat16)
            for h in range(COLUMNS)
        ]
        for first in range(0, COLUMNS, FOUR):
            result = jnp.dot(
                turned[...],
                jnp.concatenate(loaded[first : first + FOUR], axis=1),
                preferred_element_type=jnp.float32,
            )
            for h in range(FOUR):
                column = COLUMNS * g + first + h
                piece = result[:, h * lanes : (h + 1) * lanes]
                if natural:
                    place = (first + h) % 2 * columns + COLUMNS // 2 * g + (first + h) // 2
                    planes = height // 2
                    for k in range(pieces):
                        for part in range(2):
                            start = k * height * columns + part * (columns // 2) + place
                            row = k * height + part * planes
                            tall[0][pl.ds(start, planes, stride=2 * columns), :] = piece[
                                row : row + planes
                            ]
                else:
                    piece = piece.astype(jnp.bfloat16)
                    for k, (_, out) in enumerate(outs):
                        out[column] = piece[k * height : (k + 1) * height]
        return carry

    lax.fori_loop(0, columns // COLUMNS, some_columns, 0)
    if natural:
        for k, (_, out) in enumerate(outs):
            values = tall[0][k * height * columns : (k + 1) * height * columns, :]
            out[...] = values.astype(jnp.bfloat16).reshape(out.shape)


def first_x(slab, table, coeffs, planes, pieces, natural):
    _, size_x, columns, size_z = coeffs.shape
    lanes = size_z // 2
    shape = (planes, 2 * columns) if natural else (columns, 2 * planes)
    scratch = [
        pltpu.VMEM(table.shape, jnp.bfloat16),
        pltpu.VMEM((2 * size_x * (columns + 1), lanes), jnp.float32),
    ]
    if natural:
        scratch.append(pltpu.VMEM((2 * pieces * planes * columns, lanes), jnp.float32))
    out_specs = [pl.BlockSpec((*shape, lanes), lambda i: (0, 0, i))] * pieces
    out_shape = [jax.ShapeDtypeStruct((*shape, size_z), jnp.bfloat16)] * pieces
    return pl.pallas_call(
        functools.partial(first_x_kernel, pieces=pieces, natural=natural),
        grid=(2,),
        in_specs=[
            SMEM_SPEC,
            whole(table.shape),
            pl.BlockSpec((2, size_x, columns, lanes), lambda i: (0, 0, 0, i)),
        ],
        out_specs=out_specs,
        out_shape=out_shape,
        scratch_shapes=scratch,
        compiler_params=params(1),
        cost_estimate=cost(2 * size_x * pieces * planes * columns * size_z, 2 * size_x * columns * size_z),
        name="first_x",
    )(slab, table, coeffs)


def ones_at(codes, count, axis):
    shape = (codes.shape[0], count) if axis == 1 else (count, codes.shape[1])
    places = lax.broadcasted_iota(jnp.int32, shape, axis)
    return jnp.where(codes == places, 1.0, 0.0).astype(jnp.bfloat16)


def field_kernel(slab, weights, table_y, table_z, codes, sides, *refs, pieces, count, natural):
    bufs = paired(refs[:count], slab[0])
    wave, density, *rows_out, gathered, wide = refs[count:]
    _, near, size_y, size_z = wave.shape
    columns = size_y // pieces
    groups, entries, _ = codes.shape
    lanes = 128
    halves = size_z // lanes
    i, last = pl.program_id(0), pl.num_programs(0) - 1
    planes = near * (last + 1)

    @pl.when(i == 0)
    def _():
        gathered[...] = jnp.zeros_like(gathered)

    loaded = []
    if natural:
        for source, buf in bufs:
            wide[source] = buf[...]
        for h in range(near):
            loaded.append(
                [wide[:, h, s * columns : (s + 1) * columns].reshape(size_y, size_z) for s in (0, 1)]
            )
    else:
        rows = bufs[0][1].shape[1]
        pitch = rows + 1

        @pl.when(i == 0)
        def _():
            for source, buf in bufs:

                def widen(column, carry):
                    values = buf[column].astype(jnp.float32)
                    for q in range(halves):
                        wide[q, pl.ds((source * columns + column) * pitch, rows), :] = values[
                            :, q * lanes : (q + 1) * lanes
                        ]
                    return carry

                lax.fori_loop(0, columns, widen, 0, unroll=8)

        def strided(start):
            return jnp.concatenate(
                [
                    wide[q, pl.ds(start, size_y // 2, stride=2 * pitch), :]
                    for q in range(halves)
                ],
                axis=1,
            ).astype(jnp.bfloat16)

        for h in range(near):
            plane = i * near + h
            loaded.append(
                [
                    jnp.concatenate(
                        [strided(s * pitch + part * planes + plane) for part in range(2)], axis=0
                    )
                    for s in (0, 1)
                ]
            )
    even, odd = (
        jnp.dot(
            table_y[s],
            jnp.concatenate([pair[s] for pair in loaded], axis=1),
            preferred_element_type=jnp.float32,
        )
        for s in (0, 1)
    )
    low, high = (even + odd).astype(jnp.bfloat16), (even - odd).astype(jnp.bfloat16)
    middle = size_y // 2
    turned = []
    for h in range(near):
        span = slice(h * size_z, (h + 1) * size_z)
        both = [
            jnp.concatenate(
                [values[part * middle : (part + 1) * middle, span] for values in (low, high)], axis=0
            )
            for part in range(2)
        ]
        turned.append(jnp.concatenate(both, axis=1))
    result = jnp.dot(
        jnp.concatenate(turned, axis=0), table_z[...], preferred_element_type=jnp.float32
    ).astype(jnp.bfloat16)
    for h in range(near):
        total = jnp.zeros((size_y, size_z), jnp.float32)
        for part in range(2):
            values = result[h * size_y : (h + 1) * size_y, part * size_z : (part + 1) * size_z]
            wave[part, h] = values
            values = values.astype(jnp.float32)
            total += weights[0, part] * values * values
        density[h] = total.astype(jnp.bfloat16)

    used = [0] if groups == 1 else [0, 1 + (2 * i > last).astype(jnp.int32)]
    for group in used:
        places = ones_at(codes[group] - i * near * size_y, near * size_y, 1)
        gathered[group] += jnp.dot(places, result, preferred_element_type=jnp.float32)

    @pl.when(i == last)
    def _():
        for group in range(groups):
            for part in range(2):
                total = jnp.zeros((entries, lanes), jnp.float32)
                for q in range(halves):
                    start = part * size_z + q * lanes
                    total += jnp.where(
                        sides[group] == q, gathered[group, :, start : start + lanes], 0.0
                    )
                rows_out[group][part] = total.astype(jnp.bfloat16)


def make_field(slab, weights, bufs, table_y, table_z, codes, sides, planes, pieces, natural):
    size_z = bufs[0].shape[-1]
    size_y = table_y.shape[1]
    columns = size_y // pieces
    groups, entries, _ = codes.shape
    if natural:
        buf_spec = pl.BlockSpec((PLANES, 2 * columns, size_z), lambda i: (i, 0, 0))
        wide = pltpu.VMEM((pieces, PLANES, 2 * columns, size_z), jnp.bfloat16)
    else:
        buf_spec = whole(bufs[0].shape)
        wide = pltpu.VMEM((size_z // 128, (2 * planes + 1) * size_y, 128), jnp.float32)
    return pl.pallas_call(
        functools.partial(field_kernel, pieces=pieces, count=len(bufs), natural=natural),
        grid=(planes // PLANES,),
        in_specs=[SMEM_SPEC, SMEM_SPEC]
        + [whole(a.shape) for a in (table_y, table_z, codes, sides)]
        + [buf_spec] * len(bufs),
        out_specs=[
            pl.BlockSpec((2, PLANES, size_y, size_z), lambda i: (0, i, 0, 0)),
            pl.BlockSpec((PLANES, size_y, size_z), lambda i: (i, 0, 0)),
        ]
        + [whole((2, entries, 128))] * groups,
        out_shape=[
            jax.ShapeDtypeStruct((2, planes, size_y, size_z), jnp.bfloat16),
            jax.ShapeDtypeStruct((planes, size_y, size_z), jnp.bfloat16),
        ]
        + [jax.ShapeDtypeStruct((2, entries, 128), jnp.bfloat16)] * groups,
        scratch_shapes=[pltpu.VMEM((groups, entries, 2 * size_z), jnp.float32), wide],
        compiler_params=params(1),
        cost_estimate=cost(
            2 * planes * size_y * size_z * (size_y + size_z), 2 * planes * size_y * size_z
        ),
        name="make_field",
    )(slab, weights, table_y, table_z, codes, sides, *bufs)


def nonlocal_kernel(coupled, projectors, *refs):
    parts, (projections, spread) = refs[:-2], refs[-2:]
    atoms, nproj, blocks, cells = projectors.shape
    for atom in range(atoms):
        tables = [projectors[atom, j].astype(jnp.float32) for j in range(nproj)]
        place = pl.ds(atom * blocks, blocks)
        for part in range(2):
            rows = sum(p[part, place].astype(jnp.float32) for p in parts)
            tile = jnp.concatenate(
                [jnp.sum(t * rows, axis=0, keepdims=True) for t in tables], axis=0
            )
            mixed = jnp.zeros_like(tile)
            for j in range(nproj):
                mixed += coupled[j] * tile[j : j + 1]
            projections[atom, part] = jnp.broadcast_to(
                jnp.sum(tile, -1, keepdims=True), tile.shape
            )
            energy = jnp.broadcast_to(jnp.sum(mixed, -1, keepdims=True), tile.shape)
            spread[part, place] = sum(
                t * energy[j : j + 1] for j, t in enumerate(tables)
            ).astype(jnp.bfloat16)


def make_nonlocal(coupled, projectors, parts):
    atoms, nproj, _, cells = projectors.shape
    return pl.pallas_call(
        nonlocal_kernel,
        out_shape=[
            jax.ShapeDtypeStruct((atoms, 2, nproj, cells), jnp.float32),
            jax.ShapeDtypeStruct(parts[0].shape, jnp.bfloat16),
        ],
        name="make_nonlocal",
    )(coupled, projectors, *parts)


def back_kernel(slab, wave, potential, table_z, table_y, codes, sides, *refs, pieces, natural):
    groups, _, entries = codes.shape
    sources, outs = refs[:groups], refs[groups:-2]
    spread, tall = refs[-2:]
    outs = shifted(outs, slab[0])
    near, size_y, size_z = potential.shape
    lanes = 128
    halves = size_z // lanes
    i, last = pl.program_id(0), pl.num_programs(0) - 1
    planes = near * (last + 1)

    @pl.when(i == 0)
    def _():
        for group, source in enumerate(sources):
            for part in range(2):
                for q in range(halves):
                    start = part * size_z + q * lanes
                    spread[group, :, start : start + lanes] = jnp.where(
                        sides[group] == q, source[part].astype(jnp.float32), 0.0
                    ).astype(jnp.bfloat16)

    used = [0] if groups == 1 else [0, 1 + (2 * i > last).astype(jnp.int32)]
    extra = jnp.zeros((near * size_y, 2 * size_z), jnp.float32)
    for group in used:
        places = ones_at(codes[group] - i * near * size_y, near * size_y, 0)
        extra += jnp.dot(places, spread[group], preferred_element_type=jnp.float32)
    fields = []
    for h in range(near):
        local = potential[h].astype(jnp.float32)
        both = [
            local * wave[part, h].astype(jnp.float32)
            + extra[h * size_y : (h + 1) * size_y, part * size_z : (part + 1) * size_z]
            for part in range(2)
        ]
        fields.append(jnp.concatenate(both, axis=1).astype(jnp.bfloat16))
    back_z = jnp.dot(
        jnp.concatenate(fields, axis=0), table_z[...], preferred_element_type=jnp.float32
    )
    middle = size_y // 2
    folded = [[], []]
    for h in range(near):
        low = back_z[h * size_y : h * size_y + middle]
        high = back_z[h * size_y + middle : (h + 1) * size_y]
        for kept, values in zip(folded, (low + high, low - high)):
            values = values.astype(jnp.bfloat16)
            kept.append(jnp.concatenate([values[:, :size_z], values[:, size_z:]], axis=0))
    columns = size_y // pieces
    for s, kept in enumerate(folded):
        back_y = jnp.dot(
            table_y[s], jnp.concatenate(kept, axis=1), preferred_element_type=jnp.float32
        )
        if natural:
            back_y = back_y.astype(jnp.bfloat16)
            for h in range(near):
                tall[:, h, s * columns : (s + 1) * columns] = back_y[
                    :, h * size_z : (h + 1) * size_z
                ].reshape(pieces, columns, size_z)
            continue
        pitch = outs[0][1].shape[1] + 1
        for h in range(near):
            for part in range(2):
                for q in range(halves):
                    start = s * pitch + part * planes + i * near + h
                    lane = h * size_z + q * lanes
                    tall[q, pl.ds(start, middle, stride=2 * pitch), :] = back_y[
                        part * middle : (part + 1) * middle, lane : lane + lanes
                    ]

    if natural:
        for target, out in outs:
            out[...] = tall[target]
        return
    rows = outs[0][1].shape[1]

    @pl.when(i == last)
    def _():
        for target, out in outs:

            def narrow(column, carry):
                start = (target * columns + column) * pitch
                values = [tall[q, pl.ds(start, rows), :] for q in range(halves)]
                out[column] = jnp.concatenate(values, axis=1).astype(jnp.bfloat16)
                return carry

            lax.fori_loop(0, columns, narrow, 0, unroll=8)


def go_back(slab, wave, potential, table_z, table_y, codes, sides, sources, place, pieces, natural):
    _, planes, size_y, size_z = wave.shape
    columns = size_y // pieces
    groups, _, entries = codes.shape
    scratch = [pltpu.VMEM((groups, entries, 2 * size_z), jnp.bfloat16)]
    if natural:
        shape = (planes, 2 * columns, size_z)
        out_specs = [pl.BlockSpec((PLANES, 2 * columns, size_z), lambda i: (i, 0, 0))] * pieces
        scratch.append(pltpu.VMEM((pieces, PLANES, 2 * columns, size_z), jnp.bfloat16))
    else:
        shape = (columns, 2 * planes, size_z)
        out_specs = [whole(shape)] * pieces
        scratch.append(pltpu.VMEM((size_z // 128, (2 * planes + 1) * size_y, 128), jnp.float32))
    return pl.pallas_call(
        functools.partial(back_kernel, pieces=pieces, natural=natural),
        grid=(planes // PLANES,),
        in_specs=[
            SMEM_SPEC,
            pl.BlockSpec((2, PLANES, size_y, size_z), lambda i: (0, i, 0, 0)),
            pl.BlockSpec((PLANES, size_y, size_z), lambda i: (place(i), 0, 0)),
        ]
        + [whole(a.shape) for a in (table_z, table_y, codes, sides, *sources)],
        out_specs=out_specs,
        out_shape=[jax.ShapeDtypeStruct(shape, jnp.bfloat16)] * pieces,
        scratch_shapes=scratch,
        compiler_params=params(1),
        cost_estimate=cost(
            2 * planes * size_y * size_z * (size_y + size_z), 2 * planes * size_y * size_z
        ),
        name="go_back",
    )(slab, wave, potential, table_z, table_y, codes, sides, *sources)


def last_x_kernel(frequency_x, frequency_yz, table, coeffs, *refs):
    bufs, (out, tall) = refs[:-2], refs[-2:]
    parts, size_x, columns, lanes = coeffs.shape
    pitch = columns + 1

    def some_columns(g, carry):
        loaded = []
        for h in range(COLUMNS):
            loaded.append(jnp.concatenate([buf[COLUMNS * g + h] for buf in bufs], axis=0))
        for first in range(0, COLUMNS, FOUR):
            result = jnp.dot(
                table[...],
                jnp.concatenate(loaded[first : first + FOUR], axis=1),
                preferred_element_type=jnp.float32,
            )
            for h in range(FOUR):
                tall[pl.ds(COLUMNS * g + first + h, parts * size_x, stride=pitch), :] = result[
                    :, h * lanes : (h + 1) * lanes
                ]
        return carry

    lax.fori_loop(0, columns // COLUMNS, some_columns, 0)

    def finish(k, carry):
        kinetic = frequency_x[k] + frequency_yz[...]
        for part in range(parts):
            out[part, k] = (
                tall[pl.ds((part * size_x + k) * pitch, columns), :] + kinetic * coeffs[part, k].astype(jnp.float32)
            ).astype(jnp.bfloat16)
        return carry

    lax.fori_loop(0, size_x, finish, 0, unroll=8)


def last_x(frequency_x, frequency_yz, table, coeffs, bufs):
    _, size_x, columns, size_z = coeffs.shape
    lanes = size_z // 2
    spec = pl.BlockSpec((2, size_x, columns, lanes), lambda i: (0, 0, 0, i))
    return pl.pallas_call(
        last_x_kernel,
        grid=(2,),
        in_specs=[
            SMEM_SPEC,
            pl.BlockSpec((columns, lanes), lambda i: (0, i)),
            whole(table.shape),
            spec,
        ]
        + [pl.BlockSpec((*b.shape[:2], lanes), lambda i: (0, 0, i)) for b in bufs],
        out_specs=spec,
        out_shape=jax.ShapeDtypeStruct(coeffs.shape, jnp.bfloat16),
        scratch_shapes=[pltpu.VMEM((2 * size_x * (columns + 1), lanes), jnp.float32)],
        compiler_params=params(1),
        cost_estimate=cost(2 * size_x * size_x * columns * size_z, 3 * size_x * columns * size_z),
        name="last_x",
    )(frequency_x, frequency_yz, table, coeffs, *bufs)


def per_device_chunked(wave_coeffs, occupation, potential, projectors, coupling, sphere_blocks):
    pieces = lax.axis_size("fft")
    bands = lax.axis_size("band")
    slab = lax.axis_index("fft")
    coeffs = wave_coeffs[0]
    _, size_x, columns, size_z = coeffs.shape
    slab_planes, size_y, _ = potential.shape
    atom_dev, nproj, blocks, cells = projectors.shape
    zblocks = size_z // cells
    outer, inner = chunk_planes(slab_planes)
    up = [(i, (i + 1) % pieces) for i in range(pieces)]
    down = [(j, i) for i, j in up]

    inverse_x, forward_x = (real_blocks(size_x, s) for s in (1.0, -1.0))
    inverse_y, forward_y = (real_blocks(size_y, s) for s in (1.0, -1.0))
    inverse_z, forward_z = (real_blocks(size_z, s) for s in (1.0, -1.0))
    place_outer, place_inner = (
        np.arange(pieces)[:, None] * slab_planes + np.array(chunk)[None, :]
        for chunk in (outer, inner)
    )
    table_x_outer = np.stack([inverse_x[r][place_outer] for r in range(2)], 1)
    table_x_inner = np.stack([inverse_x[r][place_inner] for r in range(2)], 1)
    tables_back_x = [
        np.stack([forward_x[:, :, r][:, :, place] for r in range(2)], 3).reshape(
            2 * size_x, pieces, -1
        )
        for place in (place_outer, place_inner)
    ]
    middle = size_y // 2
    down_y = [inverse_y[:, :middle, :, s::2] for s in (0, 1)]
    back_y = [forward_y[:, s::2, :, :middle] for s in (0, 1)]
    split = (pieces, columns // 2)
    tables = [
        table_x_outer.reshape(-1, 2 * size_x),
        table_x_inner.reshape(-1, 2 * size_x),
        np.stack([t.reshape(size_y, -1) for t in down_y]),
        np.stack(
            [t.reshape(2, middle, 2, *split).swapaxes(2, 3).reshape(size_y, -1) for t in down_y]
        ),
        inverse_z.transpose(2, 3, 0, 1).reshape(2 * size_z, -1),
        forward_z.transpose(2, 3, 0, 1).reshape(2 * size_z, -1),
        np.stack([t.reshape(size_y, -1) for t in back_y]),
        np.stack([t.reshape(2, *split, -1).swapaxes(0, 1).reshape(size_y, -1) for t in back_y]),
        np.stack(
            [
                np.concatenate(
                    [t[:, (d - np.arange(pieces)) % pieces].reshape(2 * size_x, -1) for t in tables_back_x],
                    axis=1,
                )
                for d in range(pieces)
            ]
        ),
    ]
    (
        table_x_outer, table_x_inner, table_y_outer, table_y_inner, table_z,
        table_back_z, table_back_y_outer, table_back_y_inner, tables_back_x,
    ) = (jnp.asarray(t.astype(jnp.bfloat16)) for t in tables)

    table_back_x = lax.dynamic_index_in_dim(tables_back_x, slab, 0, keepdims=False)

    where = slab.reshape(1)
    section_outer = first_x(where, table_x_outer, coeffs, len(outer), pieces, False)
    section_outer, table_x_inner, sphere_blocks = lax.optimization_barrier(
        (section_outer, table_x_inner, sphere_blocks)
    )
    section_inner = first_x(where, table_x_inner, coeffs, len(inner), pieces, True)

    entries = atom_dev * blocks

    def codes_of(chunk, shift):
        owner = (slab + shift + pieces) % pieces
        numbers = lax.dynamic_slice_in_dim(sphere_blocks, owner * atom_dev, atom_dev, 0)
        plane = numbers // (size_y * zblocks) - slab * slab_planes
        rest = numbers % (size_y * zblocks)
        if chunk is outer:
            inside = ((plane >= 0) & (plane < EDGE)) | (
                (plane >= slab_planes - EDGE) & (plane < slab_planes)
            )
            plane = jnp.where(plane < EDGE, plane, plane - len(inner))
        else:
            inside = (plane >= EDGE) & (plane < slab_planes - EDGE)
            plane = plane - EDGE
        code = jnp.where(inside, plane * size_y + rest // zblocks, -1)
        return code.reshape(entries), (rest % zblocks).reshape(entries)

    found = [codes_of(outer, shift) for shift in (0, -1, 1)]
    codes_outer, sides_outer = (jnp.stack(values) for values in zip(*found))
    codes_inner, sides_inner = (values[None] for values in codes_of(inner, 0))
    sides_outer, sides_inner = sides_outer[:, :, None], sides_inner[:, :, None]
    rows_codes = [codes_outer[:, :, None], codes_inner[:, :, None]]
    lane_codes = [codes_outer[:, None, :], codes_inner[:, None, :]]
    strength = 3.0 * math.sqrt(cells * blocks) / nproj
    coupled = (coupling + coupling.T) * (0.5 * strength)
    coupled = jnp.broadcast_to(coupled.T[:, :, None], (nproj, nproj, cells))
    section_inner, rows_codes, lane_codes, sides_outer, sides_inner, coupled = (
        lax.optimization_barrier(
            (section_inner, rows_codes, lane_codes, sides_outer, sides_inner, coupled)
        )
    )

    half = pieces // 2
    near, far = list(range(1, half)), list(range(half, pieces))

    def send(block, k, *awaited):
        for row, m in awaited:
            block, row[m] = lax.optimization_barrier((block, row[m]))
        return lax.ppermute(block, "fft", [(j, j ^ k) for j in range(pieces)])

    received_outer, received_inner = (
        [section[0]] + [None] * (pieces - 1) for section in (section_outer, section_inner)
    )
    for partners in (near, far):
        queue = [(section_outer, received_outer, k) for k in partners]
        queue += [(section_inner, received_inner, k) for k in partners]
        for place, (section, received, k) in enumerate(queue):
            awaited = [queue[place - 2][1:]] if place >= 2 else []
            received[k] = send(section[k], k, *awaited)
    wave_outer, density_outer, rows_outer, to_previous, to_following = make_field(
        where, occupation, received_outer, table_y_outer, table_z, rows_codes[0],
        sides_outer, len(outer), pieces, False,
    )
    from_following = lax.ppermute(to_previous, "fft", down)
    from_previous = lax.ppermute(to_following, "fft", up)
    density_outer = lax.psum(density_outer, "band")
    wave_inner, density_inner, rows_inner = make_field(
        where, occupation, received_inner, table_y_inner, table_z, rows_codes[1],
        sides_inner, len(inner), pieces, True,
    )
    projected, spread = make_nonlocal(
        coupled, projectors, [rows_outer, rows_inner, from_following, from_previous]
    )
    spread_previous = lax.ppermute(spread, "fft", up)
    spread_following = lax.ppermute(spread, "fft", down)
    edge_steps = EDGE // PLANES
    inner_steps = len(inner) // PLANES
    back_inner = go_back(
        where, wave_inner, potential, table_back_z, table_back_y_inner, lane_codes[1],
        sides_inner, [spread], lambda i: i + edge_steps, pieces, True,
    )
    def permute_all(values):
        received = [values[0]]
        for k in range(1, pieces):
            pairs = [(j, (j + k) % pieces) for j in range(pieces)]
            received.append(lax.ppermute(values[k], "fft", pairs))
        return received

    back_inner = permute_all(back_inner)
    back_outer = go_back(
        where, wave_outer, potential, table_back_z, table_back_y_outer, lane_codes[0],
        sides_outer, [spread, spread_previous, spread_following],
        lambda i: jnp.where(i < edge_steps, i, i + inner_steps), pieces, False,
    )
    density_inner, density_outer = lax.optimization_barrier((density_inner, density_outer))
    density_inner = lax.psum(density_inner, "band")
    back_outer, density_outer = lax.optimization_barrier((back_outer, density_outer))
    back_outer = permute_all(back_outer)
    back_inner = [
        b.reshape(len(inner), 2, 2, columns // 2, size_z)
        .transpose(3, 1, 2, 0, 4)
        .reshape(columns, -1, size_z)
        for b in back_inner
    ]
    density = jnp.concatenate([density_outer[:EDGE], density_inner, density_outer[EDGE:]], axis=0)

    index_x = np.arange(size_x)
    frequency_x = jnp.asarray(
        (np.where(2 * index_x < size_x, index_x, index_x - size_x) / size_x) ** 2, jnp.float32
    )
    index_y = slab * columns + jnp.arange(columns, dtype=jnp.int32)
    index_z = jnp.arange(size_z, dtype=jnp.int32)
    frequency_yz = wave_squares(index_y, size_y)[:, None] + wave_squares(index_z, size_z)[None, :]
    coeffs, density, back_inner = lax.optimization_barrier((coeffs, density, back_inner))
    applied = last_x(frequency_x, frequency_yz, table_back_x, coeffs, back_outer + back_inner)
    return (applied[None], density, projected[None, :, :, :, 0])


def per_device(wave_coeffs, occupation, potential, projectors, coupling, sphere_blocks):
    pieces, bands = lax.axis_size("fft"), lax.axis_size("band")
    size_z = wave_coeffs.shape[4]
    columns = wave_coeffs.shape[3]
    slab_planes = potential.shape[0]
    chunked = (
        pieces >= 4
        and pieces & (pieces - 1) == 0
        and slab_planes % EDGE == 0
        and slab_planes >= 3 * EDGE
        and EDGE >= HALO
        and columns % 8 == 0
        and size_z % 256 == 0
        and projectors.shape[0] % bands == 0
        and projectors.shape[3] == 128
        and projectors.shape[1] == 8
    )
    chosen = per_device_chunked if chunked else per_device_plain
    return chosen(wave_coeffs, occupation, potential, projectors, coupling, sphere_blocks)


def solution(mesh):
    placed = (
        P("band", None, None, "fft", None),
        P("band", None),
        P("fft", None, None),
        P("fft", None, None, None),
        P(),
        P(),
    )
    return jax.shard_map(
        per_device,
        mesh=mesh,
        in_specs=placed,
        out_specs=(
            P("band", None, None, "fft", None),
            P("fft", None, None),
            P("band", "fft", None, None),
        ),
        check_vma=False,
    )
```

```python
import functools
import math

import jax
import jax.numpy as jnp
import numpy as np
from jax import lax
from jax.experimental import pallas as pl
from jax.experimental.pallas import tpu as pltpu
from jax.sharding import PartitionSpec as P

HALO = 6
EDGE = 8
PLANES = 4
COLUMNS = 8
FOUR = 4
VMEM_BYTES = 56 * 1024 * 1024


def extended(shard, sides, width):
    for axis, dim in sides:
        count, length = (lax.axis_size(axis), shard.shape[dim])
        up = [(i, (i + 1) % count) for i in range(count)]
        down = [(j, i) for i, j in up]
        last = lax.slice_in_dim(shard, length - width, length, axis=dim)
        first = lax.slice_in_dim(shard, 0, width, axis=dim)
        before = lax.ppermute(last, axis, up)
        after = lax.ppermute(first, axis, down)
        shard = jnp.concatenate([before, shard, after], axis=dim)
    return shard


def dft_table(length, sign_value):
    indices = jnp.arange(length, dtype=jnp.int32)
    phases = indices[:, None] * indices[None, :] % length
    angles = 2.0 * math.pi / length * phases.astype(jnp.float32)
    factor = 1.0 / math.sqrt(length)
    cosine = jnp.cos(angles) * factor
    sine_part = jnp.sin(angles) * (sign_value * factor)
    upper_rows = jnp.stack([cosine, -sine_part])
    bottom = jnp.stack([sine_part, cosine])
    return jnp.stack([upper_rows, bottom]).astype(jnp.bfloat16)


def wave_squares(indices, length):
    frequency = (
        jnp.where(2 * indices < length, indices, indices - length).astype(jnp.float32) / length
    )
    return frequency * frequency


def per_device_plain(wave_coeffs, occupation, potential, projectors, coupling, sphere_blocks):
    pieces = lax.axis_size("fft")
    slab_index = lax.axis_index("fft")
    coeffs = wave_coeffs[0]
    size_x = coeffs.shape[1]
    columns = coeffs.shape[2]
    size_z = coeffs.shape[3]
    slab_planes = potential.shape[0]
    size_y = potential.shape[1]
    atom_dev = projectors.shape[0]
    nproj_count = projectors.shape[1]
    block_cells = projectors.shape[3]
    zblocks = size_z // block_cells
    plane_blocks = size_y * zblocks
    total_atoms = atom_dev * pieces
    table_x = dft_table(size_x, 1.0).transpose(0, 2, 1, 3).reshape(2 * size_x, 2 * size_x)
    inverse_y = dft_table(size_y, 1.0)
    inverse_z = dft_table(size_z, 1.0)
    flattened = coeffs.reshape(2 * size_x, columns * size_z)
    along_x = jnp.dot(table_x, flattened, preferred_element_type=jnp.float32)
    along_x = along_x.reshape(2, size_x, columns, size_z).astype(jnp.bfloat16)
    along_y = jnp.einsum(
        "abyk,bxkz->axyz",
        inverse_y,
        lax.all_to_all(along_x, "fft", split_axis=1, concat_axis=2, tiled=True),
        preferred_element_type=jnp.float32,
    ).astype(jnp.bfloat16)
    wave_field = jnp.einsum(
        "abzk,bxyk->axyz", inverse_z, along_y, preferred_element_type=jnp.float32
    ).astype(jnp.bfloat16)
    weights = occupation[0]
    real_part = wave_field[0].astype(jnp.float32)
    imag_part = wave_field[1].astype(jnp.float32)
    partial_density = weights[0] * real_part * real_part + weights[1] * imag_part * imag_part
    density = lax.psum(partial_density.astype(jnp.bfloat16), "band")
    strength = 3.0 * math.sqrt(block_cells * projectors.shape[2]) / nproj_count
    coupled = (coupling + coupling.T) * (0.5 * strength)
    nearby = extended(projectors, (("fft", 0),), atom_dev)
    atom_rows = (
        slab_index * atom_dev - atom_dev + jnp.arange(3 * atom_dev, dtype=jnp.int32) + total_atoms
    ) % total_atoms
    near_blocks = sphere_blocks[atom_rows]
    plane_index = near_blocks // plane_blocks
    inside = plane_index // slab_planes == slab_index
    local_index = jnp.where(
        inside,
        (plane_index - slab_index * slab_planes) * plane_blocks + near_blocks % plane_blocks,
        0,
    )
    blocks_own = wave_field.reshape(2, slab_planes * plane_blocks, block_cells)
    gathered = blocks_own[:, local_index] * inside[None, :, :, None].astype(jnp.bfloat16)
    partial_value = jnp.einsum(
        "ajsk,bask->abj", nearby, gathered, preferred_element_type=jnp.float32
    )
    summed = extended(partial_value, (("fft", 0),), atom_dev)
    projections_own = (
        summed[:atom_dev] + summed[2 * atom_dev : 3 * atom_dev] + summed[4 * atom_dev :]
    )
    energy_own = jnp.einsum(
        "ij,abj->abi", coupled, projections_own, precision=lax.Precision.HIGHEST
    )
    energy = extended(energy_own, (("fft", 0),), atom_dev)
    spread = jnp.einsum(
        "ajsk,abj->bask", nearby.astype(jnp.float32), energy, precision=lax.Precision.HIGHEST
    )
    spread = spread * inside[None, :, :, None].astype(jnp.float32)
    accumulated = (
        jnp.zeros((2, slab_planes * plane_blocks, block_cells), jnp.float32)
        .at[:, local_index]
        .add(spread)
    )
    nonlocal_term = accumulated.reshape(2, slab_planes, size_y, size_z)
    total_field = (
        potential.astype(jnp.float32)[None] * wave_field.astype(jnp.float32) + nonlocal_term
    ).astype(jnp.bfloat16)
    forward_z = dft_table(size_z, -1.0)
    forward_y = dft_table(size_y, -1.0)
    forward_x = dft_table(size_x, -1.0)
    back_z = jnp.einsum(
        "abzk,bxyk->axyz", forward_z, total_field, preferred_element_type=jnp.float32
    ).astype(jnp.bfloat16)
    back_y = jnp.einsum(
        "abyk,bxkz->axyz", forward_y, back_z, preferred_element_type=jnp.float32
    ).astype(jnp.bfloat16)
    transformed = jnp.einsum(
        "abxk,bkyz->axyz",
        forward_x,
        lax.all_to_all(back_y, "fft", split_axis=2, concat_axis=1, tiled=True),
        preferred_element_type=jnp.float32,
    )
    index_x = jnp.arange(size_x, dtype=jnp.int32)
    index_y = slab_index * columns + jnp.arange(columns, dtype=jnp.int32)
    index_z = jnp.arange(size_z, dtype=jnp.int32)
    kinetic = (
        wave_squares(index_x, size_x)[:, None, None]
        + wave_squares(index_y, size_y)[None, :, None]
        + wave_squares(index_z, size_z)[None, None, :]
    )
    applied = (transformed + kinetic[None] * coeffs.astype(jnp.float32)).astype(jnp.bfloat16)
    return (applied[None], density, projections_own[None])


def real_blocks(length, sign):
    index = np.arange(length)
    angles = 2.0 * np.pi / length * (index[:, None] * index[None, :] % length)
    cosine = np.cos(angles) / np.sqrt(length)
    sine = sign * np.sin(angles) / np.sqrt(length)
    blocks = np.empty((2, length, 2, length))
    blocks[0, :, 0, :] = cosine
    blocks[1, :, 1, :] = cosine
    blocks[0, :, 1, :] = -sine
    blocks[1, :, 0, :] = sine
    return blocks


def chunk_planes(slab_planes):
    low, high = list(range(EDGE)), list(range(slab_planes - EDGE, slab_planes))
    return [low + high, list(range(EDGE, slab_planes - EDGE))]


def params(steps):
    return pltpu.CompilerParams(
        dimension_semantics=("arbitrary",) * steps, vmem_limit_bytes=VMEM_BYTES
    )


def cost(products, values):
    return pl.CostEstimate(flops=4 * products, bytes_accessed=4 * values, transcendentals=0)


def whole(shape):
    return pl.BlockSpec(shape, lambda i: (0,) * len(shape))


SMEM_SPEC = pl.BlockSpec(memory_space=pltpu.SMEM)


def paired(refs, slab):
    return [(lax.bitwise_xor(slab, jnp.int32(k)), ref) for k, ref in enumerate(refs)]


def shifted(refs, slab):
    return [(lax.rem(slab + k, len(refs)), ref) for k, ref in enumerate(refs)]


def first_x_kernel(slab, table_ref, coeffs_ref, *refs, pieces, natural):
    scratch = 3 if natural else 2
    outs = paired(refs[:-scratch], slab[0])
    turned, wide, *tall = refs[-scratch:]
    parts, size_x, columns, lanes = coeffs_ref.shape
    rows = parts * size_x
    height = table_ref.shape[0] // pieces

    for k, (device, _) in enumerate(outs):
        start = pl.multiple_of(device * height, 16)
        turned[k * height : (k + 1) * height, :] = table_ref[pl.ds(start, height), :]

    pitch = columns + 1

    def widen(k, carry):
        for part in range(parts):
            wide[pl.ds((part * size_x + k) * pitch, columns), :] = coeffs_ref[part, k].astype(
                jnp.float32
            )
        return carry

    lax.fori_loop(0, size_x, widen, 0, unroll=8)

    def some_columns(g, carry):
        loaded = [
            wide[pl.ds(COLUMNS * g + h, rows, stride=pitch), :].astype(jnp.bfloat16)
            for h in range(COLUMNS)
        ]
        for first in range(0, COLUMNS, FOUR):
            result = jnp.dot(
                turned[...],
                jnp.concatenate(loaded[first : first + FOUR], axis=1),
                preferred_element_type=jnp.float32,
            )
            for h in range(FOUR):
                column = COLUMNS * g + first + h
                piece = result[:, h * lanes : (h + 1) * lanes]
                if natural:
                    place = (first + h) % 2 * columns + COLUMNS // 2 * g + (first + h) // 2
                    planes = height // 2
                    for k in range(pieces):
                        for part in range(2):
                            start = k * height * columns + part * (columns // 2) + place
                            row = k * height + part * planes
                            tall[0][pl.ds(start, planes, stride=2 * columns), :] = piece[
                                row : row + planes
                            ]
                else:
                    piece = piece.astype(jnp.bfloat16)
                    for k, (_, out) in enumerate(outs):
                        out[column] = piece[k * height : (k + 1) * height]
        return carry

    lax.fori_loop(0, columns // COLUMNS, some_columns, 0)
    if natural:
        for k, (_, out) in enumerate(outs):
            values = tall[0][k * height * columns : (k + 1) * height * columns, :]
            out[...] = values.astype(jnp.bfloat16).reshape(out.shape)


def first_x(slab, table, coeffs, planes, pieces, natural):
    _, size_x, columns, size_z = coeffs.shape
    lanes = size_z // 2
    shape = (planes, 2 * columns) if natural else (columns, 2 * planes)
    scratch = [
        pltpu.VMEM(table.shape, jnp.bfloat16),
        pltpu.VMEM((2 * size_x * (columns + 1), lanes), jnp.float32),
    ]
    if natural:
        scratch.append(pltpu.VMEM((2 * pieces * planes * columns, lanes), jnp.float32))
    out_specs = [pl.BlockSpec((*shape, lanes), lambda i: (0, 0, i))] * pieces
    out_shape = [jax.ShapeDtypeStruct((*shape, size_z), jnp.bfloat16)] * pieces
    return pl.pallas_call(
        functools.partial(first_x_kernel, pieces=pieces, natural=natural),
        grid=(2,),
        in_specs=[
            SMEM_SPEC,
            whole(table.shape),
            pl.BlockSpec((2, size_x, columns, lanes), lambda i: (0, 0, 0, i)),
        ],
        out_specs=out_specs,
        out_shape=out_shape,
        scratch_shapes=scratch,
        compiler_params=params(1),
        cost_estimate=cost(2 * size_x * pieces * planes * columns * size_z, 2 * size_x * columns * size_z),
        name="first_x",
    )(slab, table, coeffs)


def ones_at(codes, count, axis):
    shape = (codes.shape[0], count) if axis == 1 else (count, codes.shape[1])
    places = lax.broadcasted_iota(jnp.int32, shape, axis)
    return jnp.where(codes == places, 1.0, 0.0).astype(jnp.bfloat16)


def field_kernel(slab, weights, table_y, table_z, codes, sides, *refs, pieces, count, natural):
    bufs = paired(refs[:count], slab[0])
    wave, density, *rows_out, gathered, wide = refs[count:]
    _, near, size_y, size_z = wave.shape
    columns = size_y // pieces
    groups, entries, _ = codes.shape
    lanes = 128
    halves = size_z // lanes
    i, last = pl.program_id(0), pl.num_programs(0) - 1
    planes = near * (last + 1)

    @pl.when(i == 0)
    def _():
        gathered[...] = jnp.zeros_like(gathered)

    loaded = []
    if natural:
        for source, buf in bufs:
            wide[source] = buf[...]
        for h in range(near):
            loaded.append(
                [wide[:, h, s * columns : (s + 1) * columns].reshape(size_y, size_z) for s in (0, 1)]
            )
    else:
        rows = bufs[0][1].shape[1]
        pitch = rows + 1

        @pl.when(i == 0)
        def _():
            for source, buf in bufs:

                def widen(column, carry):
                    values = buf[column].astype(jnp.float32)
                    for q in range(halves):
                        wide[q, pl.ds((source * columns + column) * pitch, rows), :] = values[
                            :, q * lanes : (q + 1) * lanes
                        ]
                    return carry

                lax.fori_loop(0, columns, widen, 0, unroll=8)

        def strided(start):
            return jnp.concatenate(
                [
                    wide[q, pl.ds(start, size_y // 2, stride=2 * pitch), :]
                    for q in range(halves)
                ],
                axis=1,
            ).astype(jnp.bfloat16)

        for h in range(near):
            plane = i * near + h
            loaded.append(
                [
                    jnp.concatenate(
                        [strided(s * pitch + part * planes + plane) for part in range(2)], axis=0
                    )
                    for s in (0, 1)
                ]
            )
    even, odd = (
        jnp.dot(
            table_y[s],
            jnp.concatenate([pair[s] for pair in loaded], axis=1),
            preferred_element_type=jnp.float32,
        )
        for s in (0, 1)
    )
    low, high = (even + odd).astype(jnp.bfloat16), (even - odd).astype(jnp.bfloat16)
    middle = size_y // 2
    turned = []
    for h in range(near):
        span = slice(h * size_z, (h + 1) * size_z)
        both = [
            jnp.concatenate(
                [values[part * middle : (part + 1) * middle, span] for values in (low, high)], axis=0
            )
            for part in range(2)
        ]
        turned.append(jnp.concatenate(both, axis=1))
    result = jnp.dot(
        jnp.concatenate(turned, axis=0), table_z[...], preferred_element_type=jnp.float32
    ).astype(jnp.bfloat16)
    for h in range(near):
        total = jnp.zeros((size_y, size_z), jnp.float32)
        for part in range(2):
            values = result[h * size_y : (h + 1) * size_y, part * size_z : (part + 1) * size_z]
            wave[part, h] = values
            values = values.astype(jnp.float32)
            total += weights[0, part] * values * values
        density[h] = total.astype(jnp.bfloat16)

    used = [0] if groups == 1 else [0, 1 + (2 * i > last).astype(jnp.int32)]
    for group in used:
        places = ones_at(codes[group] - i * near * size_y, near * size_y, 1)
        gathered[group] += jnp.dot(places, result, preferred_element_type=jnp.float32)

    @pl.when(i == last)
    def _():
        for group in range(groups):
            for part in range(2):
                total = jnp.zeros((entries, lanes), jnp.float32)
                for q in range(halves):
                    start = part * size_z + q * lanes
                    total += jnp.where(
                        sides[group] == q, gathered[group, :, start : start + lanes], 0.0
                    )
                rows_out[group][part] = total.astype(jnp.bfloat16)


def make_field(slab, weights, bufs, table_y, table_z, codes, sides, planes, pieces, natural):
    size_z = bufs[0].shape[-1]
    size_y = table_y.shape[1]
    columns = size_y // pieces
    groups, entries, _ = codes.shape
    if natural:
        buf_spec = pl.BlockSpec((PLANES, 2 * columns, size_z), lambda i: (i, 0, 0))
        wide = pltpu.VMEM((pieces, PLANES, 2 * columns, size_z), jnp.bfloat16)
    else:
        buf_spec = whole(bufs[0].shape)
        wide = pltpu.VMEM((size_z // 128, (2 * planes + 1) * size_y, 128), jnp.float32)
    return pl.pallas_call(
        functools.partial(field_kernel, pieces=pieces, count=len(bufs), natural=natural),
        grid=(planes // PLANES,),
        in_specs=[SMEM_SPEC, SMEM_SPEC]
        + [whole(a.shape) for a in (table_y, table_z, codes, sides)]
        + [buf_spec] * len(bufs),
        out_specs=[
            pl.BlockSpec((2, PLANES, size_y, size_z), lambda i: (0, i, 0, 0)),
            pl.BlockSpec((PLANES, size_y, size_z), lambda i: (i, 0, 0)),
        ]
        + [whole((2, entries, 128))] * groups,
        out_shape=[
            jax.ShapeDtypeStruct((2, planes, size_y, size_z), jnp.bfloat16),
            jax.ShapeDtypeStruct((planes, size_y, size_z), jnp.bfloat16),
        ]
        + [jax.ShapeDtypeStruct((2, entries, 128), jnp.bfloat16)] * groups,
        scratch_shapes=[pltpu.VMEM((groups, entries, 2 * size_z), jnp.float32), wide],
        compiler_params=params(1),
        cost_estimate=cost(
            2 * planes * size_y * size_z * (size_y + size_z), 2 * planes * size_y * size_z
        ),
        name="make_field",
    )(slab, weights, table_y, table_z, codes, sides, *bufs)


def nonlocal_kernel(coupled, projectors, *refs):
    parts, (projections, spread) = refs[:-2], refs[-2:]
    atoms, nproj, blocks, cells = projectors.shape
    for atom in range(atoms):
        tables = [projectors[atom, j].astype(jnp.float32) for j in range(nproj)]
        place = pl.ds(atom * blocks, blocks)
        for part in range(2):
            rows = sum(p[part, place].astype(jnp.float32) for p in parts)
            tile = jnp.concatenate(
                [jnp.sum(t * rows, axis=0, keepdims=True) for t in tables], axis=0
            )
            mixed = jnp.zeros_like(tile)
            for j in range(nproj):
                mixed += coupled[j] * tile[j : j + 1]
            projections[atom, part] = jnp.broadcast_to(
                jnp.sum(tile, -1, keepdims=True), tile.shape
            )
            energy = jnp.broadcast_to(jnp.sum(mixed, -1, keepdims=True), tile.shape)
            spread[part, place] = sum(
                t * energy[j : j + 1] for j, t in enumerate(tables)
            ).astype(jnp.bfloat16)


def make_nonlocal(coupled, projectors, parts):
    atoms, nproj, _, cells = projectors.shape
    return pl.pallas_call(
        nonlocal_kernel,
        out_shape=[
            jax.ShapeDtypeStruct((atoms, 2, nproj, cells), jnp.float32),
            jax.ShapeDtypeStruct(parts[0].shape, jnp.bfloat16),
        ],
        name="make_nonlocal",
    )(coupled, projectors, *parts)


def back_kernel(slab, wave, potential, table_z, table_y, codes, sides, *refs, pieces, natural):
    groups, _, entries = codes.shape
    sources, outs = refs[:groups], refs[groups:-2]
    spread, tall = refs[-2:]
    outs = shifted(outs, slab[0])
    near, size_y, size_z = potential.shape
    lanes = 128
    halves = size_z // lanes
    i, last = pl.program_id(0), pl.num_programs(0) - 1
    planes = near * (last + 1)

    @pl.when(i == 0)
    def _():
        for group, source in enumerate(sources):
            for part in range(2):
                for q in range(halves):
                    start = part * size_z + q * lanes
                    spread[group, :, start : start + lanes] = jnp.where(
                        sides[group] == q, source[part].astype(jnp.float32), 0.0
                    ).astype(jnp.bfloat16)

    used = [0] if groups == 1 else [0, 1 + (2 * i > last).astype(jnp.int32)]
    extra = jnp.zeros((near * size_y, 2 * size_z), jnp.float32)
    for group in used:
        places = ones_at(codes[group] - i * near * size_y, near * size_y, 0)
        extra += jnp.dot(places, spread[group], preferred_element_type=jnp.float32)
    fields = []
    for h in range(near):
        local = potential[h].astype(jnp.float32)
        both = [
            local * wave[part, h].astype(jnp.float32)
            + extra[h * size_y : (h + 1) * size_y, part * size_z : (part + 1) * size_z]
            for part in range(2)
        ]
        fields.append(jnp.concatenate(both, axis=1).astype(jnp.bfloat16))
    back_z = jnp.dot(
        jnp.concatenate(fields, axis=0), table_z[...], preferred_element_type=jnp.float32
    )
    middle = size_y // 2
    folded = [[], []]
    for h in range(near):
        low = back_z[h * size_y : h * size_y + middle]
        high = back_z[h * size_y + middle : (h + 1) * size_y]
        for kept, values in zip(folded, (low + high, low - high)):
            values = values.astype(jnp.bfloat16)
            kept.append(jnp.concatenate([values[:, :size_z], values[:, size_z:]], axis=0))
    columns = size_y // pieces
    for s, kept in enumerate(folded):
        back_y = jnp.dot(
            table_y[s], jnp.concatenate(kept, axis=1), preferred_element_type=jnp.float32
        )
        if natural:
            back_y = back_y.astype(jnp.bfloat16)
            for h in range(near):
                tall[:, h, s * columns : (s + 1) * columns] = back_y[
                    :, h * size_z : (h + 1) * size_z
                ].reshape(pieces, columns, size_z)
            continue
        pitch = outs[0][1].shape[1] + 1
        for h in range(near):
            for part in range(2):
                for q in range(halves):
                    start = s * pitch + part * planes + i * near + h
                    lane = h * size_z + q * lanes
                    tall[q, pl.ds(start, middle, stride=2 * pitch), :] = back_y[
                        part * middle : (part + 1) * middle, lane : lane + lanes
                    ]

    if natural:
        for target, out in outs:
            out[...] = tall[target]
        return
    rows = outs[0][1].shape[1]

    @pl.when(i == last)
    def _():
        for target, out in outs:

            def narrow(column, carry):
                start = (target * columns + column) * pitch
                values = [tall[q, pl.ds(start, rows), :] for q in range(halves)]
                out[column] = jnp.concatenate(values, axis=1).astype(jnp.bfloat16)
                return carry

            lax.fori_loop(0, columns, narrow, 0, unroll=8)


def go_back(slab, wave, potential, table_z, table_y, codes, sides, sources, place, pieces, natural):
    _, planes, size_y, size_z = wave.shape
    columns = size_y // pieces
    groups, _, entries = codes.shape
    scratch = [pltpu.VMEM((groups, entries, 2 * size_z), jnp.bfloat16)]
    if natural:
        shape = (planes, 2 * columns, size_z)
        out_specs = [pl.BlockSpec((PLANES, 2 * columns, size_z), lambda i: (i, 0, 0))] * pieces
        scratch.append(pltpu.VMEM((pieces, PLANES, 2 * columns, size_z), jnp.bfloat16))
    else:
        shape = (columns, 2 * planes, size_z)
        out_specs = [whole(shape)] * pieces
        scratch.append(pltpu.VMEM((size_z // 128, (2 * planes + 1) * size_y, 128), jnp.float32))
    return pl.pallas_call(
        functools.partial(back_kernel, pieces=pieces, natural=natural),
        grid=(planes // PLANES,),
        in_specs=[
            SMEM_SPEC,
            pl.BlockSpec((2, PLANES, size_y, size_z), lambda i: (0, i, 0, 0)),
            pl.BlockSpec((PLANES, size_y, size_z), lambda i: (place(i), 0, 0)),
        ]
        + [whole(a.shape) for a in (table_z, table_y, codes, sides, *sources)],
        out_specs=out_specs,
        out_shape=[jax.ShapeDtypeStruct(shape, jnp.bfloat16)] * pieces,
        scratch_shapes=scratch,
        compiler_params=params(1),
        cost_estimate=cost(
            2 * planes * size_y * size_z * (size_y + size_z), 2 * planes * size_y * size_z
        ),
        name="go_back",
    )(slab, wave, potential, table_z, table_y, codes, sides, *sources)


def last_x_kernel(frequency_x, frequency_yz, table, coeffs, *refs):
    bufs, (out, tall) = refs[:-2], refs[-2:]
    parts, size_x, columns, lanes = coeffs.shape
    pitch = columns + 1

    def some_columns(g, carry):
        loaded = []
        for h in range(COLUMNS):
            loaded.append(jnp.concatenate([buf[COLUMNS * g + h] for buf in bufs], axis=0))
        for first in range(0, COLUMNS, FOUR):
            result = jnp.dot(
                table[...],
                jnp.concatenate(loaded[first : first + FOUR], axis=1),
                preferred_element_type=jnp.float32,
            )
            for h in range(FOUR):
                tall[pl.ds(COLUMNS * g + first + h, parts * size_x, stride=pitch), :] = result[
                    :, h * lanes : (h + 1) * lanes
                ]
        return carry

    lax.fori_loop(0, columns // COLUMNS, some_columns, 0)

    def finish(k, carry):
        kinetic = frequency_x[k] + frequency_yz[...]
        for part in range(parts):
            out[part, k] = (
                tall[pl.ds((part * size_x + k) * pitch, columns), :] + kinetic * coeffs[part, k].astype(jnp.float32)
            ).astype(jnp.bfloat16)
        return carry

    lax.fori_loop(0, size_x, finish, 0, unroll=8)


def last_x(frequency_x, frequency_yz, table, coeffs, bufs):
    _, size_x, columns, size_z = coeffs.shape
    lanes = size_z // 2
    spec = pl.BlockSpec((2, size_x, columns, lanes), lambda i: (0, 0, 0, i))
    return pl.pallas_call(
        last_x_kernel,
        grid=(2,),
        in_specs=[
            SMEM_SPEC,
            pl.BlockSpec((columns, lanes), lambda i: (0, i)),
            whole(table.shape),
            spec,
        ]
        + [pl.BlockSpec((*b.shape[:2], lanes), lambda i: (0, 0, i)) for b in bufs],
        out_specs=spec,
        out_shape=jax.ShapeDtypeStruct(coeffs.shape, jnp.bfloat16),
        scratch_shapes=[pltpu.VMEM((2 * size_x * (columns + 1), lanes), jnp.float32)],
        compiler_params=params(1),
        cost_estimate=cost(2 * size_x * size_x * columns * size_z, 3 * size_x * columns * size_z),
        name="last_x",
    )(frequency_x, frequency_yz, table, coeffs, *bufs)


def per_device_chunked(wave_coeffs, occupation, potential, projectors, coupling, sphere_blocks):
    pieces = lax.axis_size("fft")
    bands = lax.axis_size("band")
    slab = lax.axis_index("fft")
    coeffs = wave_coeffs[0]
    _, size_x, columns, size_z = coeffs.shape
    slab_planes, size_y, _ = potential.shape
    atom_dev, nproj, blocks, cells = projectors.shape
    zblocks = size_z // cells
    outer, inner = chunk_planes(slab_planes)
    up = [(i, (i + 1) % pieces) for i in range(pieces)]
    down = [(j, i) for i, j in up]

    inverse_x, forward_x = (real_blocks(size_x, s) for s in (1.0, -1.0))
    inverse_y, forward_y = (real_blocks(size_y, s) for s in (1.0, -1.0))
    inverse_z, forward_z = (real_blocks(size_z, s) for s in (1.0, -1.0))
    place_outer, place_inner = (
        np.arange(pieces)[:, None] * slab_planes + np.array(chunk)[None, :]
        for chunk in (outer, inner)
    )
    table_x_outer = np.stack([inverse_x[r][place_outer] for r in range(2)], 1)
    table_x_inner = np.stack([inverse_x[r][place_inner] for r in range(2)], 1)
    tables_back_x = [
        np.stack([forward_x[:, :, r][:, :, place] for r in range(2)], 3).reshape(
            2 * size_x, pieces, -1
        )
        for place in (place_outer, place_inner)
    ]
    middle = size_y // 2
    down_y = [inverse_y[:, :middle, :, s::2] for s in (0, 1)]
    back_y = [forward_y[:, s::2, :, :middle] for s in (0, 1)]
    split = (pieces, columns // 2)
    tables = [
        table_x_outer.reshape(-1, 2 * size_x),
        table_x_inner.reshape(-1, 2 * size_x),
        np.stack([t.reshape(size_y, -1) for t in down_y]),
        np.stack(
            [t.reshape(2, middle, 2, *split).swapaxes(2, 3).reshape(size_y, -1) for t in down_y]
        ),
        inverse_z.transpose(2, 3, 0, 1).reshape(2 * size_z, -1),
        forward_z.transpose(2, 3, 0, 1).reshape(2 * size_z, -1),
        np.stack([t.reshape(size_y, -1) for t in back_y]),
        np.stack([t.reshape(2, *split, -1).swapaxes(0, 1).reshape(size_y, -1) for t in back_y]),
        np.stack(
            [
                np.concatenate(
                    [t[:, (d - np.arange(pieces)) % pieces].reshape(2 * size_x, -1) for t in tables_back_x],
                    axis=1,
                )
                for d in range(pieces)
            ]
        ),
    ]
    (
        table_x_outer, table_x_inner, table_y_outer, table_y_inner, table_z,
        table_back_z, table_back_y_outer, table_back_y_inner, tables_back_x,
    ) = (jnp.asarray(t.astype(jnp.bfloat16)) for t in tables)

    table_back_x = lax.dynamic_index_in_dim(tables_back_x, slab, 0, keepdims=False)

    where = slab.reshape(1)
    section_outer = first_x(where, table_x_outer, coeffs, len(outer), pieces, False)
    section_outer, table_x_inner, sphere_blocks = lax.optimization_barrier(
        (section_outer, table_x_inner, sphere_blocks)
    )
    section_inner = first_x(where, table_x_inner, coeffs, len(inner), pieces, True)

    entries = atom_dev * blocks

    def codes_of(chunk, shift):
        owner = (slab + shift + pieces) % pieces
        numbers = lax.dynamic_slice_in_dim(sphere_blocks, owner * atom_dev, atom_dev, 0)
        plane = numbers // (size_y * zblocks) - slab * slab_planes
        rest = numbers % (size_y * zblocks)
        if chunk is outer:
            inside = ((plane >= 0) & (plane < EDGE)) | (
                (plane >= slab_planes - EDGE) & (plane < slab_planes)
            )
            plane = jnp.where(plane < EDGE, plane, plane - len(inner))
        else:
            inside = (plane >= EDGE) & (plane < slab_planes - EDGE)
            plane = plane - EDGE
        code = jnp.where(inside, plane * size_y + rest // zblocks, -1)
        return code.reshape(entries), (rest % zblocks).reshape(entries)

    found = [codes_of(outer, shift) for shift in (0, -1, 1)]
    codes_outer, sides_outer = (jnp.stack(values) for values in zip(*found))
    codes_inner, sides_inner = (values[None] for values in codes_of(inner, 0))
    sides_outer, sides_inner = sides_outer[:, :, None], sides_inner[:, :, None]
    rows_codes = [codes_outer[:, :, None], codes_inner[:, :, None]]
    lane_codes = [codes_outer[:, None, :], codes_inner[:, None, :]]
    strength = 3.0 * math.sqrt(cells * blocks) / nproj
    coupled = (coupling + coupling.T) * (0.5 * strength)
    coupled = jnp.broadcast_to(coupled.T[:, :, None], (nproj, nproj, cells))
    section_inner, rows_codes, lane_codes, sides_outer, sides_inner, coupled = (
        lax.optimization_barrier(
            (section_inner, rows_codes, lane_codes, sides_outer, sides_inner, coupled)
        )
    )

    half = pieces // 2
    near, far = list(range(1, half)), list(range(half, pieces))

    def send(block, k, *awaited):
        for row, m in awaited:
            block, row[m] = lax.optimization_barrier((block, row[m]))
        return lax.ppermute(block, "fft", [(j, j ^ k) for j in range(pieces)])

    received_outer, received_inner = (
        [section[0]] + [None] * (pieces - 1) for section in (section_outer, section_inner)
    )
    for partners in (near, far):
        queue = [(section_outer, received_outer, k) for k in partners]
        queue += [(section_inner, received_inner, k) for k in partners]
        for place, (section, received, k) in enumerate(queue):
            awaited = [queue[place - 2][1:]] if place >= 2 else []
            received[k] = send(section[k], k, *awaited)
    wave_outer, density_outer, rows_outer, to_previous, to_following = make_field(
        where, occupation, received_outer, table_y_outer, table_z, rows_codes[0],
        sides_outer, len(outer), pieces, False,
    )
    from_following = lax.ppermute(to_previous, "fft", down)
    from_previous = lax.ppermute(to_following, "fft", up)
    density_outer = lax.psum(density_outer, "band")
    wave_inner, density_inner, rows_inner = make_field(
        where, occupation, received_inner, table_y_inner, table_z, rows_codes[1],
        sides_inner, len(inner), pieces, True,
    )
    projected, spread = make_nonlocal(
        coupled, projectors, [rows_outer, rows_inner, from_following, from_previous]
    )
    spread_previous = lax.ppermute(spread, "fft", up)
    spread_following = lax.ppermute(spread, "fft", down)
    edge_steps = EDGE // PLANES
    inner_steps = len(inner) // PLANES
    back_inner = go_back(
        where, wave_inner, potential, table_back_z, table_back_y_inner, lane_codes[1],
        sides_inner, [spread], lambda i: i + edge_steps, pieces, True,
    )
    distances = sorted(range(1, pieces), key=lambda k: abs(k - half))

    def permute_all(values):
        received = [values[0]] + [None] * (pieces - 1)
        for k in distances:
            pairs = [(j, (j + k) % pieces) for j in range(pieces)]
            received[k] = lax.ppermute(values[k], "fft", pairs)
        return received

    back_inner = permute_all(back_inner)
    back_outer = go_back(
        where, wave_outer, potential, table_back_z, table_back_y_outer, lane_codes[0],
        sides_outer, [spread, spread_previous, spread_following],
        lambda i: jnp.where(i < edge_steps, i, i + inner_steps), pieces, False,
    )
    density_inner, density_outer = lax.optimization_barrier((density_inner, density_outer))
    density_inner = lax.psum(density_inner, "band")
    back_outer, density_outer = lax.optimization_barrier((back_outer, density_outer))
    back_outer = permute_all(back_outer)
    back_inner = [
        b.reshape(len(inner), 2, 2, columns // 2, size_z)
        .transpose(3, 1, 2, 0, 4)
        .reshape(columns, -1, size_z)
        for b in back_inner
    ]
    density = jnp.concatenate([density_outer[:EDGE], density_inner, density_outer[EDGE:]], axis=0)

    index_x = np.arange(size_x)
    frequency_x = jnp.asarray(
        (np.where(2 * index_x < size_x, index_x, index_x - size_x) / size_x) ** 2, jnp.float32
    )
    index_y = slab * columns + jnp.arange(columns, dtype=jnp.int32)
    index_z = jnp.arange(size_z, dtype=jnp.int32)
    frequency_yz = wave_squares(index_y, size_y)[:, None] + wave_squares(index_z, size_z)[None, :]
    coeffs, density, back_inner = lax.optimization_barrier((coeffs, density, back_inner))
    applied = last_x(frequency_x, frequency_yz, table_back_x, coeffs, back_outer + back_inner)
    return (applied[None], density, projected[None, :, :, :, 0])


def per_device(wave_coeffs, occupation, potential, projectors, coupling, sphere_blocks):
    pieces, bands = lax.axis_size("fft"), lax.axis_size("band")
    size_z = wave_coeffs.shape[4]
    columns = wave_coeffs.shape[3]
    slab_planes = potential.shape[0]
    chunked = (
        pieces >= 4
        and pieces & (pieces - 1) == 0
        and slab_planes % EDGE == 0
        and slab_planes >= 3 * EDGE
        and EDGE >= HALO
        and columns % 8 == 0
        and size_z % 256 == 0
        and projectors.shape[0] % bands == 0
        and projectors.shape[3] == 128
        and projectors.shape[1] == 8
    )
    chosen = per_device_chunked if chunked else per_device_plain
    return chosen(wave_coeffs, occupation, potential, projectors, coupling, sphere_blocks)


def solution(mesh):
    placed = (
        P("band", None, None, "fft", None),
        P("band", None),
        P("fft", None, None),
        P("fft", None, None, None),
        P(),
        P(),
    )
    return jax.shard_map(
        per_device,
        mesh=mesh,
        in_specs=placed,
        out_specs=(
            P("band", None, None, "fft", None),
            P("fft", None, None),
            P("band", "fft", None, None),
        ),
        check_vma=False,
    )
```

```python
import functools
import math

import jax
import jax.numpy as jnp
import numpy as np
from jax import lax
from jax.experimental import pallas as pl
from jax.experimental.pallas import tpu as pltpu
from jax.sharding import PartitionSpec as P

HALO = 6
EDGE = 8
PLANES = 4
COLUMNS = 8
FOUR = 4
VMEM_BYTES = 56 * 1024 * 1024


def extended(shard, sides, width):
    for axis, dim in sides:
        count, length = (lax.axis_size(axis), shard.shape[dim])
        up = [(i, (i + 1) % count) for i in range(count)]
        down = [(j, i) for i, j in up]
        last = lax.slice_in_dim(shard, length - width, length, axis=dim)
        first = lax.slice_in_dim(shard, 0, width, axis=dim)
        before = lax.ppermute(last, axis, up)
        after = lax.ppermute(first, axis, down)
        shard = jnp.concatenate([before, shard, after], axis=dim)
    return shard


def dft_table(length, sign_value):
    indices = jnp.arange(length, dtype=jnp.int32)
    phases = indices[:, None] * indices[None, :] % length
    angles = 2.0 * math.pi / length * phases.astype(jnp.float32)
    factor = 1.0 / math.sqrt(length)
    cosine = jnp.cos(angles) * factor
    sine_part = jnp.sin(angles) * (sign_value * factor)
    upper_rows = jnp.stack([cosine, -sine_part])
    bottom = jnp.stack([sine_part, cosine])
    return jnp.stack([upper_rows, bottom]).astype(jnp.bfloat16)


def wave_squares(indices, length):
    frequency = (
        jnp.where(2 * indices < length, indices, indices - length).astype(jnp.float32) / length
    )
    return frequency * frequency


def per_device_plain(wave_coeffs, occupation, potential, projectors, coupling, sphere_blocks):
    pieces = lax.axis_size("fft")
    slab_index = lax.axis_index("fft")
    coeffs = wave_coeffs[0]
    size_x = coeffs.shape[1]
    columns = coeffs.shape[2]
    size_z = coeffs.shape[3]
    slab_planes = potential.shape[0]
    size_y = potential.shape[1]
    atom_dev = projectors.shape[0]
    nproj_count = projectors.shape[1]
    block_cells = projectors.shape[3]
    zblocks = size_z // block_cells
    plane_blocks = size_y * zblocks
    total_atoms = atom_dev * pieces
    table_x = dft_table(size_x, 1.0).transpose(0, 2, 1, 3).reshape(2 * size_x, 2 * size_x)
    inverse_y = dft_table(size_y, 1.0)
    inverse_z = dft_table(size_z, 1.0)
    flattened = coeffs.reshape(2 * size_x, columns * size_z)
    along_x = jnp.dot(table_x, flattened, preferred_element_type=jnp.float32)
    along_x = along_x.reshape(2, size_x, columns, size_z).astype(jnp.bfloat16)
    along_y = jnp.einsum(
        "abyk,bxkz->axyz",
        inverse_y,
        lax.all_to_all(along_x, "fft", split_axis=1, concat_axis=2, tiled=True),
        preferred_element_type=jnp.float32,
    ).astype(jnp.bfloat16)
    wave_field = jnp.einsum(
        "abzk,bxyk->axyz", inverse_z, along_y, preferred_element_type=jnp.float32
    ).astype(jnp.bfloat16)
    weights = occupation[0]
    real_part = wave_field[0].astype(jnp.float32)
    imag_part = wave_field[1].astype(jnp.float32)
    partial_density = weights[0] * real_part * real_part + weights[1] * imag_part * imag_part
    density = lax.psum(partial_density.astype(jnp.bfloat16), "band")
    strength = 3.0 * math.sqrt(block_cells * projectors.shape[2]) / nproj_count
    coupled = (coupling + coupling.T) * (0.5 * strength)
    nearby = extended(projectors, (("fft", 0),), atom_dev)
    atom_rows = (
        slab_index * atom_dev - atom_dev + jnp.arange(3 * atom_dev, dtype=jnp.int32) + total_atoms
    ) % total_atoms
    near_blocks = sphere_blocks[atom_rows]
    plane_index = near_blocks // plane_blocks
    inside = plane_index // slab_planes == slab_index
    local_index = jnp.where(
        inside,
        (plane_index - slab_index * slab_planes) * plane_blocks + near_blocks % plane_blocks,
        0,
    )
    blocks_own = wave_field.reshape(2, slab_planes * plane_blocks, block_cells)
    gathered = blocks_own[:, local_index] * inside[None, :, :, None].astype(jnp.bfloat16)
    partial_value = jnp.einsum(
        "ajsk,bask->abj", nearby, gathered, preferred_element_type=jnp.float32
    )
    summed = extended(partial_value, (("fft", 0),), atom_dev)
    projections_own = (
        summed[:atom_dev] + summed[2 * atom_dev : 3 * atom_dev] + summed[4 * atom_dev :]
    )
    energy_own = jnp.einsum(
        "ij,abj->abi", coupled, projections_own, precision=lax.Precision.HIGHEST
    )
    energy = extended(energy_own, (("fft", 0),), atom_dev)
    spread = jnp.einsum(
        "ajsk,abj->bask", nearby.astype(jnp.float32), energy, precision=lax.Precision.HIGHEST
    )
    spread = spread * inside[None, :, :, None].astype(jnp.float32)
    accumulated = (
        jnp.zeros((2, slab_planes * plane_blocks, block_cells), jnp.float32)
        .at[:, local_index]
        .add(spread)
    )
    nonlocal_term = accumulated.reshape(2, slab_planes, size_y, size_z)
    total_field = (
        potential.astype(jnp.float32)[None] * wave_field.astype(jnp.float32) + nonlocal_term
    ).astype(jnp.bfloat16)
    forward_z = dft_table(size_z, -1.0)
    forward_y = dft_table(size_y, -1.0)
    forward_x = dft_table(size_x, -1.0)
    back_z = jnp.einsum(
        "abzk,bxyk->axyz", forward_z, total_field, preferred_element_type=jnp.float32
    ).astype(jnp.bfloat16)
    back_y = jnp.einsum(
        "abyk,bxkz->axyz", forward_y, back_z, preferred_element_type=jnp.float32
    ).astype(jnp.bfloat16)
    transformed = jnp.einsum(
        "abxk,bkyz->axyz",
        forward_x,
        lax.all_to_all(back_y, "fft", split_axis=2, concat_axis=1, tiled=True),
        preferred_element_type=jnp.float32,
    )
    index_x = jnp.arange(size_x, dtype=jnp.int32)
    index_y = slab_index * columns + jnp.arange(columns, dtype=jnp.int32)
    index_z = jnp.arange(size_z, dtype=jnp.int32)
    kinetic = (
        wave_squares(index_x, size_x)[:, None, None]
        + wave_squares(index_y, size_y)[None, :, None]
        + wave_squares(index_z, size_z)[None, None, :]
    )
    applied = (transformed + kinetic[None] * coeffs.astype(jnp.float32)).astype(jnp.bfloat16)
    return (applied[None], density, projections_own[None])


def real_blocks(length, sign):
    index = np.arange(length)
    angles = 2.0 * np.pi / length * (index[:, None] * index[None, :] % length)
    cosine = np.cos(angles) / np.sqrt(length)
    sine = sign * np.sin(angles) / np.sqrt(length)
    blocks = np.empty((2, length, 2, length))
    blocks[0, :, 0, :] = cosine
    blocks[1, :, 1, :] = cosine
    blocks[0, :, 1, :] = -sine
    blocks[1, :, 0, :] = sine
    return blocks


def chunk_planes(slab_planes):
    low, high = list(range(EDGE)), list(range(slab_planes - EDGE, slab_planes))
    return [low + high, list(range(EDGE, slab_planes - EDGE))]


def params(steps):
    return pltpu.CompilerParams(
        dimension_semantics=("arbitrary",) * steps, vmem_limit_bytes=VMEM_BYTES
    )


def cost(products, values):
    return pl.CostEstimate(flops=4 * products, bytes_accessed=4 * values, transcendentals=0)


def whole(shape):
    return pl.BlockSpec(shape, lambda i: (0,) * len(shape))


SMEM_SPEC = pl.BlockSpec(memory_space=pltpu.SMEM)


def paired(refs, slab):
    return [(lax.bitwise_xor(slab, jnp.int32(k)), ref) for k, ref in enumerate(refs)]


def ring_order(pieces):
    return [0] + sorted(range(1, pieces), key=lambda k: abs(k - pieces // 2))


def shifted(refs, slab):
    order = ring_order(len(refs))
    return [(lax.rem(slab + k, len(refs)), ref) for k, ref in zip(order, refs)]


def first_x_kernel(slab, table_ref, coeffs_ref, *refs, pieces, natural):
    scratch = 3 if natural else 2
    outs = paired(refs[:-scratch], slab[0])
    turned, wide, *tall = refs[-scratch:]
    parts, size_x, columns, lanes = coeffs_ref.shape
    rows = parts * size_x
    height = table_ref.shape[0] // pieces

    for k, (device, _) in enumerate(outs):
        start = pl.multiple_of(device * height, 16)
        turned[k * height : (k + 1) * height, :] = table_ref[pl.ds(start, height), :]

    pitch = columns + 1

    def widen(k, carry):
        for part in range(parts):
            wide[pl.ds((part * size_x + k) * pitch, columns), :] = coeffs_ref[part, k].astype(
                jnp.float32
            )
        return carry

    lax.fori_loop(0, size_x, widen, 0, unroll=8)

    def some_columns(g, carry):
        loaded = [
            wide[pl.ds(COLUMNS * g + h, rows, stride=pitch), :].astype(jnp.bfloat16)
            for h in range(COLUMNS)
        ]
        for first in range(0, COLUMNS, FOUR):
            result = jnp.dot(
                turned[...],
                jnp.concatenate(loaded[first : first + FOUR], axis=1),
                preferred_element_type=jnp.float32,
            )
            for h in range(FOUR):
                column = COLUMNS * g + first + h
                piece = result[:, h * lanes : (h + 1) * lanes]
                if natural:
                    place = (first + h) % 2 * columns + COLUMNS // 2 * g + (first + h) // 2
                    planes = height // 2
                    for k in range(pieces):
                        for part in range(2):
                            start = k * height * columns + part * (columns // 2) + place
                            row = k * height + part * planes
                            tall[0][pl.ds(start, planes, stride=2 * columns), :] = piece[
                                row : row + planes
                            ]
                else:
                    piece = piece.astype(jnp.bfloat16)
                    for k, (_, out) in enumerate(outs):
                        out[column] = piece[k * height : (k + 1) * height]
        return carry

    lax.fori_loop(0, columns // COLUMNS, some_columns, 0)
    if natural:
        for k, (_, out) in enumerate(outs):
            values = tall[0][k * height * columns : (k + 1) * height * columns, :]
            out[...] = values.astype(jnp.bfloat16).reshape(out.shape)


def first_x(slab, table, coeffs, planes, pieces, natural):
    _, size_x, columns, size_z = coeffs.shape
    lanes = size_z // 2
    shape = (planes, 2 * columns) if natural else (columns, 2 * planes)
    scratch = [
        pltpu.VMEM(table.shape, jnp.bfloat16),
        pltpu.VMEM((2 * size_x * (columns + 1), lanes), jnp.float32),
    ]
    if natural:
        scratch.append(pltpu.VMEM((2 * pieces * planes * columns, lanes), jnp.float32))
    out_specs = [pl.BlockSpec((*shape, lanes), lambda i: (0, 0, i))] * pieces
    out_shape = [jax.ShapeDtypeStruct((*shape, size_z), jnp.bfloat16)] * pieces
    return pl.pallas_call(
        functools.partial(first_x_kernel, pieces=pieces, natural=natural),
        grid=(2,),
        in_specs=[
            SMEM_SPEC,
            whole(table.shape),
            pl.BlockSpec((2, size_x, columns, lanes), lambda i: (0, 0, 0, i)),
        ],
        out_specs=out_specs,
        out_shape=out_shape,
        scratch_shapes=scratch,
        compiler_params=params(1),
        cost_estimate=cost(2 * size_x * pieces * planes * columns * size_z, 2 * size_x * columns * size_z),
        name="first_x",
    )(slab, table, coeffs)


def ones_at(codes, count, axis):
    shape = (codes.shape[0], count) if axis == 1 else (count, codes.shape[1])
    places = lax.broadcasted_iota(jnp.int32, shape, axis)
    return jnp.where(codes == places, 1.0, 0.0).astype(jnp.bfloat16)


def field_kernel(slab, weights, table_y, table_z, codes, sides, *refs, pieces, count, natural):
    bufs = paired(refs[:count], slab[0])
    wave, density, *rows_out, gathered, wide = refs[count:]
    _, near, size_y, size_z = wave.shape
    columns = size_y // pieces
    groups, entries, _ = codes.shape
    lanes = 128
    halves = size_z // lanes
    i, last = pl.program_id(0), pl.num_programs(0) - 1
    planes = near * (last + 1)

    @pl.when(i == 0)
    def _():
        gathered[...] = jnp.zeros_like(gathered)

    loaded = []
    if natural:
        for source, buf in bufs:
            wide[source] = buf[...]
        for h in range(near):
            loaded.append(
                [wide[:, h, s * columns : (s + 1) * columns].reshape(size_y, size_z) for s in (0, 1)]
            )
    else:
        rows = bufs[0][1].shape[1]
        pitch = rows + 1

        @pl.when(i == 0)
        def _():
            for source, buf in bufs:

                def widen(column, carry):
                    values = buf[column].astype(jnp.float32)
                    for q in range(halves):
                        wide[q, pl.ds((source * columns + column) * pitch, rows), :] = values[
                            :, q * lanes : (q + 1) * lanes
                        ]
                    return carry

                lax.fori_loop(0, columns, widen, 0, unroll=8)

        def strided(start):
            return jnp.concatenate(
                [
                    wide[q, pl.ds(start, size_y // 2, stride=2 * pitch), :]
                    for q in range(halves)
                ],
                axis=1,
            ).astype(jnp.bfloat16)

        for h in range(near):
            plane = i * near + h
            loaded.append(
                [
                    jnp.concatenate(
                        [strided(s * pitch + part * planes + plane) for part in range(2)], axis=0
                    )
                    for s in (0, 1)
                ]
            )
    even, odd = (
        jnp.dot(
            table_y[s],
            jnp.concatenate([pair[s] for pair in loaded], axis=1),
            preferred_element_type=jnp.float32,
        )
        for s in (0, 1)
    )
    low, high = (even + odd).astype(jnp.bfloat16), (even - odd).astype(jnp.bfloat16)
    middle = size_y // 2
    turned = []
    for h in range(near):
        span = slice(h * size_z, (h + 1) * size_z)
        both = [
            jnp.concatenate(
                [values[part * middle : (part + 1) * middle, span] for values in (low, high)], axis=0
            )
            for part in range(2)
        ]
        turned.append(jnp.concatenate(both, axis=1))
    result = jnp.dot(
        jnp.concatenate(turned, axis=0), table_z[...], preferred_element_type=jnp.float32
    ).astype(jnp.bfloat16)
    for h in range(near):
        total = jnp.zeros((size_y, size_z), jnp.float32)
        for part in range(2):
            values = result[h * size_y : (h + 1) * size_y, part * size_z : (part + 1) * size_z]
            wave[part, h] = values
            values = values.astype(jnp.float32)
            total += weights[0, part] * values * values
        density[h] = total.astype(jnp.bfloat16)

    used = [0] if groups == 1 else [0, 1 + (2 * i > last).astype(jnp.int32)]
    for group in used:
        places = ones_at(codes[group] - i * near * size_y, near * size_y, 1)
        gathered[group] += jnp.dot(places, result, preferred_element_type=jnp.float32)

    @pl.when(i == last)
    def _():
        for group in range(groups):
            for part in range(2):
                total = jnp.zeros((entries, lanes), jnp.float32)
                for q in range(halves):
                    start = part * size_z + q * lanes
                    total += jnp.where(
                        sides[group] == q, gathered[group, :, start : start + lanes], 0.0
                    )
                rows_out[group][part] = total.astype(jnp.bfloat16)


def make_field(slab, weights, bufs, table_y, table_z, codes, sides, planes, pieces, natural):
    size_z = bufs[0].shape[-1]
    size_y = table_y.shape[1]
    columns = size_y // pieces
    groups, entries, _ = codes.shape
    if natural:
        buf_spec = pl.BlockSpec((PLANES, 2 * columns, size_z), lambda i: (i, 0, 0))
        wide = pltpu.VMEM((pieces, PLANES, 2 * columns, size_z), jnp.bfloat16)
    else:
        buf_spec = whole(bufs[0].shape)
        wide = pltpu.VMEM((size_z // 128, (2 * planes + 1) * size_y, 128), jnp.float32)
    return pl.pallas_call(
        functools.partial(field_kernel, pieces=pieces, count=len(bufs), natural=natural),
        grid=(planes // PLANES,),
        in_specs=[SMEM_SPEC, SMEM_SPEC]
        + [whole(a.shape) for a in (table_y, table_z, codes, sides)]
        + [buf_spec] * len(bufs),
        out_specs=[
            pl.BlockSpec((2, PLANES, size_y, size_z), lambda i: (0, i, 0, 0)),
            pl.BlockSpec((PLANES, size_y, size_z), lambda i: (i, 0, 0)),
        ]
        + [whole((2, entries, 128))] * groups,
        out_shape=[
            jax.ShapeDtypeStruct((2, planes, size_y, size_z), jnp.bfloat16),
            jax.ShapeDtypeStruct((planes, size_y, size_z), jnp.bfloat16),
        ]
        + [jax.ShapeDtypeStruct((2, entries, 128), jnp.bfloat16)] * groups,
        scratch_shapes=[pltpu.VMEM((groups, entries, 2 * size_z), jnp.float32), wide],
        compiler_params=params(1),
        cost_estimate=cost(
            2 * planes * size_y * size_z * (size_y + size_z), 2 * planes * size_y * size_z
        ),
        name="make_field",
    )(slab, weights, table_y, table_z, codes, sides, *bufs)


def nonlocal_kernel(coupled, projectors, *refs):
    parts, (projections, spread) = refs[:-2], refs[-2:]
    atoms, nproj, blocks, cells = projectors.shape
    for atom in range(atoms):
        tables = [projectors[atom, j].astype(jnp.float32) for j in range(nproj)]
        place = pl.ds(atom * blocks, blocks)
        for part in range(2):
            rows = sum(p[part, place].astype(jnp.float32) for p in parts)
            tile = jnp.concatenate(
                [jnp.sum(t * rows, axis=0, keepdims=True) for t in tables], axis=0
            )
            mixed = jnp.zeros_like(tile)
            for j in range(nproj):
                mixed += coupled[j] * tile[j : j + 1]
            projections[atom, part] = jnp.broadcast_to(
                jnp.sum(tile, -1, keepdims=True), tile.shape
            )
            energy = jnp.broadcast_to(jnp.sum(mixed, -1, keepdims=True), tile.shape)
            spread[part, place] = sum(
                t * energy[j : j + 1] for j, t in enumerate(tables)
            ).astype(jnp.bfloat16)


def make_nonlocal(coupled, projectors, parts):
    atoms, nproj, _, cells = projectors.shape
    return pl.pallas_call(
        nonlocal_kernel,
        out_shape=[
            jax.ShapeDtypeStruct((atoms, 2, nproj, cells), jnp.float32),
            jax.ShapeDtypeStruct(parts[0].shape, jnp.bfloat16),
        ],
        name="make_nonlocal",
    )(coupled, projectors, *parts)


def back_kernel(slab, wave, potential, table_z, table_y, codes, sides, *refs, pieces, natural):
    groups, _, entries = codes.shape
    sources, outs = refs[:groups], refs[groups:-2]
    spread, tall = refs[-2:]
    outs = shifted(outs, slab[0])
    near, size_y, size_z = potential.shape
    lanes = 128
    halves = size_z // lanes
    i, last = pl.program_id(0), pl.num_programs(0) - 1
    planes = near * (last + 1)

    @pl.when(i == 0)
    def _():
        for group, source in enumerate(sources):
            for part in range(2):
                for q in range(halves):
                    start = part * size_z + q * lanes
                    spread[group, :, start : start + lanes] = jnp.where(
                        sides[group] == q, source[part].astype(jnp.float32), 0.0
                    ).astype(jnp.bfloat16)

    used = [0] if groups == 1 else [0, 1 + (2 * i > last).astype(jnp.int32)]
    extra = jnp.zeros((near * size_y, 2 * size_z), jnp.float32)
    for group in used:
        places = ones_at(codes[group] - i * near * size_y, near * size_y, 0)
        extra += jnp.dot(places, spread[group], preferred_element_type=jnp.float32)
    fields = []
    for h in range(near):
        local = potential[h].astype(jnp.float32)
        both = [
            local * wave[part, h].astype(jnp.float32)
            + extra[h * size_y : (h + 1) * size_y, part * size_z : (part + 1) * size_z]
            for part in range(2)
        ]
        fields.append(jnp.concatenate(both, axis=1).astype(jnp.bfloat16))
    back_z = jnp.dot(
        jnp.concatenate(fields, axis=0), table_z[...], preferred_element_type=jnp.float32
    )
    middle = size_y // 2
    folded = [[], []]
    for h in range(near):
        low = back_z[h * size_y : h * size_y + middle]
        high = back_z[h * size_y + middle : (h + 1) * size_y]
        for kept, values in zip(folded, (low + high, low - high)):
            values = values.astype(jnp.bfloat16)
            kept.append(jnp.concatenate([values[:, :size_z], values[:, size_z:]], axis=0))
    columns = size_y // pieces
    for s, kept in enumerate(folded):
        back_y = jnp.dot(
            table_y[s], jnp.concatenate(kept, axis=1), preferred_element_type=jnp.float32
        )
        if natural:
            back_y = back_y.astype(jnp.bfloat16)
            for h in range(near):
                tall[:, h, s * columns : (s + 1) * columns] = back_y[
                    :, h * size_z : (h + 1) * size_z
                ].reshape(pieces, columns, size_z)
            continue
        pitch = outs[0][1].shape[1] + 1
        for h in range(near):
            for part in range(2):
                for q in range(halves):
                    start = s * pitch + part * planes + i * near + h
                    lane = h * size_z + q * lanes
                    tall[q, pl.ds(start, middle, stride=2 * pitch), :] = back_y[
                        part * middle : (part + 1) * middle, lane : lane + lanes
                    ]

    if natural:
        for target, out in outs:
            out[...] = tall[target]
        return
    rows = outs[0][1].shape[1]

    @pl.when(i == last)
    def _():
        for target, out in outs:

            def narrow(column, carry):
                start = (target * columns + column) * pitch
                values = [tall[q, pl.ds(start, rows), :] for q in range(halves)]
                out[column] = jnp.concatenate(values, axis=1).astype(jnp.bfloat16)
                return carry

            lax.fori_loop(0, columns, narrow, 0, unroll=8)


def go_back(slab, wave, potential, table_z, table_y, codes, sides, sources, place, pieces, natural):
    _, planes, size_y, size_z = wave.shape
    columns = size_y // pieces
    groups, _, entries = codes.shape
    scratch = [pltpu.VMEM((groups, entries, 2 * size_z), jnp.bfloat16)]
    if natural:
        shape = (planes, 2 * columns, size_z)
        out_specs = [pl.BlockSpec((PLANES, 2 * columns, size_z), lambda i: (i, 0, 0))] * pieces
        scratch.append(pltpu.VMEM((pieces, PLANES, 2 * columns, size_z), jnp.bfloat16))
    else:
        shape = (columns, 2 * planes, size_z)
        out_specs = [whole(shape)] * pieces
        scratch.append(pltpu.VMEM((size_z // 128, (2 * planes + 1) * size_y, 128), jnp.float32))
    return pl.pallas_call(
        functools.partial(back_kernel, pieces=pieces, natural=natural),
        grid=(planes // PLANES,),
        in_specs=[
            SMEM_SPEC,
            pl.BlockSpec((2, PLANES, size_y, size_z), lambda i: (0, i, 0, 0)),
            pl.BlockSpec((PLANES, size_y, size_z), lambda i: (place(i), 0, 0)),
        ]
        + [whole(a.shape) for a in (table_z, table_y, codes, sides, *sources)],
        out_specs=out_specs,
        out_shape=[jax.ShapeDtypeStruct(shape, jnp.bfloat16)] * pieces,
        scratch_shapes=scratch,
        compiler_params=params(1),
        cost_estimate=cost(
            2 * planes * size_y * size_z * (size_y + size_z), 2 * planes * size_y * size_z
        ),
        name="go_back",
    )(slab, wave, potential, table_z, table_y, codes, sides, *sources)


def last_x_kernel(frequency_x, frequency_yz, table, coeffs, *refs):
    bufs, (out, tall) = refs[:-2], refs[-2:]
    parts, size_x, columns, lanes = coeffs.shape
    pitch = columns + 1

    def some_columns(g, carry):
        loaded = []
        for h in range(COLUMNS):
            loaded.append(jnp.concatenate([buf[COLUMNS * g + h] for buf in bufs], axis=0))
        for first in range(0, COLUMNS, FOUR):
            result = jnp.dot(
                table[...],
                jnp.concatenate(loaded[first : first + FOUR], axis=1),
                preferred_element_type=jnp.float32,
            )
            for h in range(FOUR):
                tall[pl.ds(COLUMNS * g + first + h, parts * size_x, stride=pitch), :] = result[
                    :, h * lanes : (h + 1) * lanes
                ]
        return carry

    lax.fori_loop(0, columns // COLUMNS, some_columns, 0)

    def finish(k, carry):
        kinetic = frequency_x[k] + frequency_yz[...]
        for part in range(parts):
            out[part, k] = (
                tall[pl.ds((part * size_x + k) * pitch, columns), :] + kinetic * coeffs[part, k].astype(jnp.float32)
            ).astype(jnp.bfloat16)
        return carry

    lax.fori_loop(0, size_x, finish, 0, unroll=8)


def last_x(frequency_x, frequency_yz, table, coeffs, bufs):
    _, size_x, columns, size_z = coeffs.shape
    lanes = size_z // 2
    spec = pl.BlockSpec((2, size_x, columns, lanes), lambda i: (0, 0, 0, i))
    return pl.pallas_call(
        last_x_kernel,
        grid=(2,),
        in_specs=[
            SMEM_SPEC,
            pl.BlockSpec((columns, lanes), lambda i: (0, i)),
            whole(table.shape),
            spec,
        ]
        + [pl.BlockSpec((*b.shape[:2], lanes), lambda i: (0, 0, i)) for b in bufs],
        out_specs=spec,
        out_shape=jax.ShapeDtypeStruct(coeffs.shape, jnp.bfloat16),
        scratch_shapes=[pltpu.VMEM((2 * size_x * (columns + 1), lanes), jnp.float32)],
        compiler_params=params(1),
        cost_estimate=cost(2 * size_x * size_x * columns * size_z, 3 * size_x * columns * size_z),
        name="last_x",
    )(frequency_x, frequency_yz, table, coeffs, *bufs)


def per_device_chunked(wave_coeffs, occupation, potential, projectors, coupling, sphere_blocks):
    pieces = lax.axis_size("fft")
    bands = lax.axis_size("band")
    slab = lax.axis_index("fft")
    coeffs = wave_coeffs[0]
    _, size_x, columns, size_z = coeffs.shape
    slab_planes, size_y, _ = potential.shape
    atom_dev, nproj, blocks, cells = projectors.shape
    zblocks = size_z // cells
    outer, inner = chunk_planes(slab_planes)
    up = [(i, (i + 1) % pieces) for i in range(pieces)]
    down = [(j, i) for i, j in up]

    order = ring_order(pieces)
    inverse_x, forward_x = (real_blocks(size_x, s) for s in (1.0, -1.0))
    inverse_y, forward_y = (real_blocks(size_y, s) for s in (1.0, -1.0))
    inverse_z, forward_z = (real_blocks(size_z, s) for s in (1.0, -1.0))
    place_outer, place_inner = (
        np.arange(pieces)[:, None] * slab_planes + np.array(chunk)[None, :]
        for chunk in (outer, inner)
    )
    table_x_outer = np.stack([inverse_x[r][place_outer] for r in range(2)], 1)
    table_x_inner = np.stack([inverse_x[r][place_inner] for r in range(2)], 1)
    tables_back_x = [
        np.stack([forward_x[:, :, r][:, :, place] for r in range(2)], 3).reshape(
            2 * size_x, pieces, -1
        )
        for place in (place_outer, place_inner)
    ]
    middle = size_y // 2
    down_y = [inverse_y[:, :middle, :, s::2] for s in (0, 1)]
    back_y = [forward_y[:, s::2, :, :middle] for s in (0, 1)]
    split = (pieces, columns // 2)
    tables = [
        table_x_outer.reshape(-1, 2 * size_x),
        table_x_inner.reshape(-1, 2 * size_x),
        np.stack([t.reshape(size_y, -1) for t in down_y]),
        np.stack(
            [t.reshape(2, middle, 2, *split).swapaxes(2, 3).reshape(size_y, -1) for t in down_y]
        ),
        inverse_z.transpose(2, 3, 0, 1).reshape(2 * size_z, -1),
        forward_z.transpose(2, 3, 0, 1).reshape(2 * size_z, -1),
        np.stack([t.reshape(size_y, -1) for t in back_y]),
        np.stack([t.reshape(2, *split, -1).swapaxes(0, 1).reshape(size_y, -1) for t in back_y]),
        np.stack(
            [
                np.concatenate(
                    [t[:, (d - np.array(order)) % pieces].reshape(2 * size_x, -1) for t in tables_back_x],
                    axis=1,
                )
                for d in range(pieces)
            ]
        ),
    ]
    (
        table_x_outer, table_x_inner, table_y_outer, table_y_inner, table_z,
        table_back_z, table_back_y_outer, table_back_y_inner, tables_back_x,
    ) = (jnp.asarray(t.astype(jnp.bfloat16)) for t in tables)

    table_back_x = lax.dynamic_index_in_dim(tables_back_x, slab, 0, keepdims=False)

    where = slab.reshape(1)
    section_outer = first_x(where, table_x_outer, coeffs, len(outer), pieces, False)
    section_outer, table_x_inner, sphere_blocks = lax.optimization_barrier(
        (section_outer, table_x_inner, sphere_blocks)
    )
    section_inner = first_x(where, table_x_inner, coeffs, len(inner), pieces, True)

    entries = atom_dev * blocks

    def codes_of(chunk, shift):
        owner = (slab + shift + pieces) % pieces
        numbers = lax.dynamic_slice_in_dim(sphere_blocks, owner * atom_dev, atom_dev, 0)
        plane = numbers // (size_y * zblocks) - slab * slab_planes
        rest = numbers % (size_y * zblocks)
        if chunk is outer:
            inside = ((plane >= 0) & (plane < EDGE)) | (
                (plane >= slab_planes - EDGE) & (plane < slab_planes)
            )
            plane = jnp.where(plane < EDGE, plane, plane - len(inner))
        else:
            inside = (plane >= EDGE) & (plane < slab_planes - EDGE)
            plane = plane - EDGE
        code = jnp.where(inside, plane * size_y + rest // zblocks, -1)
        return code.reshape(entries), (rest % zblocks).reshape(entries)

    found = [codes_of(outer, shift) for shift in (0, -1, 1)]
    codes_outer, sides_outer = (jnp.stack(values) for values in zip(*found))
    codes_inner, sides_inner = (values[None] for values in codes_of(inner, 0))
    sides_outer, sides_inner = sides_outer[:, :, None], sides_inner[:, :, None]
    rows_codes = [codes_outer[:, :, None], codes_inner[:, :, None]]
    lane_codes = [codes_outer[:, None, :], codes_inner[:, None, :]]
    strength = 3.0 * math.sqrt(cells * blocks) / nproj
    coupled = (coupling + coupling.T) * (0.5 * strength)
    coupled = jnp.broadcast_to(coupled.T[:, :, None], (nproj, nproj, cells))
    section_inner, rows_codes, lane_codes, sides_outer, sides_inner, coupled = (
        lax.optimization_barrier(
            (section_inner, rows_codes, lane_codes, sides_outer, sides_inner, coupled)
        )
    )

    half = pieces // 2
    near, far = list(range(1, half)), list(range(half, pieces))

    def send(block, k, *awaited):
        for row, m in awaited:
            block, row[m] = lax.optimization_barrier((block, row[m]))
        return lax.ppermute(block, "fft", [(j, j ^ k) for j in range(pieces)])

    received_outer, received_inner = (
        [section[0]] + [None] * (pieces - 1) for section in (section_outer, section_inner)
    )
    for partners in (near, far):
        queue = [(section_outer, received_outer, k) for k in partners]
        queue += [(section_inner, received_inner, k) for k in partners]
        for place, (section, received, k) in enumerate(queue):
            awaited = [queue[place - 2][1:]] if place >= 2 else []
            received[k] = send(section[k], k, *awaited)
    wave_outer, density_outer, rows_outer, to_previous, to_following = make_field(
        where, occupation, received_outer, table_y_outer, table_z, rows_codes[0],
        sides_outer, len(outer), pieces, False,
    )
    from_following = lax.ppermute(to_previous, "fft", down)
    from_previous = lax.ppermute(to_following, "fft", up)
    density_outer = lax.psum(density_outer, "band")
    wave_inner, density_inner, rows_inner = make_field(
        where, occupation, received_inner, table_y_inner, table_z, rows_codes[1],
        sides_inner, len(inner), pieces, True,
    )
    projected, spread = make_nonlocal(
        coupled, projectors, [rows_outer, rows_inner, from_following, from_previous]
    )
    spread_previous = lax.ppermute(spread, "fft", up)
    spread_following = lax.ppermute(spread, "fft", down)
    edge_steps = EDGE // PLANES
    inner_steps = len(inner) // PLANES
    back_inner = go_back(
        where, wave_inner, potential, table_back_z, table_back_y_inner, lane_codes[1],
        sides_inner, [spread], lambda i: i + edge_steps, pieces, True,
    )
    def permute_all(values):
        received = [values[0]]
        for k, block in zip(order[1:], values[1:]):
            pairs = [(j, (j + k) % pieces) for j in range(pieces)]
            received.append(lax.ppermute(block, "fft", pairs))
        return received

    back_inner = permute_all(back_inner)
    back_outer = go_back(
        where, wave_outer, potential, table_back_z, table_back_y_outer, lane_codes[0],
        sides_outer, [spread, spread_previous, spread_following],
        lambda i: jnp.where(i < edge_steps, i, i + inner_steps), pieces, False,
    )
    density_inner, density_outer = lax.optimization_barrier((density_inner, density_outer))
    density_inner = lax.psum(density_inner, "band")
    back_outer, density_outer = lax.optimization_barrier((back_outer, density_outer))
    back_outer = permute_all(back_outer)
    back_inner = [
        b.reshape(len(inner), 2, 2, columns // 2, size_z)
        .transpose(3, 1, 2, 0, 4)
        .reshape(columns, -1, size_z)
        for b in back_inner
    ]
    density = jnp.concatenate([density_outer[:EDGE], density_inner, density_outer[EDGE:]], axis=0)

    index_x = np.arange(size_x)
    frequency_x = jnp.asarray(
        (np.where(2 * index_x < size_x, index_x, index_x - size_x) / size_x) ** 2, jnp.float32
    )
    index_y = slab * columns + jnp.arange(columns, dtype=jnp.int32)
    index_z = jnp.arange(size_z, dtype=jnp.int32)
    frequency_yz = wave_squares(index_y, size_y)[:, None] + wave_squares(index_z, size_z)[None, :]
    coeffs, density, back_inner = lax.optimization_barrier((coeffs, density, back_inner))
    applied = last_x(frequency_x, frequency_yz, table_back_x, coeffs, back_outer + back_inner)
    return (applied[None], density, projected[None, :, :, :, 0])


def per_device(wave_coeffs, occupation, potential, projectors, coupling, sphere_blocks):
    pieces, bands = lax.axis_size("fft"), lax.axis_size("band")
    size_z = wave_coeffs.shape[4]
    columns = wave_coeffs.shape[3]
    slab_planes = potential.shape[0]
    chunked = (
        pieces >= 4
        and pieces & (pieces - 1) == 0
        and slab_planes % EDGE == 0
        and slab_planes >= 3 * EDGE
        and EDGE >= HALO
        and columns % 8 == 0
        and size_z % 256 == 0
        and projectors.shape[0] % bands == 0
        and projectors.shape[3] == 128
        and projectors.shape[1] == 8
    )
    chosen = per_device_chunked if chunked else per_device_plain
    return chosen(wave_coeffs, occupation, potential, projectors, coupling, sphere_blocks)


def solution(mesh):
    placed = (
        P("band", None, None, "fft", None),
        P("band", None),
        P("fft", None, None),
        P("fft", None, None, None),
        P(),
        P(),
    )
    return jax.shard_map(
        per_device,
        mesh=mesh,
        in_specs=placed,
        out_specs=(
            P("band", None, None, "fft", None),
            P("fft", None, None),
            P("band", "fft", None, None),
        ),
        check_vma=False,
    )
```

```python
import functools
import math

import jax
import jax.numpy as jnp
import numpy as np
from jax import lax
from jax.experimental import pallas as pl
from jax.experimental.pallas import tpu as pltpu
from jax.sharding import PartitionSpec as P

HALO = 6
EDGE = 8
PLANES = 4
COLUMNS = 8
FOUR = 4
VMEM_BYTES = 56 * 1024 * 1024


def extended(shard, sides, width):
    for axis, dim in sides:
        count, length = (lax.axis_size(axis), shard.shape[dim])
        up = [(i, (i + 1) % count) for i in range(count)]
        down = [(j, i) for i, j in up]
        last = lax.slice_in_dim(shard, length - width, length, axis=dim)
        first = lax.slice_in_dim(shard, 0, width, axis=dim)
        before = lax.ppermute(last, axis, up)
        after = lax.ppermute(first, axis, down)
        shard = jnp.concatenate([before, shard, after], axis=dim)
    return shard


def dft_table(length, sign_value):
    indices = jnp.arange(length, dtype=jnp.int32)
    phases = indices[:, None] * indices[None, :] % length
    angles = 2.0 * math.pi / length * phases.astype(jnp.float32)
    factor = 1.0 / math.sqrt(length)
    cosine = jnp.cos(angles) * factor
    sine_part = jnp.sin(angles) * (sign_value * factor)
    upper_rows = jnp.stack([cosine, -sine_part])
    bottom = jnp.stack([sine_part, cosine])
    return jnp.stack([upper_rows, bottom]).astype(jnp.bfloat16)


def wave_squares(indices, length):
    frequency = (
        jnp.where(2 * indices < length, indices, indices - length).astype(jnp.float32) / length
    )
    return frequency * frequency


def per_device_plain(wave_coeffs, occupation, potential, projectors, coupling, sphere_blocks):
    pieces = lax.axis_size("fft")
    slab_index = lax.axis_index("fft")
    coeffs = wave_coeffs[0]
    size_x = coeffs.shape[1]
    columns = coeffs.shape[2]
    size_z = coeffs.shape[3]
    slab_planes = potential.shape[0]
    size_y = potential.shape[1]
    atom_dev = projectors.shape[0]
    nproj_count = projectors.shape[1]
    block_cells = projectors.shape[3]
    zblocks = size_z // block_cells
    plane_blocks = size_y * zblocks
    total_atoms = atom_dev * pieces
    table_x = dft_table(size_x, 1.0).transpose(0, 2, 1, 3).reshape(2 * size_x, 2 * size_x)
    inverse_y = dft_table(size_y, 1.0)
    inverse_z = dft_table(size_z, 1.0)
    flattened = coeffs.reshape(2 * size_x, columns * size_z)
    along_x = jnp.dot(table_x, flattened, preferred_element_type=jnp.float32)
    along_x = along_x.reshape(2, size_x, columns, size_z).astype(jnp.bfloat16)
    along_y = jnp.einsum(
        "abyk,bxkz->axyz",
        inverse_y,
        lax.all_to_all(along_x, "fft", split_axis=1, concat_axis=2, tiled=True),
        preferred_element_type=jnp.float32,
    ).astype(jnp.bfloat16)
    wave_field = jnp.einsum(
        "abzk,bxyk->axyz", inverse_z, along_y, preferred_element_type=jnp.float32
    ).astype(jnp.bfloat16)
    weights = occupation[0]
    real_part = wave_field[0].astype(jnp.float32)
    imag_part = wave_field[1].astype(jnp.float32)
    partial_density = weights[0] * real_part * real_part + weights[1] * imag_part * imag_part
    density = lax.psum(partial_density.astype(jnp.bfloat16), "band")
    strength = 3.0 * math.sqrt(block_cells * projectors.shape[2]) / nproj_count
    coupled = (coupling + coupling.T) * (0.5 * strength)
    nearby = extended(projectors, (("fft", 0),), atom_dev)
    atom_rows = (
        slab_index * atom_dev - atom_dev + jnp.arange(3 * atom_dev, dtype=jnp.int32) + total_atoms
    ) % total_atoms
    near_blocks = sphere_blocks[atom_rows]
    plane_index = near_blocks // plane_blocks
    inside = plane_index // slab_planes == slab_index
    local_index = jnp.where(
        inside,
        (plane_index - slab_index * slab_planes) * plane_blocks + near_blocks % plane_blocks,
        0,
    )
    blocks_own = wave_field.reshape(2, slab_planes * plane_blocks, block_cells)
    gathered = blocks_own[:, local_index] * inside[None, :, :, None].astype(jnp.bfloat16)
    partial_value = jnp.einsum(
        "ajsk,bask->abj", nearby, gathered, preferred_element_type=jnp.float32
    )
    summed = extended(partial_value, (("fft", 0),), atom_dev)
    projections_own = (
        summed[:atom_dev] + summed[2 * atom_dev : 3 * atom_dev] + summed[4 * atom_dev :]
    )
    energy_own = jnp.einsum(
        "ij,abj->abi", coupled, projections_own, precision=lax.Precision.HIGHEST
    )
    energy = extended(energy_own, (("fft", 0),), atom_dev)
    spread = jnp.einsum(
        "ajsk,abj->bask", nearby.astype(jnp.float32), energy, precision=lax.Precision.HIGHEST
    )
    spread = spread * inside[None, :, :, None].astype(jnp.float32)
    accumulated = (
        jnp.zeros((2, slab_planes * plane_blocks, block_cells), jnp.float32)
        .at[:, local_index]
        .add(spread)
    )
    nonlocal_term = accumulated.reshape(2, slab_planes, size_y, size_z)
    total_field = (
        potential.astype(jnp.float32)[None] * wave_field.astype(jnp.float32) + nonlocal_term
    ).astype(jnp.bfloat16)
    forward_z = dft_table(size_z, -1.0)
    forward_y = dft_table(size_y, -1.0)
    forward_x = dft_table(size_x, -1.0)
    back_z = jnp.einsum(
        "abzk,bxyk->axyz", forward_z, total_field, preferred_element_type=jnp.float32
    ).astype(jnp.bfloat16)
    back_y = jnp.einsum(
        "abyk,bxkz->axyz", forward_y, back_z, preferred_element_type=jnp.float32
    ).astype(jnp.bfloat16)
    transformed = jnp.einsum(
        "abxk,bkyz->axyz",
        forward_x,
        lax.all_to_all(back_y, "fft", split_axis=2, concat_axis=1, tiled=True),
        preferred_element_type=jnp.float32,
    )
    index_x = jnp.arange(size_x, dtype=jnp.int32)
    index_y = slab_index * columns + jnp.arange(columns, dtype=jnp.int32)
    index_z = jnp.arange(size_z, dtype=jnp.int32)
    kinetic = (
        wave_squares(index_x, size_x)[:, None, None]
        + wave_squares(index_y, size_y)[None, :, None]
        + wave_squares(index_z, size_z)[None, None, :]
    )
    applied = (transformed + kinetic[None] * coeffs.astype(jnp.float32)).astype(jnp.bfloat16)
    return (applied[None], density, projections_own[None])


def real_blocks(length, sign):
    index = np.arange(length)
    angles = 2.0 * np.pi / length * (index[:, None] * index[None, :] % length)
    cosine = np.cos(angles) / np.sqrt(length)
    sine = sign * np.sin(angles) / np.sqrt(length)
    blocks = np.empty((2, length, 2, length))
    blocks[0, :, 0, :] = cosine
    blocks[1, :, 1, :] = cosine
    blocks[0, :, 1, :] = -sine
    blocks[1, :, 0, :] = sine
    return blocks


def chunk_planes(slab_planes):
    low, high = list(range(EDGE)), list(range(slab_planes - EDGE, slab_planes))
    return [low + high, list(range(EDGE, slab_planes - EDGE))]


def params(steps):
    return pltpu.CompilerParams(
        dimension_semantics=("arbitrary",) * steps, vmem_limit_bytes=VMEM_BYTES
    )


def cost(products, values):
    return pl.CostEstimate(flops=4 * products, bytes_accessed=4 * values, transcendentals=0)


def whole(shape):
    return pl.BlockSpec(shape, lambda i: (0,) * len(shape))


SMEM_SPEC = pl.BlockSpec(memory_space=pltpu.SMEM)


def paired(refs, slab):
    return [(lax.bitwise_xor(slab, jnp.int32(k)), ref) for k, ref in enumerate(refs)]


def ring_order(pieces):
    return [0] + sorted(range(1, pieces), key=lambda k: abs(k - pieces // 2))


def shifted(refs, slab):
    order = ring_order(len(refs))
    return [(lax.rem(slab + k, len(refs)), ref) for k, ref in zip(order, refs)]


def first_x_kernel(slab, table_ref, coeffs_ref, *refs, pieces, natural):
    scratch = 3 if natural else 2
    outs = paired(refs[:-scratch], slab[0])
    turned, wide, *tall = refs[-scratch:]
    parts, size_x, columns, lanes = coeffs_ref.shape
    rows = parts * size_x
    height = table_ref.shape[0] // pieces

    for k, (device, _) in enumerate(outs):
        start = pl.multiple_of(device * height, 16)
        turned[k * height : (k + 1) * height, :] = table_ref[pl.ds(start, height), :]

    pitch = columns + 1

    def widen(k, carry):
        for part in range(parts):
            wide[pl.ds((part * size_x + k) * pitch, columns), :] = coeffs_ref[part, k].astype(
                jnp.float32
            )
        return carry

    lax.fori_loop(0, size_x, widen, 0, unroll=8)

    def some_columns(g, carry):
        loaded = [
            wide[pl.ds(COLUMNS * g + h, rows, stride=pitch), :].astype(jnp.bfloat16)
            for h in range(COLUMNS)
        ]
        for first in range(0, COLUMNS, FOUR):
            result = jnp.dot(
                turned[...],
                jnp.concatenate(loaded[first : first + FOUR], axis=1),
                preferred_element_type=jnp.float32,
            )
            for h in range(FOUR):
                column = COLUMNS * g + first + h
                piece = result[:, h * lanes : (h + 1) * lanes]
                if natural:
                    place = (first + h) % 2 * columns + COLUMNS // 2 * g + (first + h) // 2
                    planes = height // 2
                    for k in range(pieces):
                        for part in range(2):
                            start = k * height * columns + part * (columns // 2) + place
                            row = k * height + part * planes
                            tall[0][pl.ds(start, planes, stride=2 * columns), :] = piece[
                                row : row + planes
                            ]
                else:
                    piece = piece.astype(jnp.bfloat16)
                    for k, (_, out) in enumerate(outs):
                        out[column] = piece[k * height : (k + 1) * height]
        return carry

    lax.fori_loop(0, columns // COLUMNS, some_columns, 0)
    if natural:
        for k, (_, out) in enumerate(outs):
            values = tall[0][k * height * columns : (k + 1) * height * columns, :]
            out[...] = values.astype(jnp.bfloat16).reshape(out.shape)


def first_x(slab, table, coeffs, planes, pieces, natural):
    _, size_x, columns, size_z = coeffs.shape
    lanes = size_z // 2
    shape = (planes, 2 * columns) if natural else (columns, 2 * planes)
    scratch = [
        pltpu.VMEM(table.shape, jnp.bfloat16),
        pltpu.VMEM((2 * size_x * (columns + 1), lanes), jnp.float32),
    ]
    if natural:
        scratch.append(pltpu.VMEM((2 * pieces * planes * columns, lanes), jnp.float32))
    out_specs = [pl.BlockSpec((*shape, lanes), lambda i: (0, 0, i))] * pieces
    out_shape = [jax.ShapeDtypeStruct((*shape, size_z), jnp.bfloat16)] * pieces
    return pl.pallas_call(
        functools.partial(first_x_kernel, pieces=pieces, natural=natural),
        grid=(2,),
        in_specs=[
            SMEM_SPEC,
            whole(table.shape),
            pl.BlockSpec((2, size_x, columns, lanes), lambda i: (0, 0, 0, i)),
        ],
        out_specs=out_specs,
        out_shape=out_shape,
        scratch_shapes=scratch,
        compiler_params=params(1),
        cost_estimate=cost(2 * size_x * pieces * planes * columns * size_z, 2 * size_x * columns * size_z),
        name="first_x",
    )(slab, table, coeffs)


def ones_at(codes, count, axis):
    shape = (codes.shape[0], count) if axis == 1 else (count, codes.shape[1])
    places = lax.broadcasted_iota(jnp.int32, shape, axis)
    return jnp.where(codes == places, 1.0, 0.0).astype(jnp.bfloat16)


def field_kernel(slab, weights, table_y, table_z, codes, sides, *refs, pieces, count, natural):
    bufs = paired(refs[:count], slab[0])
    wave, density, *rows_out, gathered, wide = refs[count:]
    _, near, size_y, size_z = wave.shape
    columns = size_y // pieces
    groups, entries, _ = codes.shape
    lanes = 128
    halves = size_z // lanes
    i, last = pl.program_id(0), pl.num_programs(0) - 1
    planes = near * (last + 1)

    @pl.when(i == 0)
    def _():
        gathered[...] = jnp.zeros_like(gathered)

    loaded = []
    if natural:
        for source, buf in bufs:
            wide[source] = buf[...]
        for h in range(near):
            loaded.append(
                [wide[:, h, s * columns : (s + 1) * columns].reshape(size_y, size_z) for s in (0, 1)]
            )
    else:
        rows = bufs[0][1].shape[1]
        pitch = rows + 1

        @pl.when(i == 0)
        def _():
            for source, buf in bufs:

                def widen(column, carry):
                    values = buf[column].astype(jnp.float32)
                    for q in range(halves):
                        wide[q, pl.ds((source * columns + column) * pitch, rows), :] = values[
                            :, q * lanes : (q + 1) * lanes
                        ]
                    return carry

                lax.fori_loop(0, columns, widen, 0, unroll=8)

        def strided(start):
            return jnp.concatenate(
                [
                    wide[q, pl.ds(start, size_y // 2, stride=2 * pitch), :]
                    for q in range(halves)
                ],
                axis=1,
            ).astype(jnp.bfloat16)

        for h in range(near):
            plane = i * near + h
            loaded.append(
                [
                    jnp.concatenate(
                        [strided(s * pitch + part * planes + plane) for part in range(2)], axis=0
                    )
                    for s in (0, 1)
                ]
            )
    even, odd = (
        jnp.dot(
            table_y[s],
            jnp.concatenate([pair[s] for pair in loaded], axis=1),
            preferred_element_type=jnp.float32,
        )
        for s in (0, 1)
    )
    low, high = (even + odd).astype(jnp.bfloat16), (even - odd).astype(jnp.bfloat16)
    middle = size_y // 2
    turned = []
    for h in range(near):
        span = slice(h * size_z, (h + 1) * size_z)
        both = [
            jnp.concatenate(
                [values[part * middle : (part + 1) * middle, span] for values in (low, high)], axis=0
            )
            for part in range(2)
        ]
        turned.append(jnp.concatenate(both, axis=1))
    result = jnp.dot(
        jnp.concatenate(turned, axis=0), table_z[...], preferred_element_type=jnp.float32
    ).astype(jnp.bfloat16)
    for h in range(near):
        total = jnp.zeros((size_y, size_z), jnp.float32)
        for part in range(2):
            values = result[h * size_y : (h + 1) * size_y, part * size_z : (part + 1) * size_z]
            wave[part, h] = values
            values = values.astype(jnp.float32)
            total += weights[0, part] * values * values
        density[h] = total.astype(jnp.bfloat16)

    used = [0] if groups == 1 else [0, 1 + (2 * i > last).astype(jnp.int32)]
    for group in used:
        places = ones_at(codes[group] - i * near * size_y, near * size_y, 1)
        gathered[group] += jnp.dot(places, result, preferred_element_type=jnp.float32)

    @pl.when(i == last)
    def _():
        for group in range(groups):
            for part in range(2):
                total = jnp.zeros((entries, lanes), jnp.float32)
                for q in range(halves):
                    start = part * size_z + q * lanes
                    total += jnp.where(
                        sides[group] == q, gathered[group, :, start : start + lanes], 0.0
                    )
                rows_out[group][part] = total.astype(jnp.bfloat16)


def make_field(slab, weights, bufs, table_y, table_z, codes, sides, planes, pieces, natural):
    size_z = bufs[0].shape[-1]
    size_y = table_y.shape[1]
    columns = size_y // pieces
    groups, entries, _ = codes.shape
    if natural:
        buf_spec = pl.BlockSpec((PLANES, 2 * columns, size_z), lambda i: (i, 0, 0))
        wide = pltpu.VMEM((pieces, PLANES, 2 * columns, size_z), jnp.bfloat16)
    else:
        buf_spec = whole(bufs[0].shape)
        wide = pltpu.VMEM((size_z // 128, (2 * planes + 1) * size_y, 128), jnp.float32)
    return pl.pallas_call(
        functools.partial(field_kernel, pieces=pieces, count=len(bufs), natural=natural),
        grid=(planes // PLANES,),
        in_specs=[SMEM_SPEC, SMEM_SPEC]
        + [whole(a.shape) for a in (table_y, table_z, codes, sides)]
        + [buf_spec] * len(bufs),
        out_specs=[
            pl.BlockSpec((2, PLANES, size_y, size_z), lambda i: (0, i, 0, 0)),
            pl.BlockSpec((PLANES, size_y, size_z), lambda i: (i, 0, 0)),
        ]
        + [whole((2, entries, 128))] * groups,
        out_shape=[
            jax.ShapeDtypeStruct((2, planes, size_y, size_z), jnp.bfloat16),
            jax.ShapeDtypeStruct((planes, size_y, size_z), jnp.bfloat16),
        ]
        + [jax.ShapeDtypeStruct((2, entries, 128), jnp.bfloat16)] * groups,
        scratch_shapes=[pltpu.VMEM((groups, entries, 2 * size_z), jnp.float32), wide],
        compiler_params=params(1),
        cost_estimate=cost(
            2 * planes * size_y * size_z * (size_y + size_z), 2 * planes * size_y * size_z
        ),
        name="make_field",
    )(slab, weights, table_y, table_z, codes, sides, *bufs)


def nonlocal_kernel(coupled, projectors, *refs):
    parts, (projections, spread) = refs[:-2], refs[-2:]
    atoms, nproj, blocks, cells = projectors.shape
    for atom in range(atoms):
        tables = [projectors[atom, j].astype(jnp.float32) for j in range(nproj)]
        place = pl.ds(atom * blocks, blocks)
        for part in range(2):
            rows = sum(p[part, place].astype(jnp.float32) for p in parts)
            tile = jnp.concatenate(
                [jnp.sum(t * rows, axis=0, keepdims=True) for t in tables], axis=0
            )
            mixed = jnp.zeros_like(tile)
            for j in range(nproj):
                mixed += coupled[j] * tile[j : j + 1]
            projections[atom, part] = jnp.broadcast_to(
                jnp.sum(tile, -1, keepdims=True), tile.shape
            )
            energy = jnp.broadcast_to(jnp.sum(mixed, -1, keepdims=True), tile.shape)
            spread[part, place] = sum(
                t * energy[j : j + 1] for j, t in enumerate(tables)
            ).astype(jnp.bfloat16)


def make_nonlocal(coupled, projectors, parts):
    atoms, nproj, _, cells = projectors.shape
    return pl.pallas_call(
        nonlocal_kernel,
        out_shape=[
            jax.ShapeDtypeStruct((atoms, 2, nproj, cells), jnp.float32),
            jax.ShapeDtypeStruct(parts[0].shape, jnp.bfloat16),
        ],
        name="make_nonlocal",
    )(coupled, projectors, *parts)


def back_kernel(slab, wave, potential, table_z, table_y, codes, sides, *refs, pieces, natural):
    groups, _, entries = codes.shape
    sources, outs = refs[:groups], refs[groups:-2]
    spread, tall = refs[-2:]
    outs = shifted(outs, slab[0])
    near, size_y, size_z = potential.shape
    lanes = 128
    halves = size_z // lanes
    i, last = pl.program_id(0), pl.num_programs(0) - 1
    planes = near * (last + 1)

    @pl.when(i == 0)
    def _():
        for group, source in enumerate(sources):
            for part in range(2):
                for q in range(halves):
                    start = part * size_z + q * lanes
                    spread[group, :, start : start + lanes] = jnp.where(
                        sides[group] == q, source[part].astype(jnp.float32), 0.0
                    ).astype(jnp.bfloat16)

    used = [0] if groups == 1 else [0, 1 + (2 * i > last).astype(jnp.int32)]
    extra = jnp.zeros((near * size_y, 2 * size_z), jnp.float32)
    for group in used:
        places = ones_at(codes[group] - i * near * size_y, near * size_y, 0)
        extra += jnp.dot(places, spread[group], preferred_element_type=jnp.float32)
    fields = []
    for h in range(near):
        local = potential[h].astype(jnp.float32)
        both = [
            local * wave[part, h].astype(jnp.float32)
            + extra[h * size_y : (h + 1) * size_y, part * size_z : (part + 1) * size_z]
            for part in range(2)
        ]
        fields.append(jnp.concatenate(both, axis=1).astype(jnp.bfloat16))
    back_z = jnp.dot(
        jnp.concatenate(fields, axis=0), table_z[...], preferred_element_type=jnp.float32
    )
    middle = size_y // 2
    folded = [[], []]
    for h in range(near):
        low = back_z[h * size_y : h * size_y + middle]
        high = back_z[h * size_y + middle : (h + 1) * size_y]
        for kept, values in zip(folded, (low + high, low - high)):
            values = values.astype(jnp.bfloat16)
            kept.append(jnp.concatenate([values[:, :size_z], values[:, size_z:]], axis=0))
    columns = size_y // pieces
    for s, kept in enumerate(folded):
        back_y = jnp.dot(
            table_y[s], jnp.concatenate(kept, axis=1), preferred_element_type=jnp.float32
        )
        if natural:
            back_y = back_y.astype(jnp.bfloat16)
            for h in range(near):
                tall[:, h, s * columns : (s + 1) * columns] = back_y[
                    :, h * size_z : (h + 1) * size_z
                ].reshape(pieces, columns, size_z)
            continue
        pitch = outs[0][1].shape[1] + 1
        for h in range(near):
            for part in range(2):
                for q in range(halves):
                    start = s * pitch + part * planes + i * near + h
                    lane = h * size_z + q * lanes
                    tall[q, pl.ds(start, middle, stride=2 * pitch), :] = back_y[
                        part * middle : (part + 1) * middle, lane : lane + lanes
                    ]

    if natural:
        for target, out in outs:
            out[...] = tall[target]
        return
    rows = outs[0][1].shape[1]

    @pl.when(i == last)
    def _():
        for target, out in outs:

            def narrow(column, carry):
                start = (target * columns + column) * pitch
                values = [tall[q, pl.ds(start, rows), :] for q in range(halves)]
                out[column] = jnp.concatenate(values, axis=1).astype(jnp.bfloat16)
                return carry

            lax.fori_loop(0, columns, narrow, 0, unroll=8)


def go_back(slab, wave, potential, table_z, table_y, codes, sides, sources, place, pieces, natural):
    _, planes, size_y, size_z = wave.shape
    columns = size_y // pieces
    groups, _, entries = codes.shape
    scratch = [pltpu.VMEM((groups, entries, 2 * size_z), jnp.bfloat16)]
    if natural:
        shape = (planes, 2 * columns, size_z)
        out_specs = [pl.BlockSpec((PLANES, 2 * columns, size_z), lambda i: (i, 0, 0))] * pieces
        scratch.append(pltpu.VMEM((pieces, PLANES, 2 * columns, size_z), jnp.bfloat16))
    else:
        shape = (columns, 2 * planes, size_z)
        out_specs = [whole(shape)] * pieces
        scratch.append(pltpu.VMEM((size_z // 128, (2 * planes + 1) * size_y, 128), jnp.float32))
    return pl.pallas_call(
        functools.partial(back_kernel, pieces=pieces, natural=natural),
        grid=(planes // PLANES,),
        in_specs=[
            SMEM_SPEC,
            pl.BlockSpec((2, PLANES, size_y, size_z), lambda i: (0, i, 0, 0)),
            pl.BlockSpec((PLANES, size_y, size_z), lambda i: (place(i), 0, 0)),
        ]
        + [whole(a.shape) for a in (table_z, table_y, codes, sides, *sources)],
        out_specs=out_specs,
        out_shape=[jax.ShapeDtypeStruct(shape, jnp.bfloat16)] * pieces,
        scratch_shapes=scratch,
        compiler_params=params(1),
        cost_estimate=cost(
            2 * planes * size_y * size_z * (size_y + size_z), 2 * planes * size_y * size_z
        ),
        name="go_back",
    )(slab, wave, potential, table_z, table_y, codes, sides, *sources)


def last_x_kernel(frequency_x, frequency_yz, table, coeffs, *refs):
    bufs, (out, tall) = refs[:-2], refs[-2:]
    parts, size_x, columns, lanes = coeffs.shape
    pitch = columns + 1

    def some_columns(g, carry):
        loaded = []
        for h in range(COLUMNS):
            loaded.append(jnp.concatenate([buf[COLUMNS * g + h] for buf in bufs], axis=0))
        for first in range(0, COLUMNS, FOUR):
            result = jnp.dot(
                table[...],
                jnp.concatenate(loaded[first : first + FOUR], axis=1),
                preferred_element_type=jnp.float32,
            )
            for h in range(FOUR):
                tall[pl.ds(COLUMNS * g + first + h, parts * size_x, stride=pitch), :] = result[
                    :, h * lanes : (h + 1) * lanes
                ]
        return carry

    lax.fori_loop(0, columns // COLUMNS, some_columns, 0)

    def finish(k, carry):
        kinetic = frequency_x[k] + frequency_yz[...]
        for part in range(parts):
            out[part, k] = (
                tall[pl.ds((part * size_x + k) * pitch, columns), :] + kinetic * coeffs[part, k].astype(jnp.float32)
            ).astype(jnp.bfloat16)
        return carry

    lax.fori_loop(0, size_x, finish, 0, unroll=8)


def last_x(frequency_x, frequency_yz, table, coeffs, bufs):
    _, size_x, columns, size_z = coeffs.shape
    lanes = size_z // 2
    spec = pl.BlockSpec((2, size_x, columns, lanes), lambda i: (0, 0, 0, i))
    return pl.pallas_call(
        last_x_kernel,
        grid=(2,),
        in_specs=[
            SMEM_SPEC,
            pl.BlockSpec((columns, lanes), lambda i: (0, i)),
            whole(table.shape),
            spec,
        ]
        + [pl.BlockSpec((*b.shape[:2], lanes), lambda i: (0, 0, i)) for b in bufs],
        out_specs=spec,
        out_shape=jax.ShapeDtypeStruct(coeffs.shape, jnp.bfloat16),
        scratch_shapes=[pltpu.VMEM((2 * size_x * (columns + 1), lanes), jnp.float32)],
        compiler_params=params(1),
        cost_estimate=cost(2 * size_x * size_x * columns * size_z, 3 * size_x * columns * size_z),
        name="last_x",
    )(frequency_x, frequency_yz, table, coeffs, *bufs)


def per_device_chunked(wave_coeffs, occupation, potential, projectors, coupling, sphere_blocks):
    pieces = lax.axis_size("fft")
    bands = lax.axis_size("band")
    slab = lax.axis_index("fft")
    coeffs = wave_coeffs[0]
    _, size_x, columns, size_z = coeffs.shape
    slab_planes, size_y, _ = potential.shape
    atom_dev, nproj, blocks, cells = projectors.shape
    zblocks = size_z // cells
    outer, inner = chunk_planes(slab_planes)
    up = [(i, (i + 1) % pieces) for i in range(pieces)]
    down = [(j, i) for i, j in up]

    order = ring_order(pieces)
    inverse_x, forward_x = (real_blocks(size_x, s) for s in (1.0, -1.0))
    inverse_y, forward_y = (real_blocks(size_y, s) for s in (1.0, -1.0))
    inverse_z, forward_z = (real_blocks(size_z, s) for s in (1.0, -1.0))
    place_outer, place_inner = (
        np.arange(pieces)[:, None] * slab_planes + np.array(chunk)[None, :]
        for chunk in (outer, inner)
    )
    table_x_outer = np.stack([inverse_x[r][place_outer] for r in range(2)], 1)
    table_x_inner = np.stack([inverse_x[r][place_inner] for r in range(2)], 1)
    tables_back_x = [
        np.stack([forward_x[:, :, r][:, :, place] for r in range(2)], 3).reshape(
            2 * size_x, pieces, -1
        )
        for place in (place_outer, place_inner)
    ]
    middle = size_y // 2
    down_y = [inverse_y[:, :middle, :, s::2] for s in (0, 1)]
    back_y = [forward_y[:, s::2, :, :middle] for s in (0, 1)]
    split = (pieces, columns // 2)
    tables = [
        table_x_outer.reshape(-1, 2 * size_x),
        table_x_inner.reshape(-1, 2 * size_x),
        np.stack([t.reshape(size_y, -1) for t in down_y]),
        np.stack(
            [t.reshape(2, middle, 2, *split).swapaxes(2, 3).reshape(size_y, -1) for t in down_y]
        ),
        inverse_z.transpose(2, 3, 0, 1).reshape(2 * size_z, -1),
        forward_z.transpose(2, 3, 0, 1).reshape(2 * size_z, -1),
        np.stack([t.reshape(size_y, -1) for t in back_y]),
        np.stack([t.reshape(2, *split, -1).swapaxes(0, 1).reshape(size_y, -1) for t in back_y]),
        np.stack(
            [
                np.concatenate(
                    [t[:, (d - np.array(order)) % pieces].reshape(2 * size_x, -1) for t in tables_back_x],
                    axis=1,
                )
                for d in range(pieces)
            ]
        ),
    ]
    (
        table_x_outer, table_x_inner, table_y_outer, table_y_inner, table_z,
        table_back_z, table_back_y_outer, table_back_y_inner, tables_back_x,
    ) = (jnp.asarray(t.astype(jnp.bfloat16)) for t in tables)

    table_back_x = lax.dynamic_index_in_dim(tables_back_x, slab, 0, keepdims=False)

    where = slab.reshape(1)
    section_outer = first_x(where, table_x_outer, coeffs, len(outer), pieces, False)
    section_outer, table_x_inner, sphere_blocks = lax.optimization_barrier(
        (section_outer, table_x_inner, sphere_blocks)
    )
    section_inner = first_x(where, table_x_inner, coeffs, len(inner), pieces, False)

    entries = atom_dev * blocks

    def codes_of(chunk, shift):
        owner = (slab + shift + pieces) % pieces
        numbers = lax.dynamic_slice_in_dim(sphere_blocks, owner * atom_dev, atom_dev, 0)
        plane = numbers // (size_y * zblocks) - slab * slab_planes
        rest = numbers % (size_y * zblocks)
        if chunk is outer:
            inside = ((plane >= 0) & (plane < EDGE)) | (
                (plane >= slab_planes - EDGE) & (plane < slab_planes)
            )
            plane = jnp.where(plane < EDGE, plane, plane - len(inner))
        else:
            inside = (plane >= EDGE) & (plane < slab_planes - EDGE)
            plane = plane - EDGE
        code = jnp.where(inside, plane * size_y + rest // zblocks, -1)
        return code.reshape(entries), (rest % zblocks).reshape(entries)

    found = [codes_of(outer, shift) for shift in (0, -1, 1)]
    codes_outer, sides_outer = (jnp.stack(values) for values in zip(*found))
    codes_inner, sides_inner = (values[None] for values in codes_of(inner, 0))
    sides_outer, sides_inner = sides_outer[:, :, None], sides_inner[:, :, None]
    rows_codes = [codes_outer[:, :, None], codes_inner[:, :, None]]
    lane_codes = [codes_outer[:, None, :], codes_inner[:, None, :]]
    strength = 3.0 * math.sqrt(cells * blocks) / nproj
    coupled = (coupling + coupling.T) * (0.5 * strength)
    coupled = jnp.broadcast_to(coupled.T[:, :, None], (nproj, nproj, cells))
    section_inner, rows_codes, lane_codes, sides_outer, sides_inner, coupled = (
        lax.optimization_barrier(
            (section_inner, rows_codes, lane_codes, sides_outer, sides_inner, coupled)
        )
    )

    half = pieces // 2
    near, far = list(range(1, half)), list(range(half, pieces))

    def send(block, k, *awaited):
        for row, m in awaited:
            block, row[m] = lax.optimization_barrier((block, row[m]))
        return lax.ppermute(block, "fft", [(j, j ^ k) for j in range(pieces)])

    received_outer, received_inner = (
        [section[0]] + [None] * (pieces - 1) for section in (section_outer, section_inner)
    )
    for partners in (near, far):
        queue = [(section_outer, received_outer, k) for k in partners]
        queue += [(section_inner, received_inner, k) for k in partners]
        for place, (section, received, k) in enumerate(queue):
            awaited = [queue[place - 2][1:]] if place >= 2 else []
            received[k] = send(section[k], k, *awaited)
    wave_outer, density_outer, rows_outer, to_previous, to_following = make_field(
        where, occupation, received_outer, table_y_outer, table_z, rows_codes[0],
        sides_outer, len(outer), pieces, False,
    )
    from_following = lax.ppermute(to_previous, "fft", down)
    from_previous = lax.ppermute(to_following, "fft", up)
    density_outer = lax.psum(density_outer, "band")
    wave_inner, density_inner, rows_inner = make_field(
        where, occupation, received_inner, table_y_outer, table_z, rows_codes[1],
        sides_inner, len(inner), pieces, False,
    )
    projected, spread = make_nonlocal(
        coupled, projectors, [rows_outer, rows_inner, from_following, from_previous]
    )
    spread_previous = lax.ppermute(spread, "fft", up)
    spread_following = lax.ppermute(spread, "fft", down)
    edge_steps = EDGE // PLANES
    inner_steps = len(inner) // PLANES
    back_inner = go_back(
        where, wave_inner, potential, table_back_z, table_back_y_outer, lane_codes[1],
        sides_inner, [spread], lambda i: i + edge_steps, pieces, False,
    )
    def permute_all(values):
        received = [values[0]]
        for k, block in zip(order[1:], values[1:]):
            pairs = [(j, (j + k) % pieces) for j in range(pieces)]
            received.append(lax.ppermute(block, "fft", pairs))
        return received

    back_inner = permute_all(back_inner)
    back_outer = go_back(
        where, wave_outer, potential, table_back_z, table_back_y_outer, lane_codes[0],
        sides_outer, [spread, spread_previous, spread_following],
        lambda i: jnp.where(i < edge_steps, i, i + inner_steps), pieces, False,
    )
    density_inner, density_outer = lax.optimization_barrier((density_inner, density_outer))
    density_inner = lax.psum(density_inner, "band")
    back_outer, density_outer = lax.optimization_barrier((back_outer, density_outer))
    back_outer = permute_all(back_outer)
    density = jnp.concatenate([density_outer[:EDGE], density_inner, density_outer[EDGE:]], axis=0)

    index_x = np.arange(size_x)
    frequency_x = jnp.asarray(
        (np.where(2 * index_x < size_x, index_x, index_x - size_x) / size_x) ** 2, jnp.float32
    )
    index_y = slab * columns + jnp.arange(columns, dtype=jnp.int32)
    index_z = jnp.arange(size_z, dtype=jnp.int32)
    frequency_yz = wave_squares(index_y, size_y)[:, None] + wave_squares(index_z, size_z)[None, :]
    coeffs, density, back_inner = lax.optimization_barrier((coeffs, density, back_inner))
    applied = last_x(frequency_x, frequency_yz, table_back_x, coeffs, back_outer + back_inner)
    return (applied[None], density, projected[None, :, :, :, 0])


def per_device(wave_coeffs, occupation, potential, projectors, coupling, sphere_blocks):
    pieces, bands = lax.axis_size("fft"), lax.axis_size("band")
    size_z = wave_coeffs.shape[4]
    columns = wave_coeffs.shape[3]
    slab_planes = potential.shape[0]
    chunked = (
        pieces >= 4
        and pieces & (pieces - 1) == 0
        and slab_planes % EDGE == 0
        and slab_planes >= 3 * EDGE
        and EDGE >= HALO
        and columns % 8 == 0
        and size_z % 256 == 0
        and projectors.shape[0] % bands == 0
        and projectors.shape[3] == 128
        and projectors.shape[1] == 8
    )
    chosen = per_device_chunked if chunked else per_device_plain
    return chosen(wave_coeffs, occupation, potential, projectors, coupling, sphere_blocks)


def solution(mesh):
    placed = (
        P("band", None, None, "fft", None),
        P("band", None),
        P("fft", None, None),
        P("fft", None, None, None),
        P(),
        P(),
    )
    return jax.shard_map(
        per_device,
        mesh=mesh,
        in_specs=placed,
        out_specs=(
            P("band", None, None, "fft", None),
            P("fft", None, None),
            P("band", "fft", None, None),
        ),
        check_vma=False,
    )
```

```python
import functools
import math

import jax
import jax.numpy as jnp
import numpy as np
from jax import lax
from jax.experimental import pallas as pl
from jax.experimental.pallas import tpu as pltpu
from jax.sharding import PartitionSpec as P

HALO = 6
EDGE = 8
PLANES = 4
COLUMNS = 8
FOUR = 4
VMEM_BYTES = 56 * 1024 * 1024


def extended(shard, sides, width):
    for axis, dim in sides:
        count, length = (lax.axis_size(axis), shard.shape[dim])
        up = [(i, (i + 1) % count) for i in range(count)]
        down = [(j, i) for i, j in up]
        last = lax.slice_in_dim(shard, length - width, length, axis=dim)
        first = lax.slice_in_dim(shard, 0, width, axis=dim)
        before = lax.ppermute(last, axis, up)
        after = lax.ppermute(first, axis, down)
        shard = jnp.concatenate([before, shard, after], axis=dim)
    return shard


def dft_table(length, sign_value):
    indices = jnp.arange(length, dtype=jnp.int32)
    phases = indices[:, None] * indices[None, :] % length
    angles = 2.0 * math.pi / length * phases.astype(jnp.float32)
    factor = 1.0 / math.sqrt(length)
    cosine = jnp.cos(angles) * factor
    sine_part = jnp.sin(angles) * (sign_value * factor)
    upper_rows = jnp.stack([cosine, -sine_part])
    bottom = jnp.stack([sine_part, cosine])
    return jnp.stack([upper_rows, bottom]).astype(jnp.bfloat16)


def wave_squares(indices, length):
    frequency = (
        jnp.where(2 * indices < length, indices, indices - length).astype(jnp.float32) / length
    )
    return frequency * frequency


def per_device_plain(wave_coeffs, occupation, potential, projectors, coupling, sphere_blocks):
    pieces = lax.axis_size("fft")
    slab_index = lax.axis_index("fft")
    coeffs = wave_coeffs[0]
    size_x = coeffs.shape[1]
    columns = coeffs.shape[2]
    size_z = coeffs.shape[3]
    slab_planes = potential.shape[0]
    size_y = potential.shape[1]
    atom_dev = projectors.shape[0]
    nproj_count = projectors.shape[1]
    block_cells = projectors.shape[3]
    zblocks = size_z // block_cells
    plane_blocks = size_y * zblocks
    total_atoms = atom_dev * pieces
    table_x = dft_table(size_x, 1.0).transpose(0, 2, 1, 3).reshape(2 * size_x, 2 * size_x)
    inverse_y = dft_table(size_y, 1.0)
    inverse_z = dft_table(size_z, 1.0)
    flattened = coeffs.reshape(2 * size_x, columns * size_z)
    along_x = jnp.dot(table_x, flattened, preferred_element_type=jnp.float32)
    along_x = along_x.reshape(2, size_x, columns, size_z).astype(jnp.bfloat16)
    along_y = jnp.einsum(
        "abyk,bxkz->axyz",
        inverse_y,
        lax.all_to_all(along_x, "fft", split_axis=1, concat_axis=2, tiled=True),
        preferred_element_type=jnp.float32,
    ).astype(jnp.bfloat16)
    wave_field = jnp.einsum(
        "abzk,bxyk->axyz", inverse_z, along_y, preferred_element_type=jnp.float32
    ).astype(jnp.bfloat16)
    weights = occupation[0]
    real_part = wave_field[0].astype(jnp.float32)
    imag_part = wave_field[1].astype(jnp.float32)
    partial_density = weights[0] * real_part * real_part + weights[1] * imag_part * imag_part
    density = lax.psum(partial_density.astype(jnp.bfloat16), "band")
    strength = 3.0 * math.sqrt(block_cells * projectors.shape[2]) / nproj_count
    coupled = (coupling + coupling.T) * (0.5 * strength)
    nearby = extended(projectors, (("fft", 0),), atom_dev)
    atom_rows = (
        slab_index * atom_dev - atom_dev + jnp.arange(3 * atom_dev, dtype=jnp.int32) + total_atoms
    ) % total_atoms
    near_blocks = sphere_blocks[atom_rows]
    plane_index = near_blocks // plane_blocks
    inside = plane_index // slab_planes == slab_index
    local_index = jnp.where(
        inside,
        (plane_index - slab_index * slab_planes) * plane_blocks + near_blocks % plane_blocks,
        0,
    )
    blocks_own = wave_field.reshape(2, slab_planes * plane_blocks, block_cells)
    gathered = blocks_own[:, local_index] * inside[None, :, :, None].astype(jnp.bfloat16)
    partial_value = jnp.einsum(
        "ajsk,bask->abj", nearby, gathered, preferred_element_type=jnp.float32
    )
    summed = extended(partial_value, (("fft", 0),), atom_dev)
    projections_own = (
        summed[:atom_dev] + summed[2 * atom_dev : 3 * atom_dev] + summed[4 * atom_dev :]
    )
    energy_own = jnp.einsum(
        "ij,abj->abi", coupled, projections_own, precision=lax.Precision.HIGHEST
    )
    energy = extended(energy_own, (("fft", 0),), atom_dev)
    spread = jnp.einsum(
        "ajsk,abj->bask", nearby.astype(jnp.float32), energy, precision=lax.Precision.HIGHEST
    )
    spread = spread * inside[None, :, :, None].astype(jnp.float32)
    accumulated = (
        jnp.zeros((2, slab_planes * plane_blocks, block_cells), jnp.float32)
        .at[:, local_index]
        .add(spread)
    )
    nonlocal_term = accumulated.reshape(2, slab_planes, size_y, size_z)
    total_field = (
        potential.astype(jnp.float32)[None] * wave_field.astype(jnp.float32) + nonlocal_term
    ).astype(jnp.bfloat16)
    forward_z = dft_table(size_z, -1.0)
    forward_y = dft_table(size_y, -1.0)
    forward_x = dft_table(size_x, -1.0)
    back_z = jnp.einsum(
        "abzk,bxyk->axyz", forward_z, total_field, preferred_element_type=jnp.float32
    ).astype(jnp.bfloat16)
    back_y = jnp.einsum(
        "abyk,bxkz->axyz", forward_y, back_z, preferred_element_type=jnp.float32
    ).astype(jnp.bfloat16)
    transformed = jnp.einsum(
        "abxk,bkyz->axyz",
        forward_x,
        lax.all_to_all(back_y, "fft", split_axis=2, concat_axis=1, tiled=True),
        preferred_element_type=jnp.float32,
    )
    index_x = jnp.arange(size_x, dtype=jnp.int32)
    index_y = slab_index * columns + jnp.arange(columns, dtype=jnp.int32)
    index_z = jnp.arange(size_z, dtype=jnp.int32)
    kinetic = (
        wave_squares(index_x, size_x)[:, None, None]
        + wave_squares(index_y, size_y)[None, :, None]
        + wave_squares(index_z, size_z)[None, None, :]
    )
    applied = (transformed + kinetic[None] * coeffs.astype(jnp.float32)).astype(jnp.bfloat16)
    return (applied[None], density, projections_own[None])


def real_blocks(length, sign):
    index = np.arange(length)
    angles = 2.0 * np.pi / length * (index[:, None] * index[None, :] % length)
    cosine = np.cos(angles) / np.sqrt(length)
    sine = sign * np.sin(angles) / np.sqrt(length)
    blocks = np.empty((2, length, 2, length))
    blocks[0, :, 0, :] = cosine
    blocks[1, :, 1, :] = cosine
    blocks[0, :, 1, :] = -sine
    blocks[1, :, 0, :] = sine
    return blocks


def chunk_planes(slab_planes):
    low, high = list(range(EDGE)), list(range(slab_planes - EDGE, slab_planes))
    return [low + high, list(range(EDGE, slab_planes - EDGE))]


def params(steps):
    return pltpu.CompilerParams(
        dimension_semantics=("arbitrary",) * steps, vmem_limit_bytes=VMEM_BYTES
    )


def cost(products, values):
    return pl.CostEstimate(flops=4 * products, bytes_accessed=4 * values, transcendentals=0)


def whole(shape):
    return pl.BlockSpec(shape, lambda i: (0,) * len(shape))


SMEM_SPEC = pl.BlockSpec(memory_space=pltpu.SMEM)


def paired(refs, slab):
    return [(lax.bitwise_xor(slab, jnp.int32(k)), ref) for k, ref in enumerate(refs)]


def ring_order(pieces):
    return [0] + sorted(range(1, pieces), key=lambda k: abs(k - pieces // 2))


def shifted(refs, slab):
    order = ring_order(len(refs))
    return [(lax.rem(slab + k, len(refs)), ref) for k, ref in zip(order, refs)]


def first_x_kernel(slab, table_ref, coeffs_ref, *refs, pieces, natural):
    scratch = 3 if natural else 2
    outs = paired(refs[:-scratch], slab[0])
    turned, wide, *tall = refs[-scratch:]
    parts, size_x, columns, lanes = coeffs_ref.shape
    rows = parts * size_x
    height = table_ref.shape[0] // pieces

    for k, (device, _) in enumerate(outs):
        start = pl.multiple_of(device * height, 16)
        turned[k * height : (k + 1) * height, :] = table_ref[pl.ds(start, height), :]

    pitch = columns + 1

    def widen(k, carry):
        for part in range(parts):
            wide[pl.ds((part * size_x + k) * pitch, columns), :] = coeffs_ref[part, k].astype(
                jnp.float32
            )
        return carry

    lax.fori_loop(0, size_x, widen, 0, unroll=8)

    def some_columns(g, carry):
        loaded = [
            wide[pl.ds(COLUMNS * g + h, rows, stride=pitch), :].astype(jnp.bfloat16)
            for h in range(COLUMNS)
        ]
        for first in range(0, COLUMNS, FOUR):
            result = jnp.dot(
                turned[...],
                jnp.concatenate(loaded[first : first + FOUR], axis=1),
                preferred_element_type=jnp.float32,
            )
            for h in range(FOUR):
                column = COLUMNS * g + first + h
                piece = result[:, h * lanes : (h + 1) * lanes]
                if natural:
                    place = (first + h) % 2 * columns + COLUMNS // 2 * g + (first + h) // 2
                    planes = height // 2
                    for k in range(pieces):
                        for part in range(2):
                            start = k * height * columns + part * (columns // 2) + place
                            row = k * height + part * planes
                            tall[0][pl.ds(start, planes, stride=2 * columns), :] = piece[
                                row : row + planes
                            ]
                else:
                    piece = piece.astype(jnp.bfloat16)
                    for k, (_, out) in enumerate(outs):
                        out[column] = piece[k * height : (k + 1) * height]
        return carry

    lax.fori_loop(0, columns // COLUMNS, some_columns, 0)
    if natural:
        for k, (_, out) in enumerate(outs):
            values = tall[0][k * height * columns : (k + 1) * height * columns, :]
            out[...] = values.astype(jnp.bfloat16).reshape(out.shape)


def first_x(slab, table, coeffs, planes, pieces, natural):
    _, size_x, columns, size_z = coeffs.shape
    lanes = size_z // 2
    shape = (planes, 2 * columns) if natural else (columns, 2 * planes)
    scratch = [
        pltpu.VMEM(table.shape, jnp.bfloat16),
        pltpu.VMEM((2 * size_x * (columns + 1), lanes), jnp.float32),
    ]
    if natural:
        scratch.append(pltpu.VMEM((2 * pieces * planes * columns, lanes), jnp.float32))
    out_specs = [pl.BlockSpec((*shape, lanes), lambda i: (0, 0, i))] * pieces
    out_shape = [jax.ShapeDtypeStruct((*shape, size_z), jnp.bfloat16)] * pieces
    return pl.pallas_call(
        functools.partial(first_x_kernel, pieces=pieces, natural=natural),
        grid=(2,),
        in_specs=[
            SMEM_SPEC,
            whole(table.shape),
            pl.BlockSpec((2, size_x, columns, lanes), lambda i: (0, 0, 0, i)),
        ],
        out_specs=out_specs,
        out_shape=out_shape,
        scratch_shapes=scratch,
        compiler_params=params(1),
        cost_estimate=cost(2 * size_x * pieces * planes * columns * size_z, 2 * size_x * columns * size_z),
        name="first_x",
    )(slab, table, coeffs)


def ones_at(codes, count, axis):
    shape = (codes.shape[0], count) if axis == 1 else (count, codes.shape[1])
    places = lax.broadcasted_iota(jnp.int32, shape, axis)
    return jnp.where(codes == places, 1.0, 0.0).astype(jnp.bfloat16)


def field_kernel(slab, weights, table_y, table_z, codes, sides, *refs, pieces, count, natural):
    bufs = paired(refs[:count], slab[0])
    wave, density, *rows_out, gathered, wide = refs[count:]
    _, near, size_y, size_z = wave.shape
    columns = size_y // pieces
    groups, entries, _ = codes.shape
    lanes = 128
    halves = size_z // lanes
    i, last = pl.program_id(0), pl.num_programs(0) - 1
    planes = near * (last + 1)

    @pl.when(i == 0)
    def _():
        gathered[...] = jnp.zeros_like(gathered)

    loaded = []
    if natural:
        for source, buf in bufs:
            wide[source] = buf[...]
        for h in range(near):
            loaded.append(
                [wide[:, h, s * columns : (s + 1) * columns].reshape(size_y, size_z) for s in (0, 1)]
            )
    else:
        rows = bufs[0][1].shape[1]
        pitch = rows + 1

        @pl.when(i == 0)
        def _():
            for source, buf in bufs:

                def widen(column, carry):
                    values = buf[column].astype(jnp.float32)
                    for q in range(halves):
                        wide[q, pl.ds((source * columns + column) * pitch, rows), :] = values[
                            :, q * lanes : (q + 1) * lanes
                        ]
                    return carry

                lax.fori_loop(0, columns, widen, 0, unroll=8)

        def strided(start):
            return jnp.concatenate(
                [
                    wide[q, pl.ds(start, size_y // 2, stride=2 * pitch), :]
                    for q in range(halves)
                ],
                axis=1,
            ).astype(jnp.bfloat16)

        for h in range(near):
            plane = i * near + h
            loaded.append(
                [
                    jnp.concatenate(
                        [strided(s * pitch + part * planes + plane) for part in range(2)], axis=0
                    )
                    for s in (0, 1)
                ]
            )
    even, odd = (
        jnp.dot(
            table_y[s],
            jnp.concatenate([pair[s] for pair in loaded], axis=1),
            preferred_element_type=jnp.float32,
        )
        for s in (0, 1)
    )
    low, high = (even + odd).astype(jnp.bfloat16), (even - odd).astype(jnp.bfloat16)
    middle = size_y // 2
    turned = []
    for h in range(near):
        span = slice(h * size_z, (h + 1) * size_z)
        both = [
            jnp.concatenate(
                [values[part * middle : (part + 1) * middle, span] for values in (low, high)], axis=0
            )
            for part in range(2)
        ]
        turned.append(jnp.concatenate(both, axis=1))
    result = jnp.dot(
        jnp.concatenate(turned, axis=0), table_z[...], preferred_element_type=jnp.float32
    ).astype(jnp.bfloat16)
    for h in range(near):
        total = jnp.zeros((size_y, size_z), jnp.float32)
        for part in range(2):
            values = result[h * size_y : (h + 1) * size_y, part * size_z : (part + 1) * size_z]
            wave[part, h] = values
            values = values.astype(jnp.float32)
            total += weights[0, part] * values * values
        density[h] = total.astype(jnp.bfloat16)

    used = [0] if groups == 1 else [0, 1 + (2 * i > last).astype(jnp.int32)]
    for group in used:
        places = ones_at(codes[group][:, :1] - i * near * size_y, near * size_y, 1)
        gathered[group] += jnp.dot(places, result, preferred_element_type=jnp.float32)

    @pl.when(i == last)
    def _():
        for group in range(groups):
            for part in range(2):
                total = jnp.zeros((entries, lanes), jnp.float32)
                for q in range(halves):
                    start = part * size_z + q * lanes
                    total += jnp.where(
                        sides[group] == q, gathered[group, :, start : start + lanes], 0.0
                    )
                rows_out[group][part] = total.astype(jnp.bfloat16)


def make_field(slab, weights, bufs, table_y, table_z, codes, sides, planes, pieces, natural):
    size_z = bufs[0].shape[-1]
    size_y = table_y.shape[1]
    columns = size_y // pieces
    groups, entries, _ = codes.shape
    if natural:
        buf_spec = pl.BlockSpec((PLANES, 2 * columns, size_z), lambda i: (i, 0, 0))
        wide = pltpu.VMEM((pieces, PLANES, 2 * columns, size_z), jnp.bfloat16)
    else:
        buf_spec = whole(bufs[0].shape)
        wide = pltpu.VMEM((size_z // 128, (2 * planes + 1) * size_y, 128), jnp.float32)
    return pl.pallas_call(
        functools.partial(field_kernel, pieces=pieces, count=len(bufs), natural=natural),
        grid=(planes // PLANES,),
        in_specs=[SMEM_SPEC, SMEM_SPEC]
        + [whole(a.shape) for a in (table_y, table_z, codes, sides)]
        + [buf_spec] * len(bufs),
        out_specs=[
            pl.BlockSpec((2, PLANES, size_y, size_z), lambda i: (0, i, 0, 0)),
            pl.BlockSpec((PLANES, size_y, size_z), lambda i: (i, 0, 0)),
        ]
        + [whole((2, entries, 128))] * groups,
        out_shape=[
            jax.ShapeDtypeStruct((2, planes, size_y, size_z), jnp.bfloat16),
            jax.ShapeDtypeStruct((planes, size_y, size_z), jnp.bfloat16),
        ]
        + [jax.ShapeDtypeStruct((2, entries, 128), jnp.bfloat16)] * groups,
        scratch_shapes=[pltpu.VMEM((groups, entries, 2 * size_z), jnp.float32), wide],
        compiler_params=params(1),
        cost_estimate=cost(
            2 * planes * size_y * size_z * (size_y + size_z), 2 * planes * size_y * size_z
        ),
        name="make_field",
    )(slab, weights, table_y, table_z, codes, sides, *bufs)


def nonlocal_kernel(coupled, projectors, *refs):
    parts, (projections, spread) = refs[:-2], refs[-2:]
    atoms, nproj, blocks, cells = projectors.shape
    for atom in range(atoms):
        tables = [projectors[atom, j].astype(jnp.float32) for j in range(nproj)]
        place = pl.ds(atom * blocks, blocks)
        for part in range(2):
            rows = sum(p[part, place].astype(jnp.float32) for p in parts)
            tile = jnp.concatenate(
                [jnp.sum(t * rows, axis=0, keepdims=True) for t in tables], axis=0
            )
            mixed = jnp.zeros_like(tile)
            for j in range(nproj):
                mixed += coupled[j] * tile[j : j + 1]
            projections[atom, part] = jnp.broadcast_to(
                jnp.sum(tile, -1, keepdims=True), tile.shape
            )
            energy = jnp.broadcast_to(jnp.sum(mixed, -1, keepdims=True), tile.shape)
            spread[part, place] = sum(
                t * energy[j : j + 1] for j, t in enumerate(tables)
            ).astype(jnp.bfloat16)


def make_nonlocal(coupled, projectors, parts):
    atoms, nproj, _, cells = projectors.shape
    return pl.pallas_call(
        nonlocal_kernel,
        out_shape=[
            jax.ShapeDtypeStruct((atoms, 2, nproj, cells), jnp.float32),
            jax.ShapeDtypeStruct(parts[0].shape, jnp.bfloat16),
        ],
        name="make_nonlocal",
    )(coupled, projectors, *parts)


def back_kernel(slab, wave, potential, table_z, table_y, codes, sides, *refs, pieces, natural):
    groups, _, entries = codes.shape
    sources, outs = refs[:groups], refs[groups:-2]
    spread, tall = refs[-2:]
    outs = shifted(outs, slab[0])
    near, size_y, size_z = potential.shape
    lanes = 128
    halves = size_z // lanes
    i, last = pl.program_id(0), pl.num_programs(0) - 1
    planes = near * (last + 1)

    @pl.when(i == 0)
    def _():
        for group, source in enumerate(sources):
            for part in range(2):
                for q in range(halves):
                    start = part * size_z + q * lanes
                    spread[group, :, start : start + lanes] = jnp.where(
                        sides[group] == q, source[part].astype(jnp.float32), 0.0
                    ).astype(jnp.bfloat16)

    used = [0] if groups == 1 else [0, 1 + (2 * i > last).astype(jnp.int32)]
    extra = jnp.zeros((near * size_y, 2 * size_z), jnp.float32)
    for group in used:
        places = ones_at(codes[group] - i * near * size_y, near * size_y, 0)
        extra += jnp.dot(places, spread[group], preferred_element_type=jnp.float32)
    fields = []
    for h in range(near):
        local = potential[h].astype(jnp.float32)
        both = [
            local * wave[part, h].astype(jnp.float32)
            + extra[h * size_y : (h + 1) * size_y, part * size_z : (part + 1) * size_z]
            for part in range(2)
        ]
        fields.append(jnp.concatenate(both, axis=1).astype(jnp.bfloat16))
    back_z = jnp.dot(
        jnp.concatenate(fields, axis=0), table_z[...], preferred_element_type=jnp.float32
    )
    middle = size_y // 2
    folded = [[], []]
    for h in range(near):
        low = back_z[h * size_y : h * size_y + middle]
        high = back_z[h * size_y + middle : (h + 1) * size_y]
        for kept, values in zip(folded, (low + high, low - high)):
            values = values.astype(jnp.bfloat16)
            kept.append(jnp.concatenate([values[:, :size_z], values[:, size_z:]], axis=0))
    columns = size_y // pieces
    for s, kept in enumerate(folded):
        back_y = jnp.dot(
            table_y[s], jnp.concatenate(kept, axis=1), preferred_element_type=jnp.float32
        )
        if natural:
            back_y = back_y.astype(jnp.bfloat16)
            for h in range(near):
                tall[:, h, s * columns : (s + 1) * columns] = back_y[
                    :, h * size_z : (h + 1) * size_z
                ].reshape(pieces, columns, size_z)
            continue
        pitch = outs[0][1].shape[1] + 1
        for h in range(near):
            for part in range(2):
                for q in range(halves):
                    start = s * pitch + part * planes + i * near + h
                    lane = h * size_z + q * lanes
                    tall[q, pl.ds(start, middle, stride=2 * pitch), :] = back_y[
                        part * middle : (part + 1) * middle, lane : lane + lanes
                    ]

    if natural:
        for target, out in outs:
            out[...] = tall[target]
        return
    rows = outs[0][1].shape[1]

    @pl.when(i == last)
    def _():
        for target, out in outs:

            def narrow(column, carry):
                start = (target * columns + column) * pitch
                values = [tall[q, pl.ds(start, rows), :] for q in range(halves)]
                out[column] = jnp.concatenate(values, axis=1).astype(jnp.bfloat16)
                return carry

            lax.fori_loop(0, columns, narrow, 0, unroll=8)


def go_back(slab, wave, potential, table_z, table_y, codes, sides, sources, place, pieces, natural):
    _, planes, size_y, size_z = wave.shape
    columns = size_y // pieces
    groups, _, entries = codes.shape
    scratch = [pltpu.VMEM((groups, entries, 2 * size_z), jnp.bfloat16)]
    if natural:
        shape = (planes, 2 * columns, size_z)
        out_specs = [pl.BlockSpec((PLANES, 2 * columns, size_z), lambda i: (i, 0, 0))] * pieces
        scratch.append(pltpu.VMEM((pieces, PLANES, 2 * columns, size_z), jnp.bfloat16))
    else:
        shape = (columns, 2 * planes, size_z)
        out_specs = [whole(shape)] * pieces
        scratch.append(pltpu.VMEM((size_z // 128, (2 * planes + 1) * size_y, 128), jnp.float32))
    return pl.pallas_call(
        functools.partial(back_kernel, pieces=pieces, natural=natural),
        grid=(planes // PLANES,),
        in_specs=[
            SMEM_SPEC,
            pl.BlockSpec((2, PLANES, size_y, size_z), lambda i: (0, i, 0, 0)),
            pl.BlockSpec((PLANES, size_y, size_z), lambda i: (place(i), 0, 0)),
        ]
        + [whole(a.shape) for a in (table_z, table_y, codes, sides, *sources)],
        out_specs=out_specs,
        out_shape=[jax.ShapeDtypeStruct(shape, jnp.bfloat16)] * pieces,
        scratch_shapes=scratch,
        compiler_params=params(1),
        cost_estimate=cost(
            2 * planes * size_y * size_z * (size_y + size_z), 2 * planes * size_y * size_z
        ),
        name="go_back",
    )(slab, wave, potential, table_z, table_y, codes, sides, *sources)


def last_x_kernel(frequency_x, frequency_yz, table, coeffs, *refs):
    bufs, (out, tall) = refs[:-2], refs[-2:]
    parts, size_x, columns, lanes = coeffs.shape
    pitch = columns + 1

    def some_columns(g, carry):
        loaded = []
        for h in range(COLUMNS):
            loaded.append(jnp.concatenate([buf[COLUMNS * g + h] for buf in bufs], axis=0))
        for first in range(0, COLUMNS, FOUR):
            result = jnp.dot(
                table[...],
                jnp.concatenate(loaded[first : first + FOUR], axis=1),
                preferred_element_type=jnp.float32,
            )
            for h in range(FOUR):
                tall[pl.ds(COLUMNS * g + first + h, parts * size_x, stride=pitch), :] = result[
                    :, h * lanes : (h + 1) * lanes
                ]
        return carry

    lax.fori_loop(0, columns // COLUMNS, some_columns, 0)

    def finish(k, carry):
        kinetic = frequency_x[k] + frequency_yz[...]
        for part in range(parts):
            out[part, k] = (
                tall[pl.ds((part * size_x + k) * pitch, columns), :] + kinetic * coeffs[part, k].astype(jnp.float32)
            ).astype(jnp.bfloat16)
        return carry

    lax.fori_loop(0, size_x, finish, 0, unroll=8)


def last_x(frequency_x, frequency_yz, table, coeffs, bufs):
    _, size_x, columns, size_z = coeffs.shape
    lanes = size_z // 2
    spec = pl.BlockSpec((2, size_x, columns, lanes), lambda i: (0, 0, 0, i))
    return pl.pallas_call(
        last_x_kernel,
        grid=(2,),
        in_specs=[
            SMEM_SPEC,
            pl.BlockSpec((columns, lanes), lambda i: (0, i)),
            whole(table.shape),
            spec,
        ]
        + [pl.BlockSpec((*b.shape[:2], lanes), lambda i: (0, 0, i)) for b in bufs],
        out_specs=spec,
        out_shape=jax.ShapeDtypeStruct(coeffs.shape, jnp.bfloat16),
        scratch_shapes=[pltpu.VMEM((2 * size_x * (columns + 1), lanes), jnp.float32)],
        compiler_params=params(1),
        cost_estimate=cost(2 * size_x * size_x * columns * size_z, 3 * size_x * columns * size_z),
        name="last_x",
    )(frequency_x, frequency_yz, table, coeffs, *bufs)


def per_device_chunked(wave_coeffs, occupation, potential, projectors, coupling, sphere_blocks):
    pieces = lax.axis_size("fft")
    bands = lax.axis_size("band")
    slab = lax.axis_index("fft")
    coeffs = wave_coeffs[0]
    _, size_x, columns, size_z = coeffs.shape
    slab_planes, size_y, _ = potential.shape
    atom_dev, nproj, blocks, cells = projectors.shape
    zblocks = size_z // cells
    outer, inner = chunk_planes(slab_planes)
    up = [(i, (i + 1) % pieces) for i in range(pieces)]
    down = [(j, i) for i, j in up]

    order = ring_order(pieces)
    inverse_x, forward_x = (real_blocks(size_x, s) for s in (1.0, -1.0))
    inverse_y, forward_y = (real_blocks(size_y, s) for s in (1.0, -1.0))
    inverse_z, forward_z = (real_blocks(size_z, s) for s in (1.0, -1.0))
    place_outer, place_inner = (
        np.arange(pieces)[:, None] * slab_planes + np.array(chunk)[None, :]
        for chunk in (outer, inner)
    )
    table_x_outer = np.stack([inverse_x[r][place_outer] for r in range(2)], 1)
    table_x_inner = np.stack([inverse_x[r][place_inner] for r in range(2)], 1)
    tables_back_x = [
        np.stack([forward_x[:, :, r][:, :, place] for r in range(2)], 3).reshape(
            2 * size_x, pieces, -1
        )
        for place in (place_outer, place_inner)
    ]
    middle = size_y // 2
    down_y = [inverse_y[:, :middle, :, s::2] for s in (0, 1)]
    back_y = [forward_y[:, s::2, :, :middle] for s in (0, 1)]
    split = (pieces, columns // 2)
    tables = [
        table_x_outer.reshape(-1, 2 * size_x),
        table_x_inner.reshape(-1, 2 * size_x),
        np.stack([t.reshape(size_y, -1) for t in down_y]),
        np.stack(
            [t.reshape(2, middle, 2, *split).swapaxes(2, 3).reshape(size_y, -1) for t in down_y]
        ),
        inverse_z.transpose(2, 3, 0, 1).reshape(2 * size_z, -1),
        forward_z.transpose(2, 3, 0, 1).reshape(2 * size_z, -1),
        np.stack([t.reshape(size_y, -1) for t in back_y]),
        np.stack([t.reshape(2, *split, -1).swapaxes(0, 1).reshape(size_y, -1) for t in back_y]),
        np.stack(
            [
                np.concatenate(
                    [t[:, (d - np.array(order)) % pieces].reshape(2 * size_x, -1) for t in tables_back_x],
                    axis=1,
                )
                for d in range(pieces)
            ]
        ),
    ]
    (
        table_x_outer, table_x_inner, table_y_outer, table_y_inner, table_z,
        table_back_z, table_back_y_outer, table_back_y_inner, tables_back_x,
    ) = (jnp.asarray(t.astype(jnp.bfloat16)) for t in tables)

    table_back_x = lax.dynamic_index_in_dim(tables_back_x, slab, 0, keepdims=False)

    where = slab.reshape(1)
    section_outer = first_x(where, table_x_outer, coeffs, len(outer), pieces, False)
    section_outer, table_x_inner, sphere_blocks = lax.optimization_barrier(
        (section_outer, table_x_inner, sphere_blocks)
    )
    section_inner = first_x(where, table_x_inner, coeffs, len(inner), pieces, False)

    entries = atom_dev * blocks

    def codes_of(chunk, shift):
        owner = (slab + shift + pieces) % pieces
        numbers = lax.dynamic_slice_in_dim(sphere_blocks, owner * atom_dev, atom_dev, 0)
        plane = numbers // (size_y * zblocks) - slab * slab_planes
        rest = numbers % (size_y * zblocks)
        if chunk is outer:
            inside = ((plane >= 0) & (plane < EDGE)) | (
                (plane >= slab_planes - EDGE) & (plane < slab_planes)
            )
            plane = jnp.where(plane < EDGE, plane, plane - len(inner))
        else:
            inside = (plane >= EDGE) & (plane < slab_planes - EDGE)
            plane = plane - EDGE
        code = jnp.where(inside, plane * size_y + rest // zblocks, -1)
        return code.reshape(entries), (rest % zblocks).reshape(entries)

    found = [codes_of(outer, shift) for shift in (0, -1, 1)]
    codes_outer, sides_outer = (jnp.stack(values) for values in zip(*found))
    codes_inner, sides_inner = (values[None] for values in codes_of(inner, 0))

    def on_lanes(values):
        return jnp.broadcast_to(values[:, :, None], (*values.shape, cells))

    sides_outer, sides_inner = on_lanes(sides_outer), on_lanes(sides_inner)
    rows_codes = [on_lanes(codes_outer), on_lanes(codes_inner)]
    lane_codes = [codes_outer[:, None, :], codes_inner[:, None, :]]
    strength = 3.0 * math.sqrt(cells * blocks) / nproj
    coupled = (coupling + coupling.T) * (0.5 * strength)
    coupled = jnp.broadcast_to(coupled.T[:, :, None], (nproj, nproj, cells))
    section_inner, rows_codes, lane_codes, sides_outer, sides_inner, coupled = (
        lax.optimization_barrier(
            (section_inner, rows_codes, lane_codes, sides_outer, sides_inner, coupled)
        )
    )

    half = pieces // 2
    near, far = list(range(1, half)), list(range(half, pieces))

    def send(block, k, *awaited):
        for row, m in awaited:
            block, row[m] = lax.optimization_barrier((block, row[m]))
        return lax.ppermute(block, "fft", [(j, j ^ k) for j in range(pieces)])

    received_outer, received_inner = (
        [section[0]] + [None] * (pieces - 1) for section in (section_outer, section_inner)
    )
    for partners in (near, far):
        queue = [(section_outer, received_outer, k) for k in partners]
        queue += [(section_inner, received_inner, k) for k in partners]
        for place, (section, received, k) in enumerate(queue):
            awaited = [queue[place - 2][1:]] if place >= 2 else []
            received[k] = send(section[k], k, *awaited)
    wave_outer, density_outer, rows_outer, to_previous, to_following = make_field(
        where, occupation, received_outer, table_y_outer, table_z, rows_codes[0],
        sides_outer, len(outer), pieces, False,
    )
    from_following = lax.ppermute(to_previous, "fft", down)
    from_previous = lax.ppermute(to_following, "fft", up)
    density_outer = lax.psum(density_outer, "band")
    wave_inner, density_inner, rows_inner = make_field(
        where, occupation, received_inner, table_y_outer, table_z, rows_codes[1],
        sides_inner, len(inner), pieces, False,
    )
    projected, spread = make_nonlocal(
        coupled, projectors, [rows_outer, rows_inner, from_following, from_previous]
    )
    spread_previous = lax.ppermute(spread, "fft", up)
    spread_following = lax.ppermute(spread, "fft", down)
    edge_steps = EDGE // PLANES
    inner_steps = len(inner) // PLANES
    back_inner = go_back(
        where, wave_inner, potential, table_back_z, table_back_y_outer, lane_codes[1],
        sides_inner, [spread], lambda i: i + edge_steps, pieces, False,
    )
    def permute_all(values):
        received = [values[0]]
        for k, block in zip(order[1:], values[1:]):
            pairs = [(j, (j + k) % pieces) for j in range(pieces)]
            received.append(lax.ppermute(block, "fft", pairs))
        return received

    back_inner = permute_all(back_inner)
    back_outer = go_back(
        where, wave_outer, potential, table_back_z, table_back_y_outer, lane_codes[0],
        sides_outer, [spread, spread_previous, spread_following],
        lambda i: jnp.where(i < edge_steps, i, i + inner_steps), pieces, False,
    )
    density_inner, density_outer = lax.optimization_barrier((density_inner, density_outer))
    density_inner = lax.psum(density_inner, "band")
    back_outer, density_outer = lax.optimization_barrier((back_outer, density_outer))
    back_outer = permute_all(back_outer)
    density = jnp.concatenate([density_outer[:EDGE], density_inner, density_outer[EDGE:]], axis=0)

    index_x = np.arange(size_x)
    frequency_x = jnp.asarray(
        (np.where(2 * index_x < size_x, index_x, index_x - size_x) / size_x) ** 2, jnp.float32
    )
    index_y = slab * columns + jnp.arange(columns, dtype=jnp.int32)
    index_z = jnp.arange(size_z, dtype=jnp.int32)
    frequency_yz = wave_squares(index_y, size_y)[:, None] + wave_squares(index_z, size_z)[None, :]
    coeffs, density, back_inner = lax.optimization_barrier((coeffs, density, back_inner))
    applied = last_x(frequency_x, frequency_yz, table_back_x, coeffs, back_outer + back_inner)
    return (applied[None], density, projected[None, :, :, :, 0])


def per_device(wave_coeffs, occupation, potential, projectors, coupling, sphere_blocks):
    pieces, bands = lax.axis_size("fft"), lax.axis_size("band")
    size_z = wave_coeffs.shape[4]
    columns = wave_coeffs.shape[3]
    slab_planes = potential.shape[0]
    chunked = (
        pieces >= 4
        and pieces & (pieces - 1) == 0
        and slab_planes % EDGE == 0
        and slab_planes >= 3 * EDGE
        and EDGE >= HALO
        and columns % 8 == 0
        and size_z % 256 == 0
        and projectors.shape[0] % bands == 0
        and projectors.shape[3] == 128
        and projectors.shape[1] == 8
    )
    chosen = per_device_chunked if chunked else per_device_plain
    return chosen(wave_coeffs, occupation, potential, projectors, coupling, sphere_blocks)


def solution(mesh):
    placed = (
        P("band", None, None, "fft", None),
        P("band", None),
        P("fft", None, None),
        P("fft", None, None, None),
        P(),
        P(),
    )
    return jax.shard_map(
        per_device,
        mesh=mesh,
        in_specs=placed,
        out_specs=(
            P("band", None, None, "fft", None),
            P("fft", None, None),
            P("band", "fft", None, None),
        ),
        check_vma=False,
    )
```

```python
import functools
import math

import jax
import jax.numpy as jnp
import numpy as np
from jax import lax
from jax.experimental import pallas as pl
from jax.experimental.pallas import tpu as pltpu
from jax.sharding import PartitionSpec as P

HALO = 6
EDGE = 8
PLANES = 4
COLUMNS = 8
FOUR = 4
VMEM_BYTES = 61 * 1024 * 1024


def extended(shard, sides, width):
    for axis, dim in sides:
        count, length = (lax.axis_size(axis), shard.shape[dim])
        up = [(i, (i + 1) % count) for i in range(count)]
        down = [(j, i) for i, j in up]
        last = lax.slice_in_dim(shard, length - width, length, axis=dim)
        first = lax.slice_in_dim(shard, 0, width, axis=dim)
        before = lax.ppermute(last, axis, up)
        after = lax.ppermute(first, axis, down)
        shard = jnp.concatenate([before, shard, after], axis=dim)
    return shard


def dft_table(length, sign_value):
    indices = jnp.arange(length, dtype=jnp.int32)
    phases = indices[:, None] * indices[None, :] % length
    angles = 2.0 * math.pi / length * phases.astype(jnp.float32)
    factor = 1.0 / math.sqrt(length)
    cosine = jnp.cos(angles) * factor
    sine_part = jnp.sin(angles) * (sign_value * factor)
    upper_rows = jnp.stack([cosine, -sine_part])
    bottom = jnp.stack([sine_part, cosine])
    return jnp.stack([upper_rows, bottom]).astype(jnp.bfloat16)


def wave_squares(indices, length):
    frequency = (
        jnp.where(2 * indices < length, indices, indices - length).astype(jnp.float32) / length
    )
    return frequency * frequency


def per_device_plain(wave_coeffs, occupation, potential, projectors, coupling, sphere_blocks):
    pieces = lax.axis_size("fft")
    slab_index = lax.axis_index("fft")
    coeffs = wave_coeffs[0]
    size_x = coeffs.shape[1]
    columns = coeffs.shape[2]
    size_z = coeffs.shape[3]
    slab_planes = potential.shape[0]
    size_y = potential.shape[1]
    atom_dev = projectors.shape[0]
    nproj_count = projectors.shape[1]
    block_cells = projectors.shape[3]
    zblocks = size_z // block_cells
    plane_blocks = size_y * zblocks
    total_atoms = atom_dev * pieces
    table_x = dft_table(size_x, 1.0).transpose(0, 2, 1, 3).reshape(2 * size_x, 2 * size_x)
    inverse_y = dft_table(size_y, 1.0)
    inverse_z = dft_table(size_z, 1.0)
    flattened = coeffs.reshape(2 * size_x, columns * size_z)
    along_x = jnp.dot(table_x, flattened, preferred_element_type=jnp.float32)
    along_x = along_x.reshape(2, size_x, columns, size_z).astype(jnp.bfloat16)
    along_y = jnp.einsum(
        "abyk,bxkz->axyz",
        inverse_y,
        lax.all_to_all(along_x, "fft", split_axis=1, concat_axis=2, tiled=True),
        preferred_element_type=jnp.float32,
    ).astype(jnp.bfloat16)
    wave_field = jnp.einsum(
        "abzk,bxyk->axyz", inverse_z, along_y, preferred_element_type=jnp.float32
    ).astype(jnp.bfloat16)
    weights = occupation[0]
    real_part = wave_field[0].astype(jnp.float32)
    imag_part = wave_field[1].astype(jnp.float32)
    partial_density = weights[0] * real_part * real_part + weights[1] * imag_part * imag_part
    density = lax.psum(partial_density.astype(jnp.bfloat16), "band")
    strength = 3.0 * math.sqrt(block_cells * projectors.shape[2]) / nproj_count
    coupled = (coupling + coupling.T) * (0.5 * strength)
    nearby = extended(projectors, (("fft", 0),), atom_dev)
    atom_rows = (
        slab_index * atom_dev - atom_dev + jnp.arange(3 * atom_dev, dtype=jnp.int32) + total_atoms
    ) % total_atoms
    near_blocks = sphere_blocks[atom_rows]
    plane_index = near_blocks // plane_blocks
    inside = plane_index // slab_planes == slab_index
    local_index = jnp.where(
        inside,
        (plane_index - slab_index * slab_planes) * plane_blocks + near_blocks % plane_blocks,
        0,
    )
    blocks_own = wave_field.reshape(2, slab_planes * plane_blocks, block_cells)
    gathered = blocks_own[:, local_index] * inside[None, :, :, None].astype(jnp.bfloat16)
    partial_value = jnp.einsum(
        "ajsk,bask->abj", nearby, gathered, preferred_element_type=jnp.float32
    )
    summed = extended(partial_value, (("fft", 0),), atom_dev)
    projections_own = (
        summed[:atom_dev] + summed[2 * atom_dev : 3 * atom_dev] + summed[4 * atom_dev :]
    )
    energy_own = jnp.einsum(
        "ij,abj->abi", coupled, projections_own, precision=lax.Precision.HIGHEST
    )
    energy = extended(energy_own, (("fft", 0),), atom_dev)
    spread = jnp.einsum(
        "ajsk,abj->bask", nearby.astype(jnp.float32), energy, precision=lax.Precision.HIGHEST
    )
    spread = spread * inside[None, :, :, None].astype(jnp.float32)
    accumulated = (
        jnp.zeros((2, slab_planes * plane_blocks, block_cells), jnp.float32)
        .at[:, local_index]
        .add(spread)
    )
    nonlocal_term = accumulated.reshape(2, slab_planes, size_y, size_z)
    total_field = (
        potential.astype(jnp.float32)[None] * wave_field.astype(jnp.float32) + nonlocal_term
    ).astype(jnp.bfloat16)
    forward_z = dft_table(size_z, -1.0)
    forward_y = dft_table(size_y, -1.0)
    forward_x = dft_table(size_x, -1.0)
    back_z = jnp.einsum(
        "abzk,bxyk->axyz", forward_z, total_field, preferred_element_type=jnp.float32
    ).astype(jnp.bfloat16)
    back_y = jnp.einsum(
        "abyk,bxkz->axyz", forward_y, back_z, preferred_element_type=jnp.float32
    ).astype(jnp.bfloat16)
    transformed = jnp.einsum(
        "abxk,bkyz->axyz",
        forward_x,
        lax.all_to_all(back_y, "fft", split_axis=2, concat_axis=1, tiled=True),
        preferred_element_type=jnp.float32,
    )
    index_x = jnp.arange(size_x, dtype=jnp.int32)
    index_y = slab_index * columns + jnp.arange(columns, dtype=jnp.int32)
    index_z = jnp.arange(size_z, dtype=jnp.int32)
    kinetic = (
        wave_squares(index_x, size_x)[:, None, None]
        + wave_squares(index_y, size_y)[None, :, None]
        + wave_squares(index_z, size_z)[None, None, :]
    )
    applied = (transformed + kinetic[None] * coeffs.astype(jnp.float32)).astype(jnp.bfloat16)
    return (applied[None], density, projections_own[None])


def real_blocks(length, sign):
    index = np.arange(length)
    angles = 2.0 * np.pi / length * (index[:, None] * index[None, :] % length)
    cosine = np.cos(angles) / np.sqrt(length)
    sine = sign * np.sin(angles) / np.sqrt(length)
    blocks = np.empty((2, length, 2, length))
    blocks[0, :, 0, :] = cosine
    blocks[1, :, 1, :] = cosine
    blocks[0, :, 1, :] = -sine
    blocks[1, :, 0, :] = sine
    return blocks


def chunk_planes(slab_planes):
    low, high = list(range(EDGE)), list(range(slab_planes - EDGE, slab_planes))
    return [low + high, list(range(EDGE, slab_planes - EDGE))]


def params(steps):
    return pltpu.CompilerParams(
        dimension_semantics=("arbitrary",) * steps, vmem_limit_bytes=VMEM_BYTES
    )


def cost(products, values):
    return pl.CostEstimate(flops=4 * products, bytes_accessed=4 * values, transcendentals=0)


def whole(shape):
    return pl.BlockSpec(shape, lambda i: (0,) * len(shape))


SMEM_SPEC = pl.BlockSpec(memory_space=pltpu.SMEM)


def paired(refs, slab):
    return [(lax.bitwise_xor(slab, jnp.int32(k)), ref) for k, ref in enumerate(refs)]


def ring_order(pieces):
    return [0] + sorted(range(1, pieces), key=lambda k: abs(k - pieces // 2))


def shifted(refs, slab):
    order = ring_order(len(refs))
    return [(lax.rem(slab + k, len(refs)), ref) for k, ref in zip(order, refs)]


def first_x_kernel(slab, table_ref, coeffs_ref, *refs, pieces, natural):
    scratch = 3 if natural else 2
    outs = paired(refs[:-scratch], slab[0])
    turned, wide, *tall = refs[-scratch:]
    parts, size_x, columns, lanes = coeffs_ref.shape
    rows = parts * size_x
    height = table_ref.shape[0] // pieces

    for k, (device, _) in enumerate(outs):
        start = pl.multiple_of(device * height, 16)
        turned[k * height : (k + 1) * height, :] = table_ref[pl.ds(start, height), :]

    pitch = columns + 1

    def widen(k, carry):
        for part in range(parts):
            wide[pl.ds((part * size_x + k) * pitch, columns), :] = coeffs_ref[part, k].astype(
                jnp.float32
            )
        return carry

    lax.fori_loop(0, size_x, widen, 0, unroll=8)

    def some_columns(g, carry):
        loaded = [
            wide[pl.ds(COLUMNS * g + h, rows, stride=pitch), :].astype(jnp.bfloat16)
            for h in range(COLUMNS)
        ]
        for first in range(0, COLUMNS, FOUR):
            result = jnp.dot(
                turned[...],
                jnp.concatenate(loaded[first : first + FOUR], axis=1),
                preferred_element_type=jnp.float32,
            )
            for h in range(FOUR):
                column = COLUMNS * g + first + h
                piece = result[:, h * lanes : (h + 1) * lanes]
                if natural:
                    place = (first + h) % 2 * columns + COLUMNS // 2 * g + (first + h) // 2
                    planes = height // 2
                    for k in range(pieces):
                        for part in range(2):
                            start = k * height * columns + part * (columns // 2) + place
                            row = k * height + part * planes
                            tall[0][pl.ds(start, planes, stride=2 * columns), :] = piece[
                                row : row + planes
                            ]
                else:
                    piece = piece.astype(jnp.bfloat16)
                    for k, (_, out) in enumerate(outs):
                        out[column] = piece[k * height : (k + 1) * height]
        return carry

    lax.fori_loop(0, columns // COLUMNS, some_columns, 0)
    if natural:
        for k, (_, out) in enumerate(outs):
            values = tall[0][k * height * columns : (k + 1) * height * columns, :]
            out[...] = values.astype(jnp.bfloat16).reshape(out.shape)


def first_x(slab, table, coeffs, planes, pieces, natural):
    _, size_x, columns, size_z = coeffs.shape
    lanes = size_z // 2
    shape = (planes, 2 * columns) if natural else (columns, 2 * planes)
    scratch = [
        pltpu.VMEM(table.shape, jnp.bfloat16),
        pltpu.VMEM((2 * size_x * (columns + 1), lanes), jnp.float32),
    ]
    if natural:
        scratch.append(pltpu.VMEM((2 * pieces * planes * columns, lanes), jnp.float32))
    out_specs = [pl.BlockSpec((*shape, lanes), lambda i: (0, 0, i))] * pieces
    out_shape = [jax.ShapeDtypeStruct((*shape, size_z), jnp.bfloat16)] * pieces
    return pl.pallas_call(
        functools.partial(first_x_kernel, pieces=pieces, natural=natural),
        grid=(2,),
        in_specs=[
            SMEM_SPEC,
            whole(table.shape),
            pl.BlockSpec((2, size_x, columns, lanes), lambda i: (0, 0, 0, i)),
        ],
        out_specs=out_specs,
        out_shape=out_shape,
        scratch_shapes=scratch,
        compiler_params=params(1),
        cost_estimate=cost(2 * size_x * pieces * planes * columns * size_z, 2 * size_x * columns * size_z),
        name="first_x",
    )(slab, table, coeffs)


def ones_at(codes, count, axis):
    shape = (codes.shape[0], count) if axis == 1 else (count, codes.shape[1])
    places = lax.broadcasted_iota(jnp.int32, shape, axis)
    return jnp.where(codes == places, 1.0, 0.0).astype(jnp.bfloat16)


def field_kernel(slab, weights, table_y, table_z, codes, sides, *refs, pieces, count, natural):
    bufs = paired(refs[:count], slab[0])
    wave, density, *rows_out, gathered, wide = refs[count:]
    _, near, size_y, size_z = wave.shape
    columns = size_y // pieces
    groups, entries, _ = codes.shape
    lanes = 128
    halves = size_z // lanes
    i, last = pl.program_id(0), pl.num_programs(0) - 1
    planes = near * (last + 1)

    @pl.when(i == 0)
    def _():
        gathered[...] = jnp.zeros_like(gathered)

    loaded = []
    if natural:
        for source, buf in bufs:
            wide[source] = buf[...]
        for h in range(near):
            loaded.append(
                [wide[:, h, s * columns : (s + 1) * columns].reshape(size_y, size_z) for s in (0, 1)]
            )
    else:
        rows = bufs[0][1].shape[1]
        pitch = rows + 1

        @pl.when(i == 0)
        def _():
            for source, buf in bufs:

                def widen(column, carry):
                    values = buf[column].astype(jnp.float32)
                    for q in range(halves):
                        wide[q, pl.ds((source * columns + column) * pitch, rows), :] = values[
                            :, q * lanes : (q + 1) * lanes
                        ]
                    return carry

                lax.fori_loop(0, columns, widen, 0, unroll=8)

        def strided(start):
            return jnp.concatenate(
                [
                    wide[q, pl.ds(start, size_y // 2, stride=2 * pitch), :]
                    for q in range(halves)
                ],
                axis=1,
            ).astype(jnp.bfloat16)

        for h in range(near):
            plane = i * near + h
            loaded.append(
                [
                    jnp.concatenate(
                        [strided(s * pitch + part * planes + plane) for part in range(2)], axis=0
                    )
                    for s in (0, 1)
                ]
            )
    even, odd = (
        jnp.dot(
            table_y[s],
            jnp.concatenate([pair[s] for pair in loaded], axis=1),
            preferred_element_type=jnp.float32,
        )
        for s in (0, 1)
    )
    low, high = (even + odd).astype(jnp.bfloat16), (even - odd).astype(jnp.bfloat16)
    middle = size_y // 2
    turned = []
    for h in range(near):
        span = slice(h * size_z, (h + 1) * size_z)
        both = [
            jnp.concatenate(
                [values[part * middle : (part + 1) * middle, span] for values in (low, high)], axis=0
            )
            for part in range(2)
        ]
        turned.append(jnp.concatenate(both, axis=1))
    result = jnp.dot(
        jnp.concatenate(turned, axis=0), table_z[...], preferred_element_type=jnp.float32
    ).astype(jnp.bfloat16)
    for h in range(near):
        total = jnp.zeros((size_y, size_z), jnp.float32)
        for part in range(2):
            values = result[h * size_y : (h + 1) * size_y, part * size_z : (part + 1) * size_z]
            wave[part, h] = values
            values = values.astype(jnp.float32)
            total += weights[0, part] * values * values
        density[h] = total.astype(jnp.bfloat16)

    used = [0] if groups == 1 else [0, 1 + (2 * i > last).astype(jnp.int32)]
    for group in used:
        places = ones_at(codes[group] - i * near * size_y, near * size_y, 1)
        gathered[group] += jnp.dot(places, result, preferred_element_type=jnp.float32)

    @pl.when(i == last)
    def _():
        for group in range(groups):
            for part in range(2):
                total = jnp.zeros((entries, lanes), jnp.float32)
                for q in range(halves):
                    start = part * size_z + q * lanes
                    total += jnp.where(
                        sides[group] == q, gathered[group, :, start : start + lanes], 0.0
                    )
                rows_out[group][part] = total.astype(jnp.bfloat16)


def make_field(slab, weights, bufs, table_y, table_z, codes, sides, planes, pieces, natural):
    size_z = bufs[0].shape[-1]
    size_y = table_y.shape[1]
    columns = size_y // pieces
    groups, entries, _ = codes.shape
    if natural:
        buf_spec = pl.BlockSpec((PLANES, 2 * columns, size_z), lambda i: (i, 0, 0))
        wide = pltpu.VMEM((pieces, PLANES, 2 * columns, size_z), jnp.bfloat16)
    else:
        buf_spec = whole(bufs[0].shape)
        wide = pltpu.VMEM((size_z // 128, (2 * planes + 1) * size_y, 128), jnp.float32)
    return pl.pallas_call(
        functools.partial(field_kernel, pieces=pieces, count=len(bufs), natural=natural),
        grid=(planes // PLANES,),
        in_specs=[SMEM_SPEC, SMEM_SPEC]
        + [whole(a.shape) for a in (table_y, table_z, codes, sides)]
        + [buf_spec] * len(bufs),
        out_specs=[
            pl.BlockSpec((2, PLANES, size_y, size_z), lambda i: (0, i, 0, 0)),
            pl.BlockSpec((PLANES, size_y, size_z), lambda i: (i, 0, 0)),
        ]
        + [whole((2, entries, 128))] * groups,
        out_shape=[
            jax.ShapeDtypeStruct((2, planes, size_y, size_z), jnp.bfloat16),
            jax.ShapeDtypeStruct((planes, size_y, size_z), jnp.bfloat16),
        ]
        + [jax.ShapeDtypeStruct((2, entries, 128), jnp.bfloat16)] * groups,
        scratch_shapes=[pltpu.VMEM((groups, entries, 2 * size_z), jnp.float32), wide],
        compiler_params=params(1),
        cost_estimate=cost(
            2 * planes * size_y * size_z * (size_y + size_z), 2 * planes * size_y * size_z
        ),
        name="make_field",
    )(slab, weights, table_y, table_z, codes, sides, *bufs)


def nonlocal_kernel(coupled, projectors, *refs):
    parts, (projections, spread) = refs[:-2], refs[-2:]
    atoms, nproj, blocks, cells = projectors.shape
    for atom in range(atoms):
        tables = [projectors[atom, j].astype(jnp.float32) for j in range(nproj)]
        place = pl.ds(atom * blocks, blocks)
        for part in range(2):
            rows = sum(p[part, place].astype(jnp.float32) for p in parts)
            tile = jnp.concatenate(
                [jnp.sum(t * rows, axis=0, keepdims=True) for t in tables], axis=0
            )
            mixed = jnp.zeros_like(tile)
            for j in range(nproj):
                mixed += coupled[j] * tile[j : j + 1]
            projections[atom, part] = jnp.broadcast_to(
                jnp.sum(tile, -1, keepdims=True), tile.shape
            )
            energy = jnp.broadcast_to(jnp.sum(mixed, -1, keepdims=True), tile.shape)
            spread[part, place] = sum(
                t * energy[j : j + 1] for j, t in enumerate(tables)
            ).astype(jnp.bfloat16)


def make_nonlocal(coupled, projectors, parts):
    atoms, nproj, _, cells = projectors.shape
    return pl.pallas_call(
        nonlocal_kernel,
        out_shape=[
            jax.ShapeDtypeStruct((atoms, 2, nproj, cells), jnp.float32),
            jax.ShapeDtypeStruct(parts[0].shape, jnp.bfloat16),
        ],
        name="make_nonlocal",
    )(coupled, projectors, *parts)


def back_kernel(slab, wave, potential, table_z, table_y, codes, sides, *refs, pieces, natural):
    groups, _, entries = codes.shape
    sources, outs = refs[:groups], refs[groups:-2]
    spread, tall = refs[-2:]
    outs = shifted(outs, slab[0])
    near, size_y, size_z = potential.shape
    lanes = 128
    halves = size_z // lanes
    i, last = pl.program_id(0), pl.num_programs(0) - 1
    planes = near * (last + 1)

    @pl.when(i == 0)
    def _():
        for group, source in enumerate(sources):
            for part in range(2):
                for q in range(halves):
                    start = part * size_z + q * lanes
                    spread[group, :, start : start + lanes] = jnp.where(
                        sides[group] == q, source[part].astype(jnp.float32), 0.0
                    ).astype(jnp.bfloat16)

    used = [0] if groups == 1 else [0, 1 + (2 * i > last).astype(jnp.int32)]
    extra = jnp.zeros((near * size_y, 2 * size_z), jnp.float32)
    for group in used:
        places = ones_at(codes[group] - i * near * size_y, near * size_y, 0)
        extra += jnp.dot(places, spread[group], preferred_element_type=jnp.float32)
    fields = []
    for h in range(near):
        local = potential[h].astype(jnp.float32)
        both = [
            local * wave[part, h].astype(jnp.float32)
            + extra[h * size_y : (h + 1) * size_y, part * size_z : (part + 1) * size_z]
            for part in range(2)
        ]
        fields.append(jnp.concatenate(both, axis=1).astype(jnp.bfloat16))
    back_z = jnp.dot(
        jnp.concatenate(fields, axis=0), table_z[...], preferred_element_type=jnp.float32
    )
    middle = size_y // 2
    folded = [[], []]
    for h in range(near):
        low = back_z[h * size_y : h * size_y + middle]
        high = back_z[h * size_y + middle : (h + 1) * size_y]
        for kept, values in zip(folded, (low + high, low - high)):
            values = values.astype(jnp.bfloat16)
            kept.append(jnp.concatenate([values[:, :size_z], values[:, size_z:]], axis=0))
    columns = size_y // pieces
    for s, kept in enumerate(folded):
        back_y = jnp.dot(
            table_y[s], jnp.concatenate(kept, axis=1), preferred_element_type=jnp.float32
        )
        if natural:
            back_y = back_y.astype(jnp.bfloat16)
            for h in range(near):
                tall[:, h, s * columns : (s + 1) * columns] = back_y[
                    :, h * size_z : (h + 1) * size_z
                ].reshape(pieces, columns, size_z)
            continue
        pitch = outs[0][1].shape[1] + 1
        for h in range(near):
            for part in range(2):
                for q in range(halves):
                    start = s * pitch + part * planes + i * near + h
                    lane = h * size_z + q * lanes
                    tall[q, pl.ds(start, middle, stride=2 * pitch), :] = back_y[
                        part * middle : (part + 1) * middle, lane : lane + lanes
                    ]

    if natural:
        for target, out in outs:
            out[...] = tall[target]
        return
    rows = outs[0][1].shape[1]

    @pl.when(i == last)
    def _():
        for target, out in outs:

            def narrow(column, carry):
                start = (target * columns + column) * pitch
                values = [tall[q, pl.ds(start, rows), :] for q in range(halves)]
                out[column] = jnp.concatenate(values, axis=1).astype(jnp.bfloat16)
                return carry

            lax.fori_loop(0, columns, narrow, 0, unroll=8)


def go_back(slab, wave, potential, table_z, table_y, codes, sides, sources, place, pieces, natural):
    _, planes, size_y, size_z = wave.shape
    columns = size_y // pieces
    groups, _, entries = codes.shape
    scratch = [pltpu.VMEM((groups, entries, 2 * size_z), jnp.bfloat16)]
    if natural:
        shape = (planes, 2 * columns, size_z)
        out_specs = [pl.BlockSpec((PLANES, 2 * columns, size_z), lambda i: (i, 0, 0))] * pieces
        scratch.append(pltpu.VMEM((pieces, PLANES, 2 * columns, size_z), jnp.bfloat16))
    else:
        shape = (columns, 2 * planes, size_z)
        out_specs = [whole(shape)] * pieces
        scratch.append(pltpu.VMEM((size_z // 128, (2 * planes + 1) * size_y, 128), jnp.float32))
    return pl.pallas_call(
        functools.partial(back_kernel, pieces=pieces, natural=natural),
        grid=(planes // PLANES,),
        in_specs=[
            SMEM_SPEC,
            pl.BlockSpec((2, PLANES, size_y, size_z), lambda i: (0, i, 0, 0)),
            pl.BlockSpec((PLANES, size_y, size_z), lambda i: (place(i), 0, 0)),
        ]
        + [whole(a.shape) for a in (table_z, table_y, codes, sides, *sources)],
        out_specs=out_specs,
        out_shape=[jax.ShapeDtypeStruct(shape, jnp.bfloat16)] * pieces,
        scratch_shapes=scratch,
        compiler_params=params(1),
        cost_estimate=cost(
            2 * planes * size_y * size_z * (size_y + size_z), 2 * planes * size_y * size_z
        ),
        name="go_back",
    )(slab, wave, potential, table_z, table_y, codes, sides, *sources)


def last_x_kernel(frequency_x, frequency_yz, table, coeffs, *refs):
    bufs, (out, tall) = refs[:-2], refs[-2:]
    parts, size_x, columns, lanes = coeffs.shape
    pitch = columns + 1

    def some_columns(g, carry):
        loaded = []
        for h in range(COLUMNS):
            loaded.append(jnp.concatenate([buf[COLUMNS * g + h] for buf in bufs], axis=0))
        for first in range(0, COLUMNS, FOUR):
            result = jnp.dot(
                table[...],
                jnp.concatenate(loaded[first : first + FOUR], axis=1),
                preferred_element_type=jnp.float32,
            )
            for h in range(FOUR):
                tall[pl.ds(COLUMNS * g + first + h, parts * size_x, stride=pitch), :] = result[
                    :, h * lanes : (h + 1) * lanes
                ]
        return carry

    lax.fori_loop(0, columns // COLUMNS, some_columns, 0)

    def finish(k, carry):
        kinetic = frequency_x[k] + frequency_yz[...]
        for part in range(parts):
            out[part, k] = (
                tall[pl.ds((part * size_x + k) * pitch, columns), :] + kinetic * coeffs[part, k].astype(jnp.float32)
            ).astype(jnp.bfloat16)
        return carry

    lax.fori_loop(0, size_x, finish, 0, unroll=8)


def last_x(frequency_x, frequency_yz, table, coeffs, bufs):
    _, size_x, columns, size_z = coeffs.shape
    lanes = size_z // 2
    spec = pl.BlockSpec((2, size_x, columns, lanes), lambda i: (0, 0, 0, i))
    return pl.pallas_call(
        last_x_kernel,
        grid=(2,),
        in_specs=[
            SMEM_SPEC,
            pl.BlockSpec((columns, lanes), lambda i: (0, i)),
            whole(table.shape),
            spec,
        ]
        + [pl.BlockSpec((*b.shape[:2], lanes), lambda i: (0, 0, i)) for b in bufs],
        out_specs=spec,
        out_shape=jax.ShapeDtypeStruct(coeffs.shape, jnp.bfloat16),
        scratch_shapes=[pltpu.VMEM((2 * size_x * (columns + 1), lanes), jnp.float32)],
        compiler_params=params(1),
        cost_estimate=cost(2 * size_x * size_x * columns * size_z, 3 * size_x * columns * size_z),
        name="last_x",
    )(frequency_x, frequency_yz, table, coeffs, *bufs)


def per_device_chunked(wave_coeffs, occupation, potential, projectors, coupling, sphere_blocks):
    pieces = lax.axis_size("fft")
    bands = lax.axis_size("band")
    slab = lax.axis_index("fft")
    coeffs = wave_coeffs[0]
    _, size_x, columns, size_z = coeffs.shape
    slab_planes, size_y, _ = potential.shape
    atom_dev, nproj, blocks, cells = projectors.shape
    zblocks = size_z // cells
    outer, inner = chunk_planes(slab_planes)
    up = [(i, (i + 1) % pieces) for i in range(pieces)]
    down = [(j, i) for i, j in up]

    order = ring_order(pieces)
    inverse_x, forward_x = (real_blocks(size_x, s) for s in (1.0, -1.0))
    inverse_y, forward_y = (real_blocks(size_y, s) for s in (1.0, -1.0))
    inverse_z, forward_z = (real_blocks(size_z, s) for s in (1.0, -1.0))
    place_outer, place_inner = (
        np.arange(pieces)[:, None] * slab_planes + np.array(chunk)[None, :]
        for chunk in (outer, inner)
    )
    table_x_outer = np.stack([inverse_x[r][place_outer] for r in range(2)], 1)
    table_x_inner = np.stack([inverse_x[r][place_inner] for r in range(2)], 1)
    tables_back_x = [
        np.stack([forward_x[:, :, r][:, :, place] for r in range(2)], 3).reshape(
            2 * size_x, pieces, -1
        )
        for place in (place_outer, place_inner)
    ]
    middle = size_y // 2
    down_y = [inverse_y[:, :middle, :, s::2] for s in (0, 1)]
    back_y = [forward_y[:, s::2, :, :middle] for s in (0, 1)]
    split = (pieces, columns // 2)
    tables = [
        table_x_outer.reshape(-1, 2 * size_x),
        table_x_inner.reshape(-1, 2 * size_x),
        np.stack([t.reshape(size_y, -1) for t in down_y]),
        np.stack(
            [t.reshape(2, middle, 2, *split).swapaxes(2, 3).reshape(size_y, -1) for t in down_y]
        ),
        inverse_z.transpose(2, 3, 0, 1).reshape(2 * size_z, -1),
        forward_z.transpose(2, 3, 0, 1).reshape(2 * size_z, -1),
        np.stack([t.reshape(size_y, -1) for t in back_y]),
        np.stack([t.reshape(2, *split, -1).swapaxes(0, 1).reshape(size_y, -1) for t in back_y]),
        np.stack(
            [
                np.concatenate(
                    [t[:, (d - np.array(order)) % pieces].reshape(2 * size_x, -1) for t in tables_back_x],
                    axis=1,
                )
                for d in range(pieces)
            ]
        ),
    ]
    (
        table_x_outer, table_x_inner, table_y_outer, table_y_inner, table_z,
        table_back_z, table_back_y_outer, table_back_y_inner, tables_back_x,
    ) = (jnp.asarray(t.astype(jnp.bfloat16)) for t in tables)

    table_back_x = lax.dynamic_index_in_dim(tables_back_x, slab, 0, keepdims=False)

    where = slab.reshape(1)
    section_outer = first_x(where, table_x_outer, coeffs, len(outer), pieces, False)
    section_outer, table_x_inner, sphere_blocks = lax.optimization_barrier(
        (section_outer, table_x_inner, sphere_blocks)
    )
    section_inner = first_x(where, table_x_inner, coeffs, len(inner), pieces, False)

    entries = atom_dev * blocks

    def codes_of(chunk, shift):
        owner = (slab + shift + pieces) % pieces
        numbers = lax.dynamic_slice_in_dim(sphere_blocks, owner * atom_dev, atom_dev, 0)
        plane = numbers // (size_y * zblocks) - slab * slab_planes
        rest = numbers % (size_y * zblocks)
        if chunk is outer:
            inside = ((plane >= 0) & (plane < EDGE)) | (
                (plane >= slab_planes - EDGE) & (plane < slab_planes)
            )
            plane = jnp.where(plane < EDGE, plane, plane - len(inner))
        else:
            inside = (plane >= EDGE) & (plane < slab_planes - EDGE)
            plane = plane - EDGE
        code = jnp.where(inside, plane * size_y + rest // zblocks, -1)
        return code.reshape(entries), (rest % zblocks).reshape(entries)

    found = [codes_of(outer, shift) for shift in (0, -1, 1)]
    codes_outer, sides_outer = (jnp.stack(values) for values in zip(*found))
    codes_inner, sides_inner = (values[None] for values in codes_of(inner, 0))
    sides_outer, sides_inner = sides_outer[:, :, None], sides_inner[:, :, None]
    rows_codes = [codes_outer[:, :, None], codes_inner[:, :, None]]
    lane_codes = [codes_outer[:, None, :], codes_inner[:, None, :]]
    strength = 3.0 * math.sqrt(cells * blocks) / nproj
    coupled = (coupling + coupling.T) * (0.5 * strength)
    coupled = jnp.broadcast_to(coupled.T[:, :, None], (nproj, nproj, cells))
    section_inner, rows_codes, lane_codes, sides_outer, sides_inner, coupled = (
        lax.optimization_barrier(
            (section_inner, rows_codes, lane_codes, sides_outer, sides_inner, coupled)
        )
    )

    half = pieces // 2
    near, far = list(range(1, half)), list(range(half, pieces))

    def send(block, k, *awaited):
        for row, m in awaited:
            block, row[m] = lax.optimization_barrier((block, row[m]))
        return lax.ppermute(block, "fft", [(j, j ^ k) for j in range(pieces)])

    received_outer, received_inner = (
        [section[0]] + [None] * (pieces - 1) for section in (section_outer, section_inner)
    )
    for partners in (near, far):
        queue = [(section_outer, received_outer, k) for k in partners]
        queue += [(section_inner, received_inner, k) for k in partners]
        for place, (section, received, k) in enumerate(queue):
            awaited = [queue[place - 2][1:]] if place >= 2 else []
            received[k] = send(section[k], k, *awaited)
    wave_outer, density_outer, rows_outer, to_previous, to_following = make_field(
        where, occupation, received_outer, table_y_outer, table_z, rows_codes[0],
        sides_outer, len(outer), pieces, False,
    )
    from_following = lax.ppermute(to_previous, "fft", down)
    from_previous = lax.ppermute(to_following, "fft", up)
    density_outer = lax.psum(density_outer, "band")
    wave_inner, density_inner, rows_inner = make_field(
        where, occupation, received_inner, table_y_outer, table_z, rows_codes[1],
        sides_inner, len(inner), pieces, False,
    )
    projected, spread = make_nonlocal(
        coupled, projectors, [rows_outer, rows_inner, from_following, from_previous]
    )
    spread_previous = lax.ppermute(spread, "fft", up)
    spread_following = lax.ppermute(spread, "fft", down)
    edge_steps = EDGE // PLANES
    inner_steps = len(inner) // PLANES
    back_inner = go_back(
        where, wave_inner, potential, table_back_z, table_back_y_outer, lane_codes[1],
        sides_inner, [spread], lambda i: i + edge_steps, pieces, False,
    )
    def permute_all(values):
        received = [values[0]]
        for k, block in zip(order[1:], values[1:]):
            pairs = [(j, (j + k) % pieces) for j in range(pieces)]
            received.append(lax.ppermute(block, "fft", pairs))
        return received

    back_inner = permute_all(back_inner)
    back_outer = go_back(
        where, wave_outer, potential, table_back_z, table_back_y_outer, lane_codes[0],
        sides_outer, [spread, spread_previous, spread_following],
        lambda i: jnp.where(i < edge_steps, i, i + inner_steps), pieces, False,
    )
    density_inner, density_outer = lax.optimization_barrier((density_inner, density_outer))
    density_inner = lax.psum(density_inner, "band")
    back_outer, density_outer = lax.optimization_barrier((back_outer, density_outer))
    back_outer = permute_all(back_outer)
    density = jnp.concatenate([density_outer[:EDGE], density_inner, density_outer[EDGE:]], axis=0)

    index_x = np.arange(size_x)
    frequency_x = jnp.asarray(
        (np.where(2 * index_x < size_x, index_x, index_x - size_x) / size_x) ** 2, jnp.float32
    )
    index_y = slab * columns + jnp.arange(columns, dtype=jnp.int32)
    index_z = jnp.arange(size_z, dtype=jnp.int32)
    frequency_yz = wave_squares(index_y, size_y)[:, None] + wave_squares(index_z, size_z)[None, :]
    coeffs, density, back_inner = lax.optimization_barrier((coeffs, density, back_inner))
    applied = last_x(frequency_x, frequency_yz, table_back_x, coeffs, back_outer + back_inner)
    return (applied[None], density, projected[None, :, :, :, 0])


def per_device(wave_coeffs, occupation, potential, projectors, coupling, sphere_blocks):
    pieces, bands = lax.axis_size("fft"), lax.axis_size("band")
    size_z = wave_coeffs.shape[4]
    columns = wave_coeffs.shape[3]
    slab_planes = potential.shape[0]
    chunked = (
        pieces >= 4
        and pieces & (pieces - 1) == 0
        and slab_planes % EDGE == 0
        and slab_planes >= 3 * EDGE
        and EDGE >= HALO
        and columns % 8 == 0
        and size_z % 256 == 0
        and projectors.shape[0] % bands == 0
        and projectors.shape[3] == 128
        and projectors.shape[1] == 8
    )
    chosen = per_device_chunked if chunked else per_device_plain
    return chosen(wave_coeffs, occupation, potential, projectors, coupling, sphere_blocks)


def solution(mesh):
    placed = (
        P("band", None, None, "fft", None),
        P("band", None),
        P("fft", None, None),
        P("fft", None, None, None),
        P(),
        P(),
    )
    return jax.shard_map(
        per_device,
        mesh=mesh,
        in_specs=placed,
        out_specs=(
            P("band", None, None, "fft", None),
            P("fft", None, None),
            P("band", "fft", None, None),
        ),
        check_vma=False,
    )
```
